128 devices in a mesh: sp: 4 (over z), ctx: 8 (over x_hi, y), wa: 4 (over x_lo, core).
Axes of the slice: x: 4 (x_hi: 2, x_lo: 2; x = x_hi * 2 + x_lo), y: 4, z: 4, core: 2. Of those that a mesh axis runs over, the one named last changes fastest.
Arguments:
- tokens: bfloat16 [4096, 2048], P(('sp', 'ctx')), may hold values from -6 to 6
- cotangent: bfloat16 [4096, 2048], P(('sp', 'ctx')), may hold values from -6 to 6
- routes: int32 [4096, 6], P(('sp', 'ctx')), may hold values from 0 to 63, all different within a row; in each aligned block of 128 rows (0 to 127, 128 to 255, ...) at most 16 rows name the same one
- attn_gain: bfloat16 [2048], P(('sp', 'ctx')), may hold values from 0.5 to 1.5
- query_weight: bfloat16 [2048, 2048], P(('sp', 'ctx'), 'wa'), may hold values from -0.125 to 0.125
- key_weight: bfloat16 [2048, 2048], P(('sp', 'ctx'), 'wa'), may hold values from -0.125 to 0.125
- value_weight: bfloat16 [2048, 2048], P(('sp', 'ctx'), 'wa'), may hold values from -0.125 to 0.125
- output_weight: bfloat16 [2048, 2048], P('wa', ('sp', 'ctx')), may hold values from -2 to 2
- mlp_gain: bfloat16 [2048], P(('sp', 'ctx')), may hold values from 0.5 to 1.5
- router_weight: bfloat16 [2048, 64], P(('sp', 'ctx')), may hold values from -0.0625 to 0.0625
- shared_gate: bfloat16 [2048, 2816], P(('sp', 'ctx'), 'wa'), may hold values from -0.125 to 0.125
- shared_up: bfloat16 [2048, 2816], P(('sp', 'ctx'), 'wa'), may hold values from -0.125 to 0.125
- shared_down: bfloat16 [2816, 2048], P('wa', ('sp', 'ctx')), may hold values from -0.21875 to 0.21875
- expert_gate: bfloat16 [64, 2048, 1408], P(('sp', 'ctx'), None, 'wa'), may hold values from -0.125 to 0.125
- expert_up: bfloat16 [64, 2048, 1408], P(('sp', 'ctx'), None, 'wa'), may hold values from -0.125 to 0.125
- expert_down: bfloat16 [64, 1408, 2048], P(('sp', 'ctx'), 'wa'), may hold values from -6 to 6
Outputs:
- block_out: bfloat16 [4096, 2048], P(('sp', 'ctx'))
- tokens_grad: bfloat16 [4096, 2048], P(('sp', 'ctx'))
- attn_gain_grad: float32 [2048], P(('sp', 'ctx'))
- query_weight_grad: float32 [2048, 2048], P(('sp', 'ctx'), 'wa')
- key_weight_grad: float32 [2048, 2048], P(('sp', 'ctx'), 'wa')
- value_weight_grad: float32 [2048, 2048], P(('sp', 'ctx'), 'wa')
- output_weight_grad: float32 [2048, 2048], P('wa', ('sp', 'ctx'))
- mlp_gain_grad: float32 [2048], P(('sp', 'ctx'))
- router_weight_grad: float32 [2048, 64], P(('sp', 'ctx'))
- shared_gate_grad: float32 [2048, 2816], P(('sp', 'ctx'), 'wa')
- shared_up_grad: float32 [2048, 2816], P(('sp', 'ctx'), 'wa')
- shared_down_grad: float32 [2816, 2048], P('wa', ('sp', 'ctx'))
- expert_gate_grad: float32 [64, 2048, 1408], P(('sp', 'ctx'), None, 'wa')
- expert_up_grad: float32 [64, 2048, 1408], P(('sp', 'ctx'), None, 'wa')
- expert_down_grad: float32 [64, 1408, 2048], P(('sp', 'ctx'), 'wa')
The draws below stay inside these ranges and needn't reach their ends.
Inputs may be any that keep to these rules, and one draw needn't show every extreme that they name: `routes`: each row names 6 different experts and every expert is named by some row. In each aligned block of 128 rows no expert is named more than 16 times, a bound that some block reaches.
All inputs are finite; a program needn't handle non-finite values.
Results may differ from the reference program's by a relative error of at most 0.035.
Values may be sent and summed in bfloat16 or wider, within the bound.
A program may use at most 256 MiB of HBM per device.

```python
import math
import jax
import jax.numpy as jnp
import numpy as np
from jax import lax

D = 2048
H = 16
HD = 128
F = 1408
TOP = 6
TOK_DEV = 128
FS = 2816
E = 64
SEQ = 4096
CAP = 16


def steps_of(stream_key, dims, pieces, smallest, high):
    level, own = 1.0, jax.random.fold_in(stream_key, 6)
    for axis_at, shards_of in pieces:
        draws = jnp.exp(jax.random.uniform(jax.random.fold_in(own, axis_at), (shards_of,), jnp.float32, smallest / len(pieces), high / len(pieces)))
        level = level * jnp.repeat(draws, dims[axis_at] // shards_of).reshape([-1 if axis == axis_at else 1 for axis in range(len(dims))])
    return level


def assign_block(own_key, own, number, rows, count, top, bound, skew):
    ranking = jax.random.permutation(own_key, count)
    heavy_load, usual = portions_of(count, rows * top, bound, skew, True), portions_of(count, rows * top, bound, skew, False)
    places = jnp.arange(count)

    def named(tallies, offset_by):
        used = int((tallies > 0).sum())
        fixed = max(1, used // 4)
        passed = fixed + (places - fixed + offset_by * (used - fixed)) % max(1, count - fixed)
        return jnp.zeros((count,), jnp.int32).at[ranking[jnp.where(places < fixed, places, passed)]].set(jnp.asarray(tallies, jnp.int32))

    tallies = jnp.where(number % 4 == 0, named(heavy_load, number // 4), named(usual, number - number // 4 - 1))
    mixed = jax.random.permutation(jax.random.fold_in(own, 3), count)
    donor, receiver = mixed[0:count // 2 * 2:2], mixed[1:count // 2 * 2:2]
    slack = jnp.minimum(tallies[donor] - 1, bound - tallies[receiver]) // 2
    slack = jnp.where((donor == ranking[0]) | (receiver == ranking[0]) | (tallies[receiver] == 0), 0, jnp.maximum(slack, 0))
    passed = jax.random.randint(jax.random.fold_in(own, 4), (count // 2,), 0, 1 << 20) % (slack + 1)
    tallies = tallies.at[donor].add(-passed).at[receiver].add(passed)
    members = jnp.searchsorted(jnp.cumsum(tallies), jnp.arange(rows * top), side="right").astype(jnp.int32)
    grid = members.reshape(top, rows).T
    grid = grid[jax.random.permutation(jax.random.fold_in(own, 1), rows)]
    offset_by = jax.random.randint(jax.random.fold_in(own, 2), (rows, 1), 0, top)
    return jnp.take_along_axis(grid, (jnp.arange(top)[None, :] + offset_by) % top, axis=1)


def portions_of(amount, total, bound, lean, full):
    loads = [(1 << 20) // math.isqrt(standing ** lean) + 1 for standing in range(1, amount + 1)]
    largest = bound if full else min(bound, max(-(-total // amount), total * loads[0] // sum(loads)))
    least = 1 if total - largest >= amount - 1 else 0
    counts, rest = [largest] + [least] * (amount - 1), total - largest - least * (amount - 1)
    while rest > 0:
        movable = [i for i in range(1, amount) if counts[i] < largest] or [i for i in range(1, amount) if counts[i] < bound]
        mass, remaining = sum([loads[i] for i in movable]), rest
        for i in movable:
            addition = min(bound - counts[i], max(1, remaining * loads[i] // mass), rest)
            counts[i] = counts[i] + addition
            rest = rest - addition
    return np.array(counts)


def centred(rng, dims, width, bound, cuts=(), held_as=jnp.bfloat16):
    loudness = steps_of(rng, dims, cuts, -0.22, 0.18) if cuts else 1.0
    values = jax.random.normal(rng, dims, jnp.float32) * width * loudness
    return jnp.minimum(jnp.maximum(values, -bound), bound).astype(held_as)


def setup_inputs(seed: int = 0) -> dict:
    arg_keys = jax.random.split(jax.random.key(seed), 17)
    tokens = centred(arg_keys[0], (SEQ, D), 1.0, 6.0, ((0, 32),))
    cotangent = centred(arg_keys[1], (SEQ, D), 1.0, 6.0, ((0, 32),))
    routes_keys = jax.random.split(jax.random.fold_in(arg_keys[2], 1), SEQ // TOK_DEV)
    routes_turns = jax.random.permutation(jax.random.fold_in(arg_keys[2], 3), SEQ // TOK_DEV)
    routes = jax.vmap(lambda own, number: assign_block(jax.random.fold_in(arg_keys[2], 2), own, number, TOK_DEV, E, TOP, CAP, 1))(routes_keys, routes_turns).reshape((SEQ, TOP))
    attn_gain = jnp.clip(1.0 + 0.1 * jax.random.normal(arg_keys[3], (D,), jnp.float32), 0.5, 1.5).astype(jnp.bfloat16)
    query_weight = centred(arg_keys[4], (D, H * HD), D ** -0.5, 0.125, ((0, 32), (1, 4)))
    key_weight = centred(arg_keys[5], (D, H * HD), D ** -0.5, 0.125, ((0, 32), (1, 4)))
    value_weight = centred(arg_keys[6], (D, H * HD), D ** -0.5, 0.125, ((0, 32), (1, 4)))
    output_weight = centred(arg_keys[7], (H * HD, D), (max(1, H * HD // 256)) ** -0.5, 2.0, ((0, 4), (1, 32)))
    mlp_gain = jnp.clip(1.0 + 0.1 * jax.random.normal(arg_keys[8], (D,), jnp.float32), 0.5, 1.5).astype(jnp.bfloat16)
    router_weight = centred(arg_keys[9], (D, E), (4 * D) ** -0.5, 0.0625, ((0, 32),))
    shared_gate = centred(arg_keys[10], (D, FS), D ** -0.5, 0.125, ((0, 32), (1, 4)))
    shared_up = centred(arg_keys[11], (D, FS), D ** -0.5, 0.125, ((0, 32), (1, 4)))
    shared_down = centred(arg_keys[12], (FS, D), (FS // 4) ** -0.5, 0.21875, ((0, 4), (1, 32)))
    expert_gate = centred(arg_keys[13], (E, D, F), D ** -0.5, 0.125, ((0, 32), (2, 4)))
    expert_up = centred(arg_keys[14], (E, D, F), D ** -0.5, 0.125, ((0, 32), (2, 4)))
    expert_down = centred(arg_keys[15], (E, F, D), (max(1, 4096 // (E * E))) ** -0.5, 6.0, ((0, 32), (1, 4)))
    return dict(tokens=tokens, cotangent=cotangent, routes=routes, attn_gain=attn_gain, query_weight=query_weight, key_weight=key_weight, value_weight=value_weight, output_weight=output_weight, mlp_gain=mlp_gain, router_weight=router_weight, shared_gate=shared_gate, shared_up=shared_up, shared_down=shared_down, expert_gate=expert_gate, expert_up=expert_up, expert_down=expert_down)


EPSILON = 1e-06
ROPE_BASE = 10000.0
MASKED = -1e+30
PRECISE = lax.Precision.HIGHEST

@jax.custom_vjp
def low(v):
    return lax.optimization_barrier(v.astype(jnp.bfloat16)).astype(jnp.float32)

@jax.custom_vjp
def low_back(v):
    return v

def low_keep(v):
    return (low(v), None)

def low_pass(kept, grad):
    return (grad,)

def back_keep(v):
    return (v, None)

def back_low(kept, grad):
    return (low(grad),)
low.defvjp(low_keep, low_pass)
low_back.defvjp(back_keep, back_low)

def matmul(left, right):
    return jnp.dot(left, right, precision=PRECISE)

def swish_act(values):
    return values * jax.nn.sigmoid(values)

def softmax_rows(logits):
    row_max = lax.optimization_barrier(jnp.max(logits, axis=-1, keepdims=True))
    weights = jnp.exp(logits - row_max)
    return weights / lax.optimization_barrier(jnp.sum(weights, axis=-1, keepdims=True))

def rms_normed(values, gain):
    return values * lax.rsqrt(lax.optimization_barrier(jnp.mean(values * values, axis=-1, keepdims=True)) + EPSILON) * gain

def rotate(values, positions):
    half_width = HD // 2
    inverse = 1.0 / ROPE_BASE ** (jnp.arange(half_width, dtype=jnp.float32) * 2.0 / HD)
    angles = positions[:, None] * inverse[None, :]
    cosine = jnp.cos(angles)[:, None, :]
    sine_part = jnp.sin(angles)[:, None, :]
    leading = values[..., :half_width]
    trailing = values[..., half_width:]
    return jnp.concatenate([leading * cosine - trailing * sine_part, trailing * cosine + leading * sine_part], axis=-1)

def slot_tables(routes):
    block_count = SEQ // TOK_DEV
    chosen = (routes[:, :, None] == jnp.arange(E, dtype=jnp.int32)[None, None, :]).astype(jnp.int32)
    running = jnp.cumsum(chosen.reshape(block_count, TOK_DEV * TOP, E), axis=1).reshape(SEQ, TOP, E)
    slot_index = lax.optimization_barrier(jnp.sum((running - 1) * chosen, axis=-1))
    block_index = (jnp.arange(SEQ, dtype=jnp.int32) // TOK_DEV)[:, None]
    destination = ((routes * block_count + block_index) * CAP + slot_index).astype(jnp.int32)
    token_ids = jnp.broadcast_to(jnp.arange(SEQ, dtype=jnp.int32)[:, None], (SEQ, TOP))
    owner_token = jnp.zeros((E * block_count * CAP,), jnp.int32).at[destination.reshape(-1)].set(token_ids.reshape(-1))
    filled = jnp.zeros((E * block_count * CAP,), jnp.float32).at[destination.reshape(-1)].set(1.0)
    return (destination, owner_token.reshape(E, block_count * CAP), filled.reshape(E, block_count * CAP))

def forward(tokens, attn_gain, query_weight, key_weight, value_weight, output_weight, mlp_gain, router_weight, shared_gate, shared_up, shared_down, expert_gate, expert_up, expert_down, routes):
    score_scale = HD ** (-0.5)
    positions = jnp.arange(SEQ, dtype=jnp.int32).astype(jnp.float32)
    normed = low(rms_normed(tokens, attn_gain))
    queries = low_back(low(rotate(low_back(matmul(normed, query_weight)).reshape(SEQ, H, HD), positions)))
    keys = low_back(low(rotate(low_back(matmul(normed, key_weight)).reshape(SEQ, H, HD), positions)))
    values = low_back(low(matmul(normed, value_weight))).reshape(SEQ, H, HD)
    block_rows = min(512, SEQ)
    key_index = jnp.arange(SEQ, dtype=jnp.int32)

    def attend(query_block, block_start):
        scores = low_back(jnp.einsum('qhd,khd->hqk', query_block, keys, precision=PRECISE) * score_scale)
        query_pos = block_start + jnp.arange(block_rows, dtype=jnp.int32)
        visible = key_index[None, :] <= query_pos[:, None]
        scores = jnp.where(visible[None], scores, MASKED)
        attn_probs = low(softmax_rows(scores))
        return jnp.einsum('hqk,khd->qhd', attn_probs, values, precision=PRECISE)
    checked = jax.checkpoint(attend)
    query_blocks = queries.reshape(SEQ // block_rows, block_rows, H, HD)
    block_starts = jnp.arange(SEQ // block_rows, dtype=jnp.int32) * block_rows
    attended = lax.map(lambda packed: checked(packed[0], packed[1]), (query_blocks, block_starts))
    attended = low_back(low(attended.reshape(SEQ, H * HD)))
    hidden_state = tokens + low_back(matmul(attended, output_weight))
    mlp_in = low(rms_normed(hidden_state, mlp_gain))
    router_probs = softmax_rows(matmul(mlp_in, router_weight))
    chosen = (routes[:, :, None] == jnp.arange(E, dtype=jnp.int32)[None, None, :]).astype(jnp.float32)
    gate_values = lax.optimization_barrier(jnp.sum(chosen * router_probs[:, None, :], axis=-1))
    shared_pre = low_back(matmul(mlp_in, shared_gate))
    shared_lin = low_back(matmul(mlp_in, shared_up))
    shared_act = low(swish_act(shared_pre) * shared_lin)
    shared_out = low_back(matmul(shared_act, shared_down))
    destination, owner_token, filled = slot_tables(routes)

    def expert_apply(packed):
        gate_matrix, up_matrix, down_matrix, owner_rows, filled_rows = packed
        inputs = low_back(mlp_in[owner_rows] * filled_rows[:, None])
        expert_pre = low_back(matmul(inputs, gate_matrix))
        expert_lin = low_back(matmul(inputs, up_matrix))
        activation = low(swish_act(expert_pre) * expert_lin)
        return low_back(low(matmul(activation, down_matrix)))
    expert_rows = lax.map(jax.checkpoint(expert_apply), (expert_gate, expert_up, expert_down, owner_token, filled))
    picked = expert_rows.reshape(-1, D)[destination]
    routed = lax.optimization_barrier(jnp.sum(gate_values[:, :, None] * picked, axis=1))
    return hidden_state + (routed + shared_out)

def reference(tokens, cotangent, routes, attn_gain, query_weight, key_weight, value_weight, output_weight, mlp_gain, router_weight, shared_gate, shared_up, shared_down, expert_gate, expert_up, expert_down):
    floats = tuple((array_in.astype(jnp.float32) for array_in in (tokens, attn_gain, query_weight, key_weight, value_weight, output_weight, mlp_gain, router_weight, shared_gate, shared_up, shared_down, expert_gate, expert_up, expert_down)))

    def wrapped(*params):
        return forward(*params, routes)
    result, pullback = jax.vjp(wrapped, *floats)
    gradients = pullback(cotangent.astype(jnp.float32))
    return (result.astype(jnp.bfloat16), gradients[0].astype(jnp.bfloat16), gradients[1], gradients[2], gradients[3], gradients[4], gradients[5], gradients[6], gradients[7], gradients[8], gradients[9], gradients[10], gradients[11], gradients[12], gradients[13])
```

```python
import functools

import jax
import jax.numpy as jnp
from jax import lax
from jax.experimental import pallas as pl
from jax.experimental.pallas import tpu as pltpu
from jax.sharding import PartitionSpec as P

D = 2048
HD = 128
TOP = 6


EPSILON = 1e-06
ROPE_BASE = 10000.0
MASKED = -1e30
PRECISE = lax.Precision.HIGHEST


MESH = pl.DeviceIdType.MESH
VMEM_LIMIT = 60 * 1024 * 1024

ORDERS = (
    (("z", "A"), ("z", "B"), ("y", "A"), ("y", "B")),
    (("z", "B"), ("z", "A"), ("y", "B"), ("y", "A")),
    (("y", "A"), ("y", "B"), ("z", "A"), ("z", "B")),
    (("y", "B"), ("y", "A"), ("z", "B"), ("z", "A")),
)


def paired(i, kind):
    return i + 1 - 2 * (i % 2) if kind == "A" else 3 - i


def own_place():
    c = lax.axis_index("ctx")
    return lax.axis_index("sp"), c // 4, c % 4


def neighbour(axis, kind):
    z, xh, y = own_place()
    if axis == "z":
        return {"sp": paired(z, kind)}
    if axis == "y":
        return {"ctx": 4 * xh + paired(y, kind)}
    return {"ctx": 4 * (1 - xh) + y}


def greet_cube():
    barrier = pltpu.get_barrier_semaphore()
    for axis in ("z", "y"):
        for kind in ("A", "B"):
            pl.semaphore_signal(barrier, inc=1, device_id=neighbour(axis, kind), device_id_type=MESH)
    pl.semaphore_signal(barrier, inc=1, device_id=neighbour("x", "A"), device_id_type=MESH)
    pl.semaphore_wait(barrier, 5)


def pair_slots(i, kind):
    if kind == "A":
        return [(pl.ds((i // 2) * 2, 2), pl.ds(0, 2))]
    return [(pl.ds(i, 1), pl.ds(0, 1)), (pl.ds(3 - i, 1), pl.ds(1, 1))]


def pair_members(i, kind):
    if kind == "A":
        return [(i // 2) * 2, (i // 2) * 2 + 1]
    return [i, 3 - i]


def slot_in_pair(i, kind):
    return i % 2 if kind == "A" else 0


def gather_kernel(parts, count, *refs):
    ins, outs = refs[:count], refs[count : 2 * count]
    send_sem, recv_sem, local_sem = refs[2 * count :]
    z, xh, y = own_place()
    used = [0]
    started = []

    def start(src, dst, where):
        k = used[0]
        used[0] += 1
        copy = pltpu.make_async_remote_copy(
            src_ref=src, dst_ref=dst, send_sem=send_sem.at[k], recv_sem=recv_sem.at[k],
            device_id=where, device_id_type=MESH,
        )
        copy.start()
        started.append(copy)
        return copy

    def step(lane, p, s):
        ring1, ring2 = ORDERS[p][0][0], ORDERS[p][2][0]
        axis, kind = ORDERS[p][s]
        where = neighbour(axis, kind)
        xl = xh if lane == 0 else 1 - xh
        zs, ys = [pl.ds(z, 1)], [pl.ds(y, 1)]
        full = [pl.ds(0, 4)]
        if s == 1:
            other = [d for d, _ in pair_slots(z if ring1 == "z" else y, ORDERS[p][0][1])]
            zs, ys = (other, ys) if ring1 == "z" else (zs, other)
        if s >= 2:
            zs, ys = (full, ys) if ring1 == "z" else (zs, full)
        if s == 3:
            other = [d for d, _ in pair_slots(z if ring2 == "z" else y, ORDERS[p][2][1])]
            zs, ys = (other, ys) if ring2 == "z" else (zs, other)
        copies = []
        for a, rows, cols in parts[p]:
            for zd in zs:
                for yd in ys:
                    place = outs[a].at[zd, pl.ds(xl, 1), yd, rows, cols]
                    copies.append(start(place, place, where))
        return copies

    greet_cube()
    local = [
        pltpu.make_async_copy(ins[a], outs[a].at[z, xh, y], local_sem.at[a]) for a in range(count)
    ]
    for copy in local:
        copy.start()
    across = [
        [
            start(ins[a].at[rows, cols], outs[a].at[z, xh, y, rows, cols], neighbour("x", "A"))
            for a, rows, cols in part
        ]
        for part in parts
    ]
    for copy in local:
        copy.wait()
    flying = {}

    def advance(lane, s):
        for p in range(4):
            if s == 0 and lane == 1:
                for copy in across[p]:
                    copy.wait_recv()
            if s > 0:
                for copy in flying[lane, p]:
                    copy.wait_recv()
            flying[lane, p] = step(lane, p, s) if s < 4 else []

    advance(0, 0)
    advance(0, 1)
    advance(1, 0)
    advance(0, 2)
    advance(1, 1)
    advance(0, 3)
    advance(1, 2)
    advance(1, 3)
    advance(0, 4)
    advance(1, 4)
    for copy in started:
        copy.wait_send()


def gather_cube(arrays, parts, collective_id, name):
    count = len(arrays)
    copies = 11 * sum(len(part) for part in parts)
    return pl.pallas_call(
        functools.partial(gather_kernel, parts, count),
        out_shape=[jax.ShapeDtypeStruct((4, 2, 4, *a.shape), a.dtype) for a in arrays],
        in_specs=[pl.BlockSpec(memory_space=pl.ANY)] * count,
        out_specs=[pl.BlockSpec(memory_space=pl.ANY)] * count,
        scratch_shapes=[
            pltpu.SemaphoreType.DMA((copies,)),
            pltpu.SemaphoreType.DMA((copies,)),
            pltpu.SemaphoreType.DMA((count,)),
        ],
        compiler_params=pltpu.CompilerParams(collective_id=collective_id, has_side_effects=True),
        name=name,
    )(*arrays)


def reduce_kernel(parts, count, *refs):
    entries = [(p, *entry) for p in range(4) for entry in parts[p]]
    size = 5 * len(entries)
    ins, outs = refs[:count], refs[count : 2 * count]
    bufs = refs[2 * count : 2 * count + size]
    send_sem, recv_sem = refs[2 * count + size :]
    z, xh, y = own_place()
    used = [0]
    started = []
    flying = {}

    def start(src, dst, where):
        k = used[0]
        used[0] += 1
        copy = pltpu.make_async_remote_copy(
            src_ref=src, dst_ref=dst, send_sem=send_sem.at[k], recv_sem=recv_sem.at[k],
            device_id=where, device_id_type=MESH,
        )
        copy.start()
        started.append(copy)
        return copy

    def first(lane, e):
        p, a, rows, cols = entries[e]
        ring2, near = ORDERS[p][2]
        axis, kind = ORDERS[p][3]
        xl = xh if lane == 0 else 1 - xh
        theirs = paired(z if ring2 == "z" else y, kind)
        copies = []
        for src, dst in pair_slots(theirs, near):
            if ring2 == "z":
                block, place = ins[a].at[src, xl, :, rows, cols], bufs[5 * e].at[lane, dst]
            else:
                block, place = ins[a].at[:, xl, src, rows, cols], bufs[5 * e].at[lane, :, dst]
            copies.append(start(block, place, neighbour(axis, kind)))
        flying[lane, e] = copies

    def second(lane, e):
        p, a, rows, cols = entries[e]
        ring2 = ORDERS[p][2][0]
        axis, kind = ORDERS[p][2]
        xl = xh if lane == 0 else 1 - xh
        mine = z if ring2 == "z" else y
        buf = bufs[5 * e]
        for copy in flying[lane, e]:
            copy.wait_recv()
        slot = slot_in_pair(mine, kind)

        def add(j, place):
            def one(i, carry):
                if ring2 == "z":
                    buf[lane, j, i] = buf[lane, j, i] + ins[a][place, xl, i, rows, cols]
                else:
                    buf[lane, i, j] = buf[lane, i, j] + ins[a][i, xl, place, rows, cols]
                return carry

            lax.fori_loop(0, 4, one, 0)

        add(1 - slot, paired(mine, kind))
        half = buf.at[lane, 1 - slot] if ring2 == "z" else buf.at[lane, :, 1 - slot]
        flying[lane, e] = [start(half, bufs[5 * e + 1].at[lane], neighbour(axis, kind))]
        add(slot, mine)

    def third(lane, e):
        p = entries[e][0]
        ring1, ring2 = ORDERS[p][0][0], ORDERS[p][2][0]
        axis, kind = ORDERS[p][1]
        before, buf = bufs[5 * e], bufs[5 * e + 1]
        for copy in flying[lane, e]:
            copy.wait_recv()
        slot = slot_in_pair(z if ring2 == "z" else y, ORDERS[p][2][1])

        def one(i, carry):
            other = before[lane, slot, i] if ring2 == "z" else before[lane, i, slot]
            buf[lane, i] = buf[lane, i] + other
            return carry

        lax.fori_loop(0, 4, one, 0)
        theirs = paired(z if ring1 == "z" else y, kind)
        flying[lane, e] = [
            start(buf.at[lane, src], bufs[5 * e + 2].at[lane, dst], neighbour(axis, kind))
            for src, dst in pair_slots(theirs, ORDERS[p][0][1])
        ]

    def fourth(lane, e):
        p = entries[e][0]
        ring1 = ORDERS[p][0][0]
        axis, kind = ORDERS[p][0]
        mine = z if ring1 == "z" else y
        before, buf = bufs[5 * e + 1], bufs[5 * e + 2]
        for copy in flying[lane, e]:
            copy.wait_recv()
        slot = slot_in_pair(mine, kind)
        buf[lane, 1 - slot] = buf[lane, 1 - slot] + before[lane, paired(mine, kind)]
        flying[lane, e] = [
            start(buf.at[lane, 1 - slot], bufs[5 * e + 3].at[lane], neighbour(axis, kind))
        ]
        buf[lane, slot] = buf[lane, slot] + before[lane, mine]

    def last(lane, e):
        p, a, rows, cols = entries[e]
        ring1 = ORDERS[p][0][0]
        before, buf = bufs[5 * e + 2], bufs[5 * e + 3]
        for copy in flying[lane, e]:
            copy.wait_recv()
        slot = slot_in_pair(z if ring1 == "z" else y, ORDERS[p][0][1])
        if lane == 1:
            buf[1] = buf[1] + before[1, slot]
            flying["x", e] = start(buf.at[1], bufs[5 * e + 4], neighbour("x", "A"))
        else:
            flying["x", e].wait_recv()
            total = (
                buf[0].astype(jnp.float32)
                + before[0, slot].astype(jnp.float32)
                + bufs[5 * e + 4][...].astype(jnp.float32)
            )
            outs[a][rows, cols] = total.astype(outs[a].dtype)

    greet_cube()
    for stage in (first, second, third, fourth, last):
        for lane in (1, 0):
            for e in range(len(entries)):
                stage(lane, e)
    for copy in started:
        copy.wait_send()


def reduce_cube(arrays, parts, collective_id, name, dtype=jnp.float32):
    count = len(arrays)
    scratch = []
    for p in range(4):
        pair = (2, 4) if ORDERS[p][2][0] == "z" else (4, 2)
        for a, rows, cols in parts[p]:
            for lead in ((2, *pair), (2, 4), (2, 2), (2,), ()):
                scratch.append(pltpu.VMEM((*lead, rows.size, cols.size), arrays[a].dtype))
    copies = 13 * sum(len(part) for part in parts)
    return pl.pallas_call(
        functools.partial(reduce_kernel, parts, count),
        out_shape=[jax.ShapeDtypeStruct(a.shape[3:], dtype) for a in arrays],
        in_specs=[pl.BlockSpec(memory_space=pltpu.VMEM)] * count,
        out_specs=[pl.BlockSpec(memory_space=pltpu.VMEM)] * count,
        scratch_shapes=scratch
        + [pltpu.SemaphoreType.DMA((copies,)), pltpu.SemaphoreType.DMA((copies,))],
        compiler_params=pltpu.CompilerParams(
            collective_id=collective_id, has_side_effects=True, vmem_limit_bytes=VMEM_LIMIT
        ),
        name=name,
    )(*arrays)


def row_parts(arrays):
    parts = []
    for p in range(4):
        part = []
        for a, array in enumerate(arrays):
            rows, columns = array.shape[-2:]
            part.append((a, pl.ds(p * rows // 4, rows // 4), pl.ds(0, columns)))
        parts.append(part)
    return parts


def whole_parts(arrays):
    return [[(a, pl.ds(0, x.shape[-2]), pl.ds(0, x.shape[-1]))] for a, x in enumerate(arrays)]


def half_parts(arrays):
    return [
        [(a, pl.ds(0, x.shape[-2]), pl.ds(h * x.shape[-1] // 2, x.shape[-1] // 2))]
        for a, x in enumerate(arrays)
        for h in range(2)
    ]


def sum_wa_kernel(x, out, half, got, far, send_sem, recv_sem):
    w = lax.axis_index("wa")
    core = w % 2
    beside = {"wa": w + 1 - 2 * core}
    across = {"wa": (w + 2) % 4}
    width = x.shape[1] // 2
    barrier = pltpu.get_barrier_semaphore()
    for place in (beside, across):
        pl.semaphore_signal(barrier, inc=1, device_id=place, device_id_type=MESH)
    pl.semaphore_wait(barrier, 2)

    def send(src, dst, where, k):
        copy = pltpu.make_async_remote_copy(
            src_ref=src, dst_ref=dst, send_sem=send_sem.at[k], recv_sem=recv_sem.at[k],
            device_id=where, device_id_type=MESH,
        )
        copy.start()
        return copy

    mine = pl.ds(pl.multiple_of(core * width, width), width)
    theirs = pl.ds(pl.multiple_of((1 - core) * width, width), width)
    one = send(x.at[:, theirs], got, beside, 0)
    one.wait_recv()
    half[...] = x[:, mine] + got[...]
    two = send(half, far, across, 1)
    two.wait_recv()
    out[:, mine] = half[...] + far[...]
    three = send(out.at[:, mine], out.at[:, mine], beside, 2)
    three.wait_recv()
    for copy in (one, two, three):
        copy.wait_send()


def sum_wa(x, collective_id, name):
    rows, columns = x.shape
    return pl.pallas_call(
        sum_wa_kernel,
        out_shape=jax.ShapeDtypeStruct(x.shape, x.dtype),
        in_specs=[pl.BlockSpec(memory_space=pltpu.VMEM)],
        out_specs=pl.BlockSpec(memory_space=pltpu.VMEM),
        scratch_shapes=[pltpu.VMEM((rows, columns // 2), x.dtype)] * 3
        + [pltpu.SemaphoreType.DMA((3,)), pltpu.SemaphoreType.DMA((3,))],
        compiler_params=pltpu.CompilerParams(
            collective_id=collective_id, has_side_effects=True, vmem_limit_bytes=VMEM_LIMIT
        ),
        name=name,
    )(x)


def turned_gather(arrays, axis, dims):
    turned = [jnp.moveaxis(a, dim, 0) for a, dim in zip(arrays, dims)]
    widths = [t[0].size for t in turned]
    both = jnp.concatenate([t.reshape(-1, w) for t, w in zip(turned, widths)], axis=1)
    whole = lax.all_gather(both, axis, axis=0, tiled=True)
    pieces = jnp.split(whole, [sum(widths[:k]) for k in range(1, len(widths))], axis=1)
    return tuple(
        (
            jnp.moveaxis(b.reshape(-1, *t.shape[1:]), 0, dim)
            for b, t, dim in zip(pieces, turned, dims)
        )
    )


def rope_tables(positions):
    half_width = HD // 2
    inverse = 1.0 / ROPE_BASE ** (jnp.arange(half_width, dtype=jnp.float32) * 2.0 / HD)
    angles = positions[:, None] * inverse[None, :]
    return (jnp.cos(angles)[:, None, :], jnp.sin(angles)[:, None, :])


def rotate(values, cosine, sine_part, direction):
    half_width = values.shape[-1] // 2
    leading = values[..., :half_width]
    trailing = values[..., half_width:]
    return jnp.concatenate(
        [
            leading * cosine - direction * trailing * sine_part,
            trailing * cosine + direction * leading * sine_part,
        ],
        axis=-1,
    )


def send_share(rows):
    quarter = D // lax.axis_size("wa")
    start = lax.axis_index("wa") * quarter
    piece = lax.dynamic_slice_in_dim(rows, start, quarter, 1)
    moved = lax.all_to_all(piece, ("sp", "ctx"), split_axis=0, concat_axis=0, tiled=True)
    return lax.all_gather(moved, "wa", axis=1, tiled=True)


def back_share(expert_part, shared_part, collective_id, name):
    share = lax.psum_scatter(
        expert_part.astype(jnp.bfloat16), "wa", scatter_dimension=1, tiled=True
    )
    moved = lax.all_to_all(share, ("sp", "ctx"), split_axis=0, concat_axis=0, tiled=True)
    returned = lax.all_gather(moved, "wa", axis=1, tiled=True)
    shared_sum = sum_wa(shared_part.astype(jnp.bfloat16), collective_id, name).astype(jnp.float32)
    return (returned, shared_sum)


def gather_whole(arrays):
    return gather_cube(arrays, whole_parts(arrays), 1, "gather_attention_weights")


def shards(
    tokens,
    cotangent,
    routes,
    attn_gain,
    query_weight,
    key_weight,
    value_weight,
    output_weight,
    mlp_gain,
    router_weight,
    shared_gate,
    shared_up,
    shared_down,
    expert_gate,
    expert_up,
    expert_down,
):
    local_tokens = tokens.shape[0]
    heads_here = query_weight.shape[1] // HD
    head_cols = heads_here * HD
    experts_all = router_weight.shape[1]
    experts_here = expert_gate.shape[0]
    devices_seq = lax.axis_size("sp") * lax.axis_size("ctx")
    capacity = max(2, 4 * local_tokens * TOP // (3 * experts_all))
    score_scale = HD ** (-0.5)
    seq_len = local_tokens * devices_seq
    device_pos = lax.axis_index("sp") * lax.axis_size("ctx") + lax.axis_index("ctx")
    full_query, full_key, full_value, output_turned = (
        whole.reshape(D, head_cols)
        for whole in gather_whole((query_weight, key_weight, value_weight, output_weight.T))
    )
    full_sgate, full_sup, full_sdown, full_router, full_attn_gain, full_mlp_gain = turned_gather(
        (shared_gate, shared_up, shared_down, router_weight, attn_gain, mlp_gain),
        ("sp", "ctx"),
        (0, 0, 1, 0, 0, 0),
    )
    tokens_f = tokens.astype(jnp.float32)
    inv_one = lax.rsqrt(jnp.mean(tokens_f * tokens_f, axis=-1, keepdims=True) + EPSILON)
    unit_one = tokens_f * inv_one
    gain_one = full_attn_gain.astype(jnp.float32)
    normed = (unit_one * gain_one).astype(jnp.bfloat16)
    query_pos = device_pos * local_tokens + jnp.arange(local_tokens, dtype=jnp.int32)
    cosine, sine_part = rope_tables(query_pos.astype(jnp.float32))
    query_raw = jnp.dot(normed, full_query, preferred_element_type=jnp.float32).reshape(
        local_tokens, heads_here, HD
    )
    key_raw = jnp.dot(normed, full_key, preferred_element_type=jnp.float32).reshape(
        local_tokens, heads_here, HD
    )
    queries = rotate(query_raw, cosine, sine_part, 1.0).astype(jnp.bfloat16)
    keys_local = (
        rotate(key_raw, cosine, sine_part, 1.0)
        .astype(jnp.bfloat16)
        .reshape(local_tokens, head_cols)
    )
    values_local = jnp.dot(normed, full_value, preferred_element_type=jnp.float32).astype(
        jnp.bfloat16
    )
    keys_all, values_all = gather_cube(
        (keys_local, values_local), half_parts((keys_local, values_local)), 2, "gather_keys_values"
    )
    keys_all = keys_all.reshape(seq_len, heads_here, HD)
    values_all = values_all.reshape(seq_len, heads_here, HD)
    visible = jnp.arange(seq_len, dtype=jnp.int32)[None, :] <= query_pos[:, None]

    def masked_scores():
        scores = (
            jnp.einsum("qhd,khd->hqk", queries, keys_all, preferred_element_type=jnp.float32)
            * score_scale
        )
        return jnp.where(visible[None], scores, MASKED)

    scores = masked_scores()
    row_max = jnp.max(scores, axis=-1, keepdims=True)
    weights = jnp.exp(scores - row_max)
    totals = jnp.sum(weights, axis=-1, keepdims=True)
    log_total = row_max + jnp.log(totals)
    probs_low = (weights / totals).astype(jnp.bfloat16)
    attended = (
        jnp.einsum("hqk,khd->qhd", probs_low, values_all, preferred_element_type=jnp.float32)
        .astype(jnp.bfloat16)
        .reshape(local_tokens, head_cols)
    )
    attn_part = jnp.einsum(
        "tc,dc->td", attended, output_turned, preferred_element_type=jnp.float32
    )
    attn_out = sum_wa(attn_part.astype(jnp.bfloat16), 3, "sum_attention").astype(jnp.float32)
    hidden_state = tokens_f + attn_out
    inv_two = lax.rsqrt(jnp.mean(hidden_state * hidden_state, axis=-1, keepdims=True) + EPSILON)
    unit_two = hidden_state * inv_two
    gain_two = full_mlp_gain.astype(jnp.float32)
    mlp_in = (unit_two * gain_two).astype(jnp.bfloat16)
    logits = jnp.dot(mlp_in, full_router, preferred_element_type=jnp.float32)
    logit_max = jnp.max(logits, axis=-1, keepdims=True)
    logit_exp = jnp.exp(logits - logit_max)
    router_probs = logit_exp / jnp.sum(logit_exp, axis=-1, keepdims=True)
    chosen = routes[:, :, None] == jnp.arange(experts_all, dtype=jnp.int32)[None, None, :]
    chosen_float = chosen.astype(jnp.float32)
    chosen_int = chosen.astype(jnp.int32)
    gate_values = jnp.sum(chosen_float * router_probs[:, None, :], axis=-1)
    running = jnp.cumsum(chosen_int.reshape(local_tokens * TOP, experts_all), axis=0).reshape(
        local_tokens, TOP, experts_all
    )
    slot_index = jnp.sum((running - 1) * chosen_int, axis=-1)
    destination = (routes * capacity + slot_index).reshape(-1)
    assign_ids = jnp.arange(local_tokens * TOP, dtype=jnp.int32)
    owner_assign = jnp.zeros((experts_all * capacity,), jnp.int32).at[destination].set(assign_ids)
    filled = jnp.zeros((experts_all * capacity,), jnp.bfloat16).at[destination].set(1.0)
    send_rows = mlp_in[owner_assign // TOP] * filled[:, None]
    arrived = send_share(send_rows).reshape(devices_seq, experts_here, capacity, D)
    shared_pre = jnp.dot(mlp_in, full_sgate, preferred_element_type=jnp.float32)
    shared_lin = jnp.dot(mlp_in, full_sup, preferred_element_type=jnp.float32)
    shared_sig = jax.nn.sigmoid(shared_pre)
    shared_act = (shared_pre * shared_sig * shared_lin).astype(jnp.bfloat16)
    shared_part = jnp.dot(shared_act, full_sdown, preferred_element_type=jnp.float32)
    expert_pre = jnp.einsum(
        "secd,edf->secf", arrived, expert_gate, preferred_element_type=jnp.float32
    )
    expert_lin = jnp.einsum(
        "secd,edf->secf", arrived, expert_up, preferred_element_type=jnp.float32
    )
    expert_sig = jax.nn.sigmoid(expert_pre)
    expert_act = (expert_pre * expert_sig * expert_lin).astype(jnp.bfloat16)
    expert_part = jnp.einsum(
        "secf,efd->secd", expert_act, expert_down, preferred_element_type=jnp.float32
    ).reshape(-1, D)
    returned, shared_out = back_share(expert_part, shared_part, 4, "sum_shared")
    picked = returned[destination].reshape(local_tokens, TOP, D).astype(jnp.float32)
    routed = jnp.sum(gate_values[:, :, None] * picked, axis=1)
    block_out = (hidden_state + (routed + shared_out)).astype(jnp.bfloat16)
    grad_out = cotangent.astype(jnp.float32)
    gate_grads = jnp.sum(grad_out[:, None, :] * picked, axis=-1)
    routed_grads = (
        (gate_values[:, :, None] * grad_out[:, None, :])
        .astype(jnp.bfloat16)
        .reshape(local_tokens * TOP, D)
    )
    send_grads = routed_grads[owner_assign] * filled[:, None]
    arrived_grads = send_share(send_grads).reshape(devices_seq, experts_here, capacity, D)
    act_grads = jnp.einsum(
        "secd,efd->secf", arrived_grads, expert_down, preferred_element_type=jnp.float32
    )
    expert_down_grad = jnp.einsum(
        "secf,secd->efd", expert_act, arrived_grads, preferred_element_type=jnp.float32
    )
    swish_val = expert_pre * expert_sig
    swish_slope = expert_sig * (1.0 + expert_pre * (1.0 - expert_sig))
    pre_grads = (act_grads * expert_lin * swish_slope).astype(jnp.bfloat16)
    lin_grads = (act_grads * swish_val).astype(jnp.bfloat16)
    expert_gate_grad = jnp.einsum(
        "secd,secf->edf", arrived, pre_grads, preferred_element_type=jnp.float32
    )
    expert_up_grad = jnp.einsum(
        "secd,secf->edf", arrived, lin_grads, preferred_element_type=jnp.float32
    )
    rows_part = jnp.einsum(
        "secf,edf->secd", pre_grads, expert_gate, preferred_element_type=jnp.float32
    ) + jnp.einsum("secf,edf->secd", lin_grads, expert_up, preferred_element_type=jnp.float32)
    shared_act_grads = jnp.einsum(
        "td,fd->tf", cotangent, full_sdown, preferred_element_type=jnp.float32
    )
    shared_down_grad = jnp.einsum(
        "tf,td->df", shared_act, cotangent, preferred_element_type=jnp.float32
    )
    shared_slope = shared_sig * (1.0 + shared_pre * (1.0 - shared_sig))
    shared_pre_grads = (shared_act_grads * shared_lin * shared_slope).astype(jnp.bfloat16)
    shared_lin_grads = (shared_act_grads * shared_pre * shared_sig).astype(jnp.bfloat16)
    shared_in_part = jnp.einsum(
        "tf,df->td", shared_pre_grads, full_sgate, preferred_element_type=jnp.float32
    ) + jnp.einsum("tf,df->td", shared_lin_grads, full_sup, preferred_element_type=jnp.float32)
    rows_back, shared_in_grad = back_share(
        rows_part.reshape(-1, D), shared_in_part, 5, "sum_shared_grad"
    )
    routed_in_grad = jnp.sum(
        rows_back[destination].reshape(local_tokens, TOP, D).astype(jnp.float32), axis=1
    )
    prob_grads = jnp.sum(chosen_float * gate_grads[:, :, None], axis=1)
    logit_grads = router_probs * (
        prob_grads - jnp.sum(router_probs * prob_grads, axis=-1, keepdims=True)
    )
    router_float = full_router.astype(jnp.float32)
    router_in_grad = jnp.einsum("te,de->td", logit_grads, router_float, precision=PRECISE)
    beside_grads = jnp.concatenate(
        [shared_pre_grads, shared_lin_grads, logit_grads.astype(jnp.bfloat16)], axis=1
    )
    mlp_weight_grads = jnp.einsum(
        "td,tf->df", mlp_in, beside_grads, preferred_element_type=jnp.float32
    )
    mlp_in_grad = router_in_grad + shared_in_grad + routed_in_grad
    gain_two_grad = jnp.sum(mlp_in_grad * unit_two, axis=0)
    scaled_two = mlp_in_grad * gain_two
    hidden_grad = grad_out + inv_two * (
        scaled_two - unit_two * jnp.mean(scaled_two * unit_two, axis=-1, keepdims=True)
    )
    out_grad = hidden_grad.astype(jnp.bfloat16)
    output_weight_grad = jnp.einsum(
        "tc,td->dc", attended, out_grad, preferred_element_type=jnp.float32
    )
    attended_grad = (
        jnp.einsum("td,dc->tc", out_grad, output_turned, preferred_element_type=jnp.float32)
        .astype(jnp.bfloat16)
        .reshape(local_tokens, heads_here, HD)
    )
    probs_again = jnp.exp(masked_scores() - log_total)
    value_terms = jnp.einsum(
        "hqk,qhd->khd",
        probs_again.astype(jnp.bfloat16),
        attended_grad,
        preferred_element_type=jnp.float32,
    )
    prob_grad = jnp.einsum(
        "qhd,khd->hqk", attended_grad, values_all, preferred_element_type=jnp.float32
    )
    score_grads = (
        probs_again * (prob_grad - jnp.sum(probs_again * prob_grad, axis=-1, keepdims=True))
    ).astype(jnp.bfloat16)
    query_grads = (
        jnp.einsum("hqk,khd->qhd", score_grads, keys_all, preferred_element_type=jnp.float32)
        * score_scale
    ).astype(jnp.bfloat16)
    key_terms = (
        jnp.einsum("hqk,qhd->khd", score_grads, queries, preferred_element_type=jnp.float32)
        * score_scale
    )
    key_value_terms = [
        part.astype(jnp.bfloat16).reshape(4, 2, 4, local_tokens, head_cols)
        for part in (key_terms, value_terms)
    ]
    key_sum, value_sum = reduce_cube(
        key_value_terms, half_parts(key_value_terms), 6, "reduce_keys_values", jnp.bfloat16
    )
    query_in = (
        rotate(query_grads, cosine, sine_part, -1.0)
        .astype(jnp.bfloat16)
        .reshape(local_tokens, head_cols)
    )
    key_in = (
        rotate(
            key_sum.astype(jnp.float32).reshape(local_tokens, heads_here, HD),
            cosine,
            sine_part,
            -1.0,
        )
        .astype(jnp.bfloat16)
        .reshape(local_tokens, head_cols)
    )
    value_in = value_sum
    query_weight_grad = jnp.einsum(
        "td,tc->dc", normed, query_in, preferred_element_type=jnp.float32
    )
    key_weight_grad = jnp.einsum("td,tc->dc", normed, key_in, preferred_element_type=jnp.float32)
    value_weight_grad = jnp.einsum(
        "td,tc->dc", normed, value_in, preferred_element_type=jnp.float32
    )
    normed_part = (
        jnp.einsum("tc,dc->td", query_in, full_query, preferred_element_type=jnp.float32)
        + jnp.einsum("tc,dc->td", key_in, full_key, preferred_element_type=jnp.float32)
        + jnp.einsum("tc,dc->td", value_in, full_value, preferred_element_type=jnp.float32)
    )
    normed_grad = sum_wa(normed_part.astype(jnp.bfloat16), 7, "sum_normed_grad").astype(
        jnp.float32
    )
    gain_one_grad = jnp.sum(normed_grad * unit_one, axis=0)
    scaled_one = normed_grad * gain_one
    tokens_grad = (
        hidden_grad
        + inv_one
        * (scaled_one - unit_one * jnp.mean(scaled_one * unit_one, axis=-1, keepdims=True))
    ).astype(jnp.bfloat16)
    gain_grads = jnp.stack([gain_one_grad, gain_two_grad], axis=1)
    gain_grads = jnp.pad(gain_grads, ((0, 0), (0, HD - 2)))
    mlp_grads = [
        part.astype(jnp.bfloat16).reshape(4, 2, 4, D // devices_seq, -1)
        for part in (mlp_weight_grads, shared_down_grad, gain_grads)
    ]
    mlp_shares, down_share, gain_shares = reduce_cube(
        mlp_grads, row_parts(mlp_grads), 8, "reduce_mlp_grads"
    )
    attention_grads = [
        part.astype(jnp.bfloat16).reshape(4, 2, 4, D // devices_seq, -1)
        for part in (query_weight_grad, key_weight_grad, value_weight_grad, output_weight_grad)
    ]
    query_share, key_share, value_share, output_share = reduce_cube(
        attention_grads, whole_parts(attention_grads), 9, "reduce_attention_grads"
    )
    hidden_cols = shared_gate.shape[1]
    return (
        block_out,
        tokens_grad,
        gain_shares[:, 0],
        query_share,
        key_share,
        value_share,
        output_share.T,
        gain_shares[:, 1],
        mlp_shares[:, 2 * hidden_cols :],
        mlp_shares[:, :hidden_cols],
        mlp_shares[:, hidden_cols : 2 * hidden_cols],
        down_share.T,
        expert_gate_grad,
        expert_up_grad,
        expert_down_grad,
    )


def solution(mesh):
    placed = (
        P(("sp", "ctx"), None),
        P(("sp", "ctx"), None),
        P(("sp", "ctx"), None),
        P(("sp", "ctx")),
        P(("sp", "ctx"), "wa"),
        P(("sp", "ctx"), "wa"),
        P(("sp", "ctx"), "wa"),
        P("wa", ("sp", "ctx")),
        P(("sp", "ctx")),
        P(("sp", "ctx"), None),
        P(("sp", "ctx"), "wa"),
        P(("sp", "ctx"), "wa"),
        P("wa", ("sp", "ctx")),
        P(("sp", "ctx"), None, "wa"),
        P(("sp", "ctx"), None, "wa"),
        P(("sp", "ctx"), "wa", None),
    )
    return jax.shard_map(
        shards,
        mesh=mesh,
        in_specs=placed,
        out_specs=(
            P(("sp", "ctx"), None),
            P(("sp", "ctx"), None),
            P(("sp", "ctx")),
            P(("sp", "ctx"), "wa"),
            P(("sp", "ctx"), "wa"),
            P(("sp", "ctx"), "wa"),
            P("wa", ("sp", "ctx")),
            P(("sp", "ctx")),
            P(("sp", "ctx"), None),
            P(("sp", "ctx"), "wa"),
            P(("sp", "ctx"), "wa"),
            P("wa", ("sp", "ctx")),
            P(("sp", "ctx"), None, "wa"),
            P(("sp", "ctx"), None, "wa"),
            P(("sp", "ctx"), "wa", None),
        ),
        check_vma=False,
    )
```

```python
import functools

import jax
import jax.numpy as jnp
from jax import lax
from jax.experimental import pallas as pl
from jax.experimental.pallas import tpu as pltpu
from jax.sharding import PartitionSpec as P

D = 2048
HD = 128
TOP = 6


EPSILON = 1e-06
ROPE_BASE = 10000.0
MASKED = -1e30
PRECISE = lax.Precision.HIGHEST
MESH = pl.DeviceIdType.MESH
VMEM_LIMIT = 60 * 1024 * 1024

ORDERS = (
    (("z", "A"), ("z", "B"), ("y", "A"), ("y", "B")),
    (("z", "B"), ("z", "A"), ("y", "B"), ("y", "A")),
    (("y", "A"), ("y", "B"), ("z", "A"), ("z", "B")),
    (("y", "B"), ("y", "A"), ("z", "B"), ("z", "A")),
)


def paired(i, kind):
    return i + 1 - 2 * (i % 2) if kind == "A" else 3 - i


def own_place():
    c = lax.axis_index("ctx")
    return lax.axis_index("sp"), c // 4, c % 4


def neighbour(axis, kind):
    z, xh, y = own_place()
    if axis == "z":
        return {"sp": paired(z, kind)}
    if axis == "y":
        return {"ctx": 4 * xh + paired(y, kind)}
    return {"ctx": 4 * (1 - xh) + y}


def greet_cube():
    barrier = pltpu.get_barrier_semaphore()
    for axis in ("z", "y"):
        for kind in ("A", "B"):
            pl.semaphore_signal(barrier, inc=1, device_id=neighbour(axis, kind), device_id_type=MESH)
    pl.semaphore_signal(barrier, inc=1, device_id=neighbour("x", "A"), device_id_type=MESH)
    pl.semaphore_wait(barrier, 5)


def pair_slots(i, kind):
    if kind == "A":
        return [(pl.ds((i // 2) * 2, 2), pl.ds(0, 2))]
    return [(pl.ds(i, 1), pl.ds(0, 1)), (pl.ds(3 - i, 1), pl.ds(1, 1))]


def pair_members(i, kind):
    if kind == "A":
        return [(i // 2) * 2, (i // 2) * 2 + 1]
    return [i, 3 - i]


def slot_in_pair(i, kind):
    return i % 2 if kind == "A" else 0


def gather_kernel(parts, count, *refs):
    ins, outs = refs[:count], refs[count : 2 * count]
    send_sem, recv_sem, local_sem = refs[2 * count :]
    z, xh, y = own_place()
    used = [0]
    started = []

    def start(src, dst, where):
        k = used[0]
        used[0] += 1
        copy = pltpu.make_async_remote_copy(
            src_ref=src, dst_ref=dst, send_sem=send_sem.at[k], recv_sem=recv_sem.at[k],
            device_id=where, device_id_type=MESH,
        )
        copy.start()
        started.append(copy)
        return copy

    def step(lane, p, s):
        ring1, ring2 = ORDERS[p][0][0], ORDERS[p][2][0]
        axis, kind = ORDERS[p][s]
        where = neighbour(axis, kind)
        xl = xh if lane == 0 else 1 - xh
        zs, ys = [pl.ds(z, 1)], [pl.ds(y, 1)]
        full = [pl.ds(0, 4)]
        if s == 1:
            other = [d for d, _ in pair_slots(z if ring1 == "z" else y, ORDERS[p][0][1])]
            zs, ys = (other, ys) if ring1 == "z" else (zs, other)
        if s >= 2:
            zs, ys = (full, ys) if ring1 == "z" else (zs, full)
        if s == 3:
            other = [d for d, _ in pair_slots(z if ring2 == "z" else y, ORDERS[p][2][1])]
            zs, ys = (other, ys) if ring2 == "z" else (zs, other)
        copies = []
        for a, rows, cols in parts[p]:
            for zd in zs:
                for yd in ys:
                    place = outs[a].at[zd, pl.ds(xl, 1), yd, rows, cols]
                    copies.append(start(place, place, where))
        return copies

    greet_cube()
    local = [
        pltpu.make_async_copy(ins[a], outs[a].at[z, xh, y], local_sem.at[a]) for a in range(count)
    ]
    for copy in local:
        copy.start()
    across = [
        [
            start(ins[a].at[rows, cols], outs[a].at[z, xh, y, rows, cols], neighbour("x", "A"))
            for a, rows, cols in part
        ]
        for part in parts
    ]
    for copy in local:
        copy.wait()
    flying = {}

    def advance(lane, s):
        for p in range(4):
            if s == 0 and lane == 1:
                for copy in across[p]:
                    copy.wait_recv()
            if s > 0:
                for copy in flying[lane, p]:
                    copy.wait_recv()
            flying[lane, p] = step(lane, p, s) if s < 4 else []

    advance(0, 0)
    advance(0, 1)
    advance(1, 0)
    advance(0, 2)
    advance(1, 1)
    advance(0, 3)
    advance(1, 2)
    advance(1, 3)
    advance(0, 4)
    advance(1, 4)
    for copy in started:
        copy.wait_send()


def gather_cube(arrays, parts, collective_id, name):
    count = len(arrays)
    copies = 11 * sum(len(part) for part in parts)
    return pl.pallas_call(
        functools.partial(gather_kernel, parts, count),
        out_shape=[jax.ShapeDtypeStruct((4, 2, 4, *a.shape), a.dtype) for a in arrays],
        in_specs=[pl.BlockSpec(memory_space=pl.ANY)] * count,
        out_specs=[pl.BlockSpec(memory_space=pl.ANY)] * count,
        scratch_shapes=[
            pltpu.SemaphoreType.DMA((copies,)),
            pltpu.SemaphoreType.DMA((copies,)),
            pltpu.SemaphoreType.DMA((count,)),
        ],
        compiler_params=pltpu.CompilerParams(collective_id=collective_id, has_side_effects=True),
        name=name,
    )(*arrays)


def reduce_kernel(parts, count, *refs):
    entries = [(p, *entry) for p in range(4) for entry in parts[p]]
    size = 5 * len(entries)
    ins, outs = refs[:count], refs[count : 2 * count]
    bufs = refs[2 * count : 2 * count + size]
    send_sem, recv_sem = refs[2 * count + size :]
    z, xh, y = own_place()
    used = [0]
    started = []
    flying = {}

    def start(src, dst, where):
        k = used[0]
        used[0] += 1
        copy = pltpu.make_async_remote_copy(
            src_ref=src, dst_ref=dst, send_sem=send_sem.at[k], recv_sem=recv_sem.at[k],
            device_id=where, device_id_type=MESH,
        )
        copy.start()
        started.append(copy)
        return copy

    def first(lane, e):
        p, a, rows, cols = entries[e]
        ring2, near = ORDERS[p][2]
        axis, kind = ORDERS[p][3]
        xl = xh if lane == 0 else 1 - xh
        theirs = paired(z if ring2 == "z" else y, kind)
        copies = []
        for src, dst in pair_slots(theirs, near):
            if ring2 == "z":
                block, place = ins[a].at[src, xl, :, rows, cols], bufs[5 * e].at[lane, dst]
            else:
                block, place = ins[a].at[:, xl, src, rows, cols], bufs[5 * e].at[lane, :, dst]
            copies.append(start(block, place, neighbour(axis, kind)))
        flying[lane, e] = copies

    def second(lane, e):
        p, a, rows, cols = entries[e]
        ring2 = ORDERS[p][2][0]
        axis, kind = ORDERS[p][2]
        xl = xh if lane == 0 else 1 - xh
        mine = z if ring2 == "z" else y
        buf = bufs[5 * e]
        for copy in flying[lane, e]:
            copy.wait_recv()
        slot = slot_in_pair(mine, kind)

        def add(j, place):
            def one(i, carry):
                if ring2 == "z":
                    buf[lane, j, i] = buf[lane, j, i] + ins[a][place, xl, i, rows, cols]
                else:
                    buf[lane, i, j] = buf[lane, i, j] + ins[a][i, xl, place, rows, cols]
                return carry

            lax.fori_loop(0, 4, one, 0)

        add(1 - slot, paired(mine, kind))
        half = buf.at[lane, 1 - slot] if ring2 == "z" else buf.at[lane, :, 1 - slot]
        flying[lane, e] = [start(half, bufs[5 * e + 1].at[lane], neighbour(axis, kind))]
        add(slot, mine)

    def third(lane, e):
        p = entries[e][0]
        ring1, ring2 = ORDERS[p][0][0], ORDERS[p][2][0]
        axis, kind = ORDERS[p][1]
        before, buf = bufs[5 * e], bufs[5 * e + 1]
        for copy in flying[lane, e]:
            copy.wait_recv()
        slot = slot_in_pair(z if ring2 == "z" else y, ORDERS[p][2][1])

        def one(i, carry):
            other = before[lane, slot, i] if ring2 == "z" else before[lane, i, slot]
            buf[lane, i] = buf[lane, i] + other
            return carry

        lax.fori_loop(0, 4, one, 0)
        theirs = paired(z if ring1 == "z" else y, kind)
        flying[lane, e] = [
            start(buf.at[lane, src], bufs[5 * e + 2].at[lane, dst], neighbour(axis, kind))
            for src, dst in pair_slots(theirs, ORDERS[p][0][1])
        ]

    def fourth(lane, e):
        p = entries[e][0]
        ring1 = ORDERS[p][0][0]
        axis, kind = ORDERS[p][0]
        mine = z if ring1 == "z" else y
        before, buf = bufs[5 * e + 1], bufs[5 * e + 2]
        for copy in flying[lane, e]:
            copy.wait_recv()
        slot = slot_in_pair(mine, kind)
        buf[lane, 1 - slot] = buf[lane, 1 - slot] + before[lane, paired(mine, kind)]
        flying[lane, e] = [
            start(buf.at[lane, 1 - slot], bufs[5 * e + 3].at[lane], neighbour(axis, kind))
        ]
        buf[lane, slot] = buf[lane, slot] + before[lane, mine]

    def last(lane, e):
        p, a, rows, cols = entries[e]
        ring1 = ORDERS[p][0][0]
        before, buf = bufs[5 * e + 2], bufs[5 * e + 3]
        for copy in flying[lane, e]:
            copy.wait_recv()
        slot = slot_in_pair(z if ring1 == "z" else y, ORDERS[p][0][1])
        if lane == 1:
            buf[1] = buf[1] + before[1, slot]
            flying["x", e] = start(buf.at[1], bufs[5 * e + 4], neighbour("x", "A"))
        else:
            flying["x", e].wait_recv()
            total = (
                buf[0].astype(jnp.float32)
                + before[0, slot].astype(jnp.float32)
                + bufs[5 * e + 4][...].astype(jnp.float32)
            )
            outs[a][rows, cols] = total.astype(outs[a].dtype)

    greet_cube()
    for stage in (first, second, third, fourth, last):
        for lane in (1, 0):
            for e in range(len(entries)):
                stage(lane, e)
    for copy in started:
        copy.wait_send()


def reduce_cube(arrays, parts, collective_id, name, dtype=jnp.float32):
    count = len(arrays)
    scratch = []
    for p in range(4):
        pair = (2, 4) if ORDERS[p][2][0] == "z" else (4, 2)
        for a, rows, cols in parts[p]:
            for lead in ((2, *pair), (2, 4), (2, 2), (2,), ()):
                scratch.append(pltpu.VMEM((*lead, rows.size, cols.size), arrays[a].dtype))
    copies = 13 * sum(len(part) for part in parts)
    return pl.pallas_call(
        functools.partial(reduce_kernel, parts, count),
        out_shape=[jax.ShapeDtypeStruct(a.shape[3:], dtype) for a in arrays],
        in_specs=[pl.BlockSpec(memory_space=pltpu.VMEM)] * count,
        out_specs=[pl.BlockSpec(memory_space=pltpu.VMEM)] * count,
        scratch_shapes=scratch
        + [pltpu.SemaphoreType.DMA((copies,)), pltpu.SemaphoreType.DMA((copies,))],
        compiler_params=pltpu.CompilerParams(
            collective_id=collective_id, has_side_effects=True, vmem_limit_bytes=VMEM_LIMIT
        ),
        name=name,
    )(*arrays)


def row_parts(arrays):
    parts = []
    for p in range(4):
        part = []
        for a, array in enumerate(arrays):
            rows, columns = array.shape[-2:]
            part.append((a, pl.ds(p * rows // 4, rows // 4), pl.ds(0, columns)))
        parts.append(part)
    return parts


def whole_parts(arrays):
    return [[(a, pl.ds(0, x.shape[-2]), pl.ds(0, x.shape[-1]))] for a, x in enumerate(arrays)]


def half_parts(arrays):
    return [
        [(a, pl.ds(0, x.shape[-2]), pl.ds(h * x.shape[-1] // 2, x.shape[-1] // 2))]
        for a, x in enumerate(arrays)
        for h in range(2)
    ]


def sum_wa_kernel(x, out, half, got, far, send_sem, recv_sem):
    w = lax.axis_index("wa")
    core = w % 2
    beside = {"wa": w + 1 - 2 * core}
    across = {"wa": (w + 2) % 4}
    width = x.shape[1] // 2
    barrier = pltpu.get_barrier_semaphore()
    for place in (beside, across):
        pl.semaphore_signal(barrier, inc=1, device_id=place, device_id_type=MESH)
    pl.semaphore_wait(barrier, 2)

    def send(src, dst, where, k):
        copy = pltpu.make_async_remote_copy(
            src_ref=src, dst_ref=dst, send_sem=send_sem.at[k], recv_sem=recv_sem.at[k],
            device_id=where, device_id_type=MESH,
        )
        copy.start()
        return copy

    mine = pl.ds(pl.multiple_of(core * width, width), width)
    theirs = pl.ds(pl.multiple_of((1 - core) * width, width), width)
    one = send(x.at[:, theirs], got, beside, 0)
    one.wait_recv()
    half[...] = x[:, mine] + got[...]
    two = send(half, far, across, 1)
    two.wait_recv()
    out[:, mine] = half[...] + far[...]
    three = send(out.at[:, mine], out.at[:, mine], beside, 2)
    three.wait_recv()
    for copy in (one, two, three):
        copy.wait_send()


def sum_wa(x, collective_id, name):
    rows, columns = x.shape
    return pl.pallas_call(
        sum_wa_kernel,
        out_shape=jax.ShapeDtypeStruct(x.shape, x.dtype),
        in_specs=[pl.BlockSpec(memory_space=pltpu.VMEM)],
        out_specs=pl.BlockSpec(memory_space=pltpu.VMEM),
        scratch_shapes=[pltpu.VMEM((rows, columns // 2), x.dtype)] * 3
        + [pltpu.SemaphoreType.DMA((3,)), pltpu.SemaphoreType.DMA((3,))],
        compiler_params=pltpu.CompilerParams(
            collective_id=collective_id, has_side_effects=True, vmem_limit_bytes=VMEM_LIMIT
        ),
        name=name,
    )(x)


def head_columns(h):
    return pl.ds(pl.multiple_of(h * HD, HD), HD)


class Copies:
    def __init__(self, send_sem, recv_sem):
        self.send_sem, self.recv_sem, self.started = send_sem, recv_sem, []

    def start(self, src, dst, where):
        k = len(self.started)
        copy = pltpu.make_async_remote_copy(
            src_ref=src, dst_ref=dst, send_sem=self.send_sem.at[k],
            recv_sem=self.recv_sem.at[k], device_id=where, device_id_type=MESH,
        )
        copy.start()
        self.started.append(copy)
        return copy

    def finish(self):
        for copy in self.started:
            copy.wait_send()


def greet(places):
    barrier = pltpu.get_barrier_semaphore()
    for place in places:
        pl.semaphore_signal(barrier, inc=1, device_id=place, device_id_type=MESH)
    pl.semaphore_wait(barrier, len(places))


def along_z():
    z = lax.axis_index("sp")
    return [{"sp": (z + d) % 4} for d in (1, 2, 3)]


def vmem_call(kernel, out_shape, operands, scratch, collective_id, name, **params):
    return pl.pallas_call(
        kernel,
        out_shape=out_shape,
        in_specs=[pl.BlockSpec(memory_space=pltpu.VMEM)] * len(operands),
        out_specs=jax.tree.map(lambda _: pl.BlockSpec(memory_space=pltpu.VMEM), out_shape),
        scratch_shapes=scratch,
        compiler_params=pltpu.CompilerParams(
            collective_id=collective_id,
            has_side_effects=collective_id is not None,
            vmem_limit_bytes=VMEM_LIMIT,
        ),
        name=name,
        **params,
    )(*operands)


def project_kernel(normed, wq, wk, wv, cosine, sine, q, k, v):
    for weight, out in ((wq, q), (wk, k)):
        raw = jnp.dot(normed[...], weight[...], preferred_element_type=jnp.float32)
        for h in range(out.shape[1] // HD):
            one = raw[:, h * HD : (h + 1) * HD]
            turned = one * cosine[...] + pltpu.roll(one, HD // 2, 1) * sine[...]
            out[:, h * HD : (h + 1) * HD] = turned.astype(out.dtype)
    raw = jnp.dot(normed[...], wv[...], preferred_element_type=jnp.float32)
    v[...] = raw.astype(v.dtype)


def project(normed, weights, cosine, sine):
    shape = jax.ShapeDtypeStruct((normed.shape[0], weights[0].shape[1]), jnp.bfloat16)
    return vmem_call(
        project_kernel, [shape] * 3, (normed, *weights, cosine, sine), [], None, "project_heads"
    )


def turn_back_kernel(q, k, cosine, sine, q_in, k_in):
    for src, out in ((q, q_in), (k, k_in)):
        for h in range(out.shape[1] // HD):
            one = src[:, h * HD : (h + 1) * HD].astype(jnp.float32)
            turned = one * cosine[...] - pltpu.roll(one, HD // 2, 1) * sine[...]
            out[:, h * HD : (h + 1) * HD] = turned.astype(out.dtype)


def turn_back(q, k, cosine, sine):
    shape = jax.ShapeDtypeStruct(q.shape, jnp.bfloat16)
    return vmem_call(
        turn_back_kernel, [shape] * 2, (q, k, cosine, sine), [], None, "turn_back_heads"
    )


def spread_kernel(q, k, v, q_out, k_out, v_out, send_sem, recv_sem):
    z, xh, y = own_place()
    places = along_z() + [neighbour("y", "A"), neighbour("y", "B"), neighbour("x", "A")]
    greet(places)
    copies = Copies(send_sem, recv_sem)
    arriving = []
    for d in (1, 2, 3):
        there = (z + d) % 4
        cols = head_columns(there)
        for src, dst in (
            (k, k_out.at[z, xh, y]), (v, v_out.at[z, xh, y]), (q, q_out.at[z])
        ):
            arriving.append(copies.start(src.at[:, cols], dst, {"sp": there}))
    k_out[z, xh, y] = k[:, head_columns(z)]
    v_out[z, xh, y] = v[:, head_columns(z)]
    q_out[z] = q[:, head_columns(z)]
    for copy in arriving:
        copy.wait_recv()

    def block(out, xl, place):
        return out.at[:, xl, place]

    def send(out, xl, place, axis, kind):
        where = neighbour(axis, kind)
        return copies.start(block(out, xl, place), block(out, xl, place), where)

    first, across = {}, []
    for out, kind in ((k_out, "A"), (v_out, "B")):
        first[0, kind] = send(out, xh, y, "y", kind)
        across.append(send(out, xh, y, "x", "A"))
    last = []

    def onward(lane, xl):
        first[lane, "A"].wait_recv()
        for place, _ in pair_slots(y, "A"):
            last.append(send(k_out, xl, place, "y", "B"))
        first[lane, "B"].wait_recv()
        for place, _ in pair_slots(y, "B"):
            last.append(send(v_out, xl, place, "y", "A"))

    onward(0, xh)
    for copy in across:
        copy.wait_recv()
    for out, kind in ((k_out, "A"), (v_out, "B")):
        first[1, kind] = send(out, 1 - xh, y, "y", kind)
    onward(1, 1 - xh)
    for copy in last:
        copy.wait_recv()
    copies.finish()


def spread_heads(q, k, v, collective_id):
    rows = q.shape[0]
    own = jax.ShapeDtypeStruct((4, rows, HD), q.dtype)
    every = jax.ShapeDtypeStruct((4, 2, 4, rows, HD), q.dtype)
    sems = [pltpu.SemaphoreType.DMA((21,))] * 2
    return vmem_call(
        spread_kernel, [own, every, every], (q, k, v), sems, collective_id, "spread_heads"
    )


def collect_kernel(dq, dk, dv, q_out, k_out, v_out, *refs):
    bufs, sums, cross = refs[0:2], refs[2:4], refs[4:6]
    own, (send_sem, recv_sem) = refs[6:8], refs[8:]
    z, xh, y = own_place()
    greet(along_z() + [neighbour("y", "A"), neighbour("y", "B"), neighbour("x", "A")])
    copies = Copies(send_sem, recv_sem)
    ins, near, far = (dk, dv), ("A", "B"), ("B", "A")
    flying = {}
    for lane in (1, 0):
        xl = xh if lane == 0 else 1 - xh
        for a in range(2):
            theirs = paired(y, far[a])
            flying[lane, a] = [
                copies.start(ins[a].at[:, xl, src], bufs[a].at[lane, :, dst], neighbour("y", far[a]))
                for src, dst in pair_slots(theirs, near[a])
            ]
    arriving = []
    for d in (1, 2, 3):
        there = (z + d) % 4
        arriving.append(copies.start(dq.at[there], q_out.at[:, head_columns(z)], {"sp": there}))
    q_out[:, head_columns(z)] = dq[z]
    for lane in (1, 0):
        xl = xh if lane == 0 else 1 - xh
        for a in range(2):
            for copy in flying[lane, a]:
                copy.wait_recv()
            slot = slot_in_pair(y, near[a])
            there = paired(y, near[a])

            def add(j, place):
                def one(i, carry):
                    bufs[a][lane, i, j] = bufs[a][lane, i, j] + ins[a][i, xl, place]
                    return carry

                lax.fori_loop(0, 4, one, 0)

            add(1 - slot, there)
            flying[lane, a] = copies.start(
                bufs[a].at[lane, :, 1 - slot], sums[a].at[lane], neighbour("y", near[a])
            )
            add(slot, y)
    for lane in (1, 0):
        for a in range(2):
            flying[lane, a].wait_recv()
            slot = slot_in_pair(y, near[a])

            def more(i, carry):
                sums[a][lane, i] = sums[a][lane, i] + bufs[a][lane, i, slot]
                return carry

            lax.fori_loop(0, 4, more, 0)
            if lane == 1:
                flying["x", a] = copies.start(sums[a].at[1], cross[a], neighbour("x", "A"))
    for a, out in ((0, k_out), (1, v_out)):
        flying["x", a].wait_recv()

        def total(i, carry):
            own[a][i] = sums[a][0, i] + cross[a][i]
            return carry

        lax.fori_loop(0, 4, total, 0)
        for d in (1, 2, 3):
            there = (z + d) % 4
            arriving.append(copies.start(own[a].at[there], out.at[:, head_columns(z)], {"sp": there}))
        out[:, head_columns(z)] = own[a][z]
    for copy in arriving:
        copy.wait_recv()
    copies.finish()


def collect_heads(dq, dk, dv, collective_id):
    rows = dq.shape[1]
    block = (rows, HD)
    shape = jax.ShapeDtypeStruct((rows, 4 * HD), dq.dtype)
    scratch = [
        pltpu.VMEM((*lead, *block), dq.dtype) for lead in ((2, 4, 2), (2, 4), (4,), (4,)) for _ in range(2)
    ]
    sems = [pltpu.SemaphoreType.DMA((21,))] * 2
    return vmem_call(
        collect_kernel, [shape] * 3, (dq, dk, dv), scratch + sems, collective_id, "collect_heads"
    )


def heads_out_kernel(x, out, send_sem, recv_sem):
    z = lax.axis_index("sp")
    greet(along_z())
    copies = Copies(send_sem, recv_sem)
    for d in (1, 2, 3):
        there = (z + d) % 4
        copies.start(x.at[there], out.at[:, head_columns(z)], {"sp": there})
    out[:, head_columns(z)] = x[z]
    for copy in copies.started:
        copy.wait_recv()
    copies.finish()


def heads_in_kernel(x, out, send_sem, recv_sem):
    z = lax.axis_index("sp")
    greet(along_z())
    copies = Copies(send_sem, recv_sem)
    for d in (1, 2, 3):
        there = (z + d) % 4
        copies.start(x.at[:, head_columns(there)], out.at[z], {"sp": there})
    out[z] = x[:, head_columns(z)]
    for copy in copies.started:
        copy.wait_recv()
    copies.finish()


def heads_out(x, collective_id):
    shape = jax.ShapeDtypeStruct((x.shape[1], 4 * HD), x.dtype)
    sems = [pltpu.SemaphoreType.DMA((3,))] * 2
    return vmem_call(heads_out_kernel, shape, (x,), sems, collective_id, "heads_to_tokens")


def heads_in(x, collective_id):
    shape = jax.ShapeDtypeStruct((4, x.shape[0], HD), x.dtype)
    sems = [pltpu.SemaphoreType.DMA((3,))] * 2
    return vmem_call(heads_in_kernel, shape, (x,), sems, collective_id, "tokens_to_heads")


def attend_kernel(q, k, v, attended, exact, probs, scores):
    rows = q.shape[1]
    span = 8 * rows
    first = lax.axis_index("ctx") * rows
    scale = HD ** (-0.5)
    contract = (((1,), (1,)), ((), ()))
    at = 0
    for block in range(4):
        for c in range(block + 1):
            part = lax.dot_general(
                q[block], k[c * span : (c + 1) * span], contract, preferred_element_type=jnp.float32
            ) * scale
            if c == block:
                row = lax.broadcasted_iota(jnp.int32, part.shape, 0)
                col = lax.broadcasted_iota(jnp.int32, part.shape, 1)
                part = jnp.where(col <= row + first, part, MASKED)
            scores[:, c * span : (c + 1) * span] = part
        width = (block + 1) * span
        top = jnp.max(scores[:, :width], axis=1, keepdims=True)
        total = jnp.zeros_like(top)
        for c in range(block + 1):
            part = jnp.exp(scores[:, c * span : (c + 1) * span] - top)
            total = total + jnp.sum(part, axis=1, keepdims=True)
            scores[:, c * span : (c + 1) * span] = part
        scaled = 1.0 / total
        result = jnp.zeros((rows, HD), jnp.float32)
        for c in range(block + 1):
            low = (scores[:, c * span : (c + 1) * span] * scaled).astype(probs.dtype)
            probs[at] = low
            result = result + jnp.dot(
                low, v[c * span : (c + 1) * span], preferred_element_type=jnp.float32
            )
            at += 1
        exact[block] = result
        attended[block] = result.astype(attended.dtype)


def attend(q, k, v):
    rows = q.shape[1]
    out_shape = [
        jax.ShapeDtypeStruct(q.shape, q.dtype),
        jax.ShapeDtypeStruct(q.shape, jnp.float32),
        jax.ShapeDtypeStruct((10, rows, 8 * rows), q.dtype),
    ]
    scratch = [pltpu.VMEM((rows, 32 * rows), jnp.float32)]
    return vmem_call(attend_kernel, out_shape, (q, k, v), scratch, None, "attend")


def attend_back_kernel(q, k, v, probs, grad, exact, dq, dk, dv, dk_sum, dv_sum):
    rows = q.shape[1]
    span = 8 * rows
    scale = HD ** (-0.5)
    at = 0
    for block in range(4):
        low_grad = grad[block]
        delta = jnp.sum(low_grad.astype(jnp.float32) * exact[block], axis=1, keepdims=True)
        total = jnp.zeros((rows, HD), jnp.float32)
        for c in range(block + 1):
            here = slice(c * span, (c + 1) * span)
            low = probs[at]
            back = lax.dot_general(
                low_grad, v[here], (((1,), (1,)), ((), ())), preferred_element_type=jnp.float32
            )
            terms = (low.astype(jnp.float32) * (back - delta)).astype(q.dtype)
            total = total + jnp.dot(terms, k[here], preferred_element_type=jnp.float32)
            over_rows = (((0,), (0,)), ((), ()))
            key_terms = lax.dot_general(
                terms, q[block], over_rows, preferred_element_type=jnp.float32
            )
            value_terms = lax.dot_general(
                low, low_grad, over_rows, preferred_element_type=jnp.float32
            )
            if c == block:
                dk_sum[here] = key_terms
                dv_sum[here] = value_terms
            else:
                dk_sum[here] = dk_sum[here] + key_terms
                dv_sum[here] = dv_sum[here] + value_terms
            at += 1
        dq[block] = (total * scale).astype(dq.dtype)
    for c in range(4):
        here = slice(c * span, (c + 1) * span)
        dk[here] = (dk_sum[here] * scale).astype(dk.dtype)
        dv[here] = dv_sum[here].astype(dv.dtype)


def attend_back(q, k, v, probs, grad, exact):
    out_shape = [jax.ShapeDtypeStruct(x.shape, x.dtype) for x in (q, k, v)]
    scratch = [pltpu.VMEM(k.shape, jnp.float32)] * 2
    return vmem_call(
        attend_back_kernel, out_shape, (q, k, v, probs, grad, exact), scratch, None, "attend_back"
    )


SLOTS = 16


def token_places():
    z, xh, y = own_place()
    w = lax.axis_index("wa")
    return z, xh, y, w // 2, w % 2


def block_device(dz, dx, dy):
    z, xh, y, place, core = token_places()
    there_z, there_x, there_y = (z + dz) % 4, (xh + dx) % 2, (y + dy) % 4
    there = (place + dx) % 2
    where = {"sp": there_z, "ctx": 4 * there_x + there_y, "wa": 2 * there + core}
    return where, there_z * 8 + there_x * 4 + there_y


def greet_blocks():
    barrier = pltpu.get_barrier_semaphore()

    def one(i, carry):
        where, _ = block_device(i // 8, (i // 4) % 2, i % 4)
        pl.semaphore_signal(barrier, inc=1, device_id=where, device_id_type=MESH)
        return carry

    lax.fori_loop(1, 32, one, 0)
    w = lax.axis_index("wa")
    core = w % 2
    for place in (w + 1 - 2 * core, (w + 2) % 4):
        pl.semaphore_signal(barrier, inc=1, device_id={"wa": place}, device_id_type=MESH)
    pl.semaphore_wait(barrier, 33)


def quarter_columns(place, core):
    quarter = D // 4
    return pl.ds(pl.multiple_of(core * 2 * quarter + place * quarter, quarter), quarter)


def dispatch_kernel(count, *refs):
    ins, outs = refs[:count], refs[count : 2 * count]
    out_sem, in_sem, own_sem, send_sem, recv_sem = refs[2 * count :]
    z, xh, y, place, core = token_places()
    w = lax.axis_index("wa")
    beside, across = {"wa": w + 1 - 2 * core}, {"wa": (w + 2) % 4}
    greet_blocks()
    me = z * 8 + xh * 4 + y
    columns = quarter_columns(place, core)
    here = pl.ds(pl.multiple_of(me * SLOTS, SLOTS), SLOTS)
    own = []
    for a in range(count):
        copy = pltpu.make_async_copy(ins[a].at[me], outs[a].at[:, here, columns], own_sem.at[a])
        copy.start()
        own.append(copy)

        def one(i, carry):
            where, block = block_device(i // 8, (i // 4) % 2, i % 4)
            pltpu.make_async_remote_copy(
                src_ref=ins[a].at[block], dst_ref=outs[a].at[:, here, columns],
                send_sem=out_sem.at[a], recv_sem=in_sem.at[a, i // 4],
                device_id=where, device_id_type=MESH,
            ).start()
            return carry

        lax.fori_loop(1, 32, one, 0)

    copies = Copies(send_sem, recv_sem)
    items = [(a, dz, dx) for a in range(count) for dz in range(4) for dx in range(2)]
    items.sort(key=lambda item: (item[0], item[1] + item[2] == 0))
    passed, last = {}, []

    def arrived(i):
        a, dz, dx = items[i]
        rows = pl.ds(pl.multiple_of(((z - dz + 4) % 4 * 8 + (xh + dx) % 2 * 4) * SLOTS, 4 * SLOTS), 4 * SLOTS)
        few = 3 if dz + dx == 0 else 4
        sample = outs[a].at[:, pl.ds(0, few * SLOTS), columns]
        pltpu.make_async_copy(sample, sample, in_sem.at[a, dz * 2 + dx]).wait()
        if dz + dx == 0:
            own[a].wait()
        part = outs[a].at[:, rows, quarter_columns((place + dx) % 2, core)]
        passed[i] = copies.start(part, part, across)
        last.append(copies.start(part, part, beside))

    def from_across(i):
        a, dz, dx = items[i]
        rows = pl.ds(pl.multiple_of(((z - dz + 4) % 4 * 8 + (xh + dx) % 2 * 4) * SLOTS, 4 * SLOTS), 4 * SLOTS)
        passed[i].wait_recv()
        part = outs[a].at[:, rows, quarter_columns((place + dx + 1) % 2, core)]
        last.append(copies.start(part, part, beside))

    for i in range(len(items) + 2):
        if i < len(items):
            arrived(i)
        if i >= 2:
            from_across(i - 2)
    for copy in last:
        copy.wait_recv()
    copies.finish()
    for a in range(count):
        sample = ins[a].at[pl.ds(0, 31)]
        pltpu.make_async_copy(sample, sample, out_sem.at[a]).wait()


def dispatch(arrays, collective_id):
    count = len(arrays)
    shape = jax.ShapeDtypeStruct((2, 32 * SLOTS, D), arrays[0].dtype)
    return pl.pallas_call(
        functools.partial(dispatch_kernel, count),
        out_shape=[shape] * count,
        in_specs=[pl.BlockSpec(memory_space=pl.ANY)] * count,
        out_specs=[pl.BlockSpec(memory_space=pl.ANY)] * count,
        scratch_shapes=[
            pltpu.SemaphoreType.DMA((count,)),
            pltpu.SemaphoreType.DMA((count, 8)),
            pltpu.SemaphoreType.DMA((count,)),
            pltpu.SemaphoreType.DMA((24 * count,)),
            pltpu.SemaphoreType.DMA((24 * count,)),
        ],
        compiler_params=pltpu.CompilerParams(collective_id=collective_id, has_side_effects=True),
        name="dispatch_rows",
    )(*arrays)


def return_kernel(count, *refs):
    ins, outs = refs[:count], refs[count : 2 * count]
    halves, quarters = refs[2 * count : 3 * count], refs[3 * count : 4 * count]
    out_sem, in_sem, send_sem, recv_sem = refs[4 * count :]
    z, xh, y, place, core = token_places()
    w = lax.axis_index("wa")
    beside, across = {"wa": w + 1 - 2 * core}, {"wa": (w + 2) % 4}
    greet_blocks()
    me = z * 8 + xh * 4 + y
    quarter = D // 4
    group = 4 * SLOTS
    mine = pl.ds(pl.multiple_of(core * 2 * quarter, 2 * quarter), 2 * quarter)
    theirs = pl.ds(pl.multiple_of((1 - core) * 2 * quarter, 2 * quarter), 2 * quarter)
    copies = Copies(send_sem, recv_sem)
    items = [(a, dz, dx) for a in range(count) for dz in range(4) for dx in range(2)]
    items.sort(key=lambda item: (item[0], item[1] + item[2] == 0))

    def rows_of(dz, dx):
        return pl.ds(pl.multiple_of(((z + dz) % 4 * 8 + (xh + dx) % 2 * 4) * SLOTS, group), group)

    def kept(dx):
        return pl.ds(pl.multiple_of((place + dx) % 2 * quarter, quarter), quarter)

    def given(dx):
        return pl.ds(pl.multiple_of((place + dx + 1) % 2 * quarter, quarter), quarter)

    paired_up = [
        copies.start(ins[a].at[:, rows_of(dz, dx), theirs], halves[a].at[:, rows_of(dz, dx)], beside)
        for a, dz, dx in items
    ]
    passed = {}

    def add_core(i):
        a, dz, dx = items[i]
        rows = rows_of(dz, dx)
        paired_up[i].wait_recv()
        for e in range(2):
            halves[a][e, rows] = halves[a][e, rows] + ins[a][e, rows, mine]
        passed[i] = copies.start(
            halves[a].at[:, rows, given(dx)], quarters[a].at[:, rows], across
        )

    def add_across(i):
        a, dz, dx = items[i]
        rows = rows_of(dz, dx)
        passed[i].wait_recv()
        for e in range(2):
            quarters[a][e, rows] = quarters[a][e, rows] + halves[a][e, rows, kept(dx)]
        for dy in range(4):
            where, block = block_device(dz, dx, dy)
            part = pl.ds(pl.multiple_of(block * SLOTS, SLOTS), SLOTS)
            if dz + dx + dy == 0:
                outs[a][me] = quarters[a][:, part]
            else:
                pltpu.make_async_remote_copy(
                    src_ref=quarters[a].at[:, part], dst_ref=outs[a].at[me],
                    send_sem=out_sem.at[a], recv_sem=in_sem.at[a],
                    device_id=where, device_id_type=MESH,
                ).start()

    for i in range(len(items) + 1):
        if i < len(items):
            add_core(i)
        if i >= 1:
            add_across(i - 1)
    copies.finish()
    for a in range(count):
        sample = outs[a].at[pl.ds(0, 31)]
        pltpu.make_async_copy(sample, sample, in_sem.at[a]).wait()
        pltpu.make_async_copy(sample, sample, out_sem.at[a]).wait()


def give_back(arrays, collective_id):
    count = len(arrays)
    shape = jax.ShapeDtypeStruct((32, 2, SLOTS, D // 4), arrays[0].dtype)
    rows = 32 * SLOTS
    scratch = [pltpu.VMEM((2, rows, D // 2), arrays[0].dtype)] * count
    scratch += [pltpu.VMEM((2, rows, D // 4), arrays[0].dtype)] * count
    scratch += [pltpu.SemaphoreType.DMA((count,))] * 2 + [pltpu.SemaphoreType.DMA((16 * count,))] * 2
    return vmem_call(
        functools.partial(return_kernel, count), [shape] * count, arrays, scratch, collective_id,
        "return_rows",
    )


def sum_more_kernel(parts, *refs):
    ins, adds, small = refs[:parts], refs[parts : 2 * parts], refs[2 * parts]
    outs, small_out = refs[2 * parts + 1 : 3 * parts + 1], refs[3 * parts + 1]
    got, half, far = (refs[(3 + i) * parts + 2 : (4 + i) * parts + 2] for i in range(3))
    small_got, small_half, small_far, send_sem, recv_sem = refs[6 * parts + 2 :]
    w = lax.axis_index("wa")
    core, place = w % 2, w // 2
    beside, across = {"wa": w + 1 - 2 * core}, {"wa": (w + 2) % 4}
    width = D // 2
    quarter = D // 4
    mine = pl.ds(pl.multiple_of(core * width, width), width)
    theirs = pl.ds(pl.multiple_of((1 - core) * width, width), width)
    own = pl.ds(pl.multiple_of(place * quarter, quarter), quarter)
    greet([beside, across])
    copies = Copies(send_sem, recv_sem)
    one = [copies.start(ins[a].at[:, theirs], got[a], beside) for a in range(parts)]
    one.append(copies.start(small, small_got, beside))
    two = []
    for a in range(parts):
        one[a].wait_recv()
        half[a][...] = ins[a][:, mine] + got[a][...]
        half[a][:, own] = half[a][:, own] + adds[a][...]
        two.append(copies.start(half[a], far[a], across))
    one[parts].wait_recv()
    small_half[...] = small[...] + small_got[...]
    two.append(copies.start(small_half, small_far, across))
    three = []
    for a in range(parts):
        two[a].wait_recv()
        outs[a][:, mine] = half[a][...] + far[a][...]
        three.append(copies.start(outs[a].at[:, mine], outs[a].at[:, mine], beside))
    two[parts].wait_recv()
    small_out[...] = small_half[...] + small_far[...]
    for copy in three:
        copy.wait_recv()
    copies.finish()


def sum_more(arrays, adds, small, collective_id, name):
    parts = len(arrays)
    rows = arrays[0].shape[0]
    dtype = arrays[0].dtype
    scratch = [pltpu.VMEM((rows, D // 2), dtype)] * (3 * parts)
    scratch += [pltpu.VMEM(small.shape, small.dtype)] * 3
    scratch += [pltpu.SemaphoreType.DMA((3 * parts + 2,))] * 2
    out_shape = [jax.ShapeDtypeStruct(x.shape, x.dtype) for x in (*arrays, small)]
    return vmem_call(
        functools.partial(sum_more_kernel, parts), out_shape, (*arrays, *adds, small), scratch,
        collective_id, name,
    )


def over(left, right, dims):
    return lax.dot_general(
        left, right, ((dims[:1], dims[1:]), ((), ())), preferred_element_type=jnp.float32
    )


def swish_parts(pre, lin, act_grads):
    sig = jax.nn.sigmoid(pre)
    swish = pre * sig
    slope = sig * (1.0 + pre * (1.0 - sig))
    return swish * lin, act_grads * lin * slope, act_grads * swish


def expert_kernel(rows, grads, gate, up, down, part, back, gate_grad, up_grad, down_grad):
    low = part.dtype
    x, g = rows[0], grads[0]
    pre = over(x, gate[0], (1, 0))
    lin = over(x, up[0], (1, 0))
    act, pre_grad, lin_grad = swish_parts(pre, lin, over(g, down[0], (1, 1)))
    act, pre_grad, lin_grad = act.astype(low), pre_grad.astype(low), lin_grad.astype(low)
    for at in range(0, D, 512):
        here = slice(at, at + 512)
        part[0, :, here] = over(act, down[0, :, here], (1, 0)).astype(low)
        back[0, :, here] = (
            over(pre_grad, gate[0, here], (1, 1)) + over(lin_grad, up[0, here], (1, 1))
        ).astype(low)
        down_grad[0, :, here] = over(act, g[:, here], (0, 0))
        gate_grad[0, here] = over(x[:, here], pre_grad, (0, 0))
        up_grad[0, here] = over(x[:, here], lin_grad, (0, 0))


def run_experts(rows, grads, gate, up, down):
    operands = (rows, grads, gate, up, down)
    out_shape = [jax.ShapeDtypeStruct(rows.shape, rows.dtype)] * 2
    out_shape += [jax.ShapeDtypeStruct(x.shape, jnp.float32) for x in (gate, up, down)]

    def spec(x):
        return pl.BlockSpec((1, *x.shape[1:]), lambda e: (e, 0, 0))

    return pl.pallas_call(
        expert_kernel,
        grid=(rows.shape[0],),
        out_shape=out_shape,
        in_specs=[spec(x) for x in operands],
        out_specs=[spec(x) for x in out_shape],
        compiler_params=pltpu.CompilerParams(vmem_limit_bytes=VMEM_LIMIT),
        name="run_experts",
    )(*operands)


def shared_kernel(x, g, gate, up, down, part, back, gate_grad, up_grad, down_grad):
    low = part.dtype
    pre = over(x[...], gate[...], (1, 0))
    lin = over(x[...], up[...], (1, 0))
    act, pre_grad, lin_grad = swish_parts(pre, lin, over(g[...], down[...], (1, 0)))
    act, pre_grad, lin_grad = act.astype(low), pre_grad.astype(low), lin_grad.astype(low)
    for at in range(0, D, 512):
        here = slice(at, at + 512)
        part[:, here] = over(act, down[here], (1, 1)).astype(low)
        back[:, here] = (
            over(pre_grad, gate[here], (1, 1)) + over(lin_grad, up[here], (1, 1))
        ).astype(low)
        down_grad[here] = over(g[:, here], act, (0, 0)).astype(low)
        gate_grad[here] = over(x[:, here], pre_grad, (0, 0)).astype(low)
        up_grad[here] = over(x[:, here], lin_grad, (0, 0)).astype(low)


def run_shared(x, g, gate, up, down):
    out_shape = [jax.ShapeDtypeStruct(a.shape, a.dtype) for a in (x, x, gate, up, down)]
    return vmem_call(shared_kernel, out_shape, (x, g, gate, up, down), [], None, "run_shared")


def turned_gather(arrays, axis):
    widths = [a.shape[1] for a in arrays]
    whole = lax.all_gather(jnp.concatenate(arrays, axis=1), axis, axis=0, tiled=True)
    return jnp.split(whole, [sum(widths[:k]) for k in range(1, len(widths))], axis=1)


def rope_tables(positions):
    half_width = HD // 2
    inverse = 1.0 / ROPE_BASE ** (jnp.arange(half_width, dtype=jnp.float32) * 2.0 / HD)
    angles = positions[:, None] * inverse[None, :]
    cosine, sine = jnp.cos(angles), jnp.sin(angles)
    return jnp.concatenate([cosine, cosine], axis=1), jnp.concatenate([-sine, sine], axis=1)


def dot(left, right, over, dtype=jnp.float32, **kept):
    return lax.dot_general(
        left, right, ((over[:1], over[1:]), ((), ())), preferred_element_type=dtype, **kept
    )


def shards(
    tokens,
    cotangent,
    routes,
    attn_gain,
    query_weight,
    key_weight,
    value_weight,
    output_weight,
    mlp_gain,
    router_weight,
    shared_gate,
    shared_up,
    shared_down,
    expert_gate,
    expert_up,
    expert_down,
):
    low = jnp.bfloat16
    local_tokens = tokens.shape[0]
    head_cols = query_weight.shape[1]
    experts_all = router_weight.shape[1]
    groups = ("sp", "ctx")
    device_pos = lax.axis_index("sp") * lax.axis_size("ctx") + lax.axis_index("ctx")
    place, core = lax.axis_index("wa") // 2, lax.axis_index("wa") % 2
    quarter_at = core * (D // 2) + place * (D // 4)

    def quarter(x):
        return lax.dynamic_slice_in_dim(x, quarter_at, D // 4, 1)

    heads = (query_weight, key_weight, value_weight)
    gains = jnp.pad(jnp.stack([attn_gain, mlp_gain], axis=1), ((0, 0), (0, HD - 2)))
    parts = row_parts(heads)
    parts[0].append((3, pl.ds(0, gains.shape[0]), pl.ds(0, HD)))
    full_query, full_key, full_value, full_gains = (
        whole.reshape(D, -1)
        for whole in gather_cube((*heads, gains), parts, 1, "gather_head_weights")
    )
    turned, full_sgate, full_sup, turned_sdown, full_router = turned_gather(
        (
            output_weight.T,
            shared_gate,
            shared_up,
            shared_down.T,
            router_weight,
        ),
        groups,
    )
    gain_one = full_gains[:, 0].astype(jnp.float32)
    gain_two = full_gains[:, 1].astype(jnp.float32)
    tokens_f = tokens.astype(jnp.float32)
    inv_one = lax.rsqrt(jnp.mean(tokens_f * tokens_f, axis=-1, keepdims=True) + EPSILON)
    unit_one = tokens_f * inv_one
    normed = (unit_one * gain_one).astype(low)
    query_pos = device_pos * local_tokens + jnp.arange(local_tokens, dtype=jnp.int32)
    cosine, sine = rope_tables(query_pos.astype(jnp.float32))
    queries, keys, values = project(normed, (full_query, full_key, full_value), cosine, sine)
    head_queries, head_keys, head_values = spread_heads(queries, keys, values, 2)
    head_keys = head_keys.reshape(-1, HD)
    head_values = head_values.reshape(-1, HD)
    head_attended, exact, probs = attend(head_queries, head_keys, head_values)
    attended = heads_out(head_attended, 3)
    attn_part = dot(attended, turned, (1, 1)).astype(low)
    attn_out = sum_wa(attn_part, 4, "sum_attention").astype(jnp.float32)
    hidden_state = tokens_f + attn_out
    inv_two = lax.rsqrt(jnp.mean(hidden_state * hidden_state, axis=-1, keepdims=True) + EPSILON)
    unit_two = hidden_state * inv_two
    mlp_in = (unit_two * gain_two).astype(low)

    logits = dot(mlp_in, full_router, (1, 0))
    logit_exp = jnp.exp(logits - jnp.max(logits, axis=-1, keepdims=True))
    router_probs = logit_exp / jnp.sum(logit_exp, axis=-1, keepdims=True)
    experts = jnp.arange(experts_all, dtype=jnp.int32)
    chosen = jnp.zeros((local_tokens, experts_all), jnp.bool_)
    for j in range(TOP):
        chosen = chosen | (routes[:, j : j + 1] == experts[None, :])
    ids = jnp.arange(local_tokens, dtype=jnp.int32)
    before = (ids[None, :] < ids[:, None]).astype(low)
    rank = dot(before, chosen.astype(low), (1, 0))
    slot_of = jnp.where(chosen, rank, -1.0).astype(low)
    slot_ids = jnp.arange(experts_all * SLOTS, dtype=jnp.int32)
    widen = (experts[:, None] == slot_ids[None, :] // SLOTS).astype(low)
    taken = dot(slot_of, widen, (1, 0)) == (slot_ids % SLOTS).astype(jnp.float32)[None, :]
    probs_high = router_probs.astype(low)
    probs_rest = (router_probs - probs_high.astype(jnp.float32)).astype(low)
    pick = taken.astype(low)
    gate_high = jnp.where(taken, dot(probs_high, widen, (1, 0)), 0.0).astype(low)
    gate_rest = jnp.where(taken, dot(probs_rest, widen, (1, 0)), 0.0).astype(low)
    grad_quarter = quarter(cotangent)
    send_rows = dot(pick, quarter(mlp_in), (0, 0)).astype(low)
    send_grads = (
        dot(gate_high, grad_quarter, (0, 0)) + dot(gate_rest, grad_quarter, (0, 0))
    ).astype(low)
    shared_part, shared_in_part, *mlp_grads = run_shared(
        mlp_in, cotangent, full_sgate, full_sup, turned_sdown
    )
    mlp_grads = [x.reshape(4, 2, 4, x.shape[0] // 32, x.shape[1]) for x in mlp_grads]
    gate_share, up_share, down_share = reduce_cube(
        mlp_grads, row_parts(mlp_grads), 11, "reduce_mlp_grads"
    )
    by_owner = (32, 2, SLOTS, D // 4)
    rows_in, grads_in = dispatch((send_rows.reshape(by_owner), send_grads.reshape(by_owner)), 5)

    expert_part, rows_part, expert_gate_grad, expert_up_grad, expert_down_grad = run_experts(
        rows_in, grads_in, expert_gate, expert_up, expert_down
    )
    returned, rows_back = (
        x.reshape(-1, D // 4) for x in give_back((expert_part, rows_part), 6)
    )
    routed = (dot(gate_high, returned, (1, 0)) + dot(gate_rest, returned, (1, 0))).astype(low)
    routed_in = dot(pick, rows_back, (1, 0)).astype(low)
    slot_grads = jnp.where(taken, dot(grad_quarter, returned, (1, 1)), 0.0)
    prob_part = dot(slot_grads, widen.astype(jnp.float32), (1, 1), precision=PRECISE)
    prob_part = jnp.pad(prob_part, ((0, 0), (0, HD - experts_all)))
    mixed, mixed_in, prob_grads = sum_more(
        (shared_part, shared_in_part), (routed, routed_in), prob_part, 7, "sum_mlp"
    )
    block_out = (hidden_state + mixed.astype(jnp.float32)).astype(low)
    prob_grads = prob_grads[:, :experts_all]
    logit_grads = router_probs * (
        prob_grads - jnp.sum(router_probs * prob_grads, axis=-1, keepdims=True)
    )
    router_in_grad = dot(
        logit_grads, full_router.astype(jnp.float32), (1, 1), precision=PRECISE
    )
    mlp_in_grad = router_in_grad + mixed_in.astype(jnp.float32)
    gain_two_grad = jnp.sum(mlp_in_grad * unit_two, axis=0)
    scaled_two = mlp_in_grad * gain_two
    hidden_grad = cotangent.astype(jnp.float32) + inv_two * (
        scaled_two - unit_two * jnp.mean(scaled_two * unit_two, axis=-1, keepdims=True)
    )
    out_grad = hidden_grad.astype(low)
    router_grad = dot(mlp_in, logit_grads.astype(low), (0, 0))

    attended_grad = dot(out_grad, turned, (1, 0)).astype(low)
    head_grad = heads_in(attended_grad, 8)
    dq, dk, dv = attend_back(head_queries, head_keys, head_values, probs, head_grad, exact)
    by_block = (4, 2, 4, local_tokens, HD)
    query_grads, key_grads, value_in = collect_heads(
        dq, dk.reshape(by_block), dv.reshape(by_block), 9
    )
    query_in, key_in = turn_back(query_grads, key_grads, cosine, sine)
    normed_part = (
        dot(query_in, full_query, (1, 1))
        + dot(key_in, full_key, (1, 1))
        + dot(value_in, full_value, (1, 1))
    ).astype(low)
    normed_grad = sum_wa(normed_part, 10, "sum_normed_grad").astype(jnp.float32)
    gain_one_grad = jnp.sum(normed_grad * unit_one, axis=0)
    scaled_one = normed_grad * gain_one
    tokens_grad = (
        hidden_grad
        + inv_one
        * (scaled_one - unit_one * jnp.mean(scaled_one * unit_one, axis=-1, keepdims=True))
    ).astype(low)

    gain_grads = jnp.stack([gain_one_grad, gain_two_grad], axis=1)
    small_grads = jnp.pad(
        jnp.concatenate([router_grad, gain_grads], axis=1), ((0, 0), (0, HD - 2 - experts_all))
    )

    def by_shard(x):
        return x.astype(low).reshape(4, 2, 4, x.shape[0] // 32, x.shape[1])

    attention_grads = [
        by_shard(dot(left, right, (0, 0)))
        for left, right in (
            (normed, query_in),
            (normed, key_in),
            (normed, value_in),
            (out_grad, attended),
        )
    ]
    parts = whole_parts(attention_grads)
    attention_grads.append(by_shard(small_grads))
    parts[0].append((4, pl.ds(0, attention_grads[4].shape[3]), pl.ds(0, HD)))
    query_share, key_share, value_share, output_share, small_share = reduce_cube(
        attention_grads, parts, 12, "reduce_attention_grads"
    )
    return (
        block_out,
        tokens_grad,
        small_share[:, experts_all],
        query_share,
        key_share,
        value_share,
        output_share.T,
        small_share[:, experts_all + 1],
        small_share[:, :experts_all],
        gate_share,
        up_share,
        down_share.T,
        expert_gate_grad,
        expert_up_grad,
        expert_down_grad,
    )


def solution(mesh):
    placed = (
        P(("sp", "ctx"), None),
        P(("sp", "ctx"), None),
        P(("sp", "ctx"), None),
        P(("sp", "ctx")),
        P(("sp", "ctx"), "wa"),
        P(("sp", "ctx"), "wa"),
        P(("sp", "ctx"), "wa"),
        P("wa", ("sp", "ctx")),
        P(("sp", "ctx")),
        P(("sp", "ctx"), None),
        P(("sp", "ctx"), "wa"),
        P(("sp", "ctx"), "wa"),
        P("wa", ("sp", "ctx")),
        P(("sp", "ctx"), None, "wa"),
        P(("sp", "ctx"), None, "wa"),
        P(("sp", "ctx"), "wa", None),
    )
    return jax.shard_map(
        shards,
        mesh=mesh,
        in_specs=placed,
        out_specs=(
            P(("sp", "ctx"), None),
            P(("sp", "ctx"), None),
            P(("sp", "ctx")),
            P(("sp", "ctx"), "wa"),
            P(("sp", "ctx"), "wa"),
            P(("sp", "ctx"), "wa"),
            P("wa", ("sp", "ctx")),
            P(("sp", "ctx")),
            P(("sp", "ctx"), None),
            P(("sp", "ctx"), "wa"),
            P(("sp", "ctx"), "wa"),
            P("wa", ("sp", "ctx")),
            P(("sp", "ctx"), None, "wa"),
            P(("sp", "ctx"), None, "wa"),
            P(("sp", "ctx"), "wa", None),
        ),
        check_vma=False,
    )
```

```python
import functools

import jax
import jax.numpy as jnp
from jax import lax
from jax.experimental import pallas as pl
from jax.experimental.pallas import tpu as pltpu
from jax.sharding import PartitionSpec as P

D = 2048
HD = 128
TOP = 6


EPSILON = 1e-06
ROPE_BASE = 10000.0
MASKED = -1e30
PRECISE = lax.Precision.HIGHEST


MESH = pl.DeviceIdType.MESH
VMEM_LIMIT = 60 * 1024 * 1024

ORDERS = (
    (("z", "A"), ("z", "B"), ("y", "A"), ("y", "B")),
    (("z", "B"), ("z", "A"), ("y", "B"), ("y", "A")),
    (("y", "A"), ("y", "B"), ("z", "A"), ("z", "B")),
    (("y", "B"), ("y", "A"), ("z", "B"), ("z", "A")),
)


def paired(i, kind):
    return i + 1 - 2 * (i % 2) if kind == "A" else 3 - i


def own_place():
    c = lax.axis_index("ctx")
    return lax.axis_index("sp"), c // 4, c % 4


def neighbour(axis, kind):
    z, xh, y = own_place()
    if axis == "z":
        return {"sp": paired(z, kind)}
    if axis == "y":
        return {"ctx": 4 * xh + paired(y, kind)}
    return {"ctx": 4 * (1 - xh) + y}


def cube_places():
    rings = [neighbour(axis, kind) for axis in ("z", "y") for kind in ("A", "B")]
    return rings + [neighbour("x", "A")]


def pair_slots(i, kind):
    if kind == "A":
        return [(pl.ds((i // 2) * 2, 2), pl.ds(0, 2))]
    return [(pl.ds(i, 1), pl.ds(0, 1)), (pl.ds(3 - i, 1), pl.ds(1, 1))]


def pair_members(i, kind):
    if kind == "A":
        return [(i // 2) * 2, (i // 2) * 2 + 1]
    return [i, 3 - i]


def slot_in_pair(i, kind):
    return i % 2 if kind == "A" else 0

def head_columns(h):
    return pl.ds(pl.multiple_of(h * HD, HD), HD)


class Copies:
    def __init__(self, send_sem, recv_sem):
        self.send_sem, self.recv_sem, self.started = send_sem, recv_sem, []

    def start(self, src, dst, where):
        k = len(self.started)
        copy = pltpu.make_async_remote_copy(
            src_ref=src, dst_ref=dst, send_sem=self.send_sem.at[k],
            recv_sem=self.recv_sem.at[k], device_id=where, device_id_type=MESH,
        )
        copy.start()
        self.started.append(copy)
        return copy

    def finish(self):
        for copy in self.started:
            copy.wait_send()


def run(*programs):
    programs = list(programs)
    while programs:
        programs = [program for program in programs if next(program, None) is not None]


def greet(places):
    barrier = pltpu.get_barrier_semaphore()
    for place in places:
        pl.semaphore_signal(barrier, inc=1, device_id=place, device_id_type=MESH)
    pl.semaphore_wait(barrier, len(places))


def along_z():
    z = lax.axis_index("sp")
    return [{"sp": (z + d) % 4} for d in (1, 2, 3)]


def vmem_call(kernel, out_shape, operands, scratch, collective_id, name, **params):
    return pl.pallas_call(
        kernel,
        out_shape=out_shape,
        in_specs=[pl.BlockSpec(memory_space=pltpu.VMEM)] * len(operands),
        out_specs=jax.tree.map(lambda _: pl.BlockSpec(memory_space=pltpu.VMEM), out_shape),
        scratch_shapes=scratch,
        compiler_params=pltpu.CompilerParams(
            collective_id=collective_id,
            has_side_effects=collective_id is not None,
            vmem_limit_bytes=VMEM_LIMIT,
        ),
        name=name,
        **params,
    )(*operands)

def gather_steps(parts, ins, outs, copies, local_sem):
    z, xh, y = own_place()
    count = len(ins)

    def step(lane, p, s):
        ring1, ring2 = ORDERS[p][0][0], ORDERS[p][2][0]
        where = neighbour(*ORDERS[p][s])
        xl = xh if lane == 0 else 1 - xh
        zs, ys = [pl.ds(z, 1)], [pl.ds(y, 1)]
        full = [pl.ds(0, 4)]
        if s == 1:
            other = [d for d, _ in pair_slots(z if ring1 == "z" else y, ORDERS[p][0][1])]
            zs, ys = (other, ys) if ring1 == "z" else (zs, other)
        if s >= 2:
            zs, ys = (full, ys) if ring1 == "z" else (zs, full)
        if s == 3:
            other = [d for d, _ in pair_slots(z if ring2 == "z" else y, ORDERS[p][2][1])]
            zs, ys = (other, ys) if ring2 == "z" else (zs, other)
        started = []
        for a, rows, cols in parts[p]:
            for zd in zs:
                for yd in ys:
                    place = outs[a].at[zd, pl.ds(xl, 1), yd, rows, cols]
                    started.append(copies.start(place, place, where))
        return started

    local = [
        pltpu.make_async_copy(ins[a], outs[a].at[z, xh, y], local_sem.at[a]) for a in range(count)
    ]
    for copy in local:
        copy.start()
    across = [
        [
            copies.start(
                ins[a].at[rows, cols], outs[a].at[z, xh, y, rows, cols], neighbour("x", "A")
            )
            for a, rows, cols in part
        ]
        for part in parts
    ]
    for copy in local:
        copy.wait()
    flying = {}
    for lane, s in (
        (0, 0), (0, 1), (1, 0), (0, 2), (1, 1), (0, 3), (1, 2), (1, 3), (0, 4), (1, 4)
    ):
        for p in range(4):
            for copy in flying.get((lane, p), across[p] if lane == 1 else []):
                copy.wait_recv()
            flying[lane, p] = step(lane, p, s) if s < 4 else []
        yield True
    copies.finish()


def gather_kernel(parts, count, *refs):
    ins, outs = refs[:count], refs[count : 2 * count]
    send_sem, recv_sem, local_sem = refs[2 * count :]
    greet(cube_places())
    run(gather_steps(parts, ins, outs, Copies(send_sem, recv_sem), local_sem))


def gather_cube(arrays, parts, collective_id, name):
    count = len(arrays)
    copies = 11 * sum(len(part) for part in parts)
    return pl.pallas_call(
        functools.partial(gather_kernel, parts, count),
        out_shape=[jax.ShapeDtypeStruct((4, 2, 4, *a.shape), a.dtype) for a in arrays],
        in_specs=[pl.BlockSpec(memory_space=pl.ANY)] * count,
        out_specs=[pl.BlockSpec(memory_space=pl.ANY)] * count,
        scratch_shapes=[
            pltpu.SemaphoreType.DMA((copies,)),
            pltpu.SemaphoreType.DMA((copies,)),
            pltpu.SemaphoreType.DMA((count,)),
        ],
        compiler_params=pltpu.CompilerParams(collective_id=collective_id, has_side_effects=True),
        name=name,
    )(*arrays)


def entries_of(parts):
    return [(p, *entry) for p in range(4) for entry in parts[p]]


def reduce_steps(parts, ins, outs, bufs, copies):
    entries = entries_of(parts)
    z, xh, y = own_place()
    start = copies.start
    flying = {}

    def first(lane, e):
        p, a, rows, cols = entries[e]
        ring2, near = ORDERS[p][2]
        axis, kind = ORDERS[p][3]
        xl = xh if lane == 0 else 1 - xh
        theirs = paired(z if ring2 == "z" else y, kind)
        copies = []
        for src, dst in pair_slots(theirs, near):
            if ring2 == "z":
                block, place = ins[a].at[src, xl, :, rows, cols], bufs[5 * e].at[lane, dst]
            else:
                block, place = ins[a].at[:, xl, src, rows, cols], bufs[5 * e].at[lane, :, dst]
            copies.append(start(block, place, neighbour(axis, kind)))
        flying[lane, e] = copies

    def second(lane, e):
        p, a, rows, cols = entries[e]
        ring2 = ORDERS[p][2][0]
        axis, kind = ORDERS[p][2]
        xl = xh if lane == 0 else 1 - xh
        mine = z if ring2 == "z" else y
        buf = bufs[5 * e]
        for copy in flying[lane, e]:
            copy.wait_recv()
        slot = slot_in_pair(mine, kind)

        def add(j, place):
            def one(i, carry):
                if ring2 == "z":
                    buf[lane, j, i] = buf[lane, j, i] + ins[a][place, xl, i, rows, cols]
                else:
                    buf[lane, i, j] = buf[lane, i, j] + ins[a][i, xl, place, rows, cols]
                return carry

            lax.fori_loop(0, 4, one, 0)

        add(1 - slot, paired(mine, kind))
        half = buf.at[lane, 1 - slot] if ring2 == "z" else buf.at[lane, :, 1 - slot]
        flying[lane, e] = [start(half, bufs[5 * e + 1].at[lane], neighbour(axis, kind))]
        add(slot, mine)

    def third(lane, e):
        p = entries[e][0]
        ring1, ring2 = ORDERS[p][0][0], ORDERS[p][2][0]
        axis, kind = ORDERS[p][1]
        before, buf = bufs[5 * e], bufs[5 * e + 1]
        for copy in flying[lane, e]:
            copy.wait_recv()
        slot = slot_in_pair(z if ring2 == "z" else y, ORDERS[p][2][1])

        def one(i, carry):
            other = before[lane, slot, i] if ring2 == "z" else before[lane, i, slot]
            buf[lane, i] = buf[lane, i] + other
            return carry

        lax.fori_loop(0, 4, one, 0)
        theirs = paired(z if ring1 == "z" else y, kind)
        flying[lane, e] = [
            start(buf.at[lane, src], bufs[5 * e + 2].at[lane, dst], neighbour(axis, kind))
            for src, dst in pair_slots(theirs, ORDERS[p][0][1])
        ]

    def fourth(lane, e):
        p = entries[e][0]
        ring1 = ORDERS[p][0][0]
        axis, kind = ORDERS[p][0]
        mine = z if ring1 == "z" else y
        before, buf = bufs[5 * e + 1], bufs[5 * e + 2]
        for copy in flying[lane, e]:
            copy.wait_recv()
        slot = slot_in_pair(mine, kind)
        buf[lane, 1 - slot] = buf[lane, 1 - slot] + before[lane, paired(mine, kind)]
        flying[lane, e] = [
            start(buf.at[lane, 1 - slot], bufs[5 * e + 3].at[lane], neighbour(axis, kind))
        ]
        buf[lane, slot] = buf[lane, slot] + before[lane, mine]

    def last(lane, e):
        p, a, rows, cols = entries[e]
        ring1 = ORDERS[p][0][0]
        before, buf = bufs[5 * e + 2], bufs[5 * e + 3]
        for copy in flying[lane, e]:
            copy.wait_recv()
        slot = slot_in_pair(z if ring1 == "z" else y, ORDERS[p][0][1])
        if lane == 1:
            buf[1] = buf[1] + before[1, slot]
            flying["x", e] = start(buf.at[1], bufs[5 * e + 4], neighbour("x", "A"))
        else:
            flying["x", e].wait_recv()
            total = (
                buf[0].astype(jnp.float32)
                + before[0, slot].astype(jnp.float32)
                + bufs[5 * e + 4][...].astype(jnp.float32)
            )
            outs[a][rows, cols] = total.astype(outs[a].dtype)

    for stage in (first, second, third, fourth, last):
        for lane in (1, 0):
            for e in range(len(entries)):
                stage(lane, e)
            yield True
    copies.finish()


def reduce_kernel(parts, count, *refs):
    size = 5 * len(entries_of(parts))
    ins, outs = refs[:count], refs[count : 2 * count]
    bufs = refs[2 * count : 2 * count + size]
    greet(cube_places())
    run(reduce_steps(parts, ins, outs, bufs, Copies(*refs[2 * count + size :])))


def reduce_scratch(arrays, parts):
    scratch = []
    for p in range(4):
        pair = (2, 4) if ORDERS[p][2][0] == "z" else (4, 2)
        for a, rows, cols in parts[p]:
            for lead in ((2, *pair), (2, 4), (2, 2), (2,), ()):
                scratch.append(pltpu.VMEM((*lead, rows.size, cols.size), arrays[a].dtype))
    copies = 13 * sum(len(part) for part in parts)
    return scratch + [pltpu.SemaphoreType.DMA((copies,))] * 2


def reduce_cube(arrays, parts, collective_id, name, dtype=jnp.float32):
    count = len(arrays)
    scratch = reduce_scratch(arrays, parts)
    return pl.pallas_call(
        functools.partial(reduce_kernel, parts, count),
        out_shape=[jax.ShapeDtypeStruct(a.shape[3:], dtype) for a in arrays],
        in_specs=[pl.BlockSpec(memory_space=pltpu.VMEM)] * count,
        out_specs=[pl.BlockSpec(memory_space=pltpu.VMEM)] * count,
        scratch_shapes=scratch,
        compiler_params=pltpu.CompilerParams(
            collective_id=collective_id, has_side_effects=True, vmem_limit_bytes=VMEM_LIMIT
        ),
        name=name,
    )(*arrays)


def row_parts(arrays):
    parts = []
    for p in range(4):
        part = []
        for a, array in enumerate(arrays):
            rows, columns = array.shape[-2:]
            part.append((a, pl.ds(p * rows // 4, rows // 4), pl.ds(0, columns)))
        parts.append(part)
    return parts


def whole_parts(arrays):
    return [[(a, pl.ds(0, x.shape[-2]), pl.ds(0, x.shape[-1]))] for a, x in enumerate(arrays)]


def half_parts(arrays):
    return [
        [(a, pl.ds(0, x.shape[-2]), pl.ds(h * x.shape[-1] // 2, x.shape[-1] // 2))]
        for a, x in enumerate(arrays)
        for h in range(2)
    ]


def wa_places():
    w = lax.axis_index("wa")
    return [{"wa": w + 1 - 2 * (w % 2)}, {"wa": (w + 2) % 4}]


def sum_wa_steps(x, out, half, got, far, copies):
    core = lax.axis_index("wa") % 2
    beside, across = wa_places()
    width = x.shape[1] // 2
    mine = pl.ds(pl.multiple_of(core * width, width), width)
    theirs = pl.ds(pl.multiple_of((1 - core) * width, width), width)
    one = copies.start(x.at[:, theirs], got, beside)
    yield True
    one.wait_recv()
    half[...] = x[:, mine] + got[...]
    two = copies.start(half, far, across)
    yield True
    two.wait_recv()
    out[:, mine] = half[...] + far[...]
    three = copies.start(out.at[:, mine], out.at[:, mine], beside)
    yield True
    three.wait_recv()
    copies.finish()


def sum_wa_kernel(x, out, half, got, far, send_sem, recv_sem):
    greet(wa_places())
    run(sum_wa_steps(x, out, half, got, far, Copies(send_sem, recv_sem)))


def sum_wa(x, collective_id, name):
    rows, columns = x.shape
    return pl.pallas_call(
        sum_wa_kernel,
        out_shape=jax.ShapeDtypeStruct(x.shape, x.dtype),
        in_specs=[pl.BlockSpec(memory_space=pltpu.VMEM)],
        out_specs=pl.BlockSpec(memory_space=pltpu.VMEM),
        scratch_shapes=[pltpu.VMEM((rows, columns // 2), x.dtype)] * 3
        + [pltpu.SemaphoreType.DMA((3,)), pltpu.SemaphoreType.DMA((3,))],
        compiler_params=pltpu.CompilerParams(
            collective_id=collective_id, has_side_effects=True, vmem_limit_bytes=VMEM_LIMIT
        ),
        name=name,
    )(x)

def project_kernel(normed, wq, wk, wv, cosine, sine, q, k, v):
    for weight, out in ((wq, q), (wk, k)):
        raw = jnp.dot(normed[...], weight[...], preferred_element_type=jnp.float32)
        for h in range(out.shape[1] // HD):
            one = raw[:, h * HD : (h + 1) * HD]
            turned = one * cosine[...] + pltpu.roll(one, HD // 2, 1) * sine[...]
            out[:, h * HD : (h + 1) * HD] = turned.astype(out.dtype)
    raw = jnp.dot(normed[...], wv[...], preferred_element_type=jnp.float32)
    v[...] = raw.astype(v.dtype)


def project(normed, weights, cosine, sine):
    shape = jax.ShapeDtypeStruct((normed.shape[0], weights[0].shape[1]), jnp.bfloat16)
    return vmem_call(
        project_kernel, [shape] * 3, (normed, *weights, cosine, sine), [], None, "project_heads"
    )


def turn_back_kernel(q, k, cosine, sine, q_in, k_in):
    for src, out in ((q, q_in), (k, k_in)):
        for h in range(out.shape[1] // HD):
            one = src[:, h * HD : (h + 1) * HD].astype(jnp.float32)
            turned = one * cosine[...] - pltpu.roll(one, HD // 2, 1) * sine[...]
            out[:, h * HD : (h + 1) * HD] = turned.astype(out.dtype)


def turn_back(q, k, cosine, sine):
    shape = jax.ShapeDtypeStruct(q.shape, jnp.bfloat16)
    return vmem_call(
        turn_back_kernel, [shape] * 2, (q, k, cosine, sine), [], None, "turn_back_heads"
    )


def spread_kernel(q, k, v, q_out, k_out, v_out, send_sem, recv_sem):
    z, xh, y = own_place()
    places = along_z() + [neighbour("y", "A"), neighbour("y", "B"), neighbour("x", "A")]
    greet(places)
    copies = Copies(send_sem, recv_sem)
    arriving = []
    for d in (1, 2, 3):
        there = (z + d) % 4
        cols = head_columns(there)
        for src, dst in (
            (k, k_out.at[z, xh, y]), (v, v_out.at[z, xh, y]), (q, q_out.at[z])
        ):
            arriving.append(copies.start(src.at[:, cols], dst, {"sp": there}))
    k_out[z, xh, y] = k[:, head_columns(z)]
    v_out[z, xh, y] = v[:, head_columns(z)]
    q_out[z] = q[:, head_columns(z)]
    for copy in arriving:
        copy.wait_recv()

    def block(out, xl, place):
        return out.at[:, xl, place]

    def send(out, xl, place, axis, kind):
        where = neighbour(axis, kind)
        return copies.start(block(out, xl, place), block(out, xl, place), where)

    first, across = {}, []
    for out, kind in ((k_out, "A"), (v_out, "B")):
        first[0, kind] = send(out, xh, y, "y", kind)
        across.append(send(out, xh, y, "x", "A"))
    last = []

    def onward(lane, xl):
        first[lane, "A"].wait_recv()
        for place, _ in pair_slots(y, "A"):
            last.append(send(k_out, xl, place, "y", "B"))
        first[lane, "B"].wait_recv()
        for place, _ in pair_slots(y, "B"):
            last.append(send(v_out, xl, place, "y", "A"))

    onward(0, xh)
    for copy in across:
        copy.wait_recv()
    for out, kind in ((k_out, "A"), (v_out, "B")):
        first[1, kind] = send(out, 1 - xh, y, "y", kind)
    onward(1, 1 - xh)
    for copy in last:
        copy.wait_recv()
    copies.finish()


def spread_heads(q, k, v, collective_id):
    rows = q.shape[0]
    own = jax.ShapeDtypeStruct((4, rows, HD), q.dtype)
    every = jax.ShapeDtypeStruct((4, 2, 4, rows, HD), q.dtype)
    sems = [pltpu.SemaphoreType.DMA((21,))] * 2
    return vmem_call(
        spread_kernel, [own, every, every], (q, k, v), sems, collective_id, "spread_heads"
    )


def collect_kernel(dq, dk, dv, q_out, k_out, v_out, *refs):
    bufs, sums, cross = refs[0:2], refs[2:4], refs[4:6]
    own, (send_sem, recv_sem) = refs[6:8], refs[8:]
    z, xh, y = own_place()
    greet(along_z() + [neighbour("y", "A"), neighbour("y", "B"), neighbour("x", "A")])
    copies = Copies(send_sem, recv_sem)
    ins, near, far = (dk, dv), ("A", "B"), ("B", "A")
    flying = {}
    for lane in (1, 0):
        xl = xh if lane == 0 else 1 - xh
        for a in range(2):
            theirs = paired(y, far[a])
            flying[lane, a] = [
                copies.start(ins[a].at[:, xl, src], bufs[a].at[lane, :, dst], neighbour("y", far[a]))
                for src, dst in pair_slots(theirs, near[a])
            ]
    arriving = []
    for d in (1, 2, 3):
        there = (z + d) % 4
        arriving.append(copies.start(dq.at[there], q_out.at[:, head_columns(z)], {"sp": there}))
    q_out[:, head_columns(z)] = dq[z]
    for lane in (1, 0):
        xl = xh if lane == 0 else 1 - xh
        for a in range(2):
            for copy in flying[lane, a]:
                copy.wait_recv()
            slot = slot_in_pair(y, near[a])
            there = paired(y, near[a])

            def add(j, place):
                def one(i, carry):
                    bufs[a][lane, i, j] = bufs[a][lane, i, j] + ins[a][i, xl, place]
                    return carry

                lax.fori_loop(0, 4, one, 0)

            add(1 - slot, there)
            flying[lane, a] = copies.start(
                bufs[a].at[lane, :, 1 - slot], sums[a].at[lane], neighbour("y", near[a])
            )
            add(slot, y)
    for lane in (1, 0):
        for a in range(2):
            flying[lane, a].wait_recv()
            slot = slot_in_pair(y, near[a])

            def more(i, carry):
                sums[a][lane, i] = sums[a][lane, i] + bufs[a][lane, i, slot]
                return carry

            lax.fori_loop(0, 4, more, 0)
            if lane == 1:
                flying["x", a] = copies.start(sums[a].at[1], cross[a], neighbour("x", "A"))
    for a, out in ((0, k_out), (1, v_out)):
        flying["x", a].wait_recv()

        def total(i, carry):
            own[a][i] = sums[a][0, i] + cross[a][i]
            return carry

        lax.fori_loop(0, 4, total, 0)
        for d in (1, 2, 3):
            there = (z + d) % 4
            arriving.append(copies.start(own[a].at[there], out.at[:, head_columns(z)], {"sp": there}))
        out[:, head_columns(z)] = own[a][z]
    for copy in arriving:
        copy.wait_recv()
    copies.finish()


def collect_heads(dq, dk, dv, collective_id):
    rows = dq.shape[1]
    block = (rows, HD)
    shape = jax.ShapeDtypeStruct((rows, 4 * HD), dq.dtype)
    scratch = [
        pltpu.VMEM((*lead, *block), dq.dtype) for lead in ((2, 4, 2), (2, 4), (4,), (4,)) for _ in range(2)
    ]
    sems = [pltpu.SemaphoreType.DMA((21,))] * 2
    return vmem_call(
        collect_kernel, [shape] * 3, (dq, dk, dv), scratch + sems, collective_id, "collect_heads"
    )


def heads_out_kernel(x, out, send_sem, recv_sem):
    z = lax.axis_index("sp")
    greet(along_z())
    copies = Copies(send_sem, recv_sem)
    for d in (1, 2, 3):
        there = (z + d) % 4
        copies.start(x.at[there], out.at[:, head_columns(z)], {"sp": there})
    out[:, head_columns(z)] = x[z]
    for copy in copies.started:
        copy.wait_recv()
    copies.finish()


def heads_in_kernel(x, out, send_sem, recv_sem):
    z = lax.axis_index("sp")
    greet(along_z())
    copies = Copies(send_sem, recv_sem)
    for d in (1, 2, 3):
        there = (z + d) % 4
        copies.start(x.at[:, head_columns(there)], out.at[z], {"sp": there})
    out[z] = x[:, head_columns(z)]
    for copy in copies.started:
        copy.wait_recv()
    copies.finish()


def heads_out(x, collective_id):
    shape = jax.ShapeDtypeStruct((x.shape[1], 4 * HD), x.dtype)
    sems = [pltpu.SemaphoreType.DMA((3,))] * 2
    return vmem_call(heads_out_kernel, shape, (x,), sems, collective_id, "heads_to_tokens")


def heads_in(x, collective_id):
    shape = jax.ShapeDtypeStruct((4, x.shape[0], HD), x.dtype)
    sems = [pltpu.SemaphoreType.DMA((3,))] * 2
    return vmem_call(heads_in_kernel, shape, (x,), sems, collective_id, "tokens_to_heads")


def attend_kernel(q, k, v, attended, exact, probs, scores):
    rows = q.shape[1]
    span = 8 * rows
    first = lax.axis_index("ctx") * rows
    scale = HD ** (-0.5)
    contract = (((1,), (1,)), ((), ()))
    at = 0
    for block in range(4):
        for c in range(block + 1):
            part = lax.dot_general(
                q[block], k[c * span : (c + 1) * span], contract, preferred_element_type=jnp.float32
            ) * scale
            if c == block:
                row = lax.broadcasted_iota(jnp.int32, part.shape, 0)
                col = lax.broadcasted_iota(jnp.int32, part.shape, 1)
                part = jnp.where(col <= row + first, part, MASKED)
            scores[:, c * span : (c + 1) * span] = part
        width = (block + 1) * span
        top = jnp.max(scores[:, :width], axis=1, keepdims=True)
        total = jnp.zeros_like(top)
        for c in range(block + 1):
            part = jnp.exp(scores[:, c * span : (c + 1) * span] - top)
            total = total + jnp.sum(part, axis=1, keepdims=True)
            scores[:, c * span : (c + 1) * span] = part
        scaled = 1.0 / total
        result = jnp.zeros((rows, HD), jnp.float32)
        for c in range(block + 1):
            low = (scores[:, c * span : (c + 1) * span] * scaled).astype(probs.dtype)
            probs[at] = low
            result = result + jnp.dot(
                low, v[c * span : (c + 1) * span], preferred_element_type=jnp.float32
            )
            at += 1
        exact[block] = result
        attended[block] = result.astype(attended.dtype)


def attend(q, k, v):
    rows = q.shape[1]
    out_shape = [
        jax.ShapeDtypeStruct(q.shape, q.dtype),
        jax.ShapeDtypeStruct(q.shape, jnp.float32),
        jax.ShapeDtypeStruct((10, rows, 8 * rows), q.dtype),
    ]
    scratch = [pltpu.VMEM((rows, 32 * rows), jnp.float32)]
    return vmem_call(attend_kernel, out_shape, (q, k, v), scratch, None, "attend")


def attend_back_kernel(q, k, v, probs, grad, exact, dq, dk, dv, dk_sum, dv_sum):
    rows = q.shape[1]
    span = 8 * rows
    scale = HD ** (-0.5)
    at = 0
    for block in range(4):
        low_grad = grad[block]
        delta = jnp.sum(low_grad.astype(jnp.float32) * exact[block], axis=1, keepdims=True)
        total = jnp.zeros((rows, HD), jnp.float32)
        for c in range(block + 1):
            here = slice(c * span, (c + 1) * span)
            low = probs[at]
            back = lax.dot_general(
                low_grad, v[here], (((1,), (1,)), ((), ())), preferred_element_type=jnp.float32
            )
            terms = (low.astype(jnp.float32) * (back - delta)).astype(q.dtype)
            total = total + jnp.dot(terms, k[here], preferred_element_type=jnp.float32)
            over_rows = (((0,), (0,)), ((), ()))
            key_terms = lax.dot_general(
                terms, q[block], over_rows, preferred_element_type=jnp.float32
            )
            value_terms = lax.dot_general(
                low, low_grad, over_rows, preferred_element_type=jnp.float32
            )
            if c == block:
                dk_sum[here] = key_terms
                dv_sum[here] = value_terms
            else:
                dk_sum[here] = dk_sum[here] + key_terms
                dv_sum[here] = dv_sum[here] + value_terms
            at += 1
        dq[block] = (total * scale).astype(dq.dtype)
    for c in range(4):
        here = slice(c * span, (c + 1) * span)
        dk[here] = (dk_sum[here] * scale).astype(dk.dtype)
        dv[here] = dv_sum[here].astype(dv.dtype)


def attend_back(q, k, v, probs, grad, exact):
    out_shape = [jax.ShapeDtypeStruct(x.shape, x.dtype) for x in (q, k, v)]
    scratch = [pltpu.VMEM(k.shape, jnp.float32)] * 2
    return vmem_call(
        attend_back_kernel, out_shape, (q, k, v, probs, grad, exact), scratch, None, "attend_back"
    )

SLOTS = 16
GROUP_ORDER = ((0, 1), (1, 0), (3, 0), (1, 1), (3, 1), (2, 0), (2, 1), (0, 0))
SENT_AHEAD = 4


def token_places():
    z, xh, y = own_place()
    w = lax.axis_index("wa")
    return z, xh, y, w // 2, w % 2


def block_device(dz, dx, dy):
    z, xh, y, place, core = token_places()
    there_z, there_x, there_y = (z + dz) % 4, (xh + dx) % 2, (y + dy) % 4
    there = (place + dx) % 2
    where = {"sp": there_z, "ctx": 4 * there_x + there_y, "wa": 2 * there + core}
    return where, there_z * 8 + there_x * 4 + there_y


def greet_blocks(others):
    barrier = pltpu.get_barrier_semaphore()

    def one(i, carry):
        where, _ = block_device(i // 8, (i // 4) % 2, i % 4)
        pl.semaphore_signal(barrier, inc=1, device_id=where, device_id_type=MESH)
        return carry

    lax.fori_loop(1, 32, one, 0)
    others = wa_places() + others
    for place in others:
        pl.semaphore_signal(barrier, inc=1, device_id=place, device_id_type=MESH)
    pl.semaphore_wait(barrier, 31 + len(others))


def quarter_columns(place, core):
    quarter = D // 4
    return pl.ds(pl.multiple_of(core * 2 * quarter + place * quarter, quarter), quarter)


def dispatch_steps(ins, outs, out_sem, in_sem, own_sem, copies):
    count = len(ins)
    z, xh, y, place, core = token_places()
    beside, across = wa_places()
    me = z * 8 + xh * 4 + y
    columns = quarter_columns(place, core)
    here = pl.ds(pl.multiple_of(me * SLOTS, SLOTS), SLOTS)
    own = [
        pltpu.make_async_copy(ins[a].at[me], outs[a].at[:, here, columns], own_sem.at[a])
        for a in range(count)
    ]
    for copy in own:
        copy.start()
    items = [(a, dz, dx) for a in range(count) for dz, dx in GROUP_ORDER]
    passed, last = {}, []

    def send(i):
        a, dz, dx = items[i]

        def one(dy, carry):
            where, block = block_device(dz, dx, dy)
            pltpu.make_async_remote_copy(
                src_ref=ins[a].at[block], dst_ref=outs[a].at[:, here, columns],
                send_sem=out_sem.at[a], recv_sem=in_sem.at[a, dz * 2 + dx],
                device_id=where, device_id_type=MESH,
            ).start()
            return carry

        lax.fori_loop(1 if dz + dx == 0 else 0, 4, one, 0)

    def rows_of(dz, dx):
        first = ((z - dz + 4) % 4 * 8 + (xh + dx) % 2 * 4) * SLOTS
        return pl.ds(pl.multiple_of(first, 4 * SLOTS), 4 * SLOTS)

    def arrived(i):
        a, dz, dx = items[i]
        few = 3 if dz + dx == 0 else 4
        sample = outs[a].at[:, pl.ds(0, few * SLOTS), columns]
        pltpu.make_async_copy(sample, sample, in_sem.at[a, dz * 2 + dx]).wait()
        if dz + dx == 0:
            own[a].wait()
        part = outs[a].at[:, rows_of(dz, dx), quarter_columns((place + dx) % 2, core)]
        passed[i] = copies.start(part, part, across)
        last.append(copies.start(part, part, beside))

    def from_across(i):
        a, dz, dx = items[i]
        passed[i].wait_recv()
        part = outs[a].at[:, rows_of(dz, dx), quarter_columns((place + dx + 1) % 2, core)]
        last.append(copies.start(part, part, beside))

    for i in range(SENT_AHEAD):
        send(i)
    yield True
    for i in range(len(items) + 2):
        if i < len(items):
            arrived(i)
            if i + SENT_AHEAD < len(items):
                send(i + SENT_AHEAD)
        if i >= 2:
            from_across(i - 2)
        yield True
    for copy in last:
        copy.wait_recv()
    copies.finish()
    for a in range(count):
        sample = ins[a].at[pl.ds(0, 31)]
        pltpu.make_async_copy(sample, sample, out_sem.at[a]).wait()


def shared_step(width):
    return -(-width // HD) * HD


def shared_steps(x, g, weights, whole, first, part, back, gate_grad, up_grad, down_grad, sem):
    low = part.dtype
    width = gate_grad.shape[1]
    step = shared_step(width)
    gate, up, down = (slice(k * step, k * step + width) for k in range(3))
    load = pltpu.make_async_copy(whole.at[:, pl.ds(first, weights.shape[1])], weights, sem)
    load.start()
    yield True
    load.wait()
    pre = over(x[...], weights[:, gate], (1, 0))
    yield True
    lin = over(x[...], weights[:, up], (1, 0))
    yield True
    act, pre_grad, lin_grad = swish_parts(pre, lin, over(g[...], weights[:, down], (1, 0)))
    act, pre_grad, lin_grad = act.astype(low), pre_grad.astype(low), lin_grad.astype(low)
    yield True
    for at in range(0, D, 512):
        here = slice(at, at + 512)
        part[:, here] = over(act, weights[here, down], (1, 1)).astype(low)
        back[:, here] = (
            over(pre_grad, weights[here, gate], (1, 1)) + over(lin_grad, weights[here, up], (1, 1))
        ).astype(low)
        yield True
        down_grad[here] = over(g[:, here], act, (0, 0)).astype(low)
        gate_grad[here] = over(x[:, here], pre_grad, (0, 0)).astype(low)
        up_grad[here] = over(x[:, here], lin_grad, (0, 0)).astype(low)
        yield True


def dispatch_kernel(first, *refs):
    ins, (x, g, whole), outs = refs[:2], refs[2:5], refs[5:7]
    results, weights, load_sem = refs[7:12], refs[12], refs[13]
    out_sem, in_sem, own_sem, *sems = refs[14:]
    greet_blocks([])
    moving = dispatch_steps(ins, outs, out_sem, in_sem, own_sem, Copies(*sems))
    computing = shared_steps(x, g, weights, whole, first, *results, load_sem)
    run(moving, computing)


def dispatch(arrays, x, g, whole, first, width, collective_id):
    low = x.dtype
    rows = jax.ShapeDtypeStruct((2, 32 * SLOTS, D), low)
    grad = jax.ShapeDtypeStruct((D, width), low)
    anywhere, vmem = pl.BlockSpec(memory_space=pl.ANY), pl.BlockSpec(memory_space=pltpu.VMEM)
    return pl.pallas_call(
        functools.partial(dispatch_kernel, first),
        out_shape=[rows] * 2 + [jax.ShapeDtypeStruct(x.shape, low)] * 2 + [grad] * 3,
        in_specs=[anywhere] * 2 + [vmem] * 2 + [anywhere],
        out_specs=[anywhere] * 2 + [vmem] * 5,
        scratch_shapes=[
            pltpu.VMEM((D, 3 * shared_step(width)), low),
            pltpu.SemaphoreType.DMA,
            pltpu.SemaphoreType.DMA((2,)),
            pltpu.SemaphoreType.DMA((2, 8)),
            pltpu.SemaphoreType.DMA((2,)),
            pltpu.SemaphoreType.DMA((48,)),
            pltpu.SemaphoreType.DMA((48,)),
        ],
        compiler_params=pltpu.CompilerParams(
            collective_id=collective_id, has_side_effects=True, vmem_limit_bytes=VMEM_LIMIT
        ),
        name="dispatch_rows",
    )(*arrays, x, g, whole)


def expert_steps(hbm, held, part, back, kept, load_sem, finished):
    low = part.dtype
    loads = [
        [pltpu.make_async_copy(src.at[e], dst.at[e], load_sem.at[e, k]) for k, (src, dst) in enumerate(zip(hbm, held))]
        for e in range(2)
    ]
    for load in loads[0] + loads[1]:
        load.start()
    yield True
    rows, grads, gate, up, down = held
    for e in range(2):
        for load in loads[e]:
            load.wait()
        x, g = rows[e], grads[e]
        pre = over(x, gate[e], (1, 1))
        lin = over(x, up[e], (1, 1))
        yield True
        act, pre_grad, lin_grad = swish_parts(pre, lin, over(g, down[e], (1, 1)))
        act, pre_grad, lin_grad = act.astype(low), pre_grad.astype(low), lin_grad.astype(low)
        kept[0][e], kept[1][e], kept[2][e] = act, pre_grad, lin_grad
        yield True
        for at in range(0, D, 512):
            here = slice(at, at + 512)
            part[e, :, here] = over(act, down[e, :, here], (1, 0)).astype(low)
            back[e, :, here] = (
                over(pre_grad, gate[e, :, here], (1, 0)) + over(lin_grad, up[e, :, here], (1, 0))
            ).astype(low)
            if at + 512 == D:
                finished(e)
            yield True


def return_steps(ins, outs, halves, quarters, out_sem, in_sem, copies):
    z, xh, y, place, core = token_places()
    beside, across = wa_places()
    me = z * 8 + xh * 4 + y
    quarter = D // 4
    group = 4 * SLOTS
    mine = pl.ds(pl.multiple_of(core * 2 * quarter, 2 * quarter), 2 * quarter)
    theirs = pl.ds(pl.multiple_of((1 - core) * 2 * quarter, 2 * quarter), 2 * quarter)
    items = [(e, a, dz, dx) for e in range(2) for a in range(2) for dz, dx in GROUP_ORDER]
    paired_up, passed = {}, {}

    def finished(e):
        for a in range(2):
            paired_up[e, a] = copies.start(ins[a].at[e, :, theirs], halves[a].at[e], beside)

    def rows_of(dz, dx):
        return pl.ds(pl.multiple_of(((z + dz) % 4 * 8 + (xh + dx) % 2 * 4) * SLOTS, group), group)

    def kept(dx):
        return pl.ds(pl.multiple_of((place + dx) % 2 * quarter, quarter), quarter)

    def given(dx):
        return pl.ds(pl.multiple_of((place + dx + 1) % 2 * quarter, quarter), quarter)

    def add_core(i):
        e, a, dz, dx = items[i]
        rows = rows_of(dz, dx)
        if i % 8 == 0:
            paired_up[e, a].wait_recv()
        halves[a][e, rows] = halves[a][e, rows] + ins[a][e, rows, mine]
        passed[i] = copies.start(
            halves[a].at[e, rows, given(dx)], quarters[a].at[e, rows], across
        )

    def add_across(i):
        e, a, dz, dx = items[i]
        rows = rows_of(dz, dx)
        passed[i].wait_recv()
        quarters[a][e, rows] = quarters[a][e, rows] + halves[a][e, rows, kept(dx)]
        if dz + dx == 0:
            outs[a][me, e] = quarters[a][e, pl.ds(pl.multiple_of(me * SLOTS, SLOTS), SLOTS)]

        def one(dy, carry):
            where, block = block_device(dz, dx, dy)
            part = pl.ds(pl.multiple_of(block * SLOTS, SLOTS), SLOTS)
            pltpu.make_async_remote_copy(
                src_ref=quarters[a].at[e, part], dst_ref=outs[a].at[me, e],
                send_sem=out_sem.at[a], recv_sem=in_sem.at[a],
                device_id=where, device_id_type=MESH,
            ).start()
            return carry

        lax.fori_loop(1 if dz + dx == 0 else 0, 4, one, 0)

    def steps():
        for i in range(len(items) + 1):
            if i < len(items):
                add_core(i)
            if i >= 1:
                add_across(i - 1)
            yield True
        copies.finish()
        for a in range(2):
            sample = outs[a].at[pl.ds(0, 31)]
            pltpu.make_async_copy(sample, sample, in_sem.at[a]).wait()
            pltpu.make_async_copy(sample, sample, out_sem.at[a]).wait()

    return finished, steps()


EXPERT_ORDER = "RRXXXXXXX" + "TXTTXTTXTTXTTXTTXTTXT" + "TTTRTTTRTTRTTRTTRTTRTTRT"


def expert_kernel(parts, count, *refs):
    hbm, summed, refs = refs[:5], refs[5 : 5 + count], refs[5 + count :]
    outs, shares, kept, refs = refs[:2], refs[2 : 2 + count], refs[2 + count : 5 + count], refs[5 + count :]
    held, (part, back), halves, quarters = refs[:5], refs[5:7], refs[7:9], refs[9:11]
    load_sem, out_sem, in_sem, send_sem, recv_sem = refs[11:16]
    bufs, more = refs[16:-2], refs[-2:]
    greet_blocks([neighbour("x", "A")])
    finished, returning = return_steps(
        (part, back), outs, halves, quarters, out_sem, in_sem, Copies(send_sem, recv_sem)
    )
    computing = expert_steps(hbm, held, part, back, kept, load_sem, finished)
    reducing = reduce_steps(parts, summed, shares, bufs, Copies(*more))
    for turn in EXPERT_ORDER:
        next({"R": reducing, "X": computing, "T": returning}[turn], None)
    run(returning, reducing)


def run_experts(operands, summed, collective_id):
    rows = 32 * SLOTS
    low = operands[0].dtype
    hidden = operands[2].shape[1]
    parts = row_parts(summed)
    out_shape = [jax.ShapeDtypeStruct((32, 2, SLOTS, D // 4), low)] * 2
    out_shape += [jax.ShapeDtypeStruct(x.shape[3:], jnp.float32) for x in summed]
    out_shape += [jax.ShapeDtypeStruct((2, rows, hidden), low)] * 3
    scratch = [pltpu.VMEM(x.shape, low) for x in operands]
    scratch += [pltpu.VMEM((2, rows, D), low)] * 2
    scratch += [pltpu.VMEM((2, rows, D // 2), low)] * 2 + [pltpu.VMEM((2, rows, D // 4), low)] * 2
    scratch += [pltpu.SemaphoreType.DMA((2, 5))] + [pltpu.SemaphoreType.DMA((2,))] * 2
    scratch += [pltpu.SemaphoreType.DMA((36,))] * 2
    scratch += reduce_scratch(summed, parts)
    anywhere, vmem = pl.BlockSpec(memory_space=pl.ANY), pl.BlockSpec(memory_space=pltpu.VMEM)
    return pl.pallas_call(
        functools.partial(expert_kernel, parts, len(summed)),
        out_shape=out_shape,
        in_specs=[anywhere] * 5 + [vmem] * len(summed),
        out_specs=[vmem] * len(out_shape),
        scratch_shapes=scratch,
        compiler_params=pltpu.CompilerParams(
            collective_id=collective_id, has_side_effects=True, vmem_limit_bytes=VMEM_LIMIT
        ),
        name="run_experts",
    )(*operands, *summed)


def sum_more_kernel(parts, *refs):
    ins, adds, small = refs[:parts], refs[parts : 2 * parts], refs[2 * parts]
    outs, small_out = refs[2 * parts + 1 : 3 * parts + 1], refs[3 * parts + 1]
    got, half, far = (refs[(3 + i) * parts + 2 : (4 + i) * parts + 2] for i in range(3))
    small_got, small_half, small_far, send_sem, recv_sem = refs[6 * parts + 2 :]
    w = lax.axis_index("wa")
    core, place = w % 2, w // 2
    beside, across = {"wa": w + 1 - 2 * core}, {"wa": (w + 2) % 4}
    width = D // 2
    quarter = D // 4
    mine = pl.ds(pl.multiple_of(core * width, width), width)
    theirs = pl.ds(pl.multiple_of((1 - core) * width, width), width)
    own = pl.ds(pl.multiple_of(place * quarter, quarter), quarter)
    greet([beside, across])
    copies = Copies(send_sem, recv_sem)
    one = [copies.start(ins[a].at[:, theirs], got[a], beside) for a in range(parts)]
    one.append(copies.start(small, small_got, beside))
    two = []
    for a in range(parts):
        one[a].wait_recv()
        half[a][...] = ins[a][:, mine] + got[a][...]
        half[a][:, own] = half[a][:, own] + adds[a][...]
        two.append(copies.start(half[a], far[a], across))
    one[parts].wait_recv()
    small_half[...] = small[...] + small_got[...]
    two.append(copies.start(small_half, small_far, across))
    three = []
    for a in range(parts):
        two[a].wait_recv()
        outs[a][:, mine] = half[a][...] + far[a][...]
        three.append(copies.start(outs[a].at[:, mine], outs[a].at[:, mine], beside))
    two[parts].wait_recv()
    small_out[...] = small_half[...] + small_far[...]
    for copy in three:
        copy.wait_recv()
    copies.finish()


def sum_more(arrays, adds, small, collective_id, name):
    parts = len(arrays)
    rows = arrays[0].shape[0]
    dtype = arrays[0].dtype
    scratch = [pltpu.VMEM((rows, D // 2), dtype)] * (3 * parts)
    scratch += [pltpu.VMEM(small.shape, small.dtype)] * 3
    scratch += [pltpu.SemaphoreType.DMA((3 * parts + 2,))] * 2
    out_shape = [jax.ShapeDtypeStruct(x.shape, x.dtype) for x in (*arrays, small)]
    return vmem_call(
        functools.partial(sum_more_kernel, parts), out_shape, (*arrays, *adds, small), scratch,
        collective_id, name,
    )


def tail_kernel(parts, count, *refs):
    ins, x = refs[:count], refs[count]
    outs, total = refs[count + 1 : 2 * count + 1], refs[2 * count + 1]
    half, got, far, small_got, small_far = refs[2 * count + 2 : 2 * count + 7]
    bufs, more = refs[2 * count + 7 : -6], refs[-6:]
    greet(cube_places() + wa_places())
    run(
        reduce_steps(parts, ins, outs, bufs, Copies(*more[:2])),
        sum_wa_steps(x, total, half, got, far, Copies(*more[2:4])),
    )
    beside, across = wa_places()
    copies = Copies(*more[4:])
    small = outs[count - 1]
    copies.start(small, small_got, beside).wait()
    small[...] = small[...] + small_got[...]
    copies.start(small, small_far, across).wait()
    small[...] = small[...] + small_far[...]


def reduce_and_sum(arrays, parts, x, collective_id):
    count = len(arrays)
    rows, columns = x.shape
    out_shape = [jax.ShapeDtypeStruct(a.shape[3:], jnp.float32) for a in arrays]
    scratch = [pltpu.VMEM((rows, columns // 2), x.dtype)] * 3
    scratch += [pltpu.VMEM(arrays[-1].shape[3:], jnp.float32)] * 2
    scratch += reduce_scratch(arrays, parts)
    scratch += [pltpu.SemaphoreType.DMA((3,))] * 2 + [pltpu.SemaphoreType.DMA((2,))] * 2
    return vmem_call(
        functools.partial(tail_kernel, parts, count),
        [*out_shape, jax.ShapeDtypeStruct(x.shape, x.dtype)],
        (*arrays, x),
        scratch,
        collective_id,
        "reduce_attention_grads",
    )

def over(left, right, dims):
    return lax.dot_general(
        left, right, ((dims[:1], dims[1:]), ((), ())), preferred_element_type=jnp.float32
    )


def swish_parts(pre, lin, act_grads):
    sig = jax.nn.sigmoid(pre)
    swish = pre * sig
    slope = sig * (1.0 + pre * (1.0 - sig))
    return swish * lin, act_grads * lin * slope, act_grads * swish


def expert_grads_kernel(rows, grads, act, pre_grad, lin_grad, gate_grad, up_grad, down_grad):
    for at in range(0, D, 512):
        here = slice(at, at + 512)
        down_grad[0, :, here] = over(act[0], grads[0, :, here], (0, 0))
        gate_grad[0, :, here] = over(pre_grad[0], rows[0, :, here], (0, 0))
        up_grad[0, :, here] = over(lin_grad[0], rows[0, :, here], (0, 0))


def expert_grads(*operands):
    shape = jax.ShapeDtypeStruct((2, operands[2].shape[2], D), jnp.float32)

    def spec(x):
        return pl.BlockSpec((1, *x.shape[1:]), lambda e: (e, 0, 0))

    return pl.pallas_call(
        expert_grads_kernel,
        grid=(2,),
        out_shape=[shape] * 3,
        in_specs=[spec(x) for x in operands],
        out_specs=[spec(shape)] * 3,
        compiler_params=pltpu.CompilerParams(vmem_limit_bytes=VMEM_LIMIT),
        name="expert_grads",
    )(*operands)


def turned_gather(arrays, axis):
    widths = [a.shape[1] for a in arrays]
    whole = lax.all_gather(jnp.concatenate(arrays, axis=1), axis, axis=0, tiled=True)
    return jnp.split(whole, [sum(widths[:k]) for k in range(1, len(widths))], axis=1)


def rope_tables(positions):
    half_width = HD // 2
    inverse = 1.0 / ROPE_BASE ** (jnp.arange(half_width, dtype=jnp.float32) * 2.0 / HD)
    angles = positions[:, None] * inverse[None, :]
    cosine, sine = jnp.cos(angles), jnp.sin(angles)
    return jnp.concatenate([cosine, cosine], axis=1), jnp.concatenate([-sine, sine], axis=1)


def dot(left, right, over, dtype=jnp.float32, **kept):
    return lax.dot_general(
        left, right, ((over[:1], over[1:]), ((), ())), preferred_element_type=dtype, **kept
    )


def shards(
    tokens,
    cotangent,
    routes,
    attn_gain,
    query_weight,
    key_weight,
    value_weight,
    output_weight,
    mlp_gain,
    router_weight,
    shared_gate,
    shared_up,
    shared_down,
    expert_gate,
    expert_up,
    expert_down,
):
    low = jnp.bfloat16
    local_tokens = tokens.shape[0]
    head_cols = query_weight.shape[1]
    experts_all = router_weight.shape[1]
    groups = ("sp", "ctx")
    device_pos = lax.axis_index("sp") * lax.axis_size("ctx") + lax.axis_index("ctx")
    place, core = lax.axis_index("wa") // 2, lax.axis_index("wa") % 2
    quarter_at = core * (D // 2) + place * (D // 4)

    def quarter(x):
        return lax.dynamic_slice_in_dim(x, quarter_at, D // 4, 1)

    heads = (query_weight, key_weight, value_weight)
    gain_rows = attn_gain.shape[0]
    gains = jnp.pad(jnp.stack([attn_gain, mlp_gain]), ((0, 14), (0, HD - gain_rows)))
    parts = row_parts(heads)
    parts[0].append((3, pl.ds(0, 16), pl.ds(0, HD)))
    *wholes, full_gains = gather_cube((*heads, gains), parts, 1, "gather_head_weights")
    full_query, full_key, full_value = (whole.reshape(D, head_cols) for whole in wholes)
    hidden_cols = shared_gate.shape[1]
    padded = [
        jnp.pad(x, ((0, 0), (0, -x.shape[1] % HD)))
        for x in (output_weight.T, router_weight, shared_gate, shared_up, shared_down.T)
    ]
    whole = lax.all_gather(jnp.concatenate(padded, axis=1), groups, axis=0, tiled=True)
    turned = whole[:, :head_cols]
    full_router = whole[:, head_cols : head_cols + experts_all]
    shared_first = head_cols + HD
    gain_one, gain_two = (
        full_gains[..., k, :gain_rows].reshape(D).astype(jnp.float32) for k in range(2)
    )
    tokens_f = tokens.astype(jnp.float32)
    inv_one = lax.rsqrt(jnp.mean(tokens_f * tokens_f, axis=-1, keepdims=True) + EPSILON)
    unit_one = tokens_f * inv_one
    normed = (unit_one * gain_one).astype(low)
    query_pos = device_pos * local_tokens + jnp.arange(local_tokens, dtype=jnp.int32)
    cosine, sine = rope_tables(query_pos.astype(jnp.float32))
    queries, keys, values = project(normed, (full_query, full_key, full_value), cosine, sine)
    head_queries, head_keys, head_values = spread_heads(queries, keys, values, 2)
    head_keys = head_keys.reshape(-1, HD)
    head_values = head_values.reshape(-1, HD)
    head_attended, exact, probs = attend(head_queries, head_keys, head_values)
    attended = heads_out(head_attended, 3)
    attn_part = dot(attended, turned, (1, 1)).astype(low)
    attn_out = sum_wa(attn_part, 4, "sum_attention").astype(jnp.float32)
    hidden_state = tokens_f + attn_out
    inv_two = lax.rsqrt(jnp.mean(hidden_state * hidden_state, axis=-1, keepdims=True) + EPSILON)
    unit_two = hidden_state * inv_two
    mlp_in = (unit_two * gain_two).astype(low)

    logits = dot(mlp_in, full_router, (1, 0))
    logit_exp = jnp.exp(logits - jnp.max(logits, axis=-1, keepdims=True))
    router_probs = logit_exp / jnp.sum(logit_exp, axis=-1, keepdims=True)
    experts = jnp.arange(experts_all, dtype=jnp.int32)
    chosen = jnp.zeros((local_tokens, experts_all), jnp.bool_)
    for j in range(TOP):
        chosen = chosen | (routes[:, j : j + 1] == experts[None, :])
    ids = jnp.arange(local_tokens, dtype=jnp.int32)
    before = (ids[None, :] < ids[:, None]).astype(low)
    rank = dot(before, chosen.astype(low), (1, 0))
    slot_of = jnp.where(chosen, rank, -1.0).astype(low)
    slot_ids = jnp.arange(experts_all * SLOTS, dtype=jnp.int32)
    widen = (experts[:, None] == slot_ids[None, :] // SLOTS).astype(low)
    taken = dot(slot_of, widen, (1, 0)) == (slot_ids % SLOTS).astype(jnp.float32)[None, :]
    probs_high = router_probs.astype(low)
    probs_rest = (router_probs - probs_high.astype(jnp.float32)).astype(low)
    pick = taken.astype(low)
    gate_high = jnp.where(taken, dot(probs_high, widen, (1, 0)), 0.0).astype(low)
    gate_rest = jnp.where(taken, dot(probs_rest, widen, (1, 0)), 0.0).astype(low)
    grad_quarter = quarter(cotangent)
    send_rows = dot(pick, quarter(mlp_in), (0, 0)).astype(low)
    send_grads = (
        dot(gate_high, grad_quarter, (0, 0)) + dot(gate_rest, grad_quarter, (0, 0))
    ).astype(low)
    by_owner = (32, 2, SLOTS, D // 4)
    rows_in, grads_in, shared_part, shared_in_part, *mlp_grads = dispatch(
        (send_rows.reshape(by_owner), send_grads.reshape(by_owner)),
        mlp_in,
        cotangent,
        whole,
        shared_first,
        hidden_cols,
        5,
    )
    mlp_grads = [x.reshape(4, 2, 4, x.shape[0] // 32, x.shape[1]) for x in mlp_grads]

    returned, rows_back, gate_share, up_share, down_share, *kept = run_experts(
        (
            rows_in,
            grads_in,
            expert_gate.transpose(0, 2, 1),
            expert_up.transpose(0, 2, 1),
            expert_down,
        ),
        mlp_grads,
        6,
    )
    gate_grad_turned, up_grad_turned, expert_down_grad = expert_grads(rows_in, grads_in, *kept)
    returned, rows_back = returned.reshape(-1, D // 4), rows_back.reshape(-1, D // 4)

    routed = (dot(gate_high, returned, (1, 0)) + dot(gate_rest, returned, (1, 0))).astype(low)
    routed_in = dot(pick, rows_back, (1, 0)).astype(low)
    slot_grads = jnp.where(taken, dot(grad_quarter, returned, (1, 1)), 0.0)
    prob_part = dot(slot_grads, widen.astype(jnp.float32), (1, 1), precision=PRECISE)
    prob_part = jnp.pad(prob_part, ((0, 0), (0, HD - experts_all)))
    mixed, mixed_in, prob_grads = sum_more(
        (shared_part, shared_in_part), (routed, routed_in), prob_part, 7, "sum_mlp"
    )
    block_out = (hidden_state + mixed.astype(jnp.float32)).astype(low)
    prob_grads = prob_grads[:, :experts_all]
    logit_grads = router_probs * (
        prob_grads - jnp.sum(router_probs * prob_grads, axis=-1, keepdims=True)
    )
    router_in_grad = dot(
        logit_grads, full_router.astype(jnp.float32), (1, 1), precision=PRECISE
    )
    mlp_in_grad = router_in_grad + mixed_in.astype(jnp.float32)
    gain_two_grad = jnp.sum(mlp_in_grad * unit_two, axis=0)
    scaled_two = mlp_in_grad * gain_two
    hidden_grad = cotangent.astype(jnp.float32) + inv_two * (
        scaled_two - unit_two * jnp.mean(scaled_two * unit_two, axis=-1, keepdims=True)
    )
    out_grad = hidden_grad.astype(low)
    router_grad = dot(mlp_in, logit_grads.astype(low), (0, 0))

    attended_grad = dot(out_grad, turned, (1, 0)).astype(low)
    head_grad = heads_in(attended_grad, 8)
    dq, dk, dv = attend_back(head_queries, head_keys, head_values, probs, head_grad, exact)
    by_block = (4, 2, 4, local_tokens, HD)
    query_grads, key_grads, value_in = collect_heads(
        dq, dk.reshape(by_block), dv.reshape(by_block), 9
    )
    query_in, key_in = turn_back(query_grads, key_grads, cosine, sine)
    normed_part = (
        dot(query_in, full_query, (1, 1))
        + dot(key_in, full_key, (1, 1))
        + dot(value_in, full_value, (1, 1))
    ).astype(low)
    gain_one_part = jnp.sum(normed_part.astype(jnp.float32) * unit_one, axis=0)
    small_grads = jnp.concatenate(
        [0.25 * router_grad, gain_one_part[:, None], 0.25 * gain_two_grad[:, None]], axis=1
    )
    small_grads = jnp.pad(small_grads, ((0, 0), (0, HD - small_grads.shape[1])))

    def by_shard(x):
        return x.astype(low).reshape(4, 2, 4, x.shape[0] // 32, x.shape[1])

    attention_grads = [
        by_shard(dot(left, right, (0, 0)))
        for left, right in (
            (normed, query_in),
            (normed, key_in),
            (normed, value_in),
            (out_grad, attended),
        )
    ]
    parts = whole_parts(attention_grads)
    attention_grads.append(by_shard(small_grads))
    for part, (_, rows, columns) in zip(parts, sum(row_parts(attention_grads[4:]), [])):
        part.append((4, rows, columns))
    query_share, key_share, value_share, output_share, small_share, normed_sum = reduce_and_sum(
        attention_grads, parts, normed_part, 12
    )
    normed_grad = normed_sum.astype(jnp.float32)
    scaled_one = normed_grad * gain_one
    tokens_grad = (
        hidden_grad
        + inv_one
        * (scaled_one - unit_one * jnp.mean(scaled_one * unit_one, axis=-1, keepdims=True))
    ).astype(low)
    return (
        block_out,
        tokens_grad,
        small_share[:, experts_all],
        query_share,
        key_share,
        value_share,
        output_share.T,
        small_share[:, experts_all + 1],
        small_share[:, :experts_all],
        gate_share,
        up_share,
        down_share.T,
        gate_grad_turned.transpose(0, 2, 1),
        up_grad_turned.transpose(0, 2, 1),
        expert_down_grad,
    )


def solution(mesh):
    placed = (
        P(("sp", "ctx"), None),
        P(("sp", "ctx"), None),
        P(("sp", "ctx"), None),
        P(("sp", "ctx")),
        P(("sp", "ctx"), "wa"),
        P(("sp", "ctx"), "wa"),
        P(("sp", "ctx"), "wa"),
        P("wa", ("sp", "ctx")),
        P(("sp", "ctx")),
        P(("sp", "ctx"), None),
        P(("sp", "ctx"), "wa"),
        P(("sp", "ctx"), "wa"),
        P("wa", ("sp", "ctx")),
        P(("sp", "ctx"), None, "wa"),
        P(("sp", "ctx"), None, "wa"),
        P(("sp", "ctx"), "wa", None),
    )
    return jax.shard_map(
        shards,
        mesh=mesh,
        in_specs=placed,
        out_specs=(
            P(("sp", "ctx"), None),
            P(("sp", "ctx"), None),
            P(("sp", "ctx")),
            P(("sp", "ctx"), "wa"),
            P(("sp", "ctx"), "wa"),
            P(("sp", "ctx"), "wa"),
            P("wa", ("sp", "ctx")),
            P(("sp", "ctx")),
            P(("sp", "ctx"), None),
            P(("sp", "ctx"), "wa"),
            P(("sp", "ctx"), "wa"),
            P("wa", ("sp", "ctx")),
            P(("sp", "ctx"), None, "wa"),
            P(("sp", "ctx"), None, "wa"),
            P(("sp", "ctx"), "wa", None),
        ),
        check_vma=False,
    )
```

```python
import functools

import jax
import jax.numpy as jnp
from jax import lax
from jax.experimental import pallas as pl
from jax.experimental.pallas import tpu as pltpu
from jax.sharding import PartitionSpec as P

D = 2048
HD = 128
TOP = 6


EPSILON = 1e-06
ROPE_BASE = 10000.0
MASKED = -1e30
PRECISE = lax.Precision.HIGHEST


MESH = pl.DeviceIdType.MESH
VMEM_LIMIT = 60 * 1024 * 1024

ORDERS = (
    (("z", "A"), ("z", "B"), ("y", "A"), ("y", "B")),
    (("z", "B"), ("z", "A"), ("y", "B"), ("y", "A")),
    (("y", "A"), ("y", "B"), ("z", "A"), ("z", "B")),
    (("y", "B"), ("y", "A"), ("z", "B"), ("z", "A")),
)


def paired(i, kind):
    return i + 1 - 2 * (i % 2) if kind == "A" else 3 - i


def own_place():
    c = lax.axis_index("ctx")
    return lax.axis_index("sp"), c // 4, c % 4


def neighbour(axis, kind):
    z, xh, y = own_place()
    if axis == "z":
        return {"sp": paired(z, kind)}
    if axis == "y":
        return {"ctx": 4 * xh + paired(y, kind)}
    return {"ctx": 4 * (1 - xh) + y}


def cube_places():
    rings = [neighbour(axis, kind) for axis in ("z", "y") for kind in ("A", "B")]
    return rings + [neighbour("x", "A")]


def pair_slots(i, kind):
    if kind == "A":
        return [(pl.ds((i // 2) * 2, 2), pl.ds(0, 2))]
    return [(pl.ds(i, 1), pl.ds(0, 1)), (pl.ds(3 - i, 1), pl.ds(1, 1))]


def pair_members(i, kind):
    if kind == "A":
        return [(i // 2) * 2, (i // 2) * 2 + 1]
    return [i, 3 - i]


def slot_in_pair(i, kind):
    return i % 2 if kind == "A" else 0

def over(left, right, dims):
    return lax.dot_general(
        left, right, ((dims[:1], dims[1:]), ((), ())), preferred_element_type=jnp.float32
    )


def head_columns(h):
    return pl.ds(pl.multiple_of(h * HD, HD), HD)


class Copies:
    def __init__(self, send_sem, recv_sem):
        self.send_sem, self.recv_sem, self.started = send_sem, recv_sem, []

    def start(self, src, dst, where):
        k = len(self.started)
        copy = pltpu.make_async_remote_copy(
            src_ref=src, dst_ref=dst, send_sem=self.send_sem.at[k],
            recv_sem=self.recv_sem.at[k], device_id=where, device_id_type=MESH,
        )
        copy.start()
        self.started.append(copy)
        return copy

    def finish(self):
        for copy in self.started:
            copy.wait_send()


def run(*programs):
    programs = list(programs)
    while programs:
        programs = [program for program in programs if next(program, None) is not None]


def in_turn(order, programs):
    for letter in order:
        next(programs[letter], None)


def greet(places):
    barrier = pltpu.get_barrier_semaphore()
    for place in places:
        pl.semaphore_signal(barrier, inc=1, device_id=place, device_id_type=MESH)
    pl.semaphore_wait(barrier, len(places))


def along_z():
    z = lax.axis_index("sp")
    return [{"sp": (z + d) % 4} for d in (1, 2, 3)]


def vmem_call(kernel, out_shape, operands, scratch, collective_id, name, **params):
    return pl.pallas_call(
        kernel,
        out_shape=out_shape,
        in_specs=[pl.BlockSpec(memory_space=pltpu.VMEM)] * len(operands),
        out_specs=jax.tree.map(lambda _: pl.BlockSpec(memory_space=pltpu.VMEM), out_shape),
        scratch_shapes=scratch,
        compiler_params=pltpu.CompilerParams(
            collective_id=collective_id,
            has_side_effects=collective_id is not None,
            vmem_limit_bytes=VMEM_LIMIT,
        ),
        name=name,
        **params,
    )(*operands)

def gather_steps(parts, ins, outs, copies, local_sem):
    z, xh, y = own_place()
    count = len(ins)

    def step(lane, p, s):
        ring1, ring2 = ORDERS[p][0][0], ORDERS[p][2][0]
        where = neighbour(*ORDERS[p][s])
        xl = xh if lane == 0 else 1 - xh
        zs, ys = [pl.ds(z, 1)], [pl.ds(y, 1)]
        full = [pl.ds(0, 4)]
        if s == 1:
            other = [d for d, _ in pair_slots(z if ring1 == "z" else y, ORDERS[p][0][1])]
            zs, ys = (other, ys) if ring1 == "z" else (zs, other)
        if s >= 2:
            zs, ys = (full, ys) if ring1 == "z" else (zs, full)
        if s == 3:
            other = [d for d, _ in pair_slots(z if ring2 == "z" else y, ORDERS[p][2][1])]
            zs, ys = (other, ys) if ring2 == "z" else (zs, other)
        started = []
        for a, rows, cols in parts[p]:
            for zd in zs:
                for yd in ys:
                    place = outs[a].at[zd, pl.ds(xl, 1), yd, rows, cols]
                    started.append(copies.start(place, place, where))
        return started

    local = [
        pltpu.make_async_copy(ins[a], outs[a].at[z, xh, y], local_sem.at[a]) for a in range(count)
    ]
    for copy in local:
        copy.start()
    across = [
        [
            copies.start(
                ins[a].at[rows, cols], outs[a].at[z, xh, y, rows, cols], neighbour("x", "A")
            )
            for a, rows, cols in part
        ]
        for part in parts
    ]
    for copy in local:
        copy.wait()
    flying = {}
    for lane, s in (
        (0, 0), (0, 1), (1, 0), (0, 2), (1, 1), (0, 3), (1, 2), (1, 3), (0, 4), (1, 4)
    ):
        for p in range(4):
            for copy in flying.get((lane, p), across[p] if lane == 1 else []):
                copy.wait_recv()
            flying[lane, p] = step(lane, p, s) if s < 4 else []
        yield True
    copies.finish()


def gather_kernel(parts, count, *refs):
    ins, outs = refs[:count], refs[count : 2 * count]
    send_sem, recv_sem, local_sem = refs[2 * count :]
    greet(cube_places())
    run(gather_steps(parts, ins, outs, Copies(send_sem, recv_sem), local_sem))


def gather_cube(arrays, parts, collective_id, name):
    count = len(arrays)
    copies = 11 * sum(len(part) for part in parts)
    return pl.pallas_call(
        functools.partial(gather_kernel, parts, count),
        out_shape=[jax.ShapeDtypeStruct((4, 2, 4, *a.shape), a.dtype) for a in arrays],
        in_specs=[pl.BlockSpec(memory_space=pl.ANY)] * count,
        out_specs=[pl.BlockSpec(memory_space=pl.ANY)] * count,
        scratch_shapes=[
            pltpu.SemaphoreType.DMA((copies,)),
            pltpu.SemaphoreType.DMA((copies,)),
            pltpu.SemaphoreType.DMA((count,)),
        ],
        compiler_params=pltpu.CompilerParams(collective_id=collective_id, has_side_effects=True),
        name=name,
    )(*arrays)


def entries_of(parts):
    return [(p, *entry) for p in range(4) for entry in parts[p]]


CUBE_ORDER = tuple((stage, lane) for stage in range(5) for lane in (1, 0))


def reduce_steps(parts, ins, outs, bufs, copies):
    entries = entries_of(parts)
    z, xh, y = own_place()
    start = copies.start
    flying = {}

    def first(lane, e):
        p, a, rows, cols = entries[e]
        ring2, near = ORDERS[p][2]
        axis, kind = ORDERS[p][3]
        xl = xh if lane == 0 else 1 - xh
        theirs = paired(z if ring2 == "z" else y, kind)
        copies = []
        for src, dst in pair_slots(theirs, near):
            if ring2 == "z":
                block, place = ins[a].at[src, xl, :, rows, cols], bufs[5 * e].at[lane, dst]
            else:
                block, place = ins[a].at[:, xl, src, rows, cols], bufs[5 * e].at[lane, :, dst]
            copies.append(start(block, place, neighbour(axis, kind)))
        flying[lane, e] = copies

    def second(lane, e):
        p, a, rows, cols = entries[e]
        ring2 = ORDERS[p][2][0]
        axis, kind = ORDERS[p][2]
        xl = xh if lane == 0 else 1 - xh
        mine = z if ring2 == "z" else y
        buf = bufs[5 * e]
        for copy in flying[lane, e]:
            copy.wait_recv()
        slot = slot_in_pair(mine, kind)

        def add(j, place):
            def one(i, carry):
                if ring2 == "z":
                    buf[lane, j, i] = buf[lane, j, i] + ins[a][place, xl, i, rows, cols]
                else:
                    buf[lane, i, j] = buf[lane, i, j] + ins[a][i, xl, place, rows, cols]
                return carry

            lax.fori_loop(0, 4, one, 0)

        add(1 - slot, paired(mine, kind))
        half = buf.at[lane, 1 - slot] if ring2 == "z" else buf.at[lane, :, 1 - slot]
        flying[lane, e] = [start(half, bufs[5 * e + 1].at[lane], neighbour(axis, kind))]
        add(slot, mine)

    def third(lane, e):
        p = entries[e][0]
        ring1, ring2 = ORDERS[p][0][0], ORDERS[p][2][0]
        axis, kind = ORDERS[p][1]
        before, buf = bufs[5 * e], bufs[5 * e + 1]
        for copy in flying[lane, e]:
            copy.wait_recv()
        slot = slot_in_pair(z if ring2 == "z" else y, ORDERS[p][2][1])

        def one(i, carry):
            other = before[lane, slot, i] if ring2 == "z" else before[lane, i, slot]
            buf[lane, i] = buf[lane, i] + other
            return carry

        lax.fori_loop(0, 4, one, 0)
        theirs = paired(z if ring1 == "z" else y, kind)
        flying[lane, e] = [
            start(buf.at[lane, src], bufs[5 * e + 2].at[lane, dst], neighbour(axis, kind))
            for src, dst in pair_slots(theirs, ORDERS[p][0][1])
        ]

    def fourth(lane, e):
        p = entries[e][0]
        ring1 = ORDERS[p][0][0]
        axis, kind = ORDERS[p][0]
        mine = z if ring1 == "z" else y
        before, buf = bufs[5 * e + 1], bufs[5 * e + 2]
        for copy in flying[lane, e]:
            copy.wait_recv()
        slot = slot_in_pair(mine, kind)
        buf[lane, 1 - slot] = buf[lane, 1 - slot] + before[lane, paired(mine, kind)]
        flying[lane, e] = [
            start(buf.at[lane, 1 - slot], bufs[5 * e + 3].at[lane], neighbour(axis, kind))
        ]
        buf[lane, slot] = buf[lane, slot] + before[lane, mine]

    def last(lane, e):
        p, a, rows, cols = entries[e]
        ring1 = ORDERS[p][0][0]
        before, buf = bufs[5 * e + 2], bufs[5 * e + 3]
        for copy in flying[lane, e]:
            copy.wait_recv()
        slot = slot_in_pair(z if ring1 == "z" else y, ORDERS[p][0][1])
        if lane == 1:
            buf[1] = buf[1] + before[1, slot]
            flying["x", e] = start(buf.at[1], bufs[5 * e + 4], neighbour("x", "A"))
        else:
            flying["x", e].wait_recv()
            total = (
                buf[0].astype(jnp.float32)
                + before[0, slot].astype(jnp.float32)
                + bufs[5 * e + 4][...].astype(jnp.float32)
            )
            outs[a][rows, cols] = total.astype(outs[a].dtype)

    stages = (first, second, third, fourth, last)
    for at, lane in CUBE_ORDER:
        for e in range(len(entries)):
            stages[at](lane, e)
        yield True
    copies.finish()


def reduce_kernel(parts, count, *refs):
    size = 5 * len(entries_of(parts))
    ins, outs = refs[:count], refs[count : 2 * count]
    bufs = refs[2 * count : 2 * count + size]
    greet(cube_places())
    run(reduce_steps(parts, ins, outs, bufs, Copies(*refs[2 * count + size :])))


def reduce_scratch(arrays, parts):
    scratch = []
    for p in range(4):
        pair = (2, 4) if ORDERS[p][2][0] == "z" else (4, 2)
        for a, rows, cols in parts[p]:
            for lead in ((2, *pair), (2, 4), (2, 2), (2,), ()):
                scratch.append(pltpu.VMEM((*lead, rows.size, cols.size), arrays[a].dtype))
    copies = 13 * sum(len(part) for part in parts)
    return scratch + [pltpu.SemaphoreType.DMA((copies,))] * 2


def reduce_cube(arrays, parts, collective_id, name, dtype=jnp.float32):
    count = len(arrays)
    scratch = reduce_scratch(arrays, parts)
    return pl.pallas_call(
        functools.partial(reduce_kernel, parts, count),
        out_shape=[jax.ShapeDtypeStruct(a.shape[3:], dtype) for a in arrays],
        in_specs=[pl.BlockSpec(memory_space=pltpu.VMEM)] * count,
        out_specs=[pl.BlockSpec(memory_space=pltpu.VMEM)] * count,
        scratch_shapes=scratch,
        compiler_params=pltpu.CompilerParams(
            collective_id=collective_id, has_side_effects=True, vmem_limit_bytes=VMEM_LIMIT
        ),
        name=name,
    )(*arrays)


def row_parts(arrays):
    parts = []
    for p in range(4):
        part = []
        for a, array in enumerate(arrays):
            rows, columns = array.shape[-2:]
            part.append((a, pl.ds(p * rows // 4, rows // 4), pl.ds(0, columns)))
        parts.append(part)
    return parts


def whole_parts(arrays):
    return [[(a, pl.ds(0, x.shape[-2]), pl.ds(0, x.shape[-1]))] for a, x in enumerate(arrays)]


def half_parts(arrays):
    return [
        [(a, pl.ds(0, x.shape[-2]), pl.ds(h * x.shape[-1] // 2, x.shape[-1] // 2))]
        for a, x in enumerate(arrays)
        for h in range(2)
    ]


def wa_places():
    w = lax.axis_index("wa")
    return [{"wa": w + 1 - 2 * (w % 2)}, {"wa": (w + 2) % 4}]


def sum_wa_steps(x, out, half, got, far, copies):
    core = lax.axis_index("wa") % 2
    beside, across = wa_places()
    width = x.shape[1] // 2
    mine = pl.ds(pl.multiple_of(core * width, width), width)
    theirs = pl.ds(pl.multiple_of((1 - core) * width, width), width)
    one = copies.start(x.at[:, theirs], got, beside)
    yield True
    one.wait_recv()
    half[...] = x[:, mine] + got[...]
    two = copies.start(half, far, across)
    yield True
    two.wait_recv()
    out[:, mine] = half[...] + far[...]
    three = copies.start(out.at[:, mine], out.at[:, mine], beside)
    yield True
    three.wait_recv()
    copies.finish()


def sum_wa_kernel(x, out, half, got, far, send_sem, recv_sem):
    greet(wa_places())
    run(sum_wa_steps(x, out, half, got, far, Copies(send_sem, recv_sem)))


def sum_wa(x, collective_id, name):
    rows, columns = x.shape
    return pl.pallas_call(
        sum_wa_kernel,
        out_shape=jax.ShapeDtypeStruct(x.shape, x.dtype),
        in_specs=[pl.BlockSpec(memory_space=pltpu.VMEM)],
        out_specs=pl.BlockSpec(memory_space=pltpu.VMEM),
        scratch_shapes=[pltpu.VMEM((rows, columns // 2), x.dtype)] * 3
        + [pltpu.SemaphoreType.DMA((3,)), pltpu.SemaphoreType.DMA((3,))],
        compiler_params=pltpu.CompilerParams(
            collective_id=collective_id, has_side_effects=True, vmem_limit_bytes=VMEM_LIMIT
        ),
        name=name,
    )(x)

def ctx_gather_steps(parts, copies):
    z, xh, y = own_place()

    def send(part, xl, place, axis, kind):
        ref, rows = part
        block = ref.at[:, xl, place, rows]
        return copies.start(block, block, neighbour(axis, kind))

    near, far = ("A", "B"), ("B", "A")
    first, across, last = {}, [], []
    for a in range(2):
        first[0, a] = send(parts[a], xh, y, "y", near[a])
        across.append(send(parts[a], xh, y, "x", "A"))
    yield True
    for lane in range(2):
        xl = xh if lane == 0 else 1 - xh
        if lane == 1:
            for a in range(2):
                across[a].wait_recv()
                first[1, a] = send(parts[a], xl, y, "y", near[a])
            yield True
        for a in range(2):
            first[lane, a].wait_recv()
            for place, _ in pair_slots(y, near[a]):
                last.append(send(parts[a], xl, place, "y", far[a]))
        yield True
    for copy in last:
        copy.wait_recv()
    copies.finish()


CTX_ORDER = ((0, 1), (1, 1), (0, 0), (2, 1), (1, 0), (2, 0))


def ctx_reduce_steps(parts, bufs, sums, cross, own, copies):
    z, xh, y = own_place()
    near, far = ("A", "B"), ("B", "A")
    flying = {}

    def first(lane):
        xl = xh if lane == 0 else 1 - xh
        for a, (ref, rows) in enumerate(parts):
            flying[lane, a] = [
                copies.start(
                    ref.at[:, xl, src, rows], bufs[a].at[lane, :, dst], neighbour("y", far[a])
                )
                for src, dst in pair_slots(paired(y, far[a]), near[a])
            ]

    def second(lane):
        xl = xh if lane == 0 else 1 - xh
        for a, (ref, rows) in enumerate(parts):
            for copy in flying[lane, a]:
                copy.wait_recv()
            slot = slot_in_pair(y, near[a])

            def add(j, place):
                def one(i, carry):
                    bufs[a][lane, i, j] = bufs[a][lane, i, j] + ref[i, xl, place, rows]
                    return carry

                lax.fori_loop(0, 4, one, 0)

            add(1 - slot, paired(y, near[a]))
            flying[lane, a] = copies.start(
                bufs[a].at[lane, :, 1 - slot], sums[a].at[lane], neighbour("y", near[a])
            )
            add(slot, y)

    def third(lane):
        for a in range(2):
            flying[lane, a].wait_recv()
            slot = slot_in_pair(y, near[a])

            def more(i, carry):
                sums[a][lane, i] = sums[a][lane, i] + bufs[a][lane, i, slot]
                return carry

            lax.fori_loop(0, 4, more, 0)
            if lane == 1:
                flying["x", a] = copies.start(sums[a].at[1], cross[a], neighbour("x", "A"))

    for stage, lane in CTX_ORDER:
        (first, second, third)[stage](lane)
        yield True
    for a in range(2):
        flying["x", a].wait_recv()

        def total(i, carry):
            own[a][i] = sums[a][0, i] + cross[a][i]
            return carry

        lax.fori_loop(0, 4, total, 0)
    yield True
    copies.finish()


def ctx_scratch(shapes, dtype):
    scratch = [
        pltpu.VMEM((*lead, *shape), dtype) for lead in ((2, 4, 2), (2, 4), (4,), (4,)) for shape in shapes
    ]
    return scratch + [pltpu.SemaphoreType.DMA((12,))] * 2


def column_halves(width):
    return [pl.ds(0, width // 2), pl.ds(width // 2, width // 2)]


def rows_gather_steps(x, out, copies):
    z = lax.axis_index("sp")
    near, far = ("A", "B"), ("B", "A")
    halves = column_halves(x.shape[1])
    first = [
        copies.start(x.at[:, halves[a]], out.at[z, :, halves[a]], neighbour("z", near[a]))
        for a in range(2)
    ]
    out[z] = x[...]
    yield True
    last = []
    for a in range(2):
        first[a].wait_recv()
        for place, _ in pair_slots(z, near[a]):
            block = out.at[place, :, halves[a]]
            last.append(copies.start(block, block, neighbour("z", far[a])))
    yield True
    for copy in last:
        copy.wait_recv()
    copies.finish()


def rows_reduce_steps(x, out, bufs, sums, copies):
    z = lax.axis_index("sp")
    near, far = ("A", "B"), ("B", "A")
    halves = column_halves(x.shape[2])
    flying = [
        [
            copies.start(x.at[src, :, halves[a]], bufs[a].at[dst], neighbour("z", far[a]))
            for src, dst in pair_slots(paired(z, far[a]), near[a])
        ]
        for a in range(2)
    ]
    yield True
    second = []
    for a in range(2):
        for copy in flying[a]:
            copy.wait_recv()
        slot = slot_in_pair(z, near[a])
        bufs[a][1 - slot] = bufs[a][1 - slot] + x[paired(z, near[a]), :, halves[a]]
        second.append(copies.start(bufs[a].at[1 - slot], sums[a], neighbour("z", near[a])))
        bufs[a][slot] = bufs[a][slot] + x[z, :, halves[a]]
    yield True
    for a in range(2):
        second[a].wait_recv()
        slot = slot_in_pair(z, near[a])
        out[:, halves[a]] = bufs[a][slot] + sums[a][...]
    yield True
    copies.finish()


def gather_head_kernel(x, w, rows_out, weights_out, *sems):
    z, xh, y = own_place()
    greet(along_z() + [neighbour("y", "A"), neighbour("y", "B"), neighbour("x", "A")])
    turns = Copies(*sems[:2])
    heads = w.shape[1] // HD // 4

    def columns(k, h):
        return pl.ds(pl.multiple_of(k * 4 * HD + h * HD, HD), HD)

    for d in (1, 2, 3):
        there = (z + d) % 4
        for k in range(heads):
            place = weights_out.at[z, xh, y, :, pl.ds(k * HD, HD)]
            turns.start(w.at[:, columns(k, there)], place, {"sp": there})
    rows = rows_gather_steps(x, rows_out, Copies(*sems[2:4]))
    next(rows)
    for k in range(heads):
        weights_out[z, xh, y, :, k * HD : (k + 1) * HD] = w[:, columns(k, z)]
    for copy in turns.started:
        copy.wait_recv()
    half = w.shape[0] // 2
    parts = [(weights_out, pl.ds(a * half, half)) for a in range(2)]
    run(ctx_gather_steps(parts, Copies(*sems[4:6])), rows)
    turns.finish()


def gather_head(x, w, collective_id):
    out_shape = [
        jax.ShapeDtypeStruct((4, *x.shape), x.dtype),
        jax.ShapeDtypeStruct((4, 2, 4, w.shape[0], w.shape[1] // 4), w.dtype),
    ]
    sems = [pltpu.SemaphoreType.DMA((n,)) for n in (9, 9, 5, 5, 12, 12)]
    return vmem_call(gather_head_kernel, out_shape, (x, w), sems, collective_id, "gather_head")


def project_kernel(x, w, cosine, sine, q, k, v):
    raw = jnp.dot(x[...], w[...], preferred_element_type=jnp.float32)
    for at, out in enumerate((q, k)):
        one = raw[:, at * HD : (at + 1) * HD]
        out[...] = (one * cosine[...] + pltpu.roll(one, HD // 2, 1) * sine[...]).astype(out.dtype)
    v[...] = raw[:, 2 * HD :].astype(v.dtype)


def project(x, w, cosine, sine):
    shape = jax.ShapeDtypeStruct((x.shape[0], HD), x.dtype)
    return vmem_call(project_kernel, [shape] * 3, (x, w, cosine, sine), [], None, "project_head")


def attend_steps(q, k, v, blocks, exact, probs, scores):
    rows = q.shape[1]
    span = 8 * rows
    first = lax.axis_index("ctx") * rows
    scale = HD ** (-0.5)
    at = 0

    def chunk(ref, c):
        return ref[c].reshape(span, HD)

    for block in range(4):
        for c in range(block + 1):
            part = over(q[block], chunk(k, c), (1, 1)) * scale
            if c == block:
                row = lax.broadcasted_iota(jnp.int32, part.shape, 0)
                col = lax.broadcasted_iota(jnp.int32, part.shape, 1)
                part = jnp.where(col <= row + first, part, MASKED)
            scores[:, c * span : (c + 1) * span] = part
        width = (block + 1) * span
        top = jnp.max(scores[:, :width], axis=1, keepdims=True)
        total = jnp.zeros_like(top)
        for c in range(block + 1):
            part = jnp.exp(scores[:, c * span : (c + 1) * span] - top)
            total = total + jnp.sum(part, axis=1, keepdims=True)
            scores[:, c * span : (c + 1) * span] = part
        scaled = 1.0 / total
        result = jnp.zeros((rows, HD), jnp.float32)
        for c in range(block + 1):
            low = (scores[:, c * span : (c + 1) * span] * scaled).astype(probs.dtype)
            probs[at] = low
            result = result + over(low, chunk(v, c), (1, 0))
            at += 1
        exact[block] = result
        blocks[block] = result.astype(blocks.dtype)
        yield True


ATTEND_ORDER = "KGGKGKGKGK" + "AGAGAGA"


def attention_kernel(parts, q, k, v, own, total, attended, keys, values, probs, exact, whole, *refs):
    scores, blocks, part, *wa_bufs = refs[:6]
    sems = refs[6:]
    z, xh, y = own_place()
    places = along_z() + [neighbour("y", "A"), neighbour("y", "B"), neighbour("x", "A")]
    greet(places + wa_places())
    keys[:, xh, y] = k[...]
    values[:, xh, y] = v[...]
    rows = pl.ds(0, k.shape[1])
    programs = {
        "K": ctx_gather_steps([(keys, rows), (values, rows)], Copies(*sems[0:2])),
        "G": gather_steps(parts, [own], [whole], Copies(*sems[2:4]), sems[4]),
        "A": attend_steps(q, keys, values, blocks, exact, probs, scores),
    }
    in_turn(ATTEND_ORDER, programs)
    turns = Copies(*sems[5:7])
    for d in (1, 2, 3):
        there = (z + d) % 4
        turns.start(blocks.at[there], attended.at[:, head_columns(z)], {"sp": there})
    attended[:, head_columns(z)] = blocks[z]
    run(programs["G"])
    for copy in turns.started:
        copy.wait_recv()
    turns.finish()
    width = attended.shape[1]
    step = D // 4
    for i in range(4):
        weights = whole[i].reshape(step, -1)[:, :width]
        part[:, i * step : (i + 1) * step] = over(attended[...], weights, (1, 1)).astype(part.dtype)
    run(sum_wa_steps(part, total, *wa_bufs, Copies(*sems[7:9])))


def attention(q, k, v, own, collective_id):
    rows, low = q.shape[1], q.dtype
    every = jax.ShapeDtypeStruct((4, 2, 4, rows, HD), low)
    out_shape = [
        jax.ShapeDtypeStruct((rows, D), low),
        jax.ShapeDtypeStruct((rows, 4 * HD), low),
        every,
        every,
        jax.ShapeDtypeStruct((10, rows, 8 * rows), low),
        jax.ShapeDtypeStruct(q.shape, jnp.float32),
        jax.ShapeDtypeStruct((4, 2, 4, *own.shape), low),
    ]
    scratch = [pltpu.VMEM((rows, 32 * rows), jnp.float32), pltpu.VMEM(q.shape, low)]
    scratch += [pltpu.VMEM((rows, D), low)] + [pltpu.VMEM((rows, D // 2), low)] * 3
    scratch += [pltpu.SemaphoreType.DMA((n,)) for n in (12, 12, 44, 44, 1, 3, 3, 3, 3)]
    return vmem_call(
        functools.partial(attention_kernel, row_parts([own])), out_shape, (q, k, v, own), scratch,
        collective_id, "attention",
    )


def attend_back_steps(q, k, v, probs, grad, exact, dq, dk, dv, dk_sum, dv_sum):
    rows = q.shape[1]
    span = 8 * rows
    scale = HD ** (-0.5)
    at = 0

    def chunk(ref, c):
        return ref[c].reshape(span, HD)

    for block in range(4):
        low_grad = grad[block]
        delta = jnp.sum(low_grad.astype(jnp.float32) * exact[block], axis=1, keepdims=True)
        total = jnp.zeros((rows, HD), jnp.float32)
        for c in range(block + 1):
            low = probs[at]
            back = over(low_grad, chunk(v, c), (1, 1))
            terms = (low.astype(jnp.float32) * (back - delta)).astype(q.dtype)
            total = total + over(terms, chunk(k, c), (1, 0))
            key_terms = over(terms, q[block], (0, 0))
            value_terms = over(low, low_grad, (0, 0))
            if c == block:
                dk_sum[c] = key_terms
                dv_sum[c] = value_terms
            else:
                dk_sum[c] = dk_sum[c] + key_terms
                dv_sum[c] = dv_sum[c] + value_terms
            at += 1
        dq[block] = (total * scale).astype(dq.dtype)
        yield True
    for c in range(4):
        dk[c] = (dk_sum[c] * scale).astype(dk.dtype).reshape(dk.shape[1:])
        dv[c] = dv_sum[c].astype(dv.dtype).reshape(dv.shape[1:])
    yield True


def project_back_steps(dq, dk, dv, cosine, sine, x, w, back, grad):
    low = back.dtype
    rows = dq.shape[1]
    terms = []
    for src in (dq, dk):
        one = src[...].reshape(4 * rows, HD).astype(jnp.float32)
        terms.append((one * cosine[...] - pltpu.roll(one, HD // 2, 1) * sine[...]).astype(low))
    terms = jnp.concatenate([*terms, dv[...].reshape(4 * rows, HD)], axis=1)
    step = D // 4
    for i in range(4):
        here = slice(i * step, (i + 1) * step)
        back[:, :, here] = over(terms, w[here], (1, 1)).astype(low).reshape(4, rows, step)
        grad[i] = over(x[:, here], terms, (0, 0)).astype(low).reshape(grad.shape[1:])
        yield True


BACK_ORDER = "RRAAAAA" + "CRRCCRRCCRRRRCRRCC"


def attention_back_kernel(parts, count, *refs):
    attended_grad, q, keys, values, probs, exact, cosine, sine, x, w, heads, *refs = refs
    summed, refs = refs[:count], refs[count:]
    total, grad_out, gain_out, *refs = refs
    shares, refs = refs[:count], refs[count:]
    head_grad, dq, dk, dv, dk_sum, dv_sum, back, grad, mixed, *refs = refs
    z_bufs, z_sums, wa_bufs, gain_bufs = refs[0:2], refs[2:4], refs[4:7], refs[7:9]
    refs = refs[9:]
    (kv_bufs, kv_sums, kv_cross, kv_own), refs = (refs[2 * i : 2 * i + 2] for i in range(4)), refs[8:]
    kv_sems, refs = refs[:2], refs[2:]
    (bufs, sums, cross, own), refs = (refs[2 * i : 2 * i + 2] for i in range(4)), refs[8:]
    head_sems, refs = refs[:2], refs[2:]
    sems, refs = refs[:10], refs[10:]
    cube_bufs, cube_sems = refs[:-2], refs[-2:]
    z = lax.axis_index("sp")
    places = along_z() + [neighbour("y", "A"), neighbour("y", "B"), neighbour("x", "A")]
    greet(places + wa_places())
    turns = Copies(*sems[0:2])
    for d in (1, 2, 3):
        there = (z + d) % 4
        turns.start(attended_grad.at[:, head_columns(there)], head_grad.at[z], {"sp": there})
    head_grad[z] = attended_grad[:, head_columns(z)]
    rows = pl.ds(0, dq.shape[1])
    programs = {
        "R": reduce_steps(parts, summed, shares, cube_bufs, Copies(*cube_sems)),
        "A": attend_back_steps(
            q, keys, values, probs, head_grad, exact, dq, dk, dv, dk_sum, dv_sum
        ),
        "C": ctx_reduce_steps(
            [(dk, rows), (dv, rows)], kv_bufs, kv_sums, kv_cross, kv_own, Copies(*kv_sems)
        ),
    }
    in_turn("RR", programs)
    for copy in turns.started:
        copy.wait_recv()
    turns.finish()
    in_turn(BACK_ORDER, programs)
    run(programs["C"])
    run(project_back_steps(dq, *kv_own, cosine, sine, x, w, back, grad))
    half = grad.shape[3] // 2
    grad_parts = [(grad, pl.ds(a * half, half)) for a in range(2)]

    def sums_of_rows():
        yield from rows_reduce_steps(back, mixed, z_bufs, z_sums, Copies(*sems[2:4]))
        yield from sum_wa_steps(mixed, total, *wa_bufs, Copies(*sems[4:6]))

    def grads():
        yield from ctx_reduce_steps(grad_parts, bufs, sums, cross, own, Copies(*head_sems))
        turns = Copies(*sems[6:8])
        for d in (1, 2, 3):
            there = (z + d) % 4
            for a in range(2):
                turns.start(own[a].at[there], grad_out.at[z, grad_parts[a][1]], {"sp": there})
        for a in range(2):
            grad_out[z, a * half : (a + 1) * half] = own[a][z]
        yield True
        for copy in turns.started:
            copy.wait_recv()
        turns.finish()
        products = jnp.zeros(gain_out.shape, jnp.float32)
        for h in range(4):
            for k in range(grad_out.shape[2] // HD):
                ours = heads[:, (4 * k + h) * HD : (4 * k + h + 1) * HD].astype(jnp.float32)
                theirs = grad_out[h, :, k * HD : (k + 1) * HD].astype(jnp.float32)
                products = products + ours * theirs
        gain_out[...] = products
        copies = Copies(*sems[8:10])
        for place, buf in zip(wa_places(), gain_bufs):
            copy = copies.start(gain_out, buf, place)
            yield True
            copy.wait()
            gain_out[...] = gain_out[...] + buf[...]

    run(grads(), sums_of_rows(), programs["R"])


def attention_back(operands, summed, collective_id):
    attended_grad, q, keys, _, _, _, _, _, x, w, heads = operands
    rows, low = q.shape[1], q.dtype
    shard = heads.shape[0]
    parts = row_parts(summed)
    out_shape = [
        jax.ShapeDtypeStruct((rows, D), low),
        jax.ShapeDtypeStruct((4, shard, w.shape[1]), low),
        jax.ShapeDtypeStruct((shard, HD), jnp.float32),
    ]
    out_shape += [jax.ShapeDtypeStruct(a.shape[3:], jnp.float32) for a in summed]
    wide = (rows, D // 2)
    sums = pltpu.VMEM((4, 8 * rows, HD), jnp.float32)
    scratch = [pltpu.VMEM(a.shape, low) for a in (q, q, keys, keys)] + [sums, sums]
    scratch += [pltpu.VMEM((4, rows, D), low), pltpu.VMEM((4, 2, 4, shard, w.shape[1]), low)]
    scratch += [pltpu.VMEM((rows, D), low)]
    scratch += [pltpu.VMEM((2, *wide), low)] * 2 + [pltpu.VMEM(wide, low)] * 5
    scratch += [pltpu.VMEM((shard, HD), jnp.float32)] * 2
    scratch += ctx_scratch([(rows, HD)] * 2, low) + ctx_scratch([(shard // 2, w.shape[1])] * 2, low)
    scratch += [pltpu.SemaphoreType.DMA((n,)) for n in (3, 3, 5, 5, 3, 3, 6, 6, 2, 2)]
    scratch += reduce_scratch(summed, parts)
    return vmem_call(
        functools.partial(attention_back_kernel, parts, len(summed)), out_shape,
        (*operands, *summed), scratch, collective_id, "attention_back",
    )


SLOTS = 16
GROUP_ORDER = ((0, 1), (1, 0), (3, 0), (1, 1), (3, 1), (2, 0), (2, 1), (0, 0))
SENT_AHEAD = 4


def token_places():
    z, xh, y = own_place()
    w = lax.axis_index("wa")
    return z, xh, y, w // 2, w % 2


def block_device(dz, dx, dy):
    z, xh, y, place, core = token_places()
    there_z, there_x, there_y = (z + dz) % 4, (xh + dx) % 2, (y + dy) % 4
    there = (place + dx) % 2
    where = {"sp": there_z, "ctx": 4 * there_x + there_y, "wa": 2 * there + core}
    return where, there_z * 8 + there_x * 4 + there_y


def greet_blocks(others):
    barrier = pltpu.get_barrier_semaphore()

    def one(i, carry):
        where, _ = block_device(i // 8, (i // 4) % 2, i % 4)
        pl.semaphore_signal(barrier, inc=1, device_id=where, device_id_type=MESH)
        return carry

    lax.fori_loop(1, 32, one, 0)
    others = wa_places() + others
    for place in others:
        pl.semaphore_signal(barrier, inc=1, device_id=place, device_id_type=MESH)
    pl.semaphore_wait(barrier, 31 + len(others))


def quarter_columns(place, core):
    quarter = D // 4
    return pl.ds(pl.multiple_of(core * 2 * quarter + place * quarter, quarter), quarter)


def dispatch_steps(ins, outs, out_sem, in_sem, own_sem, copies):
    count = len(ins)
    z, xh, y, place, core = token_places()
    beside, across = wa_places()
    me = z * 8 + xh * 4 + y
    columns = quarter_columns(place, core)
    here = pl.ds(pl.multiple_of(me * SLOTS, SLOTS), SLOTS)
    own = [
        pltpu.make_async_copy(ins[a].at[me], outs[a].at[:, here, columns], own_sem.at[a])
        for a in range(count)
    ]
    for copy in own:
        copy.start()
    items = [(a, dz, dx) for a in range(count) for dz, dx in GROUP_ORDER]
    passed, last = {}, []

    def send(i):
        a, dz, dx = items[i]

        def one(dy, carry):
            where, block = block_device(dz, dx, dy)
            pltpu.make_async_remote_copy(
                src_ref=ins[a].at[block], dst_ref=outs[a].at[:, here, columns],
                send_sem=out_sem.at[a], recv_sem=in_sem.at[a, dz * 2 + dx],
                device_id=where, device_id_type=MESH,
            ).start()
            return carry

        lax.fori_loop(1 if dz + dx == 0 else 0, 4, one, 0)

    def rows_of(dz, dx):
        first = ((z - dz + 4) % 4 * 8 + (xh + dx) % 2 * 4) * SLOTS
        return pl.ds(pl.multiple_of(first, 4 * SLOTS), 4 * SLOTS)

    def arrived(i):
        a, dz, dx = items[i]
        few = 3 if dz + dx == 0 else 4
        sample = outs[a].at[:, pl.ds(0, few * SLOTS), columns]
        pltpu.make_async_copy(sample, sample, in_sem.at[a, dz * 2 + dx]).wait()
        if dz + dx == 0:
            own[a].wait()
        part = outs[a].at[:, rows_of(dz, dx), quarter_columns((place + dx) % 2, core)]
        passed[i] = copies.start(part, part, across)
        last.append(copies.start(part, part, beside))

    def from_across(i):
        a, dz, dx = items[i]
        passed[i].wait_recv()
        part = outs[a].at[:, rows_of(dz, dx), quarter_columns((place + dx + 1) % 2, core)]
        last.append(copies.start(part, part, beside))

    for i in range(SENT_AHEAD):
        send(i)
    yield True
    for i in range(len(items) + 2):
        if i < len(items):
            arrived(i)
            if i + SENT_AHEAD < len(items):
                send(i + SENT_AHEAD)
        if i >= 2:
            from_across(i - 2)
        yield True
    for copy in last:
        copy.wait_recv()
    copies.finish()
    for a in range(count):
        sample = ins[a].at[pl.ds(0, 31)]
        pltpu.make_async_copy(sample, sample, out_sem.at[a]).wait()


def shared_step(width):
    return -(-width // HD) * HD


def shared_steps(x, g, weights, whole, first, part, back, gate_grad, up_grad, down_grad, sem):
    low = part.dtype
    width = gate_grad.shape[1]
    step = shared_step(width)
    gate, up, down = (slice(k * step, k * step + width) for k in range(3))
    load = pltpu.make_async_copy(whole.at[:, pl.ds(first, weights.shape[1])], weights, sem)
    load.start()
    yield True
    load.wait()
    pre = over(x[...], weights[:, gate], (1, 0))
    yield True
    lin = over(x[...], weights[:, up], (1, 0))
    yield True
    act, pre_grad, lin_grad = swish_parts(pre, lin, over(g[...], weights[:, down], (1, 0)))
    act, pre_grad, lin_grad = act.astype(low), pre_grad.astype(low), lin_grad.astype(low)
    yield True
    for at in range(0, D, 512):
        here = slice(at, at + 512)
        part[:, here] = over(act, weights[here, down], (1, 1)).astype(low)
        back[:, here] = (
            over(pre_grad, weights[here, gate], (1, 1)) + over(lin_grad, weights[here, up], (1, 1))
        ).astype(low)
        yield True
        down_grad[here] = over(g[:, here], act, (0, 0)).astype(low)
        gate_grad[here] = over(x[:, here], pre_grad, (0, 0)).astype(low)
        up_grad[here] = over(x[:, here], lin_grad, (0, 0)).astype(low)
        yield True


def dispatch_kernel(first, *refs):
    ins, (x, g, whole), outs = refs[:2], refs[2:5], refs[5:7]
    results, weights, load_sem = refs[7:12], refs[12], refs[13]
    out_sem, in_sem, own_sem, *sems = refs[14:]
    greet_blocks([])
    moving = dispatch_steps(ins, outs, out_sem, in_sem, own_sem, Copies(*sems))
    computing = shared_steps(x, g, weights, whole, first, *results, load_sem)
    run(moving, computing)


def dispatch(arrays, x, g, whole, first, width, collective_id):
    low = x.dtype
    rows = jax.ShapeDtypeStruct((2, 32 * SLOTS, D), low)
    grad = jax.ShapeDtypeStruct((D, width), low)
    anywhere, vmem = pl.BlockSpec(memory_space=pl.ANY), pl.BlockSpec(memory_space=pltpu.VMEM)
    return pl.pallas_call(
        functools.partial(dispatch_kernel, first),
        out_shape=[rows] * 2 + [jax.ShapeDtypeStruct(x.shape, low)] * 2 + [grad] * 3,
        in_specs=[anywhere] * 2 + [vmem] * 2 + [anywhere],
        out_specs=[anywhere] * 2 + [vmem] * 5,
        scratch_shapes=[
            pltpu.VMEM((D, 3 * shared_step(width)), low),
            pltpu.SemaphoreType.DMA,
            pltpu.SemaphoreType.DMA((2,)),
            pltpu.SemaphoreType.DMA((2, 8)),
            pltpu.SemaphoreType.DMA((2,)),
            pltpu.SemaphoreType.DMA((48,)),
            pltpu.SemaphoreType.DMA((48,)),
        ],
        compiler_params=pltpu.CompilerParams(
            collective_id=collective_id, has_side_effects=True, vmem_limit_bytes=VMEM_LIMIT
        ),
        name="dispatch_rows",
    )(*arrays, x, g, whole)


def expert_steps(hbm, held, part, back, kept, load_sem, finished):
    low = part.dtype
    loads = [
        [pltpu.make_async_copy(src.at[e], dst.at[e], load_sem.at[e, k]) for k, (src, dst) in enumerate(zip(hbm, held))]
        for e in range(2)
    ]
    for load in loads[0] + loads[1]:
        load.start()
    yield True
    rows, grads, gate, up, down = held
    for e in range(2):
        for load in loads[e]:
            load.wait()
        x, g = rows[e], grads[e]
        pre = over(x, gate[e], (1, 1))
        lin = over(x, up[e], (1, 1))
        yield True
        act, pre_grad, lin_grad = swish_parts(pre, lin, over(g, down[e], (1, 1)))
        act, pre_grad, lin_grad = act.astype(low), pre_grad.astype(low), lin_grad.astype(low)
        kept[0][e], kept[1][e], kept[2][e] = act, pre_grad, lin_grad
        yield True
        for at in range(0, D, 512):
            here = slice(at, at + 512)
            part[e, :, here] = over(act, down[e, :, here], (1, 0)).astype(low)
            back[e, :, here] = (
                over(pre_grad, gate[e, :, here], (1, 0)) + over(lin_grad, up[e, :, here], (1, 0))
            ).astype(low)
            if at + 512 == D:
                finished(e)
            yield True


def return_steps(ins, outs, halves, quarters, out_sem, in_sem, copies):
    z, xh, y, place, core = token_places()
    beside, across = wa_places()
    me = z * 8 + xh * 4 + y
    quarter = D // 4
    group = 4 * SLOTS
    mine = pl.ds(pl.multiple_of(core * 2 * quarter, 2 * quarter), 2 * quarter)
    theirs = pl.ds(pl.multiple_of((1 - core) * 2 * quarter, 2 * quarter), 2 * quarter)
    items = [(e, a, dz, dx) for e in range(2) for a in range(2) for dz, dx in GROUP_ORDER]
    paired_up, passed = {}, {}

    def finished(e):
        for a in range(2):
            paired_up[e, a] = copies.start(ins[a].at[e, :, theirs], halves[a].at[e], beside)

    def rows_of(dz, dx):
        return pl.ds(pl.multiple_of(((z + dz) % 4 * 8 + (xh + dx) % 2 * 4) * SLOTS, group), group)

    def kept(dx):
        return pl.ds(pl.multiple_of((place + dx) % 2 * quarter, quarter), quarter)

    def given(dx):
        return pl.ds(pl.multiple_of((place + dx + 1) % 2 * quarter, quarter), quarter)

    def add_core(i):
        e, a, dz, dx = items[i]
        rows = rows_of(dz, dx)
        if i % 8 == 0:
            paired_up[e, a].wait_recv()
        halves[a][e, rows] = halves[a][e, rows] + ins[a][e, rows, mine]
        passed[i] = copies.start(
            halves[a].at[e, rows, given(dx)], quarters[a].at[e, rows], across
        )

    def add_across(i):
        e, a, dz, dx = items[i]
        rows = rows_of(dz, dx)
        passed[i].wait_recv()
        quarters[a][e, rows] = quarters[a][e, rows] + halves[a][e, rows, kept(dx)]
        if dz + dx == 0:
            outs[a][me, e] = quarters[a][e, pl.ds(pl.multiple_of(me * SLOTS, SLOTS), SLOTS)]

        def one(dy, carry):
            where, block = block_device(dz, dx, dy)
            part = pl.ds(pl.multiple_of(block * SLOTS, SLOTS), SLOTS)
            pltpu.make_async_remote_copy(
                src_ref=quarters[a].at[e, part], dst_ref=outs[a].at[me, e],
                send_sem=out_sem.at[a], recv_sem=in_sem.at[a],
                device_id=where, device_id_type=MESH,
            ).start()
            return carry

        lax.fori_loop(1 if dz + dx == 0 else 0, 4, one, 0)

    def steps():
        for i in range(len(items) + 1):
            if i < len(items):
                add_core(i)
            if i >= 1:
                add_across(i - 1)
            yield True
        copies.finish()
        for a in range(2):
            sample = outs[a].at[pl.ds(0, 31)]
            pltpu.make_async_copy(sample, sample, in_sem.at[a]).wait()
            pltpu.make_async_copy(sample, sample, out_sem.at[a]).wait()

    return finished, steps()


EXPERT_ORDER = "RRXXXXXXX" + "TXTTXTTXTTXTTXTTXTTXT" + "TTTRTTTRTTRTTRTTRTTRTTRT"


def expert_kernel(parts, count, *refs):
    hbm, summed, refs = refs[:5], refs[5 : 5 + count], refs[5 + count :]
    outs, shares, kept, refs = refs[:2], refs[2 : 2 + count], refs[2 + count : 5 + count], refs[5 + count :]
    held, (part, back), halves, quarters = refs[:5], refs[5:7], refs[7:9], refs[9:11]
    load_sem, out_sem, in_sem, send_sem, recv_sem = refs[11:16]
    bufs, more = refs[16:-2], refs[-2:]
    greet_blocks([neighbour("x", "A")])
    finished, returning = return_steps(
        (part, back), outs, halves, quarters, out_sem, in_sem, Copies(send_sem, recv_sem)
    )
    computing = expert_steps(hbm, held, part, back, kept, load_sem, finished)
    reducing = reduce_steps(parts, summed, shares, bufs, Copies(*more))
    for turn in EXPERT_ORDER:
        next({"R": reducing, "X": computing, "T": returning}[turn], None)
    run(returning, reducing)


def run_experts(operands, summed, collective_id):
    rows = 32 * SLOTS
    low = operands[0].dtype
    hidden = operands[2].shape[1]
    parts = row_parts(summed)
    out_shape = [jax.ShapeDtypeStruct((32, 2, SLOTS, D // 4), low)] * 2
    out_shape += [jax.ShapeDtypeStruct(x.shape[3:], jnp.float32) for x in summed]
    out_shape += [jax.ShapeDtypeStruct((2, rows, hidden), low)] * 3
    scratch = [pltpu.VMEM(x.shape, low) for x in operands]
    scratch += [pltpu.VMEM((2, rows, D), low)] * 2
    scratch += [pltpu.VMEM((2, rows, D // 2), low)] * 2 + [pltpu.VMEM((2, rows, D // 4), low)] * 2
    scratch += [pltpu.SemaphoreType.DMA((2, 5))] + [pltpu.SemaphoreType.DMA((2,))] * 2
    scratch += [pltpu.SemaphoreType.DMA((36,))] * 2
    scratch += reduce_scratch(summed, parts)
    anywhere, vmem = pl.BlockSpec(memory_space=pl.ANY), pl.BlockSpec(memory_space=pltpu.VMEM)
    return pl.pallas_call(
        functools.partial(expert_kernel, parts, len(summed)),
        out_shape=out_shape,
        in_specs=[anywhere] * 5 + [vmem] * len(summed),
        out_specs=[vmem] * len(out_shape),
        scratch_shapes=scratch,
        compiler_params=pltpu.CompilerParams(
            collective_id=collective_id, has_side_effects=True, vmem_limit_bytes=VMEM_LIMIT
        ),
        name="run_experts",
    )(*operands, *summed)


def sum_more_kernel(parts, *refs):
    ins, adds, small = refs[:parts], refs[parts : 2 * parts], refs[2 * parts]
    outs, small_out = refs[2 * parts + 1 : 3 * parts + 1], refs[3 * parts + 1]
    got, half, far = (refs[(3 + i) * parts + 2 : (4 + i) * parts + 2] for i in range(3))
    small_got, small_half, small_far, send_sem, recv_sem = refs[6 * parts + 2 :]
    w = lax.axis_index("wa")
    core, place = w % 2, w // 2
    beside, across = {"wa": w + 1 - 2 * core}, {"wa": (w + 2) % 4}
    width = D // 2
    quarter = D // 4
    mine = pl.ds(pl.multiple_of(core * width, width), width)
    theirs = pl.ds(pl.multiple_of((1 - core) * width, width), width)
    own = pl.ds(pl.multiple_of(place * quarter, quarter), quarter)
    greet([beside, across])
    copies = Copies(send_sem, recv_sem)
    one = [copies.start(ins[a].at[:, theirs], got[a], beside) for a in range(parts)]
    one.append(copies.start(small, small_got, beside))
    two = []
    for a in range(parts):
        one[a].wait_recv()
        half[a][...] = ins[a][:, mine] + got[a][...]
        half[a][:, own] = half[a][:, own] + adds[a][...]
        two.append(copies.start(half[a], far[a], across))
    one[parts].wait_recv()
    small_half[...] = small[...] + small_got[...]
    two.append(copies.start(small_half, small_far, across))
    three = []
    for a in range(parts):
        two[a].wait_recv()
        outs[a][:, mine] = half[a][...] + far[a][...]
        three.append(copies.start(outs[a].at[:, mine], outs[a].at[:, mine], beside))
    two[parts].wait_recv()
    small_out[...] = small_half[...] + small_far[...]
    for copy in three:
        copy.wait_recv()
    copies.finish()


def sum_more(arrays, adds, small, collective_id, name):
    parts = len(arrays)
    rows = arrays[0].shape[0]
    dtype = arrays[0].dtype
    scratch = [pltpu.VMEM((rows, D // 2), dtype)] * (3 * parts)
    scratch += [pltpu.VMEM(small.shape, small.dtype)] * 3
    scratch += [pltpu.SemaphoreType.DMA((3 * parts + 2,))] * 2
    out_shape = [jax.ShapeDtypeStruct(x.shape, x.dtype) for x in (*arrays, small)]
    return vmem_call(
        functools.partial(sum_more_kernel, parts), out_shape, (*arrays, *adds, small), scratch,
        collective_id, name,
    )


def swish_parts(pre, lin, act_grads):
    sig = jax.nn.sigmoid(pre)
    swish = pre * sig
    slope = sig * (1.0 + pre * (1.0 - sig))
    return swish * lin, act_grads * lin * slope, act_grads * swish


def expert_grads_kernel(rows, grads, act, pre_grad, lin_grad, gate_grad, up_grad, down_grad):
    for at in range(0, D, 512):
        here = slice(at, at + 512)
        down_grad[0, :, here] = over(act[0], grads[0, :, here], (0, 0))
        gate_grad[0, :, here] = over(pre_grad[0], rows[0, :, here], (0, 0))
        up_grad[0, :, here] = over(lin_grad[0], rows[0, :, here], (0, 0))


def expert_grads(*operands):
    shape = jax.ShapeDtypeStruct((2, operands[2].shape[2], D), jnp.float32)

    def spec(x):
        return pl.BlockSpec((1, *x.shape[1:]), lambda e: (e, 0, 0))

    return pl.pallas_call(
        expert_grads_kernel,
        grid=(2,),
        out_shape=[shape] * 3,
        in_specs=[spec(x) for x in operands],
        out_specs=[spec(shape)] * 3,
        compiler_params=pltpu.CompilerParams(vmem_limit_bytes=VMEM_LIMIT),
        name="expert_grads",
    )(*operands)


def turned_gather(arrays, axis):
    widths = [a.shape[1] for a in arrays]
    whole = lax.all_gather(jnp.concatenate(arrays, axis=1), axis, axis=0, tiled=True)
    return jnp.split(whole, [sum(widths[:k]) for k in range(1, len(widths))], axis=1)


def rope_tables(positions):
    half_width = HD // 2
    inverse = 1.0 / ROPE_BASE ** (jnp.arange(half_width, dtype=jnp.float32) * 2.0 / HD)
    angles = positions[:, None] * inverse[None, :]
    cosine, sine = jnp.cos(angles), jnp.sin(angles)
    return jnp.concatenate([cosine, cosine], axis=1), jnp.concatenate([-sine, sine], axis=1)


def dot(left, right, over, dtype=jnp.float32, **kept):
    return lax.dot_general(
        left, right, ((over[:1], over[1:]), ((), ())), preferred_element_type=dtype, **kept
    )


def shards(
    tokens,
    cotangent,
    routes,
    attn_gain,
    query_weight,
    key_weight,
    value_weight,
    output_weight,
    mlp_gain,
    router_weight,
    shared_gate,
    shared_up,
    shared_down,
    expert_gate,
    expert_up,
    expert_down,
):
    low = jnp.bfloat16
    local_tokens = tokens.shape[0]
    head_cols = query_weight.shape[1]
    experts_all = router_weight.shape[1]
    groups = ("sp", "ctx")
    place, core = lax.axis_index("wa") // 2, lax.axis_index("wa") % 2
    quarter_at = core * (D // 2) + place * (D // 4)

    def quarter(x):
        return lax.dynamic_slice_in_dim(x, quarter_at, D // 4, 1)

    hidden_cols = shared_gate.shape[1]
    def beside(arrays):
        return jnp.concatenate(
            [jnp.pad(x, ((0, 0), (0, -x.shape[1] % HD))) for x in arrays], axis=1
        )

    shared_whole = lax.all_gather(
        beside((shared_gate, shared_up, shared_down.T)), groups, axis=0, tiled=True
    )
    router_own = jnp.concatenate([router_weight, mlp_gain[:, None]], axis=1)
    tokens_f = tokens.astype(jnp.float32)
    inv_one = lax.rsqrt(jnp.mean(tokens_f * tokens_f, axis=-1, keepdims=True) + EPSILON)
    unit_one = tokens_f * inv_one
    gain_one = attn_gain.astype(jnp.float32)[:, None]
    heads = jnp.concatenate([query_weight, key_weight, value_weight], axis=1)
    scaled = (gain_one * heads.astype(jnp.float32)).astype(low)
    head_rows, head_weights = gather_head(unit_one.astype(low), scaled, 1)
    head_rows, head_weights = head_rows.reshape(-1, D), head_weights.reshape(D, -1)
    blocks = jnp.arange(4, dtype=jnp.int32)[:, None] * 8 + lax.axis_index("ctx")
    positions = blocks * local_tokens + jnp.arange(local_tokens, dtype=jnp.int32)[None, :]
    cosine, sine = rope_tables(positions.reshape(-1).astype(jnp.float32))
    by_head = (4, local_tokens, HD)
    head_queries, own_keys, own_values = (
        x.reshape(by_head) for x in project(head_rows, head_weights, cosine, sine)
    )
    attn_out, attended, head_keys, head_values, probs, exact, whole = attention(
        head_queries, own_keys, own_values, beside((output_weight.T, router_own)), 2
    )
    attn_out = attn_out.astype(jnp.float32)
    whole = whole.reshape(D, -1)
    turned = whole[:, :head_cols]
    full_router = whole[:, head_cols : head_cols + experts_all]
    gain_two = whole[:, head_cols + experts_all].astype(jnp.float32)
    hidden_state = tokens_f + attn_out
    inv_two = lax.rsqrt(jnp.mean(hidden_state * hidden_state, axis=-1, keepdims=True) + EPSILON)
    unit_two = hidden_state * inv_two
    mlp_in = (unit_two * gain_two).astype(low)

    logits = dot(mlp_in, full_router, (1, 0))
    logit_exp = jnp.exp(logits - jnp.max(logits, axis=-1, keepdims=True))
    router_probs = logit_exp / jnp.sum(logit_exp, axis=-1, keepdims=True)
    experts = jnp.arange(experts_all, dtype=jnp.int32)
    chosen = jnp.zeros((local_tokens, experts_all), jnp.bool_)
    for j in range(TOP):
        chosen = chosen | (routes[:, j : j + 1] == experts[None, :])
    ids = jnp.arange(local_tokens, dtype=jnp.int32)
    before = (ids[None, :] < ids[:, None]).astype(low)
    rank = dot(before, chosen.astype(low), (1, 0))
    slot_of = jnp.where(chosen, rank, -1.0).astype(low)
    slot_ids = jnp.arange(experts_all * SLOTS, dtype=jnp.int32)
    widen = (experts[:, None] == slot_ids[None, :] // SLOTS).astype(low)
    taken = dot(slot_of, widen, (1, 0)) == (slot_ids % SLOTS).astype(jnp.float32)[None, :]
    probs_high = router_probs.astype(low)
    probs_rest = (router_probs - probs_high.astype(jnp.float32)).astype(low)
    pick = taken.astype(low)
    gate_high = jnp.where(taken, dot(probs_high, widen, (1, 0)), 0.0).astype(low)
    gate_rest = jnp.where(taken, dot(probs_rest, widen, (1, 0)), 0.0).astype(low)
    grad_quarter = quarter(cotangent)
    send_rows = dot(pick, quarter(mlp_in), (0, 0)).astype(low)
    send_grads = (
        dot(gate_high, grad_quarter, (0, 0)) + dot(gate_rest, grad_quarter, (0, 0))
    ).astype(low)
    by_owner = (32, 2, SLOTS, D // 4)
    rows_in, grads_in, shared_part, shared_in_part, *mlp_grads = dispatch(
        (send_rows.reshape(by_owner), send_grads.reshape(by_owner)),
        mlp_in,
        cotangent,
        shared_whole,
        0,
        hidden_cols,
        5,
    )
    mlp_grads = [x.reshape(4, 2, 4, x.shape[0] // 32, x.shape[1]) for x in mlp_grads]

    returned, rows_back, gate_share, up_share, down_share, *kept = run_experts(
        (
            rows_in,
            grads_in,
            expert_gate.transpose(0, 2, 1),
            expert_up.transpose(0, 2, 1),
            expert_down,
        ),
        mlp_grads,
        6,
    )
    gate_grad_turned, up_grad_turned, expert_down_grad = expert_grads(rows_in, grads_in, *kept)
    returned, rows_back = returned.reshape(-1, D // 4), rows_back.reshape(-1, D // 4)

    routed = (dot(gate_high, returned, (1, 0)) + dot(gate_rest, returned, (1, 0))).astype(low)
    routed_in = dot(pick, rows_back, (1, 0)).astype(low)
    slot_grads = jnp.where(taken, dot(grad_quarter, returned, (1, 1)), 0.0)
    prob_part = dot(slot_grads, widen.astype(jnp.float32), (1, 1), precision=PRECISE)
    prob_part = jnp.pad(prob_part, ((0, 0), (0, HD - experts_all)))
    mixed, mixed_in, prob_grads = sum_more(
        (shared_part, shared_in_part), (routed, routed_in), prob_part, 7, "sum_mlp"
    )
    block_out = (hidden_state + mixed.astype(jnp.float32)).astype(low)
    prob_grads = prob_grads[:, :experts_all]
    logit_grads = router_probs * (
        prob_grads - jnp.sum(router_probs * prob_grads, axis=-1, keepdims=True)
    )
    router_in_grad = dot(
        logit_grads, full_router.astype(jnp.float32), (1, 1), precision=PRECISE
    )
    mlp_in_grad = router_in_grad + mixed_in.astype(jnp.float32)
    gain_two_grad = jnp.sum(mlp_in_grad * unit_two, axis=0)
    scaled_two = mlp_in_grad * gain_two
    hidden_grad = cotangent.astype(jnp.float32) + inv_two * (
        scaled_two - unit_two * jnp.mean(scaled_two * unit_two, axis=-1, keepdims=True)
    )
    out_grad = hidden_grad.astype(low)
    router_grad = dot(mlp_in, logit_grads.astype(low), (0, 0))

    attended_grad = dot(out_grad, turned, (1, 0)).astype(low)
    def by_shard(x):
        return x.astype(low).reshape(4, 2, 4, x.shape[0] // 32, x.shape[1])

    small_grads = jnp.concatenate([router_grad, gain_two_grad[:, None]], axis=1)
    small_grads = jnp.pad(small_grads, ((0, 0), (0, HD - small_grads.shape[1])))
    summed = [by_shard(dot(out_grad, attended, (0, 0))), by_shard(small_grads)]
    scaled_one, head_shares, gain_terms, output_share, small_share = attention_back(
        (
            attended_grad,
            head_queries,
            head_keys,
            head_values,
            probs,
            exact,
            cosine,
            sine,
            head_rows,
            head_weights,
            heads,
        ),
        summed,
        9,
    )
    scaled_one = scaled_one.astype(jnp.float32)
    tokens_grad = (
        hidden_grad
        + inv_one
        * (scaled_one - unit_one * jnp.mean(scaled_one * unit_one, axis=-1, keepdims=True))
    ).astype(low)
    head_shares = head_shares.astype(jnp.float32) * gain_one
    query_share, key_share, value_share = (
        head_shares[..., k * HD : (k + 1) * HD].swapaxes(0, 1).reshape(-1, head_cols)
        for k in range(3)
    )
    return (
        block_out,
        tokens_grad,
        jnp.sum(gain_terms, axis=1),
        query_share,
        key_share,
        value_share,
        output_share.T,
        small_share[:, experts_all],
        small_share[:, :experts_all],
        gate_share,
        up_share,
        down_share.T,
        gate_grad_turned.transpose(0, 2, 1),
        up_grad_turned.transpose(0, 2, 1),
        expert_down_grad,
    )


def solution(mesh):
    placed = (
        P(("sp", "ctx"), None),
        P(("sp", "ctx"), None),
        P(("sp", "ctx"), None),
        P(("sp", "ctx")),
        P(("sp", "ctx"), "wa"),
        P(("sp", "ctx"), "wa"),
        P(("sp", "ctx"), "wa"),
        P("wa", ("sp", "ctx")),
        P(("sp", "ctx")),
        P(("sp", "ctx"), None),
        P(("sp", "ctx"), "wa"),
        P(("sp", "ctx"), "wa"),
        P("wa", ("sp", "ctx")),
        P(("sp", "ctx"), None, "wa"),
        P(("sp", "ctx"), None, "wa"),
        P(("sp", "ctx"), "wa", None),
    )
    return jax.shard_map(
        shards,
        mesh=mesh,
        in_specs=placed,
        out_specs=(
            P(("sp", "ctx"), None),
            P(("sp", "ctx"), None),
            P(("sp", "ctx")),
            P(("sp", "ctx"), "wa"),
            P(("sp", "ctx"), "wa"),
            P(("sp", "ctx"), "wa"),
            P("wa", ("sp", "ctx")),
            P(("sp", "ctx")),
            P(("sp", "ctx"), None),
            P(("sp", "ctx"), "wa"),
            P(("sp", "ctx"), "wa"),
            P("wa", ("sp", "ctx")),
            P(("sp", "ctx"), None, "wa"),
            P(("sp", "ctx"), None, "wa"),
            P(("sp", "ctx"), "wa", None),
        ),
        check_vma=False,
    )
```

```python
import functools

import jax
import jax.numpy as jnp
from jax import lax
from jax.experimental import pallas as pl
from jax.experimental.pallas import tpu as pltpu
from jax.sharding import PartitionSpec as P

D = 2048
HD = 128
TOP = 6


EPSILON = 1e-06
ROPE_BASE = 10000.0
MASKED = -1e30
PRECISE = lax.Precision.HIGHEST


MESH = pl.DeviceIdType.MESH
VMEM_LIMIT = 63 * 1024 * 1024

ORDERS = (
    (("z", "A"), ("z", "B"), ("y", "A"), ("y", "B")),
    (("z", "B"), ("z", "A"), ("y", "B"), ("y", "A")),
    (("y", "A"), ("y", "B"), ("z", "A"), ("z", "B")),
    (("y", "B"), ("y", "A"), ("z", "B"), ("z", "A")),
)


def paired(i, kind):
    return i + 1 - 2 * (i % 2) if kind == "A" else 3 - i


def own_place():
    c = lax.axis_index("ctx")
    return lax.axis_index("sp"), c // 4, c % 4


def neighbour(axis, kind):
    z, xh, y = own_place()
    if axis == "z":
        return {"sp": paired(z, kind)}
    if axis == "y":
        return {"ctx": 4 * xh + paired(y, kind)}
    return {"ctx": 4 * (1 - xh) + y}


def cube_places():
    rings = [neighbour(axis, kind) for axis in ("z", "y") for kind in ("A", "B")]
    return rings + [neighbour("x", "A")]


def pair_slots(i, kind):
    if kind == "A":
        return [(pl.ds((i // 2) * 2, 2), pl.ds(0, 2))]
    return [(pl.ds(i, 1), pl.ds(0, 1)), (pl.ds(3 - i, 1), pl.ds(1, 1))]


def pair_members(i, kind):
    if kind == "A":
        return [(i // 2) * 2, (i // 2) * 2 + 1]
    return [i, 3 - i]


def slot_in_pair(i, kind):
    return i % 2 if kind == "A" else 0

def over(left, right, dims):
    return lax.dot_general(
        left, right, ((dims[:1], dims[1:]), ((), ())), preferred_element_type=jnp.float32
    )


def head_columns(h):
    return pl.ds(pl.multiple_of(h * HD, HD), HD)


class Copies:
    def __init__(self, send_sem, recv_sem):
        self.send_sem, self.recv_sem, self.started = send_sem, recv_sem, []

    def start(self, src, dst, where):
        k = len(self.started)
        copy = pltpu.make_async_remote_copy(
            src_ref=src, dst_ref=dst, send_sem=self.send_sem.at[k],
            recv_sem=self.recv_sem.at[k], device_id=where, device_id_type=MESH,
        )
        copy.start()
        self.started.append(copy)
        return copy

    def finish(self):
        for copy in self.started:
            copy.wait_send()


def run(*programs):
    programs = list(programs)
    while programs:
        programs = [program for program in programs if next(program, None) is not None]


def in_turn(order, programs):
    for letter in order:
        next(programs[letter], None)


def greet(places):
    barrier = pltpu.get_barrier_semaphore()
    for place in places:
        pl.semaphore_signal(barrier, inc=1, device_id=place, device_id_type=MESH)
    pl.semaphore_wait(barrier, len(places))


def along_z():
    z = lax.axis_index("sp")
    return [{"sp": (z + d) % 4} for d in (1, 2, 3)]


def vmem_call(kernel, out_shape, operands, scratch, collective_id, name, **params):
    return pl.pallas_call(
        kernel,
        out_shape=out_shape,
        in_specs=[pl.BlockSpec(memory_space=pltpu.VMEM)] * len(operands),
        out_specs=jax.tree.map(lambda _: pl.BlockSpec(memory_space=pltpu.VMEM), out_shape),
        scratch_shapes=scratch,
        compiler_params=pltpu.CompilerParams(
            collective_id=collective_id,
            has_side_effects=collective_id is not None,
            vmem_limit_bytes=VMEM_LIMIT,
        ),
        name=name,
        **params,
    )(*operands)

def gather_steps(parts, ins, outs, copies, local_sem):
    z, xh, y = own_place()
    count = len(ins)

    def step(lane, p, s):
        ring1, ring2 = ORDERS[p][0][0], ORDERS[p][2][0]
        where = neighbour(*ORDERS[p][s])
        xl = xh if lane == 0 else 1 - xh
        zs, ys = [pl.ds(z, 1)], [pl.ds(y, 1)]
        full = [pl.ds(0, 4)]
        if s == 1:
            other = [d for d, _ in pair_slots(z if ring1 == "z" else y, ORDERS[p][0][1])]
            zs, ys = (other, ys) if ring1 == "z" else (zs, other)
        if s >= 2:
            zs, ys = (full, ys) if ring1 == "z" else (zs, full)
        if s == 3:
            other = [d for d, _ in pair_slots(z if ring2 == "z" else y, ORDERS[p][2][1])]
            zs, ys = (other, ys) if ring2 == "z" else (zs, other)
        started = []
        for a, rows, cols in parts[p]:
            for zd in zs:
                for yd in ys:
                    place = outs[a].at[zd, pl.ds(xl, 1), yd, rows, cols]
                    started.append(copies.start(place, place, where))
        return started

    local = [
        pltpu.make_async_copy(ins[a], outs[a].at[z, xh, y], local_sem.at[a]) for a in range(count)
    ]
    for copy in local:
        copy.start()
    across = [
        [
            copies.start(
                ins[a].at[rows, cols], outs[a].at[z, xh, y, rows, cols], neighbour("x", "A")
            )
            for a, rows, cols in part
        ]
        for part in parts
    ]
    for copy in local:
        copy.wait()
    flying = {}
    for lane, s in (
        (0, 0), (0, 1), (1, 0), (0, 2), (1, 1), (0, 3), (1, 2), (1, 3), (0, 4), (1, 4)
    ):
        for p in range(4):
            for copy in flying.get((lane, p), across[p] if lane == 1 else []):
                copy.wait_recv()
            flying[lane, p] = step(lane, p, s) if s < 4 else []
        yield True
    copies.finish()


def gather_kernel(parts, count, *refs):
    ins, outs = refs[:count], refs[count : 2 * count]
    send_sem, recv_sem, local_sem = refs[2 * count :]
    greet(cube_places())
    run(gather_steps(parts, ins, outs, Copies(send_sem, recv_sem), local_sem))


def gather_cube(arrays, parts, collective_id, name):
    count = len(arrays)
    copies = 11 * sum(len(part) for part in parts)
    return pl.pallas_call(
        functools.partial(gather_kernel, parts, count),
        out_shape=[jax.ShapeDtypeStruct((4, 2, 4, *a.shape), a.dtype) for a in arrays],
        in_specs=[pl.BlockSpec(memory_space=pl.ANY)] * count,
        out_specs=[pl.BlockSpec(memory_space=pl.ANY)] * count,
        scratch_shapes=[
            pltpu.SemaphoreType.DMA((copies,)),
            pltpu.SemaphoreType.DMA((copies,)),
            pltpu.SemaphoreType.DMA((count,)),
        ],
        compiler_params=pltpu.CompilerParams(collective_id=collective_id, has_side_effects=True),
        name=name,
    )(*arrays)


def entries_of(parts):
    return [(p, *entry) for p in range(4) for entry in parts[p]]


CUBE_ORDER = tuple((stage, lane) for stage in range(5) for lane in (1, 0))


def reduce_steps(parts, ins, outs, bufs, copies):
    entries = entries_of(parts)
    z, xh, y = own_place()
    start = copies.start
    flying = {}

    def first(lane, e):
        p, a, rows, cols = entries[e]
        ring2, near = ORDERS[p][2]
        axis, kind = ORDERS[p][3]
        xl = xh if lane == 0 else 1 - xh
        theirs = paired(z if ring2 == "z" else y, kind)
        copies = []
        for src, dst in pair_slots(theirs, near):
            if ring2 == "z":
                block, place = ins[a].at[src, xl, :, rows, cols], bufs[5 * e].at[lane, dst]
            else:
                block, place = ins[a].at[:, xl, src, rows, cols], bufs[5 * e].at[lane, :, dst]
            copies.append(start(block, place, neighbour(axis, kind)))
        flying[lane, e] = copies

    def second(lane, e):
        p, a, rows, cols = entries[e]
        ring2 = ORDERS[p][2][0]
        axis, kind = ORDERS[p][2]
        xl = xh if lane == 0 else 1 - xh
        mine = z if ring2 == "z" else y
        buf = bufs[5 * e]
        for copy in flying[lane, e]:
            copy.wait_recv()
        slot = slot_in_pair(mine, kind)

        def add(j, place):
            def one(i, carry):
                if ring2 == "z":
                    buf[lane, j, i] = buf[lane, j, i] + ins[a][place, xl, i, rows, cols]
                else:
                    buf[lane, i, j] = buf[lane, i, j] + ins[a][i, xl, place, rows, cols]
                return carry

            lax.fori_loop(0, 4, one, 0)

        add(1 - slot, paired(mine, kind))
        half = buf.at[lane, 1 - slot] if ring2 == "z" else buf.at[lane, :, 1 - slot]
        flying[lane, e] = [start(half, bufs[5 * e + 1].at[lane], neighbour(axis, kind))]
        add(slot, mine)

    def third(lane, e):
        p = entries[e][0]
        ring1, ring2 = ORDERS[p][0][0], ORDERS[p][2][0]
        axis, kind = ORDERS[p][1]
        before, buf = bufs[5 * e], bufs[5 * e + 1]
        for copy in flying[lane, e]:
            copy.wait_recv()
        slot = slot_in_pair(z if ring2 == "z" else y, ORDERS[p][2][1])

        def one(i, carry):
            other = before[lane, slot, i] if ring2 == "z" else before[lane, i, slot]
            buf[lane, i] = buf[lane, i] + other
            return carry

        lax.fori_loop(0, 4, one, 0)
        theirs = paired(z if ring1 == "z" else y, kind)
        flying[lane, e] = [
            start(buf.at[lane, src], bufs[5 * e + 2].at[lane, dst], neighbour(axis, kind))
            for src, dst in pair_slots(theirs, ORDERS[p][0][1])
        ]

    def fourth(lane, e):
        p = entries[e][0]
        ring1 = ORDERS[p][0][0]
        axis, kind = ORDERS[p][0]
        mine = z if ring1 == "z" else y
        before, buf = bufs[5 * e + 1], bufs[5 * e + 2]
        for copy in flying[lane, e]:
            copy.wait_recv()
        slot = slot_in_pair(mine, kind)
        buf[lane, 1 - slot] = buf[lane, 1 - slot] + before[lane, paired(mine, kind)]
        flying[lane, e] = [
            start(buf.at[lane, 1 - slot], bufs[5 * e + 3].at[lane], neighbour(axis, kind))
        ]
        buf[lane, slot] = buf[lane, slot] + before[lane, mine]

    def last(lane, e):
        p, a, rows, cols = entries[e]
        ring1 = ORDERS[p][0][0]
        before, buf = bufs[5 * e + 2], bufs[5 * e + 3]
        for copy in flying[lane, e]:
            copy.wait_recv()
        slot = slot_in_pair(z if ring1 == "z" else y, ORDERS[p][0][1])
        if lane == 1:
            buf[1] = buf[1] + before[1, slot]
            flying["x", e] = start(buf.at[1], bufs[5 * e + 4], neighbour("x", "A"))
        else:
            flying["x", e].wait_recv()
            total = (
                buf[0].astype(jnp.float32)
                + before[0, slot].astype(jnp.float32)
                + bufs[5 * e + 4][...].astype(jnp.float32)
            )
            outs[a][rows, cols] = total.astype(outs[a].dtype)

    stages = (first, second, third, fourth, last)
    for at, lane in CUBE_ORDER:
        for e in range(len(entries)):
            stages[at](lane, e)
        yield True
    copies.finish()


def reduce_kernel(parts, count, *refs):
    size = 5 * len(entries_of(parts))
    ins, outs = refs[:count], refs[count : 2 * count]
    bufs = refs[2 * count : 2 * count + size]
    greet(cube_places())
    run(reduce_steps(parts, ins, outs, bufs, Copies(*refs[2 * count + size :])))


def reduce_scratch(arrays, parts):
    scratch = []
    for p in range(4):
        pair = (2, 4) if ORDERS[p][2][0] == "z" else (4, 2)
        for a, rows, cols in parts[p]:
            for lead in ((2, *pair), (2, 4), (2, 2), (2,), ()):
                scratch.append(pltpu.VMEM((*lead, rows.size, cols.size), arrays[a].dtype))
    copies = 13 * sum(len(part) for part in parts)
    return scratch + [pltpu.SemaphoreType.DMA((copies,))] * 2


def reduce_cube(arrays, parts, collective_id, name, dtype=jnp.float32):
    count = len(arrays)
    scratch = reduce_scratch(arrays, parts)
    return pl.pallas_call(
        functools.partial(reduce_kernel, parts, count),
        out_shape=[jax.ShapeDtypeStruct(a.shape[3:], dtype) for a in arrays],
        in_specs=[pl.BlockSpec(memory_space=pltpu.VMEM)] * count,
        out_specs=[pl.BlockSpec(memory_space=pltpu.VMEM)] * count,
        scratch_shapes=scratch,
        compiler_params=pltpu.CompilerParams(
            collective_id=collective_id, has_side_effects=True, vmem_limit_bytes=VMEM_LIMIT
        ),
        name=name,
    )(*arrays)


def row_parts(arrays):
    parts = []
    for p in range(4):
        part = []
        for a, array in enumerate(arrays):
            rows, columns = array.shape[-2:]
            part.append((a, pl.ds(p * rows // 4, rows // 4), pl.ds(0, columns)))
        parts.append(part)
    return parts


def whole_parts(arrays):
    return [[(a, pl.ds(0, x.shape[-2]), pl.ds(0, x.shape[-1]))] for a, x in enumerate(arrays)]


def half_parts(arrays):
    return [
        [(a, pl.ds(0, x.shape[-2]), pl.ds(h * x.shape[-1] // 2, x.shape[-1] // 2))]
        for a, x in enumerate(arrays)
        for h in range(2)
    ]


def wa_places():
    w = lax.axis_index("wa")
    return [{"wa": w + 1 - 2 * (w % 2)}, {"wa": (w + 2) % 4}]


def sum_wa_steps(x, out, half, got, far, copies):
    core = lax.axis_index("wa") % 2
    beside, across = wa_places()
    width = x.shape[1] // 2
    mine = pl.ds(pl.multiple_of(core * width, width), width)
    theirs = pl.ds(pl.multiple_of((1 - core) * width, width), width)
    one = copies.start(x.at[:, theirs], got, beside)
    yield True
    one.wait_recv()
    half[...] = x[:, mine] + got[...]
    two = copies.start(half, far, across)
    yield True
    two.wait_recv()
    out[:, mine] = half[...] + far[...]
    three = copies.start(out.at[:, mine], out.at[:, mine], beside)
    yield True
    three.wait_recv()
    copies.finish()


def sum_wa_kernel(x, out, half, got, far, send_sem, recv_sem):
    greet(wa_places())
    run(sum_wa_steps(x, out, half, got, far, Copies(send_sem, recv_sem)))


def sum_wa(x, collective_id, name):
    rows, columns = x.shape
    return pl.pallas_call(
        sum_wa_kernel,
        out_shape=jax.ShapeDtypeStruct(x.shape, x.dtype),
        in_specs=[pl.BlockSpec(memory_space=pltpu.VMEM)],
        out_specs=pl.BlockSpec(memory_space=pltpu.VMEM),
        scratch_shapes=[pltpu.VMEM((rows, columns // 2), x.dtype)] * 3
        + [pltpu.SemaphoreType.DMA((3,)), pltpu.SemaphoreType.DMA((3,))],
        compiler_params=pltpu.CompilerParams(
            collective_id=collective_id, has_side_effects=True, vmem_limit_bytes=VMEM_LIMIT
        ),
        name=name,
    )(x)

def ctx_gather_steps(parts, copies):
    z, xh, y = own_place()

    def send(part, xl, place, axis, kind):
        ref, rows = part
        block = ref.at[:, xl, place, rows]
        return copies.start(block, block, neighbour(axis, kind))

    near, far = ("A", "B"), ("B", "A")
    first, across, last = {}, [], []
    for a in range(2):
        first[0, a] = send(parts[a], xh, y, "y", near[a])
        across.append(send(parts[a], xh, y, "x", "A"))
    yield True
    for lane in range(2):
        xl = xh if lane == 0 else 1 - xh
        if lane == 1:
            for a in range(2):
                across[a].wait_recv()
                first[1, a] = send(parts[a], xl, y, "y", near[a])
            yield True
        for a in range(2):
            first[lane, a].wait_recv()
            for place, _ in pair_slots(y, near[a]):
                last.append(send(parts[a], xl, place, "y", far[a]))
        yield True
    for copy in last:
        copy.wait_recv()
    copies.finish()


CTX_ORDER = ((0, 1), (1, 1), (0, 0), (2, 1), (1, 0), (2, 0))


def ctx_reduce_steps(parts, bufs, sums, cross, own, copies):
    z, xh, y = own_place()
    near, far = ("A", "B"), ("B", "A")
    flying = {}

    def first(lane):
        xl = xh if lane == 0 else 1 - xh
        for a, (ref, rows) in enumerate(parts):
            flying[lane, a] = [
                copies.start(
                    ref.at[:, xl, src, rows], bufs[a].at[lane, :, dst], neighbour("y", far[a])
                )
                for src, dst in pair_slots(paired(y, far[a]), near[a])
            ]

    def second(lane):
        xl = xh if lane == 0 else 1 - xh
        for a, (ref, rows) in enumerate(parts):
            for copy in flying[lane, a]:
                copy.wait_recv()
            slot = slot_in_pair(y, near[a])

            def add(j, place):
                def one(i, carry):
                    bufs[a][lane, i, j] = bufs[a][lane, i, j] + ref[i, xl, place, rows]
                    return carry

                lax.fori_loop(0, 4, one, 0)

            add(1 - slot, paired(y, near[a]))
            flying[lane, a] = copies.start(
                bufs[a].at[lane, :, 1 - slot], sums[a].at[lane], neighbour("y", near[a])
            )
            add(slot, y)

    def third(lane):
        for a in range(2):
            flying[lane, a].wait_recv()
            slot = slot_in_pair(y, near[a])

            def more(i, carry):
                sums[a][lane, i] = sums[a][lane, i] + bufs[a][lane, i, slot]
                return carry

            lax.fori_loop(0, 4, more, 0)
            if lane == 1:
                flying["x", a] = copies.start(sums[a].at[1], cross[a], neighbour("x", "A"))

    for stage, lane in CTX_ORDER:
        (first, second, third)[stage](lane)
        yield True
    for a in range(2):
        flying["x", a].wait_recv()

        def total(i, carry):
            own[a][i] = sums[a][0, i] + cross[a][i]
            return carry

        lax.fori_loop(0, 4, total, 0)
    yield True
    copies.finish()


def ctx_scratch(shapes, dtype):
    scratch = [
        pltpu.VMEM((*lead, *shape), dtype) for lead in ((2, 4, 2), (2, 4), (4,), (4,)) for shape in shapes
    ]
    return scratch + [pltpu.SemaphoreType.DMA((12,))] * 2


def column_halves(width):
    return [pl.ds(0, width // 2), pl.ds(width // 2, width // 2)]


def rows_gather_steps(x, out, copies):
    z = lax.axis_index("sp")
    near, far = ("A", "B"), ("B", "A")
    halves = column_halves(x.shape[1])
    first = [
        copies.start(x.at[:, halves[a]], out.at[z, :, halves[a]], neighbour("z", near[a]))
        for a in range(2)
    ]
    out[z] = x[...]
    yield True
    last = []
    for a in range(2):
        first[a].wait_recv()
        for place, _ in pair_slots(z, near[a]):
            block = out.at[place, :, halves[a]]
            last.append(copies.start(block, block, neighbour("z", far[a])))
    yield True
    for copy in last:
        copy.wait_recv()
    copies.finish()


def rows_reduce_steps(x, out, bufs, sums, copies):
    z = lax.axis_index("sp")
    near, far = ("A", "B"), ("B", "A")
    halves = column_halves(x.shape[2])
    flying = [
        [
            copies.start(x.at[src, :, halves[a]], bufs[a].at[dst], neighbour("z", far[a]))
            for src, dst in pair_slots(paired(z, far[a]), near[a])
        ]
        for a in range(2)
    ]
    yield True
    second = []
    for a in range(2):
        for copy in flying[a]:
            copy.wait_recv()
        slot = slot_in_pair(z, near[a])
        bufs[a][1 - slot] = bufs[a][1 - slot] + x[paired(z, near[a]), :, halves[a]]
        second.append(copies.start(bufs[a].at[1 - slot], sums[a], neighbour("z", near[a])))
        bufs[a][slot] = bufs[a][slot] + x[z, :, halves[a]]
    yield True
    for a in range(2):
        second[a].wait_recv()
        slot = slot_in_pair(z, near[a])
        out[:, halves[a]] = bufs[a][slot] + sums[a][...]
    yield True
    copies.finish()


def gather_head_kernel(x, w, rows_out, weights_out, *sems):
    z, xh, y = own_place()
    greet(along_z() + [neighbour("y", "A"), neighbour("y", "B"), neighbour("x", "A")])
    turns = Copies(*sems[:2])
    heads = w.shape[1] // HD // 4

    def columns(k, h):
        return pl.ds(pl.multiple_of(k * 4 * HD + h * HD, HD), HD)

    for d in (1, 2, 3):
        there = (z + d) % 4
        for k in range(heads):
            place = weights_out.at[z, xh, y, :, pl.ds(k * HD, HD)]
            turns.start(w.at[:, columns(k, there)], place, {"sp": there})
    rows = rows_gather_steps(x, rows_out, Copies(*sems[2:4]))
    next(rows)
    for k in range(heads):
        weights_out[z, xh, y, :, k * HD : (k + 1) * HD] = w[:, columns(k, z)]
    for copy in turns.started:
        copy.wait_recv()
    half = w.shape[0] // 2
    parts = [(weights_out, pl.ds(a * half, half)) for a in range(2)]
    run(ctx_gather_steps(parts, Copies(*sems[4:6])), rows)
    turns.finish()


def gather_head(x, w, collective_id):
    out_shape = [
        jax.ShapeDtypeStruct((4, *x.shape), x.dtype),
        jax.ShapeDtypeStruct((4, 2, 4, w.shape[0], w.shape[1] // 4), w.dtype),
    ]
    sems = [pltpu.SemaphoreType.DMA((n,)) for n in (9, 9, 5, 5, 12, 12)]
    return vmem_call(gather_head_kernel, out_shape, (x, w), sems, collective_id, "gather_head")


def project_kernel(x, w, cosine, sine, q, k, v):
    raw = jnp.dot(x[...], w[...], preferred_element_type=jnp.float32)
    for at, out in enumerate((q, k)):
        one = raw[:, at * HD : (at + 1) * HD]
        out[...] = (one * cosine[...] + pltpu.roll(one, HD // 2, 1) * sine[...]).astype(out.dtype)
    v[...] = raw[:, 2 * HD :].astype(v.dtype)


def project(x, w, cosine, sine):
    shape = jax.ShapeDtypeStruct((x.shape[0], HD), x.dtype)
    return vmem_call(project_kernel, [shape] * 3, (x, w, cosine, sine), [], None, "project_head")


def attend_steps(q, k, v, blocks, exact, probs, scores):
    rows = q.shape[1]
    span = 8 * rows
    first = lax.axis_index("ctx") * rows
    scale = HD ** (-0.5)
    at = 0

    def chunk(ref, c):
        return ref[c].reshape(span, HD)

    for block in range(4):
        for c in range(block + 1):
            part = over(q[block], chunk(k, c), (1, 1)) * scale
            if c == block:
                row = lax.broadcasted_iota(jnp.int32, part.shape, 0)
                col = lax.broadcasted_iota(jnp.int32, part.shape, 1)
                part = jnp.where(col <= row + first, part, MASKED)
            scores[:, c * span : (c + 1) * span] = part
        width = (block + 1) * span
        top = jnp.max(scores[:, :width], axis=1, keepdims=True)
        total = jnp.zeros_like(top)
        for c in range(block + 1):
            part = jnp.exp(scores[:, c * span : (c + 1) * span] - top)
            total = total + jnp.sum(part, axis=1, keepdims=True)
            scores[:, c * span : (c + 1) * span] = part
        scaled = 1.0 / total
        result = jnp.zeros((rows, HD), jnp.float32)
        for c in range(block + 1):
            low = (scores[:, c * span : (c + 1) * span] * scaled).astype(probs.dtype)
            probs[at] = low
            result = result + over(low, chunk(v, c), (1, 0))
            at += 1
        exact[block] = result
        blocks[block] = result.astype(blocks.dtype)
        yield True


ATTEND_ORDER = "KGGKGKGKGK" + "AGAGAGA"


def attention_kernel(parts, q, k, v, own, total, attended, keys, values, probs, exact, whole, *refs):
    scores, blocks, part, *wa_bufs = refs[:6]
    sems = refs[6:]
    z, xh, y = own_place()
    places = along_z() + [neighbour("y", "A"), neighbour("y", "B"), neighbour("x", "A")]
    greet(places + wa_places())
    keys[:, xh, y] = k[...]
    values[:, xh, y] = v[...]
    rows = pl.ds(0, k.shape[1])
    programs = {
        "K": ctx_gather_steps([(keys, rows), (values, rows)], Copies(*sems[0:2])),
        "G": gather_steps(parts, [own], [whole], Copies(*sems[2:4]), sems[4]),
        "A": attend_steps(q, keys, values, blocks, exact, probs, scores),
    }
    in_turn(ATTEND_ORDER, programs)
    turns = Copies(*sems[5:7])
    for d in (1, 2, 3):
        there = (z + d) % 4
        turns.start(blocks.at[there], attended.at[:, head_columns(z)], {"sp": there})
    attended[:, head_columns(z)] = blocks[z]
    run(programs["G"])
    for copy in turns.started:
        copy.wait_recv()
    turns.finish()
    width = attended.shape[1]
    step = D // 4
    for i in range(4):
        weights = whole[i].reshape(step, -1)[:, :width]
        part[:, i * step : (i + 1) * step] = over(attended[...], weights, (1, 1)).astype(part.dtype)
    run(sum_wa_steps(part, total, *wa_bufs, Copies(*sems[7:9])))


def attention(q, k, v, own, collective_id):
    rows, low = q.shape[1], q.dtype
    every = jax.ShapeDtypeStruct((4, 2, 4, rows, HD), low)
    out_shape = [
        jax.ShapeDtypeStruct((rows, D), low),
        jax.ShapeDtypeStruct((rows, 4 * HD), low),
        every,
        every,
        jax.ShapeDtypeStruct((10, rows, 8 * rows), low),
        jax.ShapeDtypeStruct(q.shape, jnp.float32),
        jax.ShapeDtypeStruct((4, 2, 4, *own.shape), low),
    ]
    scratch = [pltpu.VMEM((rows, 32 * rows), jnp.float32), pltpu.VMEM(q.shape, low)]
    scratch += [pltpu.VMEM((rows, D), low)] + [pltpu.VMEM((rows, D // 2), low)] * 3
    scratch += [pltpu.SemaphoreType.DMA((n,)) for n in (12, 12, 44, 44, 1, 3, 3, 3, 3)]
    return vmem_call(
        functools.partial(attention_kernel, row_parts([own])), out_shape, (q, k, v, own), scratch,
        collective_id, "attention",
    )


def attend_back_steps(q, k, v, probs, grad, exact, dq, dk, dv, dk_sum, dv_sum):
    rows = q.shape[1]
    span = 8 * rows
    scale = HD ** (-0.5)
    at = 0

    def chunk(ref, c):
        return ref[c].reshape(span, HD)

    for block in range(4):
        low_grad = grad[block]
        delta = jnp.sum(low_grad.astype(jnp.float32) * exact[block], axis=1, keepdims=True)
        total = jnp.zeros((rows, HD), jnp.float32)
        for c in range(block + 1):
            low = probs[at]
            back = over(low_grad, chunk(v, c), (1, 1))
            terms = (low.astype(jnp.float32) * (back - delta)).astype(q.dtype)
            total = total + over(terms, chunk(k, c), (1, 0))
            key_terms = over(terms, q[block], (0, 0))
            value_terms = over(low, low_grad, (0, 0))
            if c == block:
                dk_sum[c] = key_terms
                dv_sum[c] = value_terms
            else:
                dk_sum[c] = dk_sum[c] + key_terms
                dv_sum[c] = dv_sum[c] + value_terms
            at += 1
        dq[block] = (total * scale).astype(dq.dtype)
        yield True
    for c in range(4):
        dk[c] = (dk_sum[c] * scale).astype(dk.dtype).reshape(dk.shape[1:])
        dv[c] = dv_sum[c].astype(dv.dtype).reshape(dv.shape[1:])
    yield True


def project_back_steps(dq, dk, dv, cosine, sine, x, w, back, grad):
    low = back.dtype
    rows = dq.shape[1]
    terms = []
    for src in (dq, dk):
        one = src[...].reshape(4 * rows, HD).astype(jnp.float32)
        terms.append((one * cosine[...] - pltpu.roll(one, HD // 2, 1) * sine[...]).astype(low))
    terms = jnp.concatenate([*terms, dv[...].reshape(4 * rows, HD)], axis=1)
    step = D // 4
    for i in range(4):
        here = slice(i * step, (i + 1) * step)
        back[:, :, here] = over(terms, w[here], (1, 1)).astype(low).reshape(4, rows, step)
        grad[i] = over(x[:, here], terms, (0, 0)).astype(low).reshape(grad.shape[1:])
        yield True


BACK_ORDER = "AAAAACCCCCCC"


def attention_back_kernel(parts, count, *refs):
    attended_grad, q, keys, values, probs, exact, cosine, sine, x, w, heads, *refs = refs
    summed, refs = refs[:count], refs[count:]
    total, grad_out, gain_out, *refs = refs
    shares, refs = refs[:count], refs[count:]
    head_grad, dq, dk, dv, dk_sum, dv_sum, back, grad, mixed, *refs = refs
    z_bufs, z_sums, wa_bufs, gain_bufs = refs[0:2], refs[2:4], refs[4:7], refs[7:9]
    refs = refs[9:]
    (kv_bufs, kv_sums, kv_cross, kv_own), refs = (refs[2 * i : 2 * i + 2] for i in range(4)), refs[8:]
    kv_sems, refs = refs[:2], refs[2:]
    (bufs, sums, cross, own), refs = (refs[2 * i : 2 * i + 2] for i in range(4)), refs[8:]
    head_sems, refs = refs[:2], refs[2:]
    sems, refs = refs[:10], refs[10:]
    cube_bufs, cube_sems = refs[:-2], refs[-2:]
    z = lax.axis_index("sp")
    places = along_z() + [neighbour("y", "A"), neighbour("y", "B"), neighbour("x", "A")]
    greet(places + wa_places())
    turns = Copies(*sems[0:2])
    for d in (1, 2, 3):
        there = (z + d) % 4
        turns.start(attended_grad.at[:, head_columns(there)], head_grad.at[z], {"sp": there})
    head_grad[z] = attended_grad[:, head_columns(z)]
    rows = pl.ds(0, dq.shape[1])
    programs = {
        "R": reduce_steps(parts, summed, shares, cube_bufs, Copies(*cube_sems)),
        "A": attend_back_steps(
            q, keys, values, probs, head_grad, exact, dq, dk, dv, dk_sum, dv_sum
        ),
        "C": ctx_reduce_steps(
            [(dk, rows), (dv, rows)], kv_bufs, kv_sums, kv_cross, kv_own, Copies(*kv_sems)
        ),
    }
    in_turn("RR", programs)
    for copy in turns.started:
        copy.wait_recv()
    turns.finish()
    in_turn(BACK_ORDER, programs)
    run(programs["C"])
    run(project_back_steps(dq, *kv_own, cosine, sine, x, w, back, grad))
    half = grad.shape[3] // 2
    grad_parts = [(grad, pl.ds(a * half, half)) for a in range(2)]

    def sums_of_rows():
        yield from rows_reduce_steps(back, mixed, z_bufs, z_sums, Copies(*sems[2:4]))
        yield from sum_wa_steps(mixed, total, *wa_bufs, Copies(*sems[4:6]))

    def grads():
        yield from ctx_reduce_steps(grad_parts, bufs, sums, cross, own, Copies(*head_sems))
        turns = Copies(*sems[6:8])
        for d in (1, 2, 3):
            there = (z + d) % 4
            for a in range(2):
                turns.start(own[a].at[there], grad_out.at[z, grad_parts[a][1]], {"sp": there})
        for a in range(2):
            grad_out[z, a * half : (a + 1) * half] = own[a][z]
        yield True
        for copy in turns.started:
            copy.wait_recv()
        turns.finish()
        products = jnp.zeros(gain_out.shape, jnp.float32)
        for h in range(4):
            for k in range(grad_out.shape[2] // HD):
                ours = heads[:, (4 * k + h) * HD : (4 * k + h + 1) * HD].astype(jnp.float32)
                theirs = grad_out[h, :, k * HD : (k + 1) * HD].astype(jnp.float32)
                products = products + ours * theirs
        gain_out[...] = products
        copies = Copies(*sems[8:10])
        for place, buf in zip(wa_places(), gain_bufs):
            copy = copies.start(gain_out, buf, place)
            yield True
            copy.wait()
            gain_out[...] = gain_out[...] + buf[...]

    run(grads(), sums_of_rows(), programs["R"])


def attention_back(operands, summed, collective_id):
    attended_grad, q, keys, _, _, _, _, _, x, w, heads = operands
    rows, low = q.shape[1], q.dtype
    shard = heads.shape[0]
    parts = row_parts(summed)
    out_shape = [
        jax.ShapeDtypeStruct((rows, D), low),
        jax.ShapeDtypeStruct((4, shard, w.shape[1]), low),
        jax.ShapeDtypeStruct((shard, HD), jnp.float32),
    ]
    out_shape += [jax.ShapeDtypeStruct(a.shape[3:], jnp.float32) for a in summed]
    wide = (rows, D // 2)
    sums = pltpu.VMEM((4, 8 * rows, HD), jnp.float32)
    scratch = [pltpu.VMEM(a.shape, low) for a in (q, q, keys, keys)] + [sums, sums]
    scratch += [pltpu.VMEM((4, rows, D), low), pltpu.VMEM((4, 2, 4, shard, w.shape[1]), low)]
    scratch += [pltpu.VMEM((rows, D), low)]
    scratch += [pltpu.VMEM((2, *wide), low)] * 2 + [pltpu.VMEM(wide, low)] * 5
    scratch += [pltpu.VMEM((shard, HD), jnp.float32)] * 2
    scratch += ctx_scratch([(rows, HD)] * 2, low) + ctx_scratch([(shard // 2, w.shape[1])] * 2, low)
    scratch += [pltpu.SemaphoreType.DMA((n,)) for n in (3, 3, 5, 5, 3, 3, 6, 6, 2, 2)]
    scratch += reduce_scratch(summed, parts)
    return vmem_call(
        functools.partial(attention_back_kernel, parts, len(summed)), out_shape,
        (*operands, *summed), scratch, collective_id, "attention_back",
    )


SLOTS = 16
GROUP_ORDER = ((0, 1), (1, 0), (3, 0), (1, 1), (3, 1), (2, 0), (2, 1), (0, 0))
SENT_AHEAD = 4
PASSED_BEHIND = 2
FIRST_COMPLETE = 11


def token_places():
    z, xh, y = own_place()
    w = lax.axis_index("wa")
    return z, xh, y, w // 2, w % 2


def block_device(dz, dx, dy):
    z, xh, y, place, core = token_places()
    there_z, there_x, there_y = (z + dz) % 4, (xh + dx) % 2, (y + dy) % 4
    there = (place + dx) % 2
    where = {"sp": there_z, "ctx": 4 * there_x + there_y, "wa": 2 * there + core}
    return where, there_z * 8 + there_x * 4 + there_y


def greet_blocks(others):
    barrier = pltpu.get_barrier_semaphore()

    def one(i, carry):
        where, _ = block_device(i // 8, (i // 4) % 2, i % 4)
        pl.semaphore_signal(barrier, inc=1, device_id=where, device_id_type=MESH)
        return carry

    lax.fori_loop(1, 32, one, 0)
    others = wa_places() + others
    for place in others:
        pl.semaphore_signal(barrier, inc=1, device_id=place, device_id_type=MESH)
    pl.semaphore_wait(barrier, 31 + len(others))


def quarter_columns(place, core):
    quarter = D // 4
    return pl.ds(pl.multiple_of(core * 2 * quarter + place * quarter, quarter), quarter)


def dispatch_steps(ins, outs, out_sem, in_sem, own_sem, copies):
    count = len(ins)
    z, xh, y, place, core = token_places()
    beside, across = wa_places()
    me = z * 8 + xh * 4 + y
    columns = quarter_columns(place, core)
    here = pl.ds(pl.multiple_of(me * SLOTS, SLOTS), SLOTS)
    own = [
        pltpu.make_async_copy(ins[a].at[me], outs[a].at[:, here, columns], own_sem.at[a])
        for a in range(count)
    ]
    for copy in own:
        copy.start()
    items = [(a, dz, dx) for a in range(count) for dz, dx in GROUP_ORDER]
    passed, last = {}, []
    firsts = len(GROUP_ORDER)

    def forward(part, i):
        copy = copies.start(part, part, beside)
        last.append((i // firsts, copy))

    def send(i):
        a, dz, dx = items[i]

        def one(dy, carry):
            where, block = block_device(dz, dx, dy)
            pltpu.make_async_remote_copy(
                src_ref=ins[a].at[block], dst_ref=outs[a].at[:, here, columns],
                send_sem=out_sem.at[a], recv_sem=in_sem.at[a, dz * 2 + dx],
                device_id=where, device_id_type=MESH,
            ).start()
            return carry

        lax.fori_loop(1 if dz + dx == 0 else 0, 4, one, 0)

    def rows_of(dz, dx):
        first = ((z - dz + 4) % 4 * 8 + (xh + dx) % 2 * 4) * SLOTS
        return pl.ds(pl.multiple_of(first, 4 * SLOTS), 4 * SLOTS)

    def arrived(i):
        a, dz, dx = items[i]
        few = 3 if dz + dx == 0 else 4
        sample = outs[a].at[:, pl.ds(0, few * SLOTS), columns]
        pltpu.make_async_copy(sample, sample, in_sem.at[a, dz * 2 + dx]).wait()
        if dz + dx == 0:
            own[a].wait()
        part = outs[a].at[:, rows_of(dz, dx), quarter_columns((place + dx) % 2, core)]
        passed[i] = copies.start(part, part, across)
        forward(part, i)

    def from_across(i):
        a, dz, dx = items[i]
        passed[i].wait_recv()
        part = outs[a].at[:, rows_of(dz, dx), quarter_columns((place + dx + 1) % 2, core)]
        forward(part, i)

    for i in range(SENT_AHEAD):
        send(i)
    yield True
    for i in range(len(items) + PASSED_BEHIND):
        if i < len(items):
            arrived(i)
            if i + SENT_AHEAD < len(items):
                send(i + SENT_AHEAD)
        if i >= PASSED_BEHIND:
            from_across(i - PASSED_BEHIND)
        if i == FIRST_COMPLETE:
            for a, copy in last:
                if a == 0:
                    copy.wait_recv()
        yield True
    for a, copy in last:
        if a > 0:
            copy.wait_recv()
    copies.finish()
    for a in range(count):
        sample = ins[a].at[pl.ds(0, 31)]
        pltpu.make_async_copy(sample, sample, out_sem.at[a]).wait()
    yield True


def shared_step(width):
    return -(-width // HD) * HD


def shared_steps(x, g, weights, whole, first, part, back, gate_grad, up_grad, down_grad, sem):
    low = part.dtype
    width = gate_grad.shape[1]
    step = shared_step(width)
    gate, up, down = (slice(k * step, k * step + width) for k in range(3))
    load = pltpu.make_async_copy(whole.at[:, pl.ds(first, weights.shape[1])], weights, sem.at[0])
    load.start()
    yield True
    load.wait()
    pre = over(x[...], weights[:, gate], (1, 0))
    yield True
    lin = over(x[...], weights[:, up], (1, 0))
    yield True
    act, pre_grad, lin_grad = swish_parts(pre, lin, over(g[...], weights[:, down], (1, 0)))
    act, pre_grad, lin_grad = act.astype(low), pre_grad.astype(low), lin_grad.astype(low)
    yield True
    for at in range(0, D, 512):
        here = slice(at, at + 512)
        part[:, here] = over(act, weights[here, down], (1, 1)).astype(low)
        back[:, here] = (
            over(pre_grad, weights[here, gate], (1, 1)) + over(lin_grad, weights[here, up], (1, 1))
        ).astype(low)
        yield True
        down_grad[here] = over(g[:, here], act, (0, 0)).astype(low)
        gate_grad[here] = over(x[:, here], pre_grad, (0, 0)).astype(low)
        up_grad[here] = over(x[:, here], lin_grad, (0, 0)).astype(low)
        yield True


def expert_steps(rows, grads, hbm, held, part, back, kept, load_sem, finished):
    low = rows.dtype
    hidden = hbm[0].shape[1]
    loads = [
        pltpu.make_async_copy(src, dst, load_sem.at[k]) for k, (src, dst) in enumerate(zip(hbm, held))
    ]
    for load in loads:
        load.start()
    yield True
    for load in loads:
        load.wait()
    gate, up, down = held
    chunks = [slice(at, at + 512) for at in range(0, D, 512)]
    found = []
    for e in range(2):
        pre = over(rows[e], gate[e], (1, 1))
        yield True
        lin = over(rows[e], up[e], (1, 1))
        found.append((pre, lin))
        act = (pre * jax.nn.sigmoid(pre) * lin).astype(low)
        kept[0][e] = act
        yield True
        for here in chunks:
            ref, place = part(e, here)
            ref[place] = over(act, down[e, :, here], (1, 0)).astype(low)
            if here is chunks[-1]:
                finished(e, 0)
            yield True
    for e in range(2):
        _, pre_grad, lin_grad = swish_parts(*found[e], over(grads[e], down[e], (1, 1)))
        pre_grad, lin_grad = pre_grad.astype(low), lin_grad.astype(low)
        kept[1][e], kept[2][e] = pre_grad, lin_grad
        yield True
        for here in chunks:
            ref, place = back(e, here)
            ref[place] = (
                over(pre_grad, gate[e, :, here], (1, 0)) + over(lin_grad, up[e, :, here], (1, 0))
            ).astype(low)
            if here is chunks[-1]:
                finished(e, 1)
            yield True


def return_steps(held, outs, halves, quarters, out_sem, in_sem, copies):
    z, xh, y, place, core = token_places()
    beside, across = wa_places()
    me = z * 8 + xh * 4 + y
    quarter = D // 4
    group = 4 * SLOTS
    mine = pl.ds(pl.multiple_of(core * 2 * quarter, 2 * quarter), 2 * quarter)
    theirs = pl.ds(pl.multiple_of((1 - core) * 2 * quarter, 2 * quarter), 2 * quarter)
    rows_each = halves[0].shape[1]
    items = [(e, a, dz, dx) for a in range(2) for e in range(2) for dz, dx in GROUP_ORDER]
    paired_up, passed = {}, {}

    def finished(e, a):
        rows = pl.ds((2 * a + e) * rows_each, rows_each)
        paired_up[e, a] = copies.start(held.at[rows, theirs], halves[a].at[e], beside)

    def rows_of(dz, dx):
        return pl.ds(pl.multiple_of(((z + dz) % 4 * 8 + (xh + dx) % 2 * 4) * SLOTS, group), group)

    def kept(dx):
        return pl.ds(pl.multiple_of((place + dx) % 2 * quarter, quarter), quarter)

    def given(dx):
        return pl.ds(pl.multiple_of((place + dx + 1) % 2 * quarter, quarter), quarter)

    def add_core(i):
        e, a, dz, dx = items[i]
        rows = rows_of(dz, dx)
        if i % 8 == 0:
            paired_up[e, a].wait_recv()
        first = (2 * a + e) * rows_each
        ours = held[pl.ds(pl.multiple_of(first + rows.start, group), group), mine]
        halves[a][e, rows] = halves[a][e, rows] + ours
        passed[i] = copies.start(
            halves[a].at[e, rows, given(dx)], quarters[a].at[e, rows], across
        )

    def add_across(i):
        e, a, dz, dx = items[i]
        rows = rows_of(dz, dx)
        passed[i].wait_recv()
        quarters[a][e, rows] = quarters[a][e, rows] + halves[a][e, rows, kept(dx)]
        if dz + dx == 0:
            outs[a][me, e] = quarters[a][e, pl.ds(pl.multiple_of(me * SLOTS, SLOTS), SLOTS)]

        def one(dy, carry):
            where, block = block_device(dz, dx, dy)
            part = pl.ds(pl.multiple_of(block * SLOTS, SLOTS), SLOTS)
            pltpu.make_async_remote_copy(
                src_ref=quarters[a].at[e, part], dst_ref=outs[a].at[me, e],
                send_sem=out_sem.at[a], recv_sem=in_sem.at[a],
                device_id=where, device_id_type=MESH,
            ).start()
            return carry

        lax.fori_loop(1 if dz + dx == 0 else 0, 4, one, 0)

    def steps():
        for i in range(len(items) + BEHIND):
            if i < len(items):
                add_core(i)
            if i >= BEHIND:
                add_across(i - BEHIND)
            yield True
        copies.finish()
        for a in range(2):
            sample = outs[a].at[pl.ds(0, 31)]
            pltpu.make_async_copy(sample, sample, in_sem.at[a]).wait()
            pltpu.make_async_copy(sample, sample, out_sem.at[a]).wait()

    return finished, steps()


BEHIND = 12
MLP_ORDER = (
    "XD" + "SD" * 12 + "RR" + "XD" * 6 + "XTXTXTXTXTXTD"
    + "XTXTXTTXTXT" + "XTTXTTXRTTXRTTXRTT" + "TTRTTRTTRTTRTTRTTTTRR"
)


def mlp_kernel(count, *refs):
    ins, (x, g, whole), hbm, refs = refs[:2], refs[2:5], refs[5:8], refs[8:]
    arrived, back_rows, (shared_part, shared_back), refs = refs[:2], refs[2:4], refs[4:6], refs[6:]
    shares, kept, refs = refs[:count], refs[count : count + 3], refs[count + 3 :]
    weights, shared_grads, refs = refs[0], refs[1 : 1 + count], refs[1 + count :]
    held, halves, quarters, refs = refs[:3], refs[3:5], refs[5:7], refs[7:]
    shared_sem, load_sem, out_sem, in_sem, own_sem, *refs = refs
    pass_sems, back_out_sem, back_in_sem, back_sems, refs = refs[:2], refs[2], refs[3], refs[4:6], refs[6:]
    bufs, cube_sems = refs[:-2], refs[-2:]
    greet_blocks([neighbour("x", "A")])
    rows = arrived[0].shape[1]
    results = weights.at[:, pl.ds(0, D)]

    def place_of(a):
        def place(e, here):
            first = (2 * a + e) * rows
            return weights, (slice(first, first + rows), here)

        return place

    finished, returning = return_steps(
        results, back_rows, halves, quarters, back_out_sem, back_in_sem, Copies(*back_sems)
    )
    shards = [grad.shape[0] // 32 for grad in shared_grads]
    cubes = [
        grad.reshape(4, 2, 4, shard, grad.shape[1]) for grad, shard in zip(shared_grads, shards)
    ]
    parts = row_parts(cubes)
    programs = {
        "D": dispatch_steps(ins, arrived, out_sem, in_sem, own_sem, Copies(*pass_sems)),
        "S": shared_steps(
            x, g, weights, whole, 0, shared_part, shared_back, *shared_grads, shared_sem
        ),
        "X": expert_steps(
            *arrived, hbm, held, place_of(0), place_of(1), kept, load_sem, finished
        ),
        "T": returning,
        "R": reduce_steps(parts, cubes, shares, bufs, Copies(*cube_sems)),
    }
    in_turn(MLP_ORDER, programs)
    run(programs["T"], programs["R"])


def mlp(arrays, x, g, whole, width, expert_weights, collective_id):
    low = x.dtype
    rows, count = 32 * SLOTS, 3
    hidden = expert_weights[0].shape[1]
    at_experts = jax.ShapeDtypeStruct((2, rows, D), low)
    grad = jax.ShapeDtypeStruct((D, width), low)
    cube = jax.ShapeDtypeStruct((4, 2, 4, D // 32, width), low)
    out_shape = [at_experts] * 2
    out_shape += [jax.ShapeDtypeStruct((32, 2, SLOTS, D // 4), low)] * 2
    out_shape += [jax.ShapeDtypeStruct(x.shape, low)] * 2
    out_shape += [jax.ShapeDtypeStruct((D // 32, width), jnp.float32)] * count
    out_shape += [jax.ShapeDtypeStruct((2, rows, hidden), low)] * 3
    scratch = [pltpu.VMEM((D, 3 * shared_step(width)), low)]
    scratch += [pltpu.VMEM(grad.shape, low)] * count
    scratch += [pltpu.VMEM(a.shape, low) for a in expert_weights]
    scratch += [pltpu.VMEM((2, rows, D // 2), low)] * 2 + [pltpu.VMEM((2, rows, D // 4), low)] * 2
    sems = [(1,), (3,), (2,), (2, 8), (2,), (48,), (48,), (2,), (2,), (36,), (36,)]
    scratch += [pltpu.SemaphoreType.DMA(n) for n in sems]
    scratch += reduce_scratch([cube] * count, row_parts([cube] * count))
    anywhere, vmem = pl.BlockSpec(memory_space=pl.ANY), pl.BlockSpec(memory_space=pltpu.VMEM)
    return pl.pallas_call(
        functools.partial(mlp_kernel, count),
        out_shape=out_shape,
        in_specs=[anywhere] * 2 + [vmem] * 2 + [anywhere] * 4,
        out_specs=[vmem] * len(out_shape),
        scratch_shapes=scratch,
        compiler_params=pltpu.CompilerParams(
            collective_id=collective_id, has_side_effects=True, vmem_limit_bytes=VMEM_LIMIT
        ),
        name="mlp",
    )(*arrays, x, g, whole, *expert_weights)


def sum_more_kernel(parts, *refs):
    ins, adds, small = refs[:parts], refs[parts : 2 * parts], refs[2 * parts]
    outs, small_out = refs[2 * parts + 1 : 3 * parts + 1], refs[3 * parts + 1]
    got, half, far = (refs[(3 + i) * parts + 2 : (4 + i) * parts + 2] for i in range(3))
    small_got, small_half, small_far, send_sem, recv_sem = refs[6 * parts + 2 :]
    w = lax.axis_index("wa")
    core, place = w % 2, w // 2
    beside, across = {"wa": w + 1 - 2 * core}, {"wa": (w + 2) % 4}
    width = D // 2
    quarter = D // 4
    mine = pl.ds(pl.multiple_of(core * width, width), width)
    theirs = pl.ds(pl.multiple_of((1 - core) * width, width), width)
    own = pl.ds(pl.multiple_of(place * quarter, quarter), quarter)
    greet([beside, across])
    copies = Copies(send_sem, recv_sem)
    one = [copies.start(ins[a].at[:, theirs], got[a], beside) for a in range(parts)]
    one.append(copies.start(small, small_got, beside))
    two = []
    for a in range(parts):
        one[a].wait_recv()
        half[a][...] = ins[a][:, mine] + got[a][...]
        half[a][:, own] = half[a][:, own] + adds[a][...]
        two.append(copies.start(half[a], far[a], across))
    one[parts].wait_recv()
    small_half[...] = small[...] + small_got[...]
    two.append(copies.start(small_half, small_far, across))
    three = []
    for a in range(parts):
        two[a].wait_recv()
        outs[a][:, mine] = half[a][...] + far[a][...]
        three.append(copies.start(outs[a].at[:, mine], outs[a].at[:, mine], beside))
    two[parts].wait_recv()
    small_out[...] = small_half[...] + small_far[...]
    for copy in three:
        copy.wait_recv()
    copies.finish()


def sum_more(arrays, adds, small, collective_id, name):
    parts = len(arrays)
    rows = arrays[0].shape[0]
    dtype = arrays[0].dtype
    scratch = [pltpu.VMEM((rows, D // 2), dtype)] * (3 * parts)
    scratch += [pltpu.VMEM(small.shape, small.dtype)] * 3
    scratch += [pltpu.SemaphoreType.DMA((3 * parts + 2,))] * 2
    out_shape = [jax.ShapeDtypeStruct(x.shape, x.dtype) for x in (*arrays, small)]
    return vmem_call(
        functools.partial(sum_more_kernel, parts), out_shape, (*arrays, *adds, small), scratch,
        collective_id, name,
    )


def swish_parts(pre, lin, act_grads):
    sig = jax.nn.sigmoid(pre)
    swish = pre * sig
    slope = sig * (1.0 + pre * (1.0 - sig))
    return swish * lin, act_grads * lin * slope, act_grads * swish


def expert_grads_kernel(rows, grads, act, pre_grad, lin_grad, gate_grad, up_grad, down_grad):
    for at in range(0, D, 512):
        here = slice(at, at + 512)
        down_grad[0, :, here] = over(act[0], grads[0, :, here], (0, 0))
        gate_grad[0, :, here] = over(pre_grad[0], rows[0, :, here], (0, 0))
        up_grad[0, :, here] = over(lin_grad[0], rows[0, :, here], (0, 0))


def expert_grads(*operands):
    shape = jax.ShapeDtypeStruct((2, operands[2].shape[2], D), jnp.float32)

    def spec(x):
        return pl.BlockSpec((1, *x.shape[1:]), lambda e: (e, 0, 0))

    return pl.pallas_call(
        expert_grads_kernel,
        grid=(2,),
        out_shape=[shape] * 3,
        in_specs=[spec(x) for x in operands],
        out_specs=[spec(shape)] * 3,
        compiler_params=pltpu.CompilerParams(vmem_limit_bytes=VMEM_LIMIT),
        name="expert_grads",
    )(*operands)


def turned_gather(arrays, axis):
    widths = [a.shape[1] for a in arrays]
    whole = lax.all_gather(jnp.concatenate(arrays, axis=1), axis, axis=0, tiled=True)
    return jnp.split(whole, [sum(widths[:k]) for k in range(1, len(widths))], axis=1)


def rope_tables(positions):
    half_width = HD // 2
    inverse = 1.0 / ROPE_BASE ** (jnp.arange(half_width, dtype=jnp.float32) * 2.0 / HD)
    angles = positions[:, None] * inverse[None, :]
    cosine, sine = jnp.cos(angles), jnp.sin(angles)
    return jnp.concatenate([cosine, cosine], axis=1), jnp.concatenate([-sine, sine], axis=1)


def dot(left, right, over, dtype=jnp.float32, **kept):
    return lax.dot_general(
        left, right, ((over[:1], over[1:]), ((), ())), preferred_element_type=dtype, **kept
    )


def shards(
    tokens,
    cotangent,
    routes,
    attn_gain,
    query_weight,
    key_weight,
    value_weight,
    output_weight,
    mlp_gain,
    router_weight,
    shared_gate,
    shared_up,
    shared_down,
    expert_gate,
    expert_up,
    expert_down,
):
    low = jnp.bfloat16
    local_tokens = tokens.shape[0]
    head_cols = query_weight.shape[1]
    experts_all = router_weight.shape[1]
    groups = ("sp", "ctx")
    place, core = lax.axis_index("wa") // 2, lax.axis_index("wa") % 2
    quarter_at = core * (D // 2) + place * (D // 4)

    def quarter(x):
        return lax.dynamic_slice_in_dim(x, quarter_at, D // 4, 1)

    hidden_cols = shared_gate.shape[1]
    def beside(arrays):
        return jnp.concatenate(
            [jnp.pad(x, ((0, 0), (0, -x.shape[1] % HD))) for x in arrays], axis=1
        )

    shared_whole = lax.all_gather(
        beside((shared_gate, shared_up, shared_down.T)), groups, axis=0, tiled=True
    )
    router_own = jnp.concatenate([router_weight, mlp_gain[:, None]], axis=1)
    tokens_f = tokens.astype(jnp.float32)
    inv_one = lax.rsqrt(jnp.mean(tokens_f * tokens_f, axis=-1, keepdims=True) + EPSILON)
    unit_one = tokens_f * inv_one
    gain_one = attn_gain.astype(jnp.float32)[:, None]
    heads = jnp.concatenate([query_weight, key_weight, value_weight], axis=1)
    scaled = (gain_one * heads.astype(jnp.float32)).astype(low)
    head_rows, head_weights = gather_head(unit_one.astype(low), scaled, 1)
    head_rows, head_weights = head_rows.reshape(-1, D), head_weights.reshape(D, -1)
    blocks = jnp.arange(4, dtype=jnp.int32)[:, None] * 8 + lax.axis_index("ctx")
    positions = blocks * local_tokens + jnp.arange(local_tokens, dtype=jnp.int32)[None, :]
    cosine, sine = rope_tables(positions.reshape(-1).astype(jnp.float32))
    by_head = (4, local_tokens, HD)
    head_queries, own_keys, own_values = (
        x.reshape(by_head) for x in project(head_rows, head_weights, cosine, sine)
    )
    attn_out, attended, head_keys, head_values, probs, exact, whole = attention(
        head_queries, own_keys, own_values, beside((output_weight.T, router_own)), 2
    )
    attn_out = attn_out.astype(jnp.float32)
    whole = whole.reshape(D, -1)
    turned = whole[:, :head_cols]
    full_router = whole[:, head_cols : head_cols + experts_all]
    gain_two = whole[:, head_cols + experts_all].astype(jnp.float32)
    hidden_state = tokens_f + attn_out
    inv_two = lax.rsqrt(jnp.mean(hidden_state * hidden_state, axis=-1, keepdims=True) + EPSILON)
    unit_two = hidden_state * inv_two
    mlp_in = (unit_two * gain_two).astype(low)

    logits = dot(mlp_in, full_router, (1, 0))
    logit_exp = jnp.exp(logits - jnp.max(logits, axis=-1, keepdims=True))
    router_probs = logit_exp / jnp.sum(logit_exp, axis=-1, keepdims=True)
    experts = jnp.arange(experts_all, dtype=jnp.int32)
    chosen = jnp.zeros((local_tokens, experts_all), jnp.bool_)
    for j in range(TOP):
        chosen = chosen | (routes[:, j : j + 1] == experts[None, :])
    ids = jnp.arange(local_tokens, dtype=jnp.int32)
    before = (ids[None, :] < ids[:, None]).astype(low)
    rank = dot(before, chosen.astype(low), (1, 0))
    slot_of = jnp.where(chosen, rank, -1.0).astype(low)
    slot_ids = jnp.arange(experts_all * SLOTS, dtype=jnp.int32)
    widen = (experts[:, None] == slot_ids[None, :] // SLOTS).astype(low)
    taken = dot(slot_of, widen, (1, 0)) == (slot_ids % SLOTS).astype(jnp.float32)[None, :]
    probs_high = router_probs.astype(low)
    probs_rest = (router_probs - probs_high.astype(jnp.float32)).astype(low)
    pick = taken.astype(low)
    gate_high = jnp.where(taken, dot(probs_high, widen, (1, 0)), 0.0).astype(low)
    gate_rest = jnp.where(taken, dot(probs_rest, widen, (1, 0)), 0.0).astype(low)
    grad_quarter = quarter(cotangent)
    send_rows = dot(pick, quarter(mlp_in), (0, 0)).astype(low)
    send_grads = (
        dot(gate_high, grad_quarter, (0, 0)) + dot(gate_rest, grad_quarter, (0, 0))
    ).astype(low)
    by_owner = (32, 2, SLOTS, D // 4)
    expert_weights = (expert_gate.transpose(0, 2, 1), expert_up.transpose(0, 2, 1), expert_down)
    (
        rows_in,
        grads_in,
        returned,
        rows_back,
        shared_part,
        shared_in_part,
        gate_share,
        up_share,
        down_share,
        *kept,
    ) = mlp(
        (send_rows.reshape(by_owner), send_grads.reshape(by_owner)),
        mlp_in,
        cotangent,
        shared_whole,
        hidden_cols,
        expert_weights,
        5,
    )
    gate_grad_turned, up_grad_turned, expert_down_grad = expert_grads(rows_in, grads_in, *kept)
    returned, rows_back = returned.reshape(-1, D // 4), rows_back.reshape(-1, D // 4)

    routed = (dot(gate_high, returned, (1, 0)) + dot(gate_rest, returned, (1, 0))).astype(low)
    routed_in = dot(pick, rows_back, (1, 0)).astype(low)
    slot_grads = jnp.where(taken, dot(grad_quarter, returned, (1, 1)), 0.0)
    prob_part = dot(slot_grads, widen.astype(jnp.float32), (1, 1), precision=PRECISE)
    prob_part = jnp.pad(prob_part, ((0, 0), (0, HD - experts_all)))
    mixed, mixed_in, prob_grads = sum_more(
        (shared_part, shared_in_part), (routed, routed_in), prob_part, 7, "sum_mlp"
    )
    block_out = (hidden_state + mixed.astype(jnp.float32)).astype(low)
    prob_grads = prob_grads[:, :experts_all]
    logit_grads = router_probs * (
        prob_grads - jnp.sum(router_probs * prob_grads, axis=-1, keepdims=True)
    )
    router_in_grad = dot(
        logit_grads, full_router.astype(jnp.float32), (1, 1), precision=PRECISE
    )
    mlp_in_grad = router_in_grad + mixed_in.astype(jnp.float32)
    gain_two_grad = jnp.sum(mlp_in_grad * unit_two, axis=0)
    scaled_two = mlp_in_grad * gain_two
    hidden_grad = cotangent.astype(jnp.float32) + inv_two * (
        scaled_two - unit_two * jnp.mean(scaled_two * unit_two, axis=-1, keepdims=True)
    )
    out_grad = hidden_grad.astype(low)
    router_grad = dot(mlp_in, logit_grads.astype(low), (0, 0))

    attended_grad = dot(out_grad, turned, (1, 0)).astype(low)
    def by_shard(x):
        return x.astype(low).reshape(4, 2, 4, x.shape[0] // 32, x.shape[1])

    small_grads = jnp.concatenate([router_grad, gain_two_grad[:, None]], axis=1)
    small_grads = jnp.pad(small_grads, ((0, 0), (0, HD - small_grads.shape[1])))
    summed = [by_shard(dot(out_grad, attended, (0, 0))), by_shard(small_grads)]
    scaled_one, head_shares, gain_terms, output_share, small_share = attention_back(
        (
            attended_grad,
            head_queries,
            head_keys,
            head_values,
            probs,
            exact,
            cosine,
            sine,
            head_rows,
            head_weights,
            heads,
        ),
        summed,
        9,
    )
    scaled_one = scaled_one.astype(jnp.float32)
    tokens_grad = (
        hidden_grad
        + inv_one
        * (scaled_one - unit_one * jnp.mean(scaled_one * unit_one, axis=-1, keepdims=True))
    ).astype(low)
    head_shares = head_shares.astype(jnp.float32) * gain_one
    query_share, key_share, value_share = (
        head_shares[..., k * HD : (k + 1) * HD].swapaxes(0, 1).reshape(-1, head_cols)
        for k in range(3)
    )
    return (
        block_out,
        tokens_grad,
        jnp.sum(gain_terms, axis=1),
        query_share,
        key_share,
        value_share,
        output_share.T,
        small_share[:, experts_all],
        small_share[:, :experts_all],
        gate_share,
        up_share,
        down_share.T,
        gate_grad_turned.transpose(0, 2, 1),
        up_grad_turned.transpose(0, 2, 1),
        expert_down_grad,
    )


def solution(mesh):
    placed = (
        P(("sp", "ctx"), None),
        P(("sp", "ctx"), None),
        P(("sp", "ctx"), None),
        P(("sp", "ctx")),
        P(("sp", "ctx"), "wa"),
        P(("sp", "ctx"), "wa"),
        P(("sp", "ctx"), "wa"),
        P("wa", ("sp", "ctx")),
        P(("sp", "ctx")),
        P(("sp", "ctx"), None),
        P(("sp", "ctx"), "wa"),
        P(("sp", "ctx"), "wa"),
        P("wa", ("sp", "ctx")),
        P(("sp", "ctx"), None, "wa"),
        P(("sp", "ctx"), None, "wa"),
        P(("sp", "ctx"), "wa", None),
    )
    return jax.shard_map(
        shards,
        mesh=mesh,
        in_specs=placed,
        out_specs=(
            P(("sp", "ctx"), None),
            P(("sp", "ctx"), None),
            P(("sp", "ctx")),
            P(("sp", "ctx"), "wa"),
            P(("sp", "ctx"), "wa"),
            P(("sp", "ctx"), "wa"),
            P("wa", ("sp", "ctx")),
            P(("sp", "ctx")),
            P(("sp", "ctx"), None),
            P(("sp", "ctx"), "wa"),
            P(("sp", "ctx"), "wa"),
            P("wa", ("sp", "ctx")),
            P(("sp", "ctx"), None, "wa"),
            P(("sp", "ctx"), None, "wa"),
            P(("sp", "ctx"), "wa", None),
        ),
        check_vma=False,
    )
```

```python
import functools

import jax
import jax.numpy as jnp
from jax import lax
from jax.experimental import pallas as pl
from jax.experimental.pallas import tpu as pltpu
from jax.sharding import PartitionSpec as P

D = 2048
HD = 128
TOP = 6


EPSILON = 1e-06
ROPE_BASE = 10000.0
MASKED = -1e30
PRECISE = lax.Precision.HIGHEST


MESH = pl.DeviceIdType.MESH
VMEM_LIMIT = 63 * 1024 * 1024

ORDERS = (
    (("z", "A"), ("z", "B"), ("y", "A"), ("y", "B")),
    (("z", "B"), ("z", "A"), ("y", "B"), ("y", "A")),
    (("y", "A"), ("y", "B"), ("z", "A"), ("z", "B")),
    (("y", "B"), ("y", "A"), ("z", "B"), ("z", "A")),
)


def paired(i, kind):
    return i + 1 - 2 * (i % 2) if kind == "A" else 3 - i


def own_place():
    c = lax.axis_index("ctx")
    return lax.axis_index("sp"), c // 4, c % 4


def neighbour(axis, kind):
    z, xh, y = own_place()
    if axis == "z":
        return {"sp": paired(z, kind)}
    if axis == "y":
        return {"ctx": 4 * xh + paired(y, kind)}
    return {"ctx": 4 * (1 - xh) + y}


def cube_places():
    rings = [neighbour(axis, kind) for axis in ("z", "y") for kind in ("A", "B")]
    return rings + [neighbour("x", "A")]


def pair_slots(i, kind):
    if kind == "A":
        return [(pl.ds((i // 2) * 2, 2), pl.ds(0, 2))]
    return [(pl.ds(i, 1), pl.ds(0, 1)), (pl.ds(3 - i, 1), pl.ds(1, 1))]


def pair_members(i, kind):
    if kind == "A":
        return [(i // 2) * 2, (i // 2) * 2 + 1]
    return [i, 3 - i]


def slot_in_pair(i, kind):
    return i % 2 if kind == "A" else 0

def over(left, right, dims):
    return lax.dot_general(
        left, right, ((dims[:1], dims[1:]), ((), ())), preferred_element_type=jnp.float32
    )


def head_columns(h):
    return pl.ds(pl.multiple_of(h * HD, HD), HD)


class Copies:
    def __init__(self, send_sem, recv_sem):
        self.send_sem, self.recv_sem, self.started = send_sem, recv_sem, []

    def start(self, src, dst, where):
        k = len(self.started)
        copy = pltpu.make_async_remote_copy(
            src_ref=src, dst_ref=dst, send_sem=self.send_sem.at[k],
            recv_sem=self.recv_sem.at[k], device_id=where, device_id_type=MESH,
        )
        copy.start()
        self.started.append(copy)
        return copy

    def finish(self):
        for copy in self.started:
            copy.wait_send()


def run(*programs):
    programs = list(programs)
    while programs:
        programs = [program for program in programs if next(program, None) is not None]


def in_turn(order, programs):
    for letter in order:
        next(programs[letter], None)


def greet(places):
    barrier = pltpu.get_barrier_semaphore()
    for place in places:
        pl.semaphore_signal(barrier, inc=1, device_id=place, device_id_type=MESH)
    pl.semaphore_wait(barrier, len(places))


def along_z():
    z = lax.axis_index("sp")
    return [{"sp": (z + d) % 4} for d in (1, 2, 3)]


def vmem_call(kernel, out_shape, operands, scratch, collective_id, name, **params):
    return pl.pallas_call(
        kernel,
        out_shape=out_shape,
        in_specs=[pl.BlockSpec(memory_space=pltpu.VMEM)] * len(operands),
        out_specs=jax.tree.map(lambda _: pl.BlockSpec(memory_space=pltpu.VMEM), out_shape),
        scratch_shapes=scratch,
        compiler_params=pltpu.CompilerParams(
            collective_id=collective_id,
            has_side_effects=collective_id is not None,
            vmem_limit_bytes=VMEM_LIMIT,
        ),
        name=name,
        **params,
    )(*operands)

def gather_steps(parts, ins, outs, copies, local_sem):
    z, xh, y = own_place()
    count = len(ins)

    def step(lane, p, s):
        ring1, ring2 = ORDERS[p][0][0], ORDERS[p][2][0]
        where = neighbour(*ORDERS[p][s])
        xl = xh if lane == 0 else 1 - xh
        zs, ys = [pl.ds(z, 1)], [pl.ds(y, 1)]
        full = [pl.ds(0, 4)]
        if s == 1:
            other = [d for d, _ in pair_slots(z if ring1 == "z" else y, ORDERS[p][0][1])]
            zs, ys = (other, ys) if ring1 == "z" else (zs, other)
        if s >= 2:
            zs, ys = (full, ys) if ring1 == "z" else (zs, full)
        if s == 3:
            other = [d for d, _ in pair_slots(z if ring2 == "z" else y, ORDERS[p][2][1])]
            zs, ys = (other, ys) if ring2 == "z" else (zs, other)
        started = []
        for a, rows, cols in parts[p]:
            for zd in zs:
                for yd in ys:
                    place = outs[a].at[zd, pl.ds(xl, 1), yd, rows, cols]
                    started.append(copies.start(place, place, where))
        return started

    local = [
        pltpu.make_async_copy(ins[a], outs[a].at[z, xh, y], local_sem.at[a]) for a in range(count)
    ]
    for copy in local:
        copy.start()
    across = [
        [
            copies.start(
                ins[a].at[rows, cols], outs[a].at[z, xh, y, rows, cols], neighbour("x", "A")
            )
            for a, rows, cols in part
        ]
        for part in parts
    ]
    for copy in local:
        copy.wait()
    flying = {}
    for lane, s in (
        (0, 0), (0, 1), (1, 0), (0, 2), (1, 1), (0, 3), (1, 2), (1, 3), (0, 4), (1, 4)
    ):
        for p in range(4):
            for copy in flying.get((lane, p), across[p] if lane == 1 else []):
                copy.wait_recv()
            flying[lane, p] = step(lane, p, s) if s < 4 else []
        yield True
    copies.finish()


def gather_kernel(parts, count, *refs):
    ins, outs = refs[:count], refs[count : 2 * count]
    send_sem, recv_sem, local_sem = refs[2 * count :]
    greet(cube_places())
    run(gather_steps(parts, ins, outs, Copies(send_sem, recv_sem), local_sem))


def gather_cube(arrays, parts, collective_id, name):
    count = len(arrays)
    copies = 11 * sum(len(part) for part in parts)
    return pl.pallas_call(
        functools.partial(gather_kernel, parts, count),
        out_shape=[jax.ShapeDtypeStruct((4, 2, 4, *a.shape), a.dtype) for a in arrays],
        in_specs=[pl.BlockSpec(memory_space=pl.ANY)] * count,
        out_specs=[pl.BlockSpec(memory_space=pl.ANY)] * count,
        scratch_shapes=[
            pltpu.SemaphoreType.DMA((copies,)),
            pltpu.SemaphoreType.DMA((copies,)),
            pltpu.SemaphoreType.DMA((count,)),
        ],
        compiler_params=pltpu.CompilerParams(collective_id=collective_id, has_side_effects=True),
        name=name,
    )(*arrays)


def entries_of(parts):
    return [(p, *entry) for p in range(4) for entry in parts[p]]


CUBE_ORDER = tuple((stage, lane) for stage in range(5) for lane in (1, 0))


def reduce_steps(parts, ins, outs, bufs, copies):
    entries = entries_of(parts)
    z, xh, y = own_place()
    start = copies.start
    flying = {}

    def first(lane, e):
        p, a, rows, cols = entries[e]
        ring2, near = ORDERS[p][2]
        axis, kind = ORDERS[p][3]
        xl = xh if lane == 0 else 1 - xh
        theirs = paired(z if ring2 == "z" else y, kind)
        copies = []
        for src, dst in pair_slots(theirs, near):
            if ring2 == "z":
                block, place = ins[a].at[src, xl, :, rows, cols], bufs[5 * e].at[lane, dst]
            else:
                block, place = ins[a].at[:, xl, src, rows, cols], bufs[5 * e].at[lane, :, dst]
            copies.append(start(block, place, neighbour(axis, kind)))
        flying[lane, e] = copies

    def second(lane, e):
        p, a, rows, cols = entries[e]
        ring2 = ORDERS[p][2][0]
        axis, kind = ORDERS[p][2]
        xl = xh if lane == 0 else 1 - xh
        mine = z if ring2 == "z" else y
        buf = bufs[5 * e]
        for copy in flying[lane, e]:
            copy.wait_recv()
        slot = slot_in_pair(mine, kind)

        def add(j, place):
            def one(i, carry):
                if ring2 == "z":
                    buf[lane, j, i] = buf[lane, j, i] + ins[a][place, xl, i, rows, cols]
                else:
                    buf[lane, i, j] = buf[lane, i, j] + ins[a][i, xl, place, rows, cols]
                return carry

            lax.fori_loop(0, 4, one, 0)

        add(1 - slot, paired(mine, kind))
        half = buf.at[lane, 1 - slot] if ring2 == "z" else buf.at[lane, :, 1 - slot]
        flying[lane, e] = [start(half, bufs[5 * e + 1].at[lane], neighbour(axis, kind))]
        add(slot, mine)

    def third(lane, e):
        p = entries[e][0]
        ring1, ring2 = ORDERS[p][0][0], ORDERS[p][2][0]
        axis, kind = ORDERS[p][1]
        before, buf = bufs[5 * e], bufs[5 * e + 1]
        for copy in flying[lane, e]:
            copy.wait_recv()
        slot = slot_in_pair(z if ring2 == "z" else y, ORDERS[p][2][1])

        def one(i, carry):
            other = before[lane, slot, i] if ring2 == "z" else before[lane, i, slot]
            buf[lane, i] = buf[lane, i] + other
            return carry

        lax.fori_loop(0, 4, one, 0)
        theirs = paired(z if ring1 == "z" else y, kind)
        flying[lane, e] = [
            start(buf.at[lane, src], bufs[5 * e + 2].at[lane, dst], neighbour(axis, kind))
            for src, dst in pair_slots(theirs, ORDERS[p][0][1])
        ]

    def fourth(lane, e):
        p = entries[e][0]
        ring1 = ORDERS[p][0][0]
        axis, kind = ORDERS[p][0]
        mine = z if ring1 == "z" else y
        before, buf = bufs[5 * e + 1], bufs[5 * e + 2]
        for copy in flying[lane, e]:
            copy.wait_recv()
        slot = slot_in_pair(mine, kind)
        buf[lane, 1 - slot] = buf[lane, 1 - slot] + before[lane, paired(mine, kind)]
        flying[lane, e] = [
            start(buf.at[lane, 1 - slot], bufs[5 * e + 3].at[lane], neighbour(axis, kind))
        ]
        buf[lane, slot] = buf[lane, slot] + before[lane, mine]

    def last(lane, e):
        p, a, rows, cols = entries[e]
        ring1 = ORDERS[p][0][0]
        before, buf = bufs[5 * e + 2], bufs[5 * e + 3]
        for copy in flying[lane, e]:
            copy.wait_recv()
        slot = slot_in_pair(z if ring1 == "z" else y, ORDERS[p][0][1])
        if lane == 1:
            buf[1] = buf[1] + before[1, slot]
            flying["x", e] = start(buf.at[1], bufs[5 * e + 4], neighbour("x", "A"))
        else:
            flying["x", e].wait_recv()
            total = (
                buf[0].astype(jnp.float32)
                + before[0, slot].astype(jnp.float32)
                + bufs[5 * e + 4][...].astype(jnp.float32)
            )
            outs[a][rows, cols] = total.astype(outs[a].dtype)

    stages = (first, second, third, fourth, last)
    for at, lane in CUBE_ORDER:
        for e in range(len(entries)):
            stages[at](lane, e)
        yield True
    copies.finish()


def reduce_kernel(parts, count, *refs):
    size = 5 * len(entries_of(parts))
    ins, outs = refs[:count], refs[count : 2 * count]
    bufs = refs[2 * count : 2 * count + size]
    greet(cube_places())
    run(reduce_steps(parts, ins, outs, bufs, Copies(*refs[2 * count + size :])))


def reduce_scratch(arrays, parts):
    scratch = []
    for p in range(4):
        pair = (2, 4) if ORDERS[p][2][0] == "z" else (4, 2)
        for a, rows, cols in parts[p]:
            for lead in ((2, *pair), (2, 4), (2, 2), (2,), ()):
                scratch.append(pltpu.VMEM((*lead, rows.size, cols.size), arrays[a].dtype))
    copies = 13 * sum(len(part) for part in parts)
    return scratch + [pltpu.SemaphoreType.DMA((copies,))] * 2


def reduce_cube(arrays, parts, collective_id, name, dtype=jnp.float32):
    count = len(arrays)
    scratch = reduce_scratch(arrays, parts)
    return pl.pallas_call(
        functools.partial(reduce_kernel, parts, count),
        out_shape=[jax.ShapeDtypeStruct(a.shape[3:], dtype) for a in arrays],
        in_specs=[pl.BlockSpec(memory_space=pltpu.VMEM)] * count,
        out_specs=[pl.BlockSpec(memory_space=pltpu.VMEM)] * count,
        scratch_shapes=scratch,
        compiler_params=pltpu.CompilerParams(
            collective_id=collective_id, has_side_effects=True, vmem_limit_bytes=VMEM_LIMIT
        ),
        name=name,
    )(*arrays)


def row_parts(arrays):
    parts = []
    for p in range(4):
        part = []
        for a, array in enumerate(arrays):
            rows, columns = array.shape[-2:]
            part.append((a, pl.ds(p * rows // 4, rows // 4), pl.ds(0, columns)))
        parts.append(part)
    return parts


def whole_parts(arrays):
    return [[(a, pl.ds(0, x.shape[-2]), pl.ds(0, x.shape[-1]))] for a, x in enumerate(arrays)]


def half_parts(arrays):
    return [
        [(a, pl.ds(0, x.shape[-2]), pl.ds(h * x.shape[-1] // 2, x.shape[-1] // 2))]
        for a, x in enumerate(arrays)
        for h in range(2)
    ]


def wa_places():
    w = lax.axis_index("wa")
    return [{"wa": w + 1 - 2 * (w % 2)}, {"wa": (w + 2) % 4}]


def sum_wa_steps(x, out, half, got, far, copies):
    core = lax.axis_index("wa") % 2
    beside, across = wa_places()
    width = x.shape[1] // 2
    mine = pl.ds(pl.multiple_of(core * width, width), width)
    theirs = pl.ds(pl.multiple_of((1 - core) * width, width), width)
    one = copies.start(x.at[:, theirs], got, beside)
    yield True
    one.wait_recv()
    half[...] = x[:, mine] + got[...]
    two = copies.start(half, far, across)
    yield True
    two.wait_recv()
    out[:, mine] = half[...] + far[...]
    three = copies.start(out.at[:, mine], out.at[:, mine], beside)
    yield True
    three.wait_recv()
    copies.finish()


def sum_wa_kernel(x, out, half, got, far, send_sem, recv_sem):
    greet(wa_places())
    run(sum_wa_steps(x, out, half, got, far, Copies(send_sem, recv_sem)))


def sum_wa(x, collective_id, name):
    rows, columns = x.shape
    return pl.pallas_call(
        sum_wa_kernel,
        out_shape=jax.ShapeDtypeStruct(x.shape, x.dtype),
        in_specs=[pl.BlockSpec(memory_space=pltpu.VMEM)],
        out_specs=pl.BlockSpec(memory_space=pltpu.VMEM),
        scratch_shapes=[pltpu.VMEM((rows, columns // 2), x.dtype)] * 3
        + [pltpu.SemaphoreType.DMA((3,)), pltpu.SemaphoreType.DMA((3,))],
        compiler_params=pltpu.CompilerParams(
            collective_id=collective_id, has_side_effects=True, vmem_limit_bytes=VMEM_LIMIT
        ),
        name=name,
    )(x)

def ctx_gather_steps(parts, copies):
    z, xh, y = own_place()

    def send(part, xl, place, axis, kind):
        ref, rows = part
        block = ref.at[:, xl, place, rows]
        return copies.start(block, block, neighbour(axis, kind))

    near, far = ("A", "B"), ("B", "A")
    first, across, last = {}, [], []
    for a in range(2):
        first[0, a] = send(parts[a], xh, y, "y", near[a])
        across.append(send(parts[a], xh, y, "x", "A"))
    yield True
    for lane in range(2):
        xl = xh if lane == 0 else 1 - xh
        if lane == 1:
            for a in range(2):
                across[a].wait_recv()
                first[1, a] = send(parts[a], xl, y, "y", near[a])
            yield True
        for a in range(2):
            first[lane, a].wait_recv()
            for place, _ in pair_slots(y, near[a]):
                last.append(send(parts[a], xl, place, "y", far[a]))
        yield True
    for copy in last:
        copy.wait_recv()
    copies.finish()


CTX_ORDER = ((0, 1), (1, 1), (0, 0), (2, 1), (1, 0), (2, 0))


def ctx_reduce_steps(parts, bufs, sums, cross, own, copies):
    z, xh, y = own_place()
    near, far = ("A", "B"), ("B", "A")
    flying = {}

    def first(lane):
        xl = xh if lane == 0 else 1 - xh
        for a, (ref, rows) in enumerate(parts):
            flying[lane, a] = [
                copies.start(
                    ref.at[:, xl, src, rows], bufs[a].at[lane, :, dst], neighbour("y", far[a])
                )
                for src, dst in pair_slots(paired(y, far[a]), near[a])
            ]

    def second(lane):
        xl = xh if lane == 0 else 1 - xh
        for a, (ref, rows) in enumerate(parts):
            for copy in flying[lane, a]:
                copy.wait_recv()
            slot = slot_in_pair(y, near[a])

            def add(j, place):
                def one(i, carry):
                    bufs[a][lane, i, j] = bufs[a][lane, i, j] + ref[i, xl, place, rows]
                    return carry

                lax.fori_loop(0, 4, one, 0)

            add(1 - slot, paired(y, near[a]))
            flying[lane, a] = copies.start(
                bufs[a].at[lane, :, 1 - slot], sums[a].at[lane], neighbour("y", near[a])
            )
            add(slot, y)

    def third(lane):
        for a in range(2):
            flying[lane, a].wait_recv()
            slot = slot_in_pair(y, near[a])

            def more(i, carry):
                sums[a][lane, i] = sums[a][lane, i] + bufs[a][lane, i, slot]
                return carry

            lax.fori_loop(0, 4, more, 0)
            if lane == 1:
                flying["x", a] = copies.start(sums[a].at[1], cross[a], neighbour("x", "A"))

    for stage, lane in CTX_ORDER:
        (first, second, third)[stage](lane)
        yield True
    for a in range(2):
        flying["x", a].wait_recv()

        def total(i, carry):
            own[a][i] = sums[a][0, i] + cross[a][i]
            return carry

        lax.fori_loop(0, 4, total, 0)
    yield True
    copies.finish()


def ctx_scratch(shapes, dtype):
    scratch = [
        pltpu.VMEM((*lead, *shape), dtype) for lead in ((2, 4, 2), (2, 4), (4,), (4,)) for shape in shapes
    ]
    return scratch + [pltpu.SemaphoreType.DMA((12,))] * 2


def column_halves(width):
    return [pl.ds(0, width // 2), pl.ds(width // 2, width // 2)]


def rows_gather_steps(x, out, copies):
    z = lax.axis_index("sp")
    near, far = ("A", "B"), ("B", "A")
    halves = column_halves(x.shape[1])
    first = [
        copies.start(x.at[:, halves[a]], out.at[z, :, halves[a]], neighbour("z", near[a]))
        for a in range(2)
    ]
    out[z] = x[...]
    yield True
    last = []
    for a in range(2):
        first[a].wait_recv()
        for place, _ in pair_slots(z, near[a]):
            block = out.at[place, :, halves[a]]
            last.append(copies.start(block, block, neighbour("z", far[a])))
    yield True
    for copy in last:
        copy.wait_recv()
    copies.finish()


def rows_reduce_steps(x, out, bufs, sums, copies):
    z = lax.axis_index("sp")
    near, far = ("A", "B"), ("B", "A")
    halves = column_halves(x.shape[2])
    flying = [
        [
            copies.start(x.at[src, :, halves[a]], bufs[a].at[dst], neighbour("z", far[a]))
            for src, dst in pair_slots(paired(z, far[a]), near[a])
        ]
        for a in range(2)
    ]
    yield True
    second = []
    for a in range(2):
        for copy in flying[a]:
            copy.wait_recv()
        slot = slot_in_pair(z, near[a])
        bufs[a][1 - slot] = bufs[a][1 - slot] + x[paired(z, near[a]), :, halves[a]]
        second.append(copies.start(bufs[a].at[1 - slot], sums[a], neighbour("z", near[a])))
        bufs[a][slot] = bufs[a][slot] + x[z, :, halves[a]]
    yield True
    for a in range(2):
        second[a].wait_recv()
        slot = slot_in_pair(z, near[a])
        out[:, halves[a]] = bufs[a][slot] + sums[a][...]
    yield True
    copies.finish()


def gather_head_kernel(x, w, rows_out, weights_out, *sems):
    z, xh, y = own_place()
    greet(along_z() + [neighbour("y", "A"), neighbour("y", "B"), neighbour("x", "A")])
    turns = Copies(*sems[:2])
    heads = w.shape[1] // HD // 4

    def columns(k, h):
        return pl.ds(pl.multiple_of(k * 4 * HD + h * HD, HD), HD)

    for d in (1, 2, 3):
        there = (z + d) % 4
        for k in range(heads):
            place = weights_out.at[z, xh, y, :, pl.ds(k * HD, HD)]
            turns.start(w.at[:, columns(k, there)], place, {"sp": there})
    rows = rows_gather_steps(x, rows_out, Copies(*sems[2:4]))
    next(rows)
    for k in range(heads):
        weights_out[z, xh, y, :, k * HD : (k + 1) * HD] = w[:, columns(k, z)]
    for copy in turns.started:
        copy.wait_recv()
    half = w.shape[0] // 2
    parts = [(weights_out, pl.ds(a * half, half)) for a in range(2)]
    run(ctx_gather_steps(parts, Copies(*sems[4:6])), rows)
    turns.finish()


def gather_head(x, w, collective_id):
    out_shape = [
        jax.ShapeDtypeStruct((4, *x.shape), x.dtype),
        jax.ShapeDtypeStruct((4, 2, 4, w.shape[0], w.shape[1] // 4), w.dtype),
    ]
    sems = [pltpu.SemaphoreType.DMA((n,)) for n in (9, 9, 5, 5, 12, 12)]
    return vmem_call(gather_head_kernel, out_shape, (x, w), sems, collective_id, "gather_head")


def project_kernel(x, w, cosine, sine, q, k, v):
    raw = jnp.dot(x[...], w[...], preferred_element_type=jnp.float32)
    for at, out in enumerate((q, k)):
        one = raw[:, at * HD : (at + 1) * HD]
        out[...] = (one * cosine[...] + pltpu.roll(one, HD // 2, 1) * sine[...]).astype(out.dtype)
    v[...] = raw[:, 2 * HD :].astype(v.dtype)


def project(x, w, cosine, sine):
    shape = jax.ShapeDtypeStruct((x.shape[0], HD), x.dtype)
    return vmem_call(project_kernel, [shape] * 3, (x, w, cosine, sine), [], None, "project_head")


def attend_steps(q, k, v, blocks, exact, probs, scores):
    rows = q.shape[1]
    span = 8 * rows
    first = lax.axis_index("ctx") * rows
    scale = HD ** (-0.5)
    at = 0

    def chunk(ref, c):
        return ref[c].reshape(span, HD)

    for block in range(4):
        for c in range(block + 1):
            part = over(q[block], chunk(k, c), (1, 1)) * scale
            if c == block:
                row = lax.broadcasted_iota(jnp.int32, part.shape, 0)
                col = lax.broadcasted_iota(jnp.int32, part.shape, 1)
                part = jnp.where(col <= row + first, part, MASKED)
            scores[:, c * span : (c + 1) * span] = part
        width = (block + 1) * span
        top = jnp.max(scores[:, :width], axis=1, keepdims=True)
        total = jnp.zeros_like(top)
        for c in range(block + 1):
            part = jnp.exp(scores[:, c * span : (c + 1) * span] - top)
            total = total + jnp.sum(part, axis=1, keepdims=True)
            scores[:, c * span : (c + 1) * span] = part
        scaled = 1.0 / total
        result = jnp.zeros((rows, HD), jnp.float32)
        for c in range(block + 1):
            low = (scores[:, c * span : (c + 1) * span] * scaled).astype(probs.dtype)
            probs[at] = low
            result = result + over(low, chunk(v, c), (1, 0))
            at += 1
        exact[block] = result
        blocks[block] = result.astype(blocks.dtype)
        yield True


ATTEND_ORDER = "KGGKGKGKGK" + "AGAGAGA"


def attention_kernel(parts, q, k, v, own, total, attended, keys, values, probs, exact, whole, *refs):
    scores, blocks, part, *wa_bufs = refs[:6]
    sems = refs[6:]
    z, xh, y = own_place()
    places = along_z() + [neighbour("y", "A"), neighbour("y", "B"), neighbour("x", "A")]
    greet(places + wa_places())
    keys[:, xh, y] = k[...]
    values[:, xh, y] = v[...]
    rows = pl.ds(0, k.shape[1])
    programs = {
        "K": ctx_gather_steps([(keys, rows), (values, rows)], Copies(*sems[0:2])),
        "G": gather_steps(parts, [own], [whole], Copies(*sems[2:4]), sems[4]),
        "A": attend_steps(q, keys, values, blocks, exact, probs, scores),
    }
    in_turn(ATTEND_ORDER, programs)
    turns = Copies(*sems[5:7])
    for d in (1, 2, 3):
        there = (z + d) % 4
        turns.start(blocks.at[there], attended.at[:, head_columns(z)], {"sp": there})
    attended[:, head_columns(z)] = blocks[z]
    run(programs["G"])
    for copy in turns.started:
        copy.wait_recv()
    turns.finish()
    width = attended.shape[1]
    step = D // 4
    for i in range(4):
        weights = whole[i].reshape(step, -1)[:, :width]
        part[:, i * step : (i + 1) * step] = over(attended[...], weights, (1, 1)).astype(part.dtype)
    run(sum_wa_steps(part, total, *wa_bufs, Copies(*sems[7:9])))


def attention(q, k, v, own, collective_id):
    rows, low = q.shape[1], q.dtype
    every = jax.ShapeDtypeStruct((4, 2, 4, rows, HD), low)
    out_shape = [
        jax.ShapeDtypeStruct((rows, D), low),
        jax.ShapeDtypeStruct((rows, 4 * HD), low),
        every,
        every,
        jax.ShapeDtypeStruct((10, rows, 8 * rows), low),
        jax.ShapeDtypeStruct(q.shape, jnp.float32),
        jax.ShapeDtypeStruct((4, 2, 4, *own.shape), low),
    ]
    scratch = [pltpu.VMEM((rows, 32 * rows), jnp.float32), pltpu.VMEM(q.shape, low)]
    scratch += [pltpu.VMEM((rows, D), low)] + [pltpu.VMEM((rows, D // 2), low)] * 3
    scratch += [pltpu.SemaphoreType.DMA((n,)) for n in (12, 12, 44, 44, 1, 3, 3, 3, 3)]
    return vmem_call(
        functools.partial(attention_kernel, row_parts([own])), out_shape, (q, k, v, own), scratch,
        collective_id, "attention",
    )


def attend_back_steps(q, k, v, probs, grad, exact, dq, dk, dv, dk_sum, dv_sum):
    rows = q.shape[1]
    span = 8 * rows
    scale = HD ** (-0.5)
    at = 0

    def chunk(ref, c):
        return ref[c].reshape(span, HD)

    for block in range(4):
        low_grad = grad[block]
        delta = jnp.sum(low_grad.astype(jnp.float32) * exact[block], axis=1, keepdims=True)
        total = jnp.zeros((rows, HD), jnp.float32)
        for c in range(block + 1):
            low = probs[at]
            back = over(low_grad, chunk(v, c), (1, 1))
            terms = (low.astype(jnp.float32) * (back - delta)).astype(q.dtype)
            total = total + over(terms, chunk(k, c), (1, 0))
            key_terms = over(terms, q[block], (0, 0))
            value_terms = over(low, low_grad, (0, 0))
            if c == block:
                dk_sum[c] = key_terms
                dv_sum[c] = value_terms
            else:
                dk_sum[c] = dk_sum[c] + key_terms
                dv_sum[c] = dv_sum[c] + value_terms
            at += 1
        dq[block] = (total * scale).astype(dq.dtype)
        yield True
    for c in range(4):
        dk[c] = (dk_sum[c] * scale).astype(dk.dtype).reshape(dk.shape[1:])
        dv[c] = dv_sum[c].astype(dv.dtype).reshape(dv.shape[1:])
    yield True


def project_back_steps(dq, dk, dv, cosine, sine, x, w, back, grad):
    low = back.dtype
    rows = dq.shape[1]
    terms = []
    for src in (dq, dk):
        one = src[...].reshape(4 * rows, HD).astype(jnp.float32)
        terms.append((one * cosine[...] - pltpu.roll(one, HD // 2, 1) * sine[...]).astype(low))
    terms = jnp.concatenate([*terms, dv[...].reshape(4 * rows, HD)], axis=1)
    step = D // 4
    for i in range(4):
        here = slice(i * step, (i + 1) * step)
        back[:, :, here] = over(terms, w[here], (1, 1)).astype(low).reshape(4, rows, step)
        grad[i] = over(x[:, here], terms, (0, 0)).astype(low).reshape(grad.shape[1:])
        yield True


BACK_ORDER = "AAAAACCCCCCC"


def attention_back_kernel(parts, count, *refs):
    attended_grad, q, keys, values, probs, exact, cosine, sine, x, w, heads, *refs = refs
    summed, refs = refs[:count], refs[count:]
    total, grad_out, gain_out, *refs = refs
    shares, refs = refs[:count], refs[count:]
    head_grad, dq, dk, dv, dk_sum, dv_sum, back, grad, mixed, *refs = refs
    z_bufs, z_sums, wa_bufs, gain_bufs = refs[0:2], refs[2:4], refs[4:7], refs[7:9]
    refs = refs[9:]
    (kv_bufs, kv_sums, kv_cross, kv_own), refs = (refs[2 * i : 2 * i + 2] for i in range(4)), refs[8:]
    kv_sems, refs = refs[:2], refs[2:]
    (bufs, sums, cross, own), refs = (refs[2 * i : 2 * i + 2] for i in range(4)), refs[8:]
    head_sems, refs = refs[:2], refs[2:]
    sems, refs = refs[:10], refs[10:]
    cube_bufs, cube_sems = refs[:-2], refs[-2:]
    z = lax.axis_index("sp")
    places = along_z() + [neighbour("y", "A"), neighbour("y", "B"), neighbour("x", "A")]
    greet(places + wa_places())
    turns = Copies(*sems[0:2])
    for d in (1, 2, 3):
        there = (z + d) % 4
        turns.start(attended_grad.at[:, head_columns(there)], head_grad.at[z], {"sp": there})
    head_grad[z] = attended_grad[:, head_columns(z)]
    rows = pl.ds(0, dq.shape[1])
    programs = {
        "R": reduce_steps(parts, summed, shares, cube_bufs, Copies(*cube_sems)),
        "A": attend_back_steps(
            q, keys, values, probs, head_grad, exact, dq, dk, dv, dk_sum, dv_sum
        ),
        "C": ctx_reduce_steps(
            [(dk, rows), (dv, rows)], kv_bufs, kv_sums, kv_cross, kv_own, Copies(*kv_sems)
        ),
    }
    in_turn("RR", programs)
    for copy in turns.started:
        copy.wait_recv()
    turns.finish()
    in_turn(BACK_ORDER, programs)
    run(programs["C"])
    run(project_back_steps(dq, *kv_own, cosine, sine, x, w, back, grad))
    half = grad.shape[3] // 2
    grad_parts = [(grad, pl.ds(a * half, half)) for a in range(2)]

    def sums_of_rows():
        yield from rows_reduce_steps(back, mixed, z_bufs, z_sums, Copies(*sems[2:4]))
        yield from sum_wa_steps(mixed, total, *wa_bufs, Copies(*sems[4:6]))

    def grads():
        yield from ctx_reduce_steps(grad_parts, bufs, sums, cross, own, Copies(*head_sems))
        turns = Copies(*sems[6:8])
        for d in (1, 2, 3):
            there = (z + d) % 4
            for a in range(2):
                turns.start(own[a].at[there], grad_out.at[z, grad_parts[a][1]], {"sp": there})
        for a in range(2):
            grad_out[z, a * half : (a + 1) * half] = own[a][z]
        yield True
        for copy in turns.started:
            copy.wait_recv()
        turns.finish()
        products = jnp.zeros(gain_out.shape, jnp.float32)
        for h in range(4):
            for k in range(grad_out.shape[2] // HD):
                ours = heads[:, (4 * k + h) * HD : (4 * k + h + 1) * HD].astype(jnp.float32)
                theirs = grad_out[h, :, k * HD : (k + 1) * HD].astype(jnp.float32)
                products = products + ours * theirs
        gain_out[...] = products
        copies = Copies(*sems[8:10])
        for place, buf in zip(wa_places(), gain_bufs):
            copy = copies.start(gain_out, buf, place)
            yield True
            copy.wait()
            gain_out[...] = gain_out[...] + buf[...]

    run(grads(), sums_of_rows(), programs["R"])


def attention_back(operands, summed, collective_id):
    attended_grad, q, keys, _, _, _, _, _, x, w, heads = operands
    rows, low = q.shape[1], q.dtype
    shard = heads.shape[0]
    parts = row_parts(summed)
    out_shape = [
        jax.ShapeDtypeStruct((rows, D), low),
        jax.ShapeDtypeStruct((4, shard, w.shape[1]), low),
        jax.ShapeDtypeStruct((shard, HD), jnp.float32),
    ]
    out_shape += [jax.ShapeDtypeStruct(a.shape[3:], jnp.float32) for a in summed]
    wide = (rows, D // 2)
    sums = pltpu.VMEM((4, 8 * rows, HD), jnp.float32)
    scratch = [pltpu.VMEM(a.shape, low) for a in (q, q, keys, keys)] + [sums, sums]
    scratch += [pltpu.VMEM((4, rows, D), low), pltpu.VMEM((4, 2, 4, shard, w.shape[1]), low)]
    scratch += [pltpu.VMEM((rows, D), low)]
    scratch += [pltpu.VMEM((2, *wide), low)] * 2 + [pltpu.VMEM(wide, low)] * 5
    scratch += [pltpu.VMEM((shard, HD), jnp.float32)] * 2
    scratch += ctx_scratch([(rows, HD)] * 2, low) + ctx_scratch([(shard // 2, w.shape[1])] * 2, low)
    scratch += [pltpu.SemaphoreType.DMA((n,)) for n in (3, 3, 5, 5, 3, 3, 6, 6, 2, 2)]
    scratch += reduce_scratch(summed, parts)
    return vmem_call(
        functools.partial(attention_back_kernel, parts, len(summed)), out_shape,
        (*operands, *summed), scratch, collective_id, "attention_back",
    )


SLOTS = 16
GROUP_ORDER = ((0, 1), (1, 0), (3, 0), (1, 1), (3, 1), (2, 0), (2, 1), (0, 0))
SENT_AHEAD = 4
PASSED_BEHIND = 2
FIRST_COMPLETE = 11


def token_places():
    z, xh, y = own_place()
    w = lax.axis_index("wa")
    return z, xh, y, w // 2, w % 2


def block_device(dz, dx, dy):
    z, xh, y, place, core = token_places()
    there_z, there_x, there_y = (z + dz) % 4, (xh + dx) % 2, (y + dy) % 4
    there = (place + dx) % 2
    where = {"sp": there_z, "ctx": 4 * there_x + there_y, "wa": 2 * there + core}
    return where, there_z * 8 + there_x * 4 + there_y


def greet_blocks(others):
    barrier = pltpu.get_barrier_semaphore()

    def one(i, carry):
        where, _ = block_device(i // 8, (i // 4) % 2, i % 4)
        pl.semaphore_signal(barrier, inc=1, device_id=where, device_id_type=MESH)
        return carry

    lax.fori_loop(1, 32, one, 0)
    others = wa_places() + others
    for place in others:
        pl.semaphore_signal(barrier, inc=1, device_id=place, device_id_type=MESH)
    pl.semaphore_wait(barrier, 31 + len(others))


def quarter_columns(place, core):
    quarter = D // 4
    return pl.ds(pl.multiple_of(core * 2 * quarter + place * quarter, quarter), quarter)


def dispatch_steps(ins, outs, out_sem, in_sem, own_sem, copies):
    count = len(ins)
    z, xh, y, place, core = token_places()
    beside, across = wa_places()
    me = z * 8 + xh * 4 + y
    columns = quarter_columns(place, core)
    here = pl.ds(pl.multiple_of(me * SLOTS, SLOTS), SLOTS)
    own = [
        pltpu.make_async_copy(ins[a].at[me], outs[a].at[:, here, columns], own_sem.at[a])
        for a in range(count)
    ]
    for copy in own:
        copy.start()
    items = [(a, dz, dx) for a in range(count) for dz, dx in GROUP_ORDER]
    passed, last = {}, []
    firsts = len(GROUP_ORDER)

    def forward(part, i):
        copy = copies.start(part, part, beside)
        last.append((i // firsts, copy))

    def send(i):
        a, dz, dx = items[i]

        def one(dy, carry):
            where, block = block_device(dz, dx, dy)
            pltpu.make_async_remote_copy(
                src_ref=ins[a].at[block], dst_ref=outs[a].at[:, here, columns],
                send_sem=out_sem.at[a], recv_sem=in_sem.at[a, dz * 2 + dx],
                device_id=where, device_id_type=MESH,
            ).start()
            return carry

        lax.fori_loop(1 if dz + dx == 0 else 0, 4, one, 0)

    def rows_of(dz, dx):
        first = ((z - dz + 4) % 4 * 8 + (xh + dx) % 2 * 4) * SLOTS
        return pl.ds(pl.multiple_of(first, 4 * SLOTS), 4 * SLOTS)

    def arrived(i):
        a, dz, dx = items[i]
        few = 3 if dz + dx == 0 else 4
        sample = outs[a].at[:, pl.ds(0, few * SLOTS), columns]
        pltpu.make_async_copy(sample, sample, in_sem.at[a, dz * 2 + dx]).wait()
        if dz + dx == 0:
            own[a].wait()
        part = outs[a].at[:, rows_of(dz, dx), quarter_columns((place + dx) % 2, core)]
        passed[i] = copies.start(part, part, across)
        forward(part, i)

    def from_across(i):
        a, dz, dx = items[i]
        passed[i].wait_recv()
        part = outs[a].at[:, rows_of(dz, dx), quarter_columns((place + dx + 1) % 2, core)]
        forward(part, i)

    for i in range(SENT_AHEAD):
        send(i)
    yield True
    for i in range(len(items) + PASSED_BEHIND):
        if i < len(items):
            arrived(i)
            if i + SENT_AHEAD < len(items):
                send(i + SENT_AHEAD)
        if i >= PASSED_BEHIND:
            from_across(i - PASSED_BEHIND)
        if i == FIRST_COMPLETE:
            for a, copy in last:
                if a == 0:
                    copy.wait_recv()
        yield True
    for a, copy in last:
        if a > 0:
            copy.wait_recv()
    copies.finish()
    for a in range(count):
        sample = ins[a].at[pl.ds(0, 31)]
        pltpu.make_async_copy(sample, sample, out_sem.at[a]).wait()
    yield True


def shared_step(width):
    return -(-width // HD) * HD


def shared_steps(x, g, weights, whole, first, part, back, gate_grad, up_grad, down_grad, sem):
    low = part.dtype
    width = gate_grad.shape[1]
    step = shared_step(width)
    gate, up, down = (slice(k * step, k * step + width) for k in range(3))
    load = pltpu.make_async_copy(whole.at[:, pl.ds(first, weights.shape[1])], weights, sem.at[0])
    load.start()
    yield True
    load.wait()
    pre = over(x[...], weights[:, gate], (1, 0))
    yield True
    lin = over(x[...], weights[:, up], (1, 0))
    yield True
    act, pre_grad, lin_grad = swish_parts(pre, lin, over(g[...], weights[:, down], (1, 0)))
    act, pre_grad, lin_grad = act.astype(low), pre_grad.astype(low), lin_grad.astype(low)
    yield True
    for at in range(0, D, 512):
        here = slice(at, at + 512)
        part[:, here] = over(act, weights[here, down], (1, 1)).astype(low)
        back[:, here] = (
            over(pre_grad, weights[here, gate], (1, 1)) + over(lin_grad, weights[here, up], (1, 1))
        ).astype(low)
        yield True
        down_grad[here] = over(g[:, here], act, (0, 0)).astype(low)
        gate_grad[here] = over(x[:, here], pre_grad, (0, 0)).astype(low)
        up_grad[here] = over(x[:, here], lin_grad, (0, 0)).astype(low)
        yield True


def expert_steps(rows, grads, hbm, held, part, back, kept, load_sem, finished):
    low = rows.dtype
    hidden = hbm[0].shape[1]
    loads = [
        pltpu.make_async_copy(src, dst, load_sem.at[k]) for k, (src, dst) in enumerate(zip(hbm, held))
    ]
    for load in loads:
        load.start()
    yield True
    for load in loads:
        load.wait()
    gate, up, down = held
    chunks = [slice(at, at + 512) for at in range(0, D, 512)]
    found = []
    for e in range(2):
        pre = over(rows[e], gate[e], (1, 1))
        yield True
        lin = over(rows[e], up[e], (1, 1))
        found.append((pre, lin))
        act = (pre * jax.nn.sigmoid(pre) * lin).astype(low)
        kept[0][e] = act
        yield True
        for here in chunks:
            ref, place = part(e, here)
            ref[place] = over(act, down[e, :, here], (1, 0)).astype(low)
            if here is chunks[-1]:
                finished(e, 0)
            yield True
    for e in range(2):
        _, pre_grad, lin_grad = swish_parts(*found[e], over(grads[e], down[e], (1, 1)))
        pre_grad, lin_grad = pre_grad.astype(low), lin_grad.astype(low)
        kept[1][e], kept[2][e] = pre_grad, lin_grad
        yield True
        for here in chunks:
            ref, place = back(e, here)
            ref[place] = (
                over(pre_grad, gate[e, :, here], (1, 0)) + over(lin_grad, up[e, :, here], (1, 0))
            ).astype(low)
            if here is chunks[-1]:
                finished(e, 1)
            yield True


def return_steps(held, outs, halves, quarters, out_sem, in_sem, own_sem, copies):
    z, xh, y, place, core = token_places()
    beside, across = wa_places()
    me = z * 8 + xh * 4 + y
    quarter = D // 4
    group = 4 * SLOTS
    mine = pl.ds(pl.multiple_of(core * 2 * quarter, 2 * quarter), 2 * quarter)
    theirs = pl.ds(pl.multiple_of((1 - core) * 2 * quarter, 2 * quarter), 2 * quarter)
    rows_each = halves[0].shape[1]
    items = [(e, a, dz, dx) for a in range(2) for e in range(2) for dz, dx in GROUP_ORDER]
    paired_up, passed, own = {}, {}, []

    def finished(e, a):
        rows = pl.ds((2 * a + e) * rows_each, rows_each)
        paired_up[e, a] = copies.start(held.at[rows, theirs], halves[a].at[e], beside)

    def rows_of(dz, dx):
        return pl.ds(pl.multiple_of(((z + dz) % 4 * 8 + (xh + dx) % 2 * 4) * SLOTS, group), group)

    def kept(dx):
        return pl.ds(pl.multiple_of((place + dx) % 2 * quarter, quarter), quarter)

    def given(dx):
        return pl.ds(pl.multiple_of((place + dx + 1) % 2 * quarter, quarter), quarter)

    def add_core(i):
        e, a, dz, dx = items[i]
        rows = rows_of(dz, dx)
        if i % 8 == 0:
            paired_up[e, a].wait_recv()
        first = (2 * a + e) * rows_each
        ours = held[pl.ds(pl.multiple_of(first + rows.start, group), group), mine]
        halves[a][e, rows] = halves[a][e, rows] + ours
        passed[i] = copies.start(
            halves[a].at[e, rows, given(dx)], quarters[a].at[e, rows], across
        )

    def add_across(i):
        e, a, dz, dx = items[i]
        rows = rows_of(dz, dx)
        passed[i].wait_recv()
        quarters[a][e, rows] = quarters[a][e, rows] + halves[a][e, rows, kept(dx)]
        if dz + dx == 0:
            part = pl.ds(pl.multiple_of(me * SLOTS, SLOTS), SLOTS)
            copy = pltpu.make_async_copy(
                quarters[a].at[e, part], outs[a].at[me, e], own_sem.at[2 * a + e]
            )
            copy.start()
            own.append(copy)

        def one(dy, carry):
            where, block = block_device(dz, dx, dy)
            part = pl.ds(pl.multiple_of(block * SLOTS, SLOTS), SLOTS)
            pltpu.make_async_remote_copy(
                src_ref=quarters[a].at[e, part], dst_ref=outs[a].at[me, e],
                send_sem=out_sem.at[a], recv_sem=in_sem.at[a],
                device_id=where, device_id_type=MESH,
            ).start()
            return carry

        lax.fori_loop(1 if dz + dx == 0 else 0, 4, one, 0)

    def steps():
        for i in range(len(items) + BEHIND):
            if i < len(items):
                add_core(i)
            if i >= BEHIND:
                add_across(i - BEHIND)
            yield True
        copies.finish()
        for copy in own:
            copy.wait()
        for a in range(2):
            sample = outs[a].at[pl.ds(0, 31)]
            pltpu.make_async_copy(sample, sample, in_sem.at[a]).wait()
            pltpu.make_async_copy(sample, sample, out_sem.at[a]).wait()

    return finished, steps()


def quarter_sum_steps(ins, outs, got, far, copies):
    w = lax.axis_index("wa")
    core, place = w % 2, w // 2
    beside, across = wa_places()
    half, quarter = D // 2, D // 4
    mine = pl.ds(pl.multiple_of(core * half, half), half)
    theirs = pl.ds(pl.multiple_of((1 - core) * half, half), half)
    kept = pl.ds(pl.multiple_of(place * quarter, quarter), quarter)
    given = pl.ds(pl.multiple_of((1 - place) * quarter, quarter), quarter)
    one = [copies.start(x.at[:, theirs], buf, beside) for x, buf in zip(ins, got)]
    yield True
    two = []
    for a, x in enumerate(ins):
        one[a].wait_recv()
        got[a][...] = got[a][...] + x[:, mine]
        two.append(copies.start(got[a].at[:, given], far[a], across))
    yield True
    for a, out in enumerate(outs):
        two[a].wait_recv()
        out[...] = got[a][:, kept] + far[a][...]
    copies.finish()
    yield True


BEHIND = 12
MLP_ORDER = (
    "XD" + "SD" * 12 + "RRW" + "XD" * 3 + "W" + "XD" * 3 + "WXTXTXTXTXTXTD"
    + "XTXTXTTXTXT" + "XTTXTTXRTTXRTTXRTT" + "TTRTTRTTRTTRTTRTTTTRR"
)


def mlp_kernel(count, *refs):
    ins, (x, g, whole), hbm, refs = refs[:2], refs[2:5], refs[5:8], refs[8:]
    arrived, back_rows, shared_sums, refs = refs[:2], refs[2:4], refs[4:6], refs[6:]
    shares, kept, refs = refs[:count], refs[count : count + 3], refs[count + 3 :]
    weights, shared_grads, refs = refs[0], refs[1 : 1 + count], refs[1 + count :]
    held, halves, quarters, refs = refs[:3], refs[3:5], refs[5:7], refs[7:]
    shared_parts, shared_got, shared_far, refs = refs[:2], refs[2:4], refs[4:6], refs[6:]
    shared_sem, load_sem, out_sem, in_sem, own_sem, own_back_sem, *refs = refs
    sum_sems, refs = refs[:2], refs[2:]
    pass_sems, back_out_sem, back_in_sem, back_sems, refs = refs[:2], refs[2], refs[3], refs[4:6], refs[6:]
    bufs, cube_sems = refs[:-2], refs[-2:]
    greet_blocks([neighbour("x", "A")])
    rows = arrived[0].shape[1]
    results = weights.at[:, pl.ds(0, D)]

    def place_of(a):
        def place(e, here):
            first = (2 * a + e) * rows
            return weights, (slice(first, first + rows), here)

        return place

    finished, returning = return_steps(
        results, back_rows, halves, quarters, back_out_sem, back_in_sem, own_back_sem,
        Copies(*back_sems),
    )
    shards = [grad.shape[0] // 32 for grad in shared_grads]
    cubes = [
        grad.reshape(4, 2, 4, shard, grad.shape[1]) for grad, shard in zip(shared_grads, shards)
    ]
    parts = row_parts(cubes)
    programs = {
        "D": dispatch_steps(ins, arrived, out_sem, in_sem, own_sem, Copies(*pass_sems)),
        "S": shared_steps(
            x, g, weights, whole, 0, *shared_parts, *shared_grads, shared_sem
        ),
        "W": quarter_sum_steps(
            shared_parts, shared_sums, shared_got, shared_far, Copies(*sum_sems)
        ),
        "X": expert_steps(
            *arrived, hbm, held, place_of(0), place_of(1), kept, load_sem, finished
        ),
        "T": returning,
        "R": reduce_steps(parts, cubes, shares, bufs, Copies(*cube_sems)),
    }
    in_turn(MLP_ORDER, programs)
    run(programs["T"], programs["R"])


def mlp(arrays, x, g, whole, width, expert_weights, collective_id):
    low = x.dtype
    rows, count = 32 * SLOTS, 3
    hidden = expert_weights[0].shape[1]
    at_experts = jax.ShapeDtypeStruct((2, rows, D), low)
    grad = jax.ShapeDtypeStruct((D, width), low)
    cube = jax.ShapeDtypeStruct((4, 2, 4, D // 32, width), low)
    out_shape = [at_experts] * 2
    out_shape += [jax.ShapeDtypeStruct((32, 2, SLOTS, D // 4), low)] * 2
    out_shape += [jax.ShapeDtypeStruct((x.shape[0], D // 4), low)] * 2
    out_shape += [jax.ShapeDtypeStruct((D // 32, width), jnp.float32)] * count
    out_shape += [jax.ShapeDtypeStruct((2, rows, hidden), low)] * 3
    scratch = [pltpu.VMEM((D, 3 * shared_step(width)), low)]
    scratch += [pltpu.VMEM(grad.shape, low)] * count
    scratch += [pltpu.VMEM(a.shape, low) for a in expert_weights]
    scratch += [pltpu.VMEM((2, rows, D // 2), low)] * 2 + [pltpu.VMEM((2, rows, D // 4), low)] * 2
    scratch += [pltpu.VMEM((x.shape[0], D // n), low) for n in (1, 1, 2, 2, 4, 4)]
    sems = [(1,), (3,), (2,), (2, 8), (2,), (4,), (4,), (4,), (48,), (48,), (2,), (2,), (36,), (36,)]
    scratch += [pltpu.SemaphoreType.DMA(n) for n in sems]
    scratch += reduce_scratch([cube] * count, row_parts([cube] * count))
    anywhere, vmem = pl.BlockSpec(memory_space=pl.ANY), pl.BlockSpec(memory_space=pltpu.VMEM)
    return pl.pallas_call(
        functools.partial(mlp_kernel, count),
        out_shape=out_shape,
        in_specs=[anywhere] * 2 + [vmem] * 2 + [anywhere] * 4,
        out_specs=[vmem] * 2 + [anywhere] * 2 + [vmem] * (len(out_shape) - 4),
        scratch_shapes=scratch,
        compiler_params=pltpu.CompilerParams(
            collective_id=collective_id, has_side_effects=True, vmem_limit_bytes=VMEM_LIMIT
        ),
        name="mlp",
    )(*arrays, x, g, whole, *expert_weights)


def combine_kernel(
    gate_high, gate_rest, pick, widen, g, returned, back, shared, shared_back,
    mixed, mixed_in, probs, half, got, far, send_sem, recv_sem,
):
    low = mixed.dtype
    _, _, _, place, core = token_places()
    beside, across = wa_places()
    greet([beside, across])
    copies = Copies(send_sem, recv_sem)
    mine, other = quarter_columns(place, core), quarter_columns(1 - place, core)
    routed = over(gate_high[...], returned[...], (1, 0)) + over(gate_rest[...], returned[...], (1, 0))
    mixed[:, mine] = (routed + shared[...].astype(jnp.float32)).astype(low)
    first, last = [], []

    def spread(out):
        part = out.at[:, mine]
        first.append(copies.start(part, part, across))
        last.append(copies.start(part, part, beside))

    spread(mixed)
    rows = over(pick[...], back[...], (1, 0))
    mixed_in[:, mine] = (rows + shared_back[...].astype(jnp.float32)).astype(low)
    spread(mixed_in)
    rest = jnp.where(pick[...] > 0, over(g[...], returned[...], (1, 1)), 0.0)
    total = jnp.zeros(probs.shape, jnp.float32)
    for _ in range(3):
        term = rest.astype(low)
        rest = rest - term.astype(jnp.float32)
        total = total + over(term, widen[...], (1, 1))
    half[...] = total
    one = copies.start(half, got, beside)
    for copy, out in zip(first, (mixed, mixed_in)):
        copy.wait_recv()
        part = out.at[:, other]
        last.append(copies.start(part, part, beside))
    one.wait()
    half[...] = half[...] + got[...]
    two = copies.start(half, far, across)
    two.wait_recv()
    probs[...] = half[...] + far[...]
    for copy in last:
        copy.wait_recv()
    for copy in copies.started:
        if copy is not one:
            copy.wait_send()


def combine(operands, collective_id):
    tokens, low = operands[0].shape[0], operands[0].dtype
    out_shape = [jax.ShapeDtypeStruct((tokens, D), low)] * 2
    out_shape += [jax.ShapeDtypeStruct((tokens, HD), jnp.float32)]
    scratch = [pltpu.VMEM((tokens, HD), jnp.float32)] * 3 + [pltpu.SemaphoreType.DMA((8,))] * 2
    return vmem_call(combine_kernel, out_shape, operands, scratch, collective_id, "combine")


def swish_parts(pre, lin, act_grads):
    sig = jax.nn.sigmoid(pre)
    swish = pre * sig
    slope = sig * (1.0 + pre * (1.0 - sig))
    return swish * lin, act_grads * lin * slope, act_grads * swish


def expert_grads_kernel(*refs):
    hbm, outs, held, results = refs[:5], refs[5:8], refs[8:13], refs[13]
    load_sem, out_sem = refs[14:]
    loads = [
        [
            pltpu.make_async_copy(src.at[e], dst.at[e], load_sem.at[e, k])
            for k, (src, dst) in enumerate(zip(hbm, held))
        ]
        for e in range(2)
    ]
    for load in loads[0] + loads[1]:
        load.start()
    rows, grads, act, pre_grad, lin_grad = held
    stores = []
    for e in range(2):
        for load in loads[e]:
            load.wait()
        for k, (left, right) in enumerate(((pre_grad, rows), (lin_grad, rows), (act, grads))):
            results[e, k] = over(left[e], right[e], (0, 0))
            store = pltpu.make_async_copy(results.at[e, k], outs[k].at[e], out_sem.at[e, k])
            store.start()
            stores.append(store)
    for store in stores:
        store.wait()


def expert_grads(*operands):
    shape = jax.ShapeDtypeStruct((2, operands[2].shape[2], D), jnp.float32)
    scratch = [pltpu.VMEM(x.shape, x.dtype) for x in operands]
    scratch += [pltpu.VMEM((2, 3, *shape.shape[1:]), jnp.float32)]
    scratch += [pltpu.SemaphoreType.DMA((2, 5)), pltpu.SemaphoreType.DMA((2, 3))]
    anywhere = pl.BlockSpec(memory_space=pl.ANY)
    return pl.pallas_call(
        expert_grads_kernel,
        out_shape=[shape] * 3,
        in_specs=[anywhere] * 5,
        out_specs=[anywhere] * 3,
        scratch_shapes=scratch,
        compiler_params=pltpu.CompilerParams(vmem_limit_bytes=VMEM_LIMIT),
        name="expert_grads",
    )(*operands)


def turned_gather(arrays, axis):
    widths = [a.shape[1] for a in arrays]
    whole = lax.all_gather(jnp.concatenate(arrays, axis=1), axis, axis=0, tiled=True)
    return jnp.split(whole, [sum(widths[:k]) for k in range(1, len(widths))], axis=1)


def rope_tables(positions):
    half_width = HD // 2
    inverse = 1.0 / ROPE_BASE ** (jnp.arange(half_width, dtype=jnp.float32) * 2.0 / HD)
    angles = positions[:, None] * inverse[None, :]
    cosine, sine = jnp.cos(angles), jnp.sin(angles)
    return jnp.concatenate([cosine, cosine], axis=1), jnp.concatenate([-sine, sine], axis=1)


def dot(left, right, over, dtype=jnp.float32, **kept):
    return lax.dot_general(
        left, right, ((over[:1], over[1:]), ((), ())), preferred_element_type=dtype, **kept
    )


def shards(
    tokens,
    cotangent,
    routes,
    attn_gain,
    query_weight,
    key_weight,
    value_weight,
    output_weight,
    mlp_gain,
    router_weight,
    shared_gate,
    shared_up,
    shared_down,
    expert_gate,
    expert_up,
    expert_down,
):
    low = jnp.bfloat16
    local_tokens = tokens.shape[0]
    head_cols = query_weight.shape[1]
    experts_all = router_weight.shape[1]
    groups = ("sp", "ctx")
    place, core = lax.axis_index("wa") // 2, lax.axis_index("wa") % 2
    quarter_at = core * (D // 2) + place * (D // 4)

    def quarter(x):
        return lax.dynamic_slice_in_dim(x, quarter_at, D // 4, 1)

    hidden_cols = shared_gate.shape[1]
    def beside(arrays):
        return jnp.concatenate(
            [jnp.pad(x, ((0, 0), (0, -x.shape[1] % HD))) for x in arrays], axis=1
        )

    shared_whole = lax.all_gather(
        beside((shared_gate, shared_up, shared_down.T)), groups, axis=0, tiled=True
    )
    router_own = jnp.concatenate([router_weight, mlp_gain[:, None]], axis=1)
    tokens_f = tokens.astype(jnp.float32)
    inv_one = lax.rsqrt(jnp.mean(tokens_f * tokens_f, axis=-1, keepdims=True) + EPSILON)
    unit_one = tokens_f * inv_one
    gain_one = attn_gain.astype(jnp.float32)[:, None]
    heads = jnp.concatenate([query_weight, key_weight, value_weight], axis=1)
    scaled = (gain_one * heads.astype(jnp.float32)).astype(low)
    head_rows, head_weights = gather_head(unit_one.astype(low), scaled, 1)
    head_rows, head_weights = head_rows.reshape(-1, D), head_weights.reshape(D, -1)
    blocks = jnp.arange(4, dtype=jnp.int32)[:, None] * 8 + lax.axis_index("ctx")
    positions = blocks * local_tokens + jnp.arange(local_tokens, dtype=jnp.int32)[None, :]
    cosine, sine = rope_tables(positions.reshape(-1).astype(jnp.float32))
    by_head = (4, local_tokens, HD)
    head_queries, own_keys, own_values = (
        x.reshape(by_head) for x in project(head_rows, head_weights, cosine, sine)
    )
    attn_out, attended, head_keys, head_values, probs, exact, whole = attention(
        head_queries, own_keys, own_values, beside((output_weight.T, router_own)), 2
    )
    attn_out = attn_out.astype(jnp.float32)
    whole = whole.reshape(D, -1)
    turned = whole[:, :head_cols]
    full_router = whole[:, head_cols : head_cols + experts_all]
    gain_two = whole[:, head_cols + experts_all].astype(jnp.float32)
    hidden_state = tokens_f + attn_out
    inv_two = lax.rsqrt(jnp.mean(hidden_state * hidden_state, axis=-1, keepdims=True) + EPSILON)
    unit_two = hidden_state * inv_two
    mlp_in = (unit_two * gain_two).astype(low)

    logits = dot(mlp_in, full_router, (1, 0))
    logit_exp = jnp.exp(logits - jnp.max(logits, axis=-1, keepdims=True))
    router_probs = logit_exp / jnp.sum(logit_exp, axis=-1, keepdims=True)
    experts = jnp.arange(experts_all, dtype=jnp.int32)
    chosen = jnp.zeros((local_tokens, experts_all), jnp.bool_)
    for j in range(TOP):
        chosen = chosen | (routes[:, j : j + 1] == experts[None, :])
    ids = jnp.arange(local_tokens, dtype=jnp.int32)
    before = (ids[None, :] < ids[:, None]).astype(low)
    rank = dot(before, chosen.astype(low), (1, 0))
    slot_of = jnp.where(chosen, rank, -1.0).astype(low)
    slot_ids = jnp.arange(experts_all * SLOTS, dtype=jnp.int32)
    widen = (experts[:, None] == slot_ids[None, :] // SLOTS).astype(low)
    taken = dot(slot_of, widen, (1, 0)) == (slot_ids % SLOTS).astype(jnp.float32)[None, :]
    probs_high = router_probs.astype(low)
    probs_rest = (router_probs - probs_high.astype(jnp.float32)).astype(low)
    pick = taken.astype(low)
    gate_high = jnp.where(taken, dot(probs_high, widen, (1, 0)), 0.0).astype(low)
    gate_rest = jnp.where(taken, dot(probs_rest, widen, (1, 0)), 0.0).astype(low)
    grad_quarter = quarter(cotangent)
    send_rows = dot(pick, quarter(mlp_in), (0, 0)).astype(low)
    send_grads = (
        dot(gate_high, grad_quarter, (0, 0)) + dot(gate_rest, grad_quarter, (0, 0))
    ).astype(low)
    by_owner = (32, 2, SLOTS, D // 4)
    expert_weights = (expert_gate.transpose(0, 2, 1), expert_up.transpose(0, 2, 1), expert_down)
    (
        rows_in,
        grads_in,
        returned,
        rows_back,
        shared_part,
        shared_in_part,
        gate_share,
        up_share,
        down_share,
        *kept,
    ) = mlp(
        (send_rows.reshape(by_owner), send_grads.reshape(by_owner)),
        mlp_in,
        cotangent,
        shared_whole,
        hidden_cols,
        expert_weights,
        5,
    )
    gate_grad_turned, up_grad_turned, expert_down_grad = expert_grads(rows_in, grads_in, *kept)
    returned, rows_back = returned.reshape(-1, D // 4), rows_back.reshape(-1, D // 4)

    widen_all = jnp.pad(widen, ((0, HD - experts_all), (0, 0)))
    mixed, mixed_in, prob_grads = combine(
        (
            gate_high,
            gate_rest,
            pick,
            widen_all,
            grad_quarter,
            returned,
            rows_back,
            shared_part,
            shared_in_part,
        ),
        7,
    )
    block_out = (hidden_state + mixed.astype(jnp.float32)).astype(low)
    prob_grads = prob_grads[:, :experts_all]
    logit_grads = router_probs * (
        prob_grads - jnp.sum(router_probs * prob_grads, axis=-1, keepdims=True)
    )
    router_in_grad = dot(
        logit_grads, full_router.astype(jnp.float32), (1, 1), precision=PRECISE
    )
    mlp_in_grad = router_in_grad + mixed_in.astype(jnp.float32)
    gain_two_grad = jnp.sum(mlp_in_grad * unit_two, axis=0)
    scaled_two = mlp_in_grad * gain_two
    hidden_grad = cotangent.astype(jnp.float32) + inv_two * (
        scaled_two - unit_two * jnp.mean(scaled_two * unit_two, axis=-1, keepdims=True)
    )
    out_grad = hidden_grad.astype(low)
    router_grad = dot(mlp_in, logit_grads.astype(low), (0, 0))

    attended_grad = dot(out_grad, turned, (1, 0)).astype(low)
    def by_shard(x):
        return x.astype(low).reshape(4, 2, 4, x.shape[0] // 32, x.shape[1])

    small_grads = jnp.concatenate([router_grad, gain_two_grad[:, None]], axis=1)
    small_grads = jnp.pad(small_grads, ((0, 0), (0, HD - small_grads.shape[1])))
    summed = [by_shard(dot(out_grad, attended, (0, 0))), by_shard(small_grads)]
    scaled_one, head_shares, gain_terms, output_share, small_share = attention_back(
        (
            attended_grad,
            head_queries,
            head_keys,
            head_values,
            probs,
            exact,
            cosine,
            sine,
            head_rows,
            head_weights,
            heads,
        ),
        summed,
        9,
    )
    scaled_one = scaled_one.astype(jnp.float32)
    tokens_grad = (
        hidden_grad
        + inv_one
        * (scaled_one - unit_one * jnp.mean(scaled_one * unit_one, axis=-1, keepdims=True))
    ).astype(low)
    head_shares = head_shares.astype(jnp.float32) * gain_one
    query_share, key_share, value_share = (
        head_shares[..., k * HD : (k + 1) * HD].swapaxes(0, 1).reshape(-1, head_cols)
        for k in range(3)
    )
    return (
        block_out,
        tokens_grad,
        jnp.sum(gain_terms, axis=1),
        query_share,
        key_share,
        value_share,
        output_share.T,
        small_share[:, experts_all],
        small_share[:, :experts_all],
        gate_share,
        up_share,
        down_share.T,
        gate_grad_turned.transpose(0, 2, 1),
        up_grad_turned.transpose(0, 2, 1),
        expert_down_grad,
    )


def solution(mesh):
    placed = (
        P(("sp", "ctx"), None),
        P(("sp", "ctx"), None),
        P(("sp", "ctx"), None),
        P(("sp", "ctx")),
        P(("sp", "ctx"), "wa"),
        P(("sp", "ctx"), "wa"),
        P(("sp", "ctx"), "wa"),
        P("wa", ("sp", "ctx")),
        P(("sp", "ctx")),
        P(("sp", "ctx"), None),
        P(("sp", "ctx"), "wa"),
        P(("sp", "ctx"), "wa"),
        P("wa", ("sp", "ctx")),
        P(("sp", "ctx"), None, "wa"),
        P(("sp", "ctx"), None, "wa"),
        P(("sp", "ctx"), "wa", None),
    )
    return jax.shard_map(
        shards,
        mesh=mesh,
        in_specs=placed,
        out_specs=(
            P(("sp", "ctx"), None),
            P(("sp", "ctx"), None),
            P(("sp", "ctx")),
            P(("sp", "ctx"), "wa"),
            P(("sp", "ctx"), "wa"),
            P(("sp", "ctx"), "wa"),
            P("wa", ("sp", "ctx")),
            P(("sp", "ctx")),
            P(("sp", "ctx"), None),
            P(("sp", "ctx"), "wa"),
            P(("sp", "ctx"), "wa"),
            P("wa", ("sp", "ctx")),
            P(("sp", "ctx"), None, "wa"),
            P(("sp", "ctx"), None, "wa"),
            P(("sp", "ctx"), "wa", None),
        ),
        check_vma=False,
    )
```

```python
import functools

import jax
import jax.numpy as jnp
from jax import lax
from jax.experimental import pallas as pl
from jax.experimental.pallas import tpu as pltpu
from jax.sharding import PartitionSpec as P

D = 2048
HD = 128
TOP = 6


EPSILON = 1e-06
ROPE_BASE = 10000.0
MASKED = -1e30
PRECISE = lax.Precision.HIGHEST


MESH = pl.DeviceIdType.MESH
VMEM_LIMIT = 63 * 1024 * 1024

ORDERS = (
    (("z", "A"), ("z", "B"), ("y", "A"), ("y", "B")),
    (("z", "B"), ("z", "A"), ("y", "B"), ("y", "A")),
    (("y", "A"), ("y", "B"), ("z", "A"), ("z", "B")),
    (("y", "B"), ("y", "A"), ("z", "B"), ("z", "A")),
)


def paired(i, kind):
    return i + 1 - 2 * (i % 2) if kind == "A" else 3 - i


def own_place():
    c = lax.axis_index("ctx")
    return lax.axis_index("sp"), c // 4, c % 4


def neighbour(axis, kind):
    z, xh, y = own_place()
    if axis == "z":
        return {"sp": paired(z, kind)}
    if axis == "y":
        return {"ctx": 4 * xh + paired(y, kind)}
    return {"ctx": 4 * (1 - xh) + y}


def cube_places():
    rings = [neighbour(axis, kind) for axis in ("z", "y") for kind in ("A", "B")]
    return rings + [neighbour("x", "A")]


def pair_slots(i, kind):
    if kind == "A":
        return [(pl.ds((i // 2) * 2, 2), pl.ds(0, 2))]
    return [(pl.ds(i, 1), pl.ds(0, 1)), (pl.ds(3 - i, 1), pl.ds(1, 1))]


def pair_members(i, kind):
    if kind == "A":
        return [(i // 2) * 2, (i // 2) * 2 + 1]
    return [i, 3 - i]


def slot_in_pair(i, kind):
    return i % 2 if kind == "A" else 0

def over(left, right, dims):
    return lax.dot_general(
        left, right, ((dims[:1], dims[1:]), ((), ())), preferred_element_type=jnp.float32
    )


def head_columns(h):
    return pl.ds(pl.multiple_of(h * HD, HD), HD)


class Copies:
    def __init__(self, send_sem, recv_sem):
        self.send_sem, self.recv_sem, self.started = send_sem, recv_sem, []

    def start(self, src, dst, where):
        k = len(self.started)
        copy = pltpu.make_async_remote_copy(
            src_ref=src, dst_ref=dst, send_sem=self.send_sem.at[k],
            recv_sem=self.recv_sem.at[k], device_id=where, device_id_type=MESH,
        )
        copy.start()
        self.started.append(copy)
        return copy

    def finish(self):
        for copy in self.started:
            copy.wait_send()


def run(*programs):
    programs = list(programs)
    while programs:
        programs = [program for program in programs if next(program, None) is not None]


def in_turn(order, programs):
    for letter in order:
        next(programs[letter], None)


def greet(places):
    barrier = pltpu.get_barrier_semaphore()
    for place in places:
        pl.semaphore_signal(barrier, inc=1, device_id=place, device_id_type=MESH)
    pl.semaphore_wait(barrier, len(places))


def along_z():
    z = lax.axis_index("sp")
    return [{"sp": (z + d) % 4} for d in (1, 2, 3)]


def vmem_call(kernel, out_shape, operands, scratch, collective_id, name, **params):
    return pl.pallas_call(
        kernel,
        out_shape=out_shape,
        in_specs=[pl.BlockSpec(memory_space=pltpu.VMEM)] * len(operands),
        out_specs=jax.tree.map(lambda _: pl.BlockSpec(memory_space=pltpu.VMEM), out_shape),
        scratch_shapes=scratch,
        compiler_params=pltpu.CompilerParams(
            collective_id=collective_id,
            has_side_effects=collective_id is not None,
            vmem_limit_bytes=VMEM_LIMIT,
        ),
        name=name,
        **params,
    )(*operands)

def gather_steps(parts, ins, outs, copies, local_sem):
    z, xh, y = own_place()
    count = len(ins)

    def step(lane, p, s):
        ring1, ring2 = ORDERS[p][0][0], ORDERS[p][2][0]
        where = neighbour(*ORDERS[p][s])
        xl = xh if lane == 0 else 1 - xh
        zs, ys = [pl.ds(z, 1)], [pl.ds(y, 1)]
        full = [pl.ds(0, 4)]
        if s == 1:
            other = [d for d, _ in pair_slots(z if ring1 == "z" else y, ORDERS[p][0][1])]
            zs, ys = (other, ys) if ring1 == "z" else (zs, other)
        if s >= 2:
            zs, ys = (full, ys) if ring1 == "z" else (zs, full)
        if s == 3:
            other = [d for d, _ in pair_slots(z if ring2 == "z" else y, ORDERS[p][2][1])]
            zs, ys = (other, ys) if ring2 == "z" else (zs, other)
        started = []
        for a, rows, cols in parts[p]:
            for zd in zs:
                for yd in ys:
                    place = outs[a].at[zd, pl.ds(xl, 1), yd, rows, cols]
                    started.append(copies.start(place, place, where))
        return started

    local = [
        pltpu.make_async_copy(ins[a], outs[a].at[z, xh, y], local_sem.at[a]) for a in range(count)
    ]
    for copy in local:
        copy.start()
    across = [
        [
            copies.start(
                ins[a].at[rows, cols], outs[a].at[z, xh, y, rows, cols], neighbour("x", "A")
            )
            for a, rows, cols in part
        ]
        for part in parts
    ]
    for copy in local:
        copy.wait()
    flying = {}
    for lane, s in (
        (0, 0), (0, 1), (1, 0), (0, 2), (1, 1), (0, 3), (1, 2), (1, 3), (0, 4), (1, 4)
    ):
        for p in range(4):
            for copy in flying.get((lane, p), across[p] if lane == 1 else []):
                copy.wait_recv()
            flying[lane, p] = step(lane, p, s) if s < 4 else []
        yield True
    copies.finish()


def gather_kernel(parts, count, *refs):
    ins, outs = refs[:count], refs[count : 2 * count]
    send_sem, recv_sem, local_sem = refs[2 * count :]
    greet(cube_places())
    run(gather_steps(parts, ins, outs, Copies(send_sem, recv_sem), local_sem))


def gather_cube(arrays, parts, collective_id, name):
    count = len(arrays)
    copies = 11 * sum(len(part) for part in parts)
    return pl.pallas_call(
        functools.partial(gather_kernel, parts, count),
        out_shape=[jax.ShapeDtypeStruct((4, 2, 4, *a.shape), a.dtype) for a in arrays],
        in_specs=[pl.BlockSpec(memory_space=pl.ANY)] * count,
        out_specs=[pl.BlockSpec(memory_space=pl.ANY)] * count,
        scratch_shapes=[
            pltpu.SemaphoreType.DMA((copies,)),
            pltpu.SemaphoreType.DMA((copies,)),
            pltpu.SemaphoreType.DMA((count,)),
        ],
        compiler_params=pltpu.CompilerParams(collective_id=collective_id, has_side_effects=True),
        name=name,
    )(*arrays)


def entries_of(parts):
    return [(p, *entry) for p in range(4) for entry in parts[p]]


CUBE_ORDER = tuple((stage, lane) for stage in range(5) for lane in (1, 0))


def reduce_steps(parts, ins, outs, bufs, copies):
    entries = entries_of(parts)
    z, xh, y = own_place()
    start = copies.start
    flying = {}

    def first(lane, e):
        p, a, rows, cols = entries[e]
        ring2, near = ORDERS[p][2]
        axis, kind = ORDERS[p][3]
        xl = xh if lane == 0 else 1 - xh
        theirs = paired(z if ring2 == "z" else y, kind)
        copies = []
        for src, dst in pair_slots(theirs, near):
            if ring2 == "z":
                block, place = ins[a].at[src, xl, :, rows, cols], bufs[5 * e].at[lane, dst]
            else:
                block, place = ins[a].at[:, xl, src, rows, cols], bufs[5 * e].at[lane, :, dst]
            copies.append(start(block, place, neighbour(axis, kind)))
        flying[lane, e] = copies

    def second(lane, e):
        p, a, rows, cols = entries[e]
        ring2 = ORDERS[p][2][0]
        axis, kind = ORDERS[p][2]
        xl = xh if lane == 0 else 1 - xh
        mine = z if ring2 == "z" else y
        buf = bufs[5 * e]
        for copy in flying[lane, e]:
            copy.wait_recv()
        slot = slot_in_pair(mine, kind)

        def add(j, place):
            def one(i, carry):
                if ring2 == "z":
                    buf[lane, j, i] = buf[lane, j, i] + ins[a][place, xl, i, rows, cols]
                else:
                    buf[lane, i, j] = buf[lane, i, j] + ins[a][i, xl, place, rows, cols]
                return carry

            lax.fori_loop(0, 4, one, 0)

        add(1 - slot, paired(mine, kind))
        half = buf.at[lane, 1 - slot] if ring2 == "z" else buf.at[lane, :, 1 - slot]
        flying[lane, e] = [start(half, bufs[5 * e + 1].at[lane], neighbour(axis, kind))]
        add(slot, mine)

    def third(lane, e):
        p = entries[e][0]
        ring1, ring2 = ORDERS[p][0][0], ORDERS[p][2][0]
        axis, kind = ORDERS[p][1]
        before, buf = bufs[5 * e], bufs[5 * e + 1]
        for copy in flying[lane, e]:
            copy.wait_recv()
        slot = slot_in_pair(z if ring2 == "z" else y, ORDERS[p][2][1])

        def one(i, carry):
            other = before[lane, slot, i] if ring2 == "z" else before[lane, i, slot]
            buf[lane, i] = buf[lane, i] + other
            return carry

        lax.fori_loop(0, 4, one, 0)
        theirs = paired(z if ring1 == "z" else y, kind)
        flying[lane, e] = [
            start(buf.at[lane, src], bufs[5 * e + 2].at[lane, dst], neighbour(axis, kind))
            for src, dst in pair_slots(theirs, ORDERS[p][0][1])
        ]

    def fourth(lane, e):
        p = entries[e][0]
        ring1 = ORDERS[p][0][0]
        axis, kind = ORDERS[p][0]
        mine = z if ring1 == "z" else y
        before, buf = bufs[5 * e + 1], bufs[5 * e + 2]
        for copy in flying[lane, e]:
            copy.wait_recv()
        slot = slot_in_pair(mine, kind)
        buf[lane, 1 - slot] = buf[lane, 1 - slot] + before[lane, paired(mine, kind)]
        flying[lane, e] = [
            start(buf.at[lane, 1 - slot], bufs[5 * e + 3].at[lane], neighbour(axis, kind))
        ]
        buf[lane, slot] = buf[lane, slot] + before[lane, mine]

    def last(lane, e):
        p, a, rows, cols = entries[e]
        ring1 = ORDERS[p][0][0]
        before, buf = bufs[5 * e + 2], bufs[5 * e + 3]
        for copy in flying[lane, e]:
            copy.wait_recv()
        slot = slot_in_pair(z if ring1 == "z" else y, ORDERS[p][0][1])
        if lane == 1:
            buf[1] = buf[1] + before[1, slot]
            flying["x", e] = start(buf.at[1], bufs[5 * e + 4], neighbour("x", "A"))
        else:
            flying["x", e].wait_recv()
            total = (
                buf[0].astype(jnp.float32)
                + before[0, slot].astype(jnp.float32)
                + bufs[5 * e + 4][...].astype(jnp.float32)
            )
            outs[a][rows, cols] = total.astype(outs[a].dtype)

    stages = (first, second, third, fourth, last)
    for at, lane in CUBE_ORDER:
        for e in range(len(entries)):
            stages[at](lane, e)
        yield True
    copies.finish()


def reduce_kernel(parts, count, *refs):
    size = 5 * len(entries_of(parts))
    ins, outs = refs[:count], refs[count : 2 * count]
    bufs = refs[2 * count : 2 * count + size]
    greet(cube_places())
    run(reduce_steps(parts, ins, outs, bufs, Copies(*refs[2 * count + size :])))


def reduce_scratch(arrays, parts):
    scratch = []
    for p in range(4):
        pair = (2, 4) if ORDERS[p][2][0] == "z" else (4, 2)
        for a, rows, cols in parts[p]:
            for lead in ((2, *pair), (2, 4), (2, 2), (2,), ()):
                scratch.append(pltpu.VMEM((*lead, rows.size, cols.size), arrays[a].dtype))
    copies = 13 * sum(len(part) for part in parts)
    return scratch + [pltpu.SemaphoreType.DMA((copies,))] * 2


def reduce_cube(arrays, parts, collective_id, name, dtype=jnp.float32):
    count = len(arrays)
    scratch = reduce_scratch(arrays, parts)
    return pl.pallas_call(
        functools.partial(reduce_kernel, parts, count),
        out_shape=[jax.ShapeDtypeStruct(a.shape[3:], dtype) for a in arrays],
        in_specs=[pl.BlockSpec(memory_space=pltpu.VMEM)] * count,
        out_specs=[pl.BlockSpec(memory_space=pltpu.VMEM)] * count,
        scratch_shapes=scratch,
        compiler_params=pltpu.CompilerParams(
            collective_id=collective_id, has_side_effects=True, vmem_limit_bytes=VMEM_LIMIT
        ),
        name=name,
    )(*arrays)


def row_parts(arrays):
    parts = []
    for p in range(4):
        part = []
        for a, array in enumerate(arrays):
            rows, columns = array.shape[-2:]
            part.append((a, pl.ds(p * rows // 4, rows // 4), pl.ds(0, columns)))
        parts.append(part)
    return parts


def whole_parts(arrays):
    return [[(a, pl.ds(0, x.shape[-2]), pl.ds(0, x.shape[-1]))] for a, x in enumerate(arrays)]


def half_parts(arrays):
    return [
        [(a, pl.ds(0, x.shape[-2]), pl.ds(h * x.shape[-1] // 2, x.shape[-1] // 2))]
        for a, x in enumerate(arrays)
        for h in range(2)
    ]


def wa_places():
    w = lax.axis_index("wa")
    return [{"wa": w + 1 - 2 * (w % 2)}, {"wa": (w + 2) % 4}]


def sum_wa_steps(x, out, half, got, far, copies):
    core = lax.axis_index("wa") % 2
    beside, across = wa_places()
    width = x.shape[1] // 2
    mine = pl.ds(pl.multiple_of(core * width, width), width)
    theirs = pl.ds(pl.multiple_of((1 - core) * width, width), width)
    one = copies.start(x.at[:, theirs], got, beside)
    yield True
    one.wait_recv()
    half[...] = x[:, mine] + got[...]
    two = copies.start(half, far, across)
    yield True
    two.wait_recv()
    out[:, mine] = half[...] + far[...]
    three = copies.start(out.at[:, mine], out.at[:, mine], beside)
    yield True
    three.wait_recv()
    copies.finish()


def sum_wa_kernel(x, out, half, got, far, send_sem, recv_sem):
    greet(wa_places())
    run(sum_wa_steps(x, out, half, got, far, Copies(send_sem, recv_sem)))


def sum_wa(x, collective_id, name):
    rows, columns = x.shape
    return pl.pallas_call(
        sum_wa_kernel,
        out_shape=jax.ShapeDtypeStruct(x.shape, x.dtype),
        in_specs=[pl.BlockSpec(memory_space=pltpu.VMEM)],
        out_specs=pl.BlockSpec(memory_space=pltpu.VMEM),
        scratch_shapes=[pltpu.VMEM((rows, columns // 2), x.dtype)] * 3
        + [pltpu.SemaphoreType.DMA((3,)), pltpu.SemaphoreType.DMA((3,))],
        compiler_params=pltpu.CompilerParams(
            collective_id=collective_id, has_side_effects=True, vmem_limit_bytes=VMEM_LIMIT
        ),
        name=name,
    )(x)

def ctx_gather_steps(parts, copies):
    z, xh, y = own_place()

    def send(part, xl, place, axis, kind):
        ref, rows = part
        block = ref.at[:, xl, place, rows]
        return copies.start(block, block, neighbour(axis, kind))

    near, far = ("A", "B"), ("B", "A")
    first, across, last = {}, [], []
    for a in range(2):
        first[0, a] = send(parts[a], xh, y, "y", near[a])
        across.append(send(parts[a], xh, y, "x", "A"))
    yield True
    for lane in range(2):
        xl = xh if lane == 0 else 1 - xh
        if lane == 1:
            for a in range(2):
                across[a].wait_recv()
                first[1, a] = send(parts[a], xl, y, "y", near[a])
            yield True
        for a in range(2):
            first[lane, a].wait_recv()
            for place, _ in pair_slots(y, near[a]):
                last.append(send(parts[a], xl, place, "y", far[a]))
        yield True
    for copy in last:
        copy.wait_recv()
    copies.finish()


CTX_ORDER = ((0, 1), (1, 1), (0, 0), (2, 1), (1, 0), (2, 0))


def ctx_reduce_steps(parts, bufs, sums, cross, own, copies):
    z, xh, y = own_place()
    near, far = ("A", "B"), ("B", "A")
    flying = {}

    def first(lane):
        xl = xh if lane == 0 else 1 - xh
        for a, (ref, rows) in enumerate(parts):
            flying[lane, a] = [
                copies.start(
                    ref.at[:, xl, src, rows], bufs[a].at[lane, :, dst], neighbour("y", far[a])
                )
                for src, dst in pair_slots(paired(y, far[a]), near[a])
            ]

    def second(lane):
        xl = xh if lane == 0 else 1 - xh
        for a, (ref, rows) in enumerate(parts):
            for copy in flying[lane, a]:
                copy.wait_recv()
            slot = slot_in_pair(y, near[a])

            def add(j, place):
                def one(i, carry):
                    bufs[a][lane, i, j] = bufs[a][lane, i, j] + ref[i, xl, place, rows]
                    return carry

                lax.fori_loop(0, 4, one, 0)

            add(1 - slot, paired(y, near[a]))
            flying[lane, a] = copies.start(
                bufs[a].at[lane, :, 1 - slot], sums[a].at[lane], neighbour("y", near[a])
            )
            add(slot, y)

    def third(lane):
        for a in range(2):
            flying[lane, a].wait_recv()
            slot = slot_in_pair(y, near[a])

            def more(i, carry):
                sums[a][lane, i] = sums[a][lane, i] + bufs[a][lane, i, slot]
                return carry

            lax.fori_loop(0, 4, more, 0)
            if lane == 1:
                flying["x", a] = copies.start(sums[a].at[1], cross[a], neighbour("x", "A"))

    for stage, lane in CTX_ORDER:
        (first, second, third)[stage](lane)
        yield True
    for a in range(2):
        flying["x", a].wait_recv()

        def total(i, carry):
            own[a][i] = sums[a][0, i] + cross[a][i]
            return carry

        lax.fori_loop(0, 4, total, 0)
    yield True
    copies.finish()


def ctx_scratch(shapes, dtype):
    scratch = [
        pltpu.VMEM((*lead, *shape), dtype) for lead in ((2, 4, 2), (2, 4), (4,), (4,)) for shape in shapes
    ]
    return scratch + [pltpu.SemaphoreType.DMA((12,))] * 2


def column_halves(width):
    return [pl.ds(0, width // 2), pl.ds(width // 2, width // 2)]


def rows_gather_steps(x, out, copies):
    z = lax.axis_index("sp")
    near, far = ("A", "B"), ("B", "A")
    halves = column_halves(x.shape[1])
    first = [
        copies.start(x.at[:, halves[a]], out.at[z, :, halves[a]], neighbour("z", near[a]))
        for a in range(2)
    ]
    out[z] = x[...]
    yield True
    last = []
    for a in range(2):
        first[a].wait_recv()
        for place, _ in pair_slots(z, near[a]):
            block = out.at[place, :, halves[a]]
            last.append(copies.start(block, block, neighbour("z", far[a])))
    yield True
    for copy in last:
        copy.wait_recv()
    copies.finish()


def rows_reduce_steps(x, out, bufs, sums, copies):
    z = lax.axis_index("sp")
    near, far = ("A", "B"), ("B", "A")
    halves = column_halves(x.shape[2])
    flying = [
        [
            copies.start(x.at[src, :, halves[a]], bufs[a].at[dst], neighbour("z", far[a]))
            for src, dst in pair_slots(paired(z, far[a]), near[a])
        ]
        for a in range(2)
    ]
    yield True
    second = []
    for a in range(2):
        for copy in flying[a]:
            copy.wait_recv()
        slot = slot_in_pair(z, near[a])
        bufs[a][1 - slot] = bufs[a][1 - slot] + x[paired(z, near[a]), :, halves[a]]
        second.append(copies.start(bufs[a].at[1 - slot], sums[a], neighbour("z", near[a])))
        bufs[a][slot] = bufs[a][slot] + x[z, :, halves[a]]
    yield True
    for a in range(2):
        second[a].wait_recv()
        slot = slot_in_pair(z, near[a])
        out[:, halves[a]] = bufs[a][slot] + sums[a][...]
    yield True
    copies.finish()


def gather_head_kernel(x, w, rows_out, weights_out, *sems):
    z, xh, y = own_place()
    greet(along_z() + [neighbour("y", "A"), neighbour("y", "B"), neighbour("x", "A")])
    turns = Copies(*sems[:2])
    heads = w.shape[1] // HD // 4

    def columns(k, h):
        return pl.ds(pl.multiple_of(k * 4 * HD + h * HD, HD), HD)

    for d in (1, 2, 3):
        there = (z + d) % 4
        for k in range(heads):
            place = weights_out.at[z, xh, y, :, pl.ds(k * HD, HD)]
            turns.start(w.at[:, columns(k, there)], place, {"sp": there})
    rows = rows_gather_steps(x, rows_out, Copies(*sems[2:4]))
    next(rows)
    for k in range(heads):
        weights_out[z, xh, y, :, k * HD : (k + 1) * HD] = w[:, columns(k, z)]
    for copy in turns.started:
        copy.wait_recv()
    half = w.shape[0] // 2
    parts = [(weights_out, pl.ds(a * half, half)) for a in range(2)]
    run(ctx_gather_steps(parts, Copies(*sems[4:6])), rows)
    turns.finish()


def gather_head(x, w, collective_id):
    out_shape = [
        jax.ShapeDtypeStruct((4, *x.shape), x.dtype),
        jax.ShapeDtypeStruct((4, 2, 4, w.shape[0], w.shape[1] // 4), w.dtype),
    ]
    sems = [pltpu.SemaphoreType.DMA((n,)) for n in (9, 9, 5, 5, 12, 12)]
    return vmem_call(gather_head_kernel, out_shape, (x, w), sems, collective_id, "gather_head")


def project_kernel(x, w, cosine, sine, q, k, v):
    raw = jnp.dot(x[...], w[...], preferred_element_type=jnp.float32)
    for at, out in enumerate((q, k)):
        one = raw[:, at * HD : (at + 1) * HD]
        out[...] = (one * cosine[...] + pltpu.roll(one, HD // 2, 1) * sine[...]).astype(out.dtype)
    v[...] = raw[:, 2 * HD :].astype(v.dtype)


def project(x, w, cosine, sine):
    shape = jax.ShapeDtypeStruct((x.shape[0], HD), x.dtype)
    return vmem_call(project_kernel, [shape] * 3, (x, w, cosine, sine), [], None, "project_head")


def attend_steps(q, k, v, blocks, exact, probs, scores):
    rows = q.shape[1]
    span = 8 * rows
    first = lax.axis_index("ctx") * rows
    scale = HD ** (-0.5)
    at = 0

    def chunk(ref, c):
        return ref[c].reshape(span, HD)

    for block in range(4):
        for c in range(block + 1):
            part = over(q[block], chunk(k, c), (1, 1)) * scale
            if c == block:
                row = lax.broadcasted_iota(jnp.int32, part.shape, 0)
                col = lax.broadcasted_iota(jnp.int32, part.shape, 1)
                part = jnp.where(col <= row + first, part, MASKED)
            scores[:, c * span : (c + 1) * span] = part
        width = (block + 1) * span
        top = jnp.max(scores[:, :width], axis=1, keepdims=True)
        total = jnp.zeros_like(top)
        for c in range(block + 1):
            part = jnp.exp(scores[:, c * span : (c + 1) * span] - top)
            total = total + jnp.sum(part, axis=1, keepdims=True)
            scores[:, c * span : (c + 1) * span] = part
        scaled = 1.0 / total
        result = jnp.zeros((rows, HD), jnp.float32)
        for c in range(block + 1):
            low = (scores[:, c * span : (c + 1) * span] * scaled).astype(probs.dtype)
            probs[at] = low
            result = result + over(low, chunk(v, c), (1, 0))
            at += 1
        exact[block] = result
        blocks[block] = result.astype(blocks.dtype)
        yield True


ATTEND_ORDER = "KGGKGKGKGK" + "AGAGAGA"


def attention_kernel(parts, q, k, v, own, total, attended, keys, values, probs, exact, whole, *refs):
    scores, blocks, part, *wa_bufs = refs[:6]
    sems = refs[6:]
    z, xh, y = own_place()
    places = along_z() + [neighbour("y", "A"), neighbour("y", "B"), neighbour("x", "A")]
    greet(places + wa_places())
    keys[:, xh, y] = k[...]
    values[:, xh, y] = v[...]
    rows = pl.ds(0, k.shape[1])
    programs = {
        "K": ctx_gather_steps([(keys, rows), (values, rows)], Copies(*sems[0:2])),
        "G": gather_steps(parts, [own], [whole], Copies(*sems[2:4]), sems[4]),
        "A": attend_steps(q, keys, values, blocks, exact, probs, scores),
    }
    in_turn(ATTEND_ORDER, programs)
    turns = Copies(*sems[5:7])
    for d in (1, 2, 3):
        there = (z + d) % 4
        turns.start(blocks.at[there], attended.at[:, head_columns(z)], {"sp": there})
    attended[:, head_columns(z)] = blocks[z]
    run(programs["G"])
    for copy in turns.started:
        copy.wait_recv()
    turns.finish()
    width = attended.shape[1]
    step = D // 4
    for i in range(4):
        weights = whole[i].reshape(step, -1)[:, :width]
        part[:, i * step : (i + 1) * step] = over(attended[...], weights, (1, 1)).astype(part.dtype)
    run(sum_wa_steps(part, total, *wa_bufs, Copies(*sems[7:9])))


def attention(q, k, v, own, collective_id):
    rows, low = q.shape[1], q.dtype
    every = jax.ShapeDtypeStruct((4, 2, 4, rows, HD), low)
    out_shape = [
        jax.ShapeDtypeStruct((rows, D), low),
        jax.ShapeDtypeStruct((rows, 4 * HD), low),
        every,
        every,
        jax.ShapeDtypeStruct((10, rows, 8 * rows), low),
        jax.ShapeDtypeStruct(q.shape, jnp.float32),
        jax.ShapeDtypeStruct((4, 2, 4, *own.shape), low),
    ]
    scratch = [pltpu.VMEM((rows, 32 * rows), jnp.float32), pltpu.VMEM(q.shape, low)]
    scratch += [pltpu.VMEM((rows, D), low)] + [pltpu.VMEM((rows, D // 2), low)] * 3
    scratch += [pltpu.SemaphoreType.DMA((n,)) for n in (12, 12, 44, 44, 1, 3, 3, 3, 3)]
    return vmem_call(
        functools.partial(attention_kernel, row_parts([own])), out_shape, (q, k, v, own), scratch,
        collective_id, "attention",
    )


def attend_back_steps(q, k, v, probs, grad, exact, dq, dk, dv, dk_sum, dv_sum):
    rows = q.shape[1]
    span = 8 * rows
    scale = HD ** (-0.5)
    at = 0

    def chunk(ref, c):
        return ref[c].reshape(span, HD)

    for block in range(4):
        low_grad = grad[block]
        delta = jnp.sum(low_grad.astype(jnp.float32) * exact[block], axis=1, keepdims=True)
        total = jnp.zeros((rows, HD), jnp.float32)
        for c in range(block + 1):
            low = probs[at]
            back = over(low_grad, chunk(v, c), (1, 1))
            terms = (low.astype(jnp.float32) * (back - delta)).astype(q.dtype)
            total = total + over(terms, chunk(k, c), (1, 0))
            key_terms = over(terms, q[block], (0, 0))
            value_terms = over(low, low_grad, (0, 0))
            if c == block:
                dk_sum[c] = key_terms
                dv_sum[c] = value_terms
            else:
                dk_sum[c] = dk_sum[c] + key_terms
                dv_sum[c] = dv_sum[c] + value_terms
            at += 1
        dq[block] = (total * scale).astype(dq.dtype)
        yield True
    for c in range(4):
        dk[c] = (dk_sum[c] * scale).astype(dk.dtype).reshape(dk.shape[1:])
        dv[c] = dv_sum[c].astype(dv.dtype).reshape(dv.shape[1:])
    yield True


def project_back_steps(dq, dk, dv, cosine, sine, x, w, back, grad):
    low = back.dtype
    rows = dq.shape[1]
    terms = []
    for src in (dq, dk):
        one = src[...].reshape(4 * rows, HD).astype(jnp.float32)
        terms.append((one * cosine[...] - pltpu.roll(one, HD // 2, 1) * sine[...]).astype(low))
    terms = jnp.concatenate([*terms, dv[...].reshape(4 * rows, HD)], axis=1)
    step = D // 4
    for i in range(4):
        here = slice(i * step, (i + 1) * step)
        back[:, :, here] = over(terms, w[here], (1, 1)).astype(low).reshape(4, rows, step)
        grad[i] = over(x[:, here], terms, (0, 0)).astype(low).reshape(grad.shape[1:])
        yield True


BACK_ORDER = "AAAAACCCCCCC"


def attention_back_kernel(parts, count, *refs):
    attended_grad, q, keys, values, probs, exact, cosine, sine, x, w, heads, *refs = refs
    summed, refs = refs[:count], refs[count:]
    total, grad_out, gain_out, *refs = refs
    shares, refs = refs[:count], refs[count:]
    head_grad, dq, dk, dv, dk_sum, dv_sum, back, grad, mixed, *refs = refs
    z_bufs, z_sums, wa_bufs, gain_bufs = refs[0:2], refs[2:4], refs[4:7], refs[7:9]
    refs = refs[9:]
    (kv_bufs, kv_sums, kv_cross, kv_own), refs = (refs[2 * i : 2 * i + 2] for i in range(4)), refs[8:]
    kv_sems, refs = refs[:2], refs[2:]
    (bufs, sums, cross, own), refs = (refs[2 * i : 2 * i + 2] for i in range(4)), refs[8:]
    head_sems, refs = refs[:2], refs[2:]
    sems, refs = refs[:10], refs[10:]
    cube_bufs, cube_sems = refs[:-2], refs[-2:]
    z = lax.axis_index("sp")
    places = along_z() + [neighbour("y", "A"), neighbour("y", "B"), neighbour("x", "A")]
    greet(places + wa_places())
    turns = Copies(*sems[0:2])
    for d in (1, 2, 3):
        there = (z + d) % 4
        turns.start(attended_grad.at[:, head_columns(there)], head_grad.at[z], {"sp": there})
    head_grad[z] = attended_grad[:, head_columns(z)]
    rows = pl.ds(0, dq.shape[1])
    programs = {
        "R": reduce_steps(parts, summed, shares, cube_bufs, Copies(*cube_sems)),
        "A": attend_back_steps(
            q, keys, values, probs, head_grad, exact, dq, dk, dv, dk_sum, dv_sum
        ),
        "C": ctx_reduce_steps(
            [(dk, rows), (dv, rows)], kv_bufs, kv_sums, kv_cross, kv_own, Copies(*kv_sems)
        ),
    }
    in_turn("RR", programs)
    for copy in turns.started:
        copy.wait_recv()
    turns.finish()
    in_turn(BACK_ORDER, programs)
    run(programs["C"])
    run(project_back_steps(dq, *kv_own, cosine, sine, x, w, back, grad))
    half = grad.shape[3] // 2
    grad_parts = [(grad, pl.ds(a * half, half)) for a in range(2)]

    def sums_of_rows():
        yield from rows_reduce_steps(back, mixed, z_bufs, z_sums, Copies(*sems[2:4]))
        yield from sum_wa_steps(mixed, total, *wa_bufs, Copies(*sems[4:6]))

    def grads():
        yield from ctx_reduce_steps(grad_parts, bufs, sums, cross, own, Copies(*head_sems))
        turns = Copies(*sems[6:8])
        for d in (1, 2, 3):
            there = (z + d) % 4
            for a in range(2):
                turns.start(own[a].at[there], grad_out.at[z, grad_parts[a][1]], {"sp": there})
        for a in range(2):
            grad_out[z, a * half : (a + 1) * half] = own[a][z]
        yield True
        for copy in turns.started:
            copy.wait_recv()
        turns.finish()
        products = jnp.zeros(gain_out.shape, jnp.float32)
        for h in range(4):
            for k in range(grad_out.shape[2] // HD):
                ours = heads[:, (4 * k + h) * HD : (4 * k + h + 1) * HD].astype(jnp.float32)
                theirs = grad_out[h, :, k * HD : (k + 1) * HD].astype(jnp.float32)
                products = products + ours * theirs
        gain_out[...] = products
        copies = Copies(*sems[8:10])
        for place, buf in zip(wa_places(), gain_bufs):
            copy = copies.start(gain_out, buf, place)
            yield True
            copy.wait()
            gain_out[...] = gain_out[...] + buf[...]

    run(grads(), sums_of_rows(), programs["R"])


def attention_back(operands, summed, collective_id):
    attended_grad, q, keys, _, _, _, _, _, x, w, heads = operands
    rows, low = q.shape[1], q.dtype
    shard = heads.shape[0]
    parts = row_parts(summed)
    out_shape = [
        jax.ShapeDtypeStruct((rows, D), low),
        jax.ShapeDtypeStruct((4, shard, w.shape[1]), low),
        jax.ShapeDtypeStruct((shard, HD), jnp.float32),
    ]
    out_shape += [jax.ShapeDtypeStruct(a.shape[3:], jnp.float32) for a in summed]
    wide = (rows, D // 2)
    sums = pltpu.VMEM((4, 8 * rows, HD), jnp.float32)
    scratch = [pltpu.VMEM(a.shape, low) for a in (q, q, keys, keys)] + [sums, sums]
    scratch += [pltpu.VMEM((4, rows, D), low), pltpu.VMEM((4, 2, 4, shard, w.shape[1]), low)]
    scratch += [pltpu.VMEM((rows, D), low)]
    scratch += [pltpu.VMEM((2, *wide), low)] * 2 + [pltpu.VMEM(wide, low)] * 5
    scratch += [pltpu.VMEM((shard, HD), jnp.float32)] * 2
    scratch += ctx_scratch([(rows, HD)] * 2, low) + ctx_scratch([(shard // 2, w.shape[1])] * 2, low)
    scratch += [pltpu.SemaphoreType.DMA((n,)) for n in (3, 3, 5, 5, 3, 3, 6, 6, 2, 2)]
    scratch += reduce_scratch(summed, parts)
    return vmem_call(
        functools.partial(attention_back_kernel, parts, len(summed)), out_shape,
        (*operands, *summed), scratch, collective_id, "attention_back",
    )


SLOTS = 16
GROUP_ORDER = ((0, 1), (1, 0), (3, 0), (1, 1), (3, 1), (2, 0), (2, 1), (0, 0))
SENT_AHEAD = 4
PASSED_BEHIND = 2
FIRST_COMPLETE = 11


def token_places():
    z, xh, y = own_place()
    w = lax.axis_index("wa")
    return z, xh, y, w // 2, w % 2


def block_device(dz, dx, dy):
    z, xh, y, place, core = token_places()
    there_z, there_x, there_y = (z + dz) % 4, (xh + dx) % 2, (y + dy) % 4
    there = (place + dx) % 2
    where = {"sp": there_z, "ctx": 4 * there_x + there_y, "wa": 2 * there + core}
    return where, there_z * 8 + there_x * 4 + there_y


def greet_blocks(others):
    barrier = pltpu.get_barrier_semaphore()

    def one(i, carry):
        where, _ = block_device(i // 8, (i // 4) % 2, i % 4)
        pl.semaphore_signal(barrier, inc=1, device_id=where, device_id_type=MESH)
        return carry

    lax.fori_loop(1, 32, one, 0)
    others = wa_places() + others
    for place in others:
        pl.semaphore_signal(barrier, inc=1, device_id=place, device_id_type=MESH)
    pl.semaphore_wait(barrier, 31 + len(others))


def quarter_columns(place, core):
    quarter = D // 4
    return pl.ds(pl.multiple_of(core * 2 * quarter + place * quarter, quarter), quarter)


def dispatch_steps(ins, outs, out_sem, in_sem, own_sem, copies):
    count = len(ins)
    z, xh, y, place, core = token_places()
    beside, across = wa_places()
    me = z * 8 + xh * 4 + y
    columns = quarter_columns(place, core)
    here = pl.ds(pl.multiple_of(me * SLOTS, SLOTS), SLOTS)
    own = [
        pltpu.make_async_copy(ins[a].at[me], outs[a].at[:, here, columns], own_sem.at[a])
        for a in range(count)
    ]
    for copy in own:
        copy.start()
    items = [(a, dz, dx) for a in range(count) for dz, dx in GROUP_ORDER]
    passed, last = {}, []
    firsts = len(GROUP_ORDER)

    def forward(part, i):
        copy = copies.start(part, part, beside)
        last.append((i // firsts, copy))

    def send(i):
        a, dz, dx = items[i]

        def one(dy, carry):
            where, block = block_device(dz, dx, dy)
            pltpu.make_async_remote_copy(
                src_ref=ins[a].at[block], dst_ref=outs[a].at[:, here, columns],
                send_sem=out_sem.at[a], recv_sem=in_sem.at[a, dz * 2 + dx],
                device_id=where, device_id_type=MESH,
            ).start()
            return carry

        lax.fori_loop(1 if dz + dx == 0 else 0, 4, one, 0)

    def rows_of(dz, dx):
        first = ((z - dz + 4) % 4 * 8 + (xh + dx) % 2 * 4) * SLOTS
        return pl.ds(pl.multiple_of(first, 4 * SLOTS), 4 * SLOTS)

    def arrived(i):
        a, dz, dx = items[i]
        few = 3 if dz + dx == 0 else 4
        sample = outs[a].at[:, pl.ds(0, few * SLOTS), columns]
        pltpu.make_async_copy(sample, sample, in_sem.at[a, dz * 2 + dx]).wait()
        if dz + dx == 0:
            own[a].wait()
        part = outs[a].at[:, rows_of(dz, dx), quarter_columns((place + dx) % 2, core)]
        passed[i] = copies.start(part, part, across)
        forward(part, i)

    def from_across(i):
        a, dz, dx = items[i]
        passed[i].wait_recv()
        part = outs[a].at[:, rows_of(dz, dx), quarter_columns((place + dx + 1) % 2, core)]
        forward(part, i)

    for i in range(SENT_AHEAD):
        send(i)
    yield True
    for i in range(len(items) + PASSED_BEHIND):
        if i < len(items):
            arrived(i)
            if i + SENT_AHEAD < len(items):
                send(i + SENT_AHEAD)
        if i >= PASSED_BEHIND:
            from_across(i - PASSED_BEHIND)
        if i == FIRST_COMPLETE:
            for a, copy in last:
                if a == 0:
                    copy.wait_recv()
        yield True
    for a, copy in last:
        if a > 0:
            copy.wait_recv()
    copies.finish()
    for a in range(count):
        sample = ins[a].at[pl.ds(0, 31)]
        pltpu.make_async_copy(sample, sample, out_sem.at[a]).wait()
    yield True


def shared_step(width):
    return -(-width // HD) * HD


def shared_steps(x, g, weights, whole, first, part, back, gate_grad, up_grad, down_grad, sem):
    low = part.dtype
    width = gate_grad.shape[1]
    step = shared_step(width)
    gate, up, down = (slice(k * step, k * step + width) for k in range(3))
    load = pltpu.make_async_copy(whole.at[:, pl.ds(first, weights.shape[1])], weights, sem.at[0])
    load.start()
    yield True
    load.wait()
    pre = over(x[...], weights[:, gate], (1, 0))
    yield True
    lin = over(x[...], weights[:, up], (1, 0))
    yield True
    act, pre_grad, lin_grad = swish_parts(pre, lin, over(g[...], weights[:, down], (1, 0)))
    act, pre_grad, lin_grad = act.astype(low), pre_grad.astype(low), lin_grad.astype(low)
    yield True
    for at in range(0, D, 512):
        here = slice(at, at + 512)
        part[:, here] = over(act, weights[here, down], (1, 1)).astype(low)
        back[:, here] = (
            over(pre_grad, weights[here, gate], (1, 1)) + over(lin_grad, weights[here, up], (1, 1))
        ).astype(low)
        yield True
        down_grad[here] = over(g[:, here], act, (0, 0)).astype(low)
        gate_grad[here] = over(x[:, here], pre_grad, (0, 0)).astype(low)
        up_grad[here] = over(x[:, here], lin_grad, (0, 0)).astype(low)
        yield True


def expert_steps(rows, grads, hbm, held, part, back, kept, load_sem, finished):
    low = rows.dtype
    hidden = hbm[0].shape[1]
    loads = [
        pltpu.make_async_copy(src, dst, load_sem.at[k]) for k, (src, dst) in enumerate(zip(hbm, held))
    ]
    for load in loads:
        load.start()
    yield True
    for load in loads:
        load.wait()
    gate, up, down = held
    chunks = [slice(at, at + 512) for at in range(0, D, 512)]
    found = []
    for e in range(2):
        pre = over(rows[e], gate[e], (1, 1))
        yield True
        lin = over(rows[e], up[e], (1, 1))
        found.append((pre, lin))
        act = (pre * jax.nn.sigmoid(pre) * lin).astype(low)
        kept[0][e] = act
        yield True
        for here in chunks:
            ref, place = part(e, here)
            ref[place] = over(act, down[e, :, here], (1, 0)).astype(low)
            if here is chunks[-1]:
                finished(e, 0)
            yield True
    for e in range(2):
        _, pre_grad, lin_grad = swish_parts(*found[e], over(grads[e], down[e], (1, 1)))
        pre_grad, lin_grad = pre_grad.astype(low), lin_grad.astype(low)
        kept[1][e], kept[2][e] = pre_grad, lin_grad
        yield True
        for here in chunks:
            ref, place = back(e, here)
            ref[place] = (
                over(pre_grad, gate[e, :, here], (1, 0)) + over(lin_grad, up[e, :, here], (1, 0))
            ).astype(low)
            if here is chunks[-1]:
                finished(e, 1)
            yield True


def return_steps(held, outs, halves, quarters, out_sem, in_sem, own_sem, copies):
    z, xh, y, place, core = token_places()
    beside, across = wa_places()
    me = z * 8 + xh * 4 + y
    quarter = D // 4
    group = 4 * SLOTS
    mine = pl.ds(pl.multiple_of(core * 2 * quarter, 2 * quarter), 2 * quarter)
    theirs = pl.ds(pl.multiple_of((1 - core) * 2 * quarter, 2 * quarter), 2 * quarter)
    rows_each = halves[0].shape[1]
    items = [(e, a, dz, dx) for a in range(2) for e in range(2) for dz, dx in GROUP_ORDER]
    paired_up, passed, own = {}, {}, []

    def finished(e, a):
        rows = pl.ds((2 * a + e) * rows_each, rows_each)
        paired_up[e, a] = copies.start(held.at[rows, theirs], halves[a].at[e], beside)

    def rows_of(dz, dx):
        return pl.ds(pl.multiple_of(((z + dz) % 4 * 8 + (xh + dx) % 2 * 4) * SLOTS, group), group)

    def kept(dx):
        return pl.ds(pl.multiple_of((place + dx) % 2 * quarter, quarter), quarter)

    def given(dx):
        return pl.ds(pl.multiple_of((place + dx + 1) % 2 * quarter, quarter), quarter)

    def add_core(i):
        e, a, dz, dx = items[i]
        rows = rows_of(dz, dx)
        if i % 8 == 0:
            paired_up[e, a].wait_recv()
        first = (2 * a + e) * rows_each
        ours = held[pl.ds(pl.multiple_of(first + rows.start, group), group), mine]
        halves[a][e, rows] = halves[a][e, rows] + ours
        passed[i] = copies.start(
            halves[a].at[e, rows, given(dx)], quarters[a].at[e, rows], across
        )

    def add_across(i):
        e, a, dz, dx = items[i]
        rows = rows_of(dz, dx)
        passed[i].wait_recv()
        quarters[a][e, rows] = quarters[a][e, rows] + halves[a][e, rows, kept(dx)]
        if dz + dx == 0:
            part = pl.ds(pl.multiple_of(me * SLOTS, SLOTS), SLOTS)
            copy = pltpu.make_async_copy(
                quarters[a].at[e, part], outs[a].at[me, e], own_sem.at[2 * a + e]
            )
            copy.start()
            own.append(copy)

        def one(dy, carry):
            where, block = block_device(dz, dx, dy)
            part = pl.ds(pl.multiple_of(block * SLOTS, SLOTS), SLOTS)
            pltpu.make_async_remote_copy(
                src_ref=quarters[a].at[e, part], dst_ref=outs[a].at[me, e],
                send_sem=out_sem.at[a], recv_sem=in_sem.at[a],
                device_id=where, device_id_type=MESH,
            ).start()
            return carry

        lax.fori_loop(1 if dz + dx == 0 else 0, 4, one, 0)

    def steps():
        for i in range(len(items) + BEHIND):
            if i < len(items):
                add_core(i)
            if i >= BEHIND:
                add_across(i - BEHIND)
            yield True
        copies.finish()
        for copy in own:
            copy.wait()
        for a in range(2):
            sample = outs[a].at[pl.ds(0, 31)]
            pltpu.make_async_copy(sample, sample, in_sem.at[a]).wait()
            pltpu.make_async_copy(sample, sample, out_sem.at[a]).wait()

    return finished, steps()


def quarter_sum_steps(ins, outs, got, far, copies):
    w = lax.axis_index("wa")
    core, place = w % 2, w // 2
    beside, across = wa_places()
    half, quarter = D // 2, D // 4
    mine = pl.ds(pl.multiple_of(core * half, half), half)
    theirs = pl.ds(pl.multiple_of((1 - core) * half, half), half)
    kept = pl.ds(pl.multiple_of(place * quarter, quarter), quarter)
    given = pl.ds(pl.multiple_of((1 - place) * quarter, quarter), quarter)
    one = [copies.start(x.at[:, theirs], buf, beside) for x, buf in zip(ins, got)]
    yield True
    two = []
    for a, x in enumerate(ins):
        one[a].wait_recv()
        got[a][...] = got[a][...] + x[:, mine]
        two.append(copies.start(got[a].at[:, given], far[a], across))
    yield True
    for a, out in enumerate(outs):
        two[a].wait_recv()
        out[...] = got[a][:, kept] + far[a][...]
    copies.finish()
    yield True


BEHIND = 12
MLP_ORDER = (
    "XD" + "SD" * 12 + "RRW" + "XD" * 3 + "W" + "XD" * 3 + "WXTXTXTXTXTXTD"
    + "XTXTXTTXTXT" + "XTTXTTXRTTXRTTXRTT" + "TTRTTRTTRTTRTTRTTTTRR"
)


def mlp_kernel(count, *refs):
    ins, (x, g, whole), hbm, refs = refs[:2], refs[2:5], refs[5:8], refs[8:]
    arrived, back_rows, shared_sums, refs = refs[:2], refs[2:4], refs[4:6], refs[6:]
    shares, kept, refs = refs[:count], refs[count : count + 3], refs[count + 3 :]
    weights, shared_grads, refs = refs[0], refs[1 : 1 + count], refs[1 + count :]
    held, halves, quarters, refs = refs[:3], refs[3:5], refs[5:7], refs[7:]
    shared_parts, shared_got, shared_far, refs = refs[:2], refs[2:4], refs[4:6], refs[6:]
    shared_sem, load_sem, out_sem, in_sem, own_sem, own_back_sem, *refs = refs
    sum_sems, refs = refs[:2], refs[2:]
    pass_sems, back_out_sem, back_in_sem, back_sems, refs = refs[:2], refs[2], refs[3], refs[4:6], refs[6:]
    bufs, cube_sems = refs[:-2], refs[-2:]
    greet_blocks([neighbour("x", "A")])
    rows = arrived[0].shape[1]
    results = weights.at[:, pl.ds(0, D)]

    def place_of(a):
        def place(e, here):
            first = (2 * a + e) * rows
            return weights, (slice(first, first + rows), here)

        return place

    finished, returning = return_steps(
        results, back_rows, halves, quarters, back_out_sem, back_in_sem, own_back_sem,
        Copies(*back_sems),
    )
    shards = [grad.shape[0] // 32 for grad in shared_grads]
    cubes = [
        grad.reshape(4, 2, 4, shard, grad.shape[1]) for grad, shard in zip(shared_grads, shards)
    ]
    parts = row_parts(cubes)
    programs = {
        "D": dispatch_steps(ins, arrived, out_sem, in_sem, own_sem, Copies(*pass_sems)),
        "S": shared_steps(
            x, g, weights, whole, 0, *shared_parts, *shared_grads, shared_sem
        ),
        "W": quarter_sum_steps(
            shared_parts, shared_sums, shared_got, shared_far, Copies(*sum_sems)
        ),
        "X": expert_steps(
            *arrived, hbm, held, place_of(0), place_of(1), kept, load_sem, finished
        ),
        "T": returning,
        "R": reduce_steps(parts, cubes, shares, bufs, Copies(*cube_sems)),
    }
    in_turn(MLP_ORDER, programs)
    run(programs["T"], programs["R"])


def mlp(arrays, x, g, whole, width, expert_weights, collective_id):
    low = x.dtype
    rows, count = 32 * SLOTS, 3
    hidden = expert_weights[0].shape[1]
    at_experts = jax.ShapeDtypeStruct((2, rows, D), low)
    grad = jax.ShapeDtypeStruct((D, width), low)
    cube = jax.ShapeDtypeStruct((4, 2, 4, D // 32, width), low)
    out_shape = [at_experts] * 2
    out_shape += [jax.ShapeDtypeStruct((32, 2, SLOTS, D // 4), low)] * 2
    out_shape += [jax.ShapeDtypeStruct((x.shape[0], D // 4), low)] * 2
    out_shape += [jax.ShapeDtypeStruct((D // 32, width), jnp.float32)] * count
    out_shape += [jax.ShapeDtypeStruct((2, rows, hidden), low)] * 3
    scratch = [pltpu.VMEM((D, 3 * shared_step(width)), low)]
    scratch += [pltpu.VMEM(grad.shape, low)] * count
    scratch += [pltpu.VMEM(a.shape, low) for a in expert_weights]
    scratch += [pltpu.VMEM((2, rows, D // 2), low)] * 2 + [pltpu.VMEM((2, rows, D // 4), low)] * 2
    scratch += [pltpu.VMEM((x.shape[0], D // n), low) for n in (1, 1, 2, 2, 4, 4)]
    sems = [(1,), (3,), (2,), (2, 8), (2,), (4,), (4,), (4,), (48,), (48,), (2,), (2,), (36,), (36,)]
    scratch += [pltpu.SemaphoreType.DMA(n) for n in sems]
    scratch += reduce_scratch([cube] * count, row_parts([cube] * count))
    anywhere, vmem = pl.BlockSpec(memory_space=pl.ANY), pl.BlockSpec(memory_space=pltpu.VMEM)
    return pl.pallas_call(
        functools.partial(mlp_kernel, count),
        out_shape=out_shape,
        in_specs=[anywhere] * 2 + [vmem] * 2 + [anywhere] * 4,
        out_specs=[vmem] * 2 + [anywhere] * 2 + [vmem] * (len(out_shape) - 4),
        scratch_shapes=scratch,
        compiler_params=pltpu.CompilerParams(
            collective_id=collective_id, has_side_effects=True, vmem_limit_bytes=VMEM_LIMIT
        ),
        name="mlp",
    )(*arrays, x, g, whole, *expert_weights)


def combine_kernel(
    gate_high, gate_rest, pick, widen, g, returned, back, shared, shared_back,
    mixed, mixed_in, probs, half, got, far, send_sem, recv_sem,
):
    low = mixed.dtype
    _, _, _, place, core = token_places()
    beside, across = wa_places()
    greet([beside, across])
    copies = Copies(send_sem, recv_sem)
    mine, other = quarter_columns(place, core), quarter_columns(1 - place, core)
    routed = over(gate_high[...], returned[...], (1, 0)) + over(gate_rest[...], returned[...], (1, 0))
    mixed[:, mine] = (routed + shared[...].astype(jnp.float32)).astype(low)
    first, last = [], []

    def spread(out):
        part = out.at[:, mine]
        first.append(copies.start(part, part, across))
        last.append(copies.start(part, part, beside))

    spread(mixed)
    rows = over(pick[...], back[...], (1, 0))
    mixed_in[:, mine] = (rows + shared_back[...].astype(jnp.float32)).astype(low)
    spread(mixed_in)
    rest = jnp.where(pick[...] > 0, over(g[...], returned[...], (1, 1)), 0.0)
    total = jnp.zeros(probs.shape, jnp.float32)
    for _ in range(3):
        term = rest.astype(low)
        rest = rest - term.astype(jnp.float32)
        total = total + over(term, widen[...], (1, 1))
    half[...] = total
    one = copies.start(half, got, beside)
    for copy, out in zip(first, (mixed, mixed_in)):
        copy.wait_recv()
        part = out.at[:, other]
        last.append(copies.start(part, part, beside))
    one.wait()
    half[...] = half[...] + got[...]
    two = copies.start(half, far, across)
    two.wait_recv()
    probs[...] = half[...] + far[...]
    for copy in last:
        copy.wait_recv()
    for copy in copies.started:
        if copy is not one:
            copy.wait_send()


def combine(operands, collective_id):
    tokens, low = operands[0].shape[0], operands[0].dtype
    out_shape = [jax.ShapeDtypeStruct((tokens, D), low)] * 2
    out_shape += [jax.ShapeDtypeStruct((tokens, HD), jnp.float32)]
    scratch = [pltpu.VMEM((tokens, HD), jnp.float32)] * 3 + [pltpu.SemaphoreType.DMA((8,))] * 2
    return vmem_call(combine_kernel, out_shape, operands, scratch, collective_id, "combine")


def swish_parts(pre, lin, act_grads):
    sig = jax.nn.sigmoid(pre)
    swish = pre * sig
    slope = sig * (1.0 + pre * (1.0 - sig))
    return swish * lin, act_grads * lin * slope, act_grads * swish


def expert_grads_kernel(*refs):
    hbm, outs, held, results = refs[:5], refs[5:8], refs[8:13], refs[13]
    load_sem, out_sem = refs[14:]
    loads = [
        [
            pltpu.make_async_copy(src.at[e], dst.at[e], load_sem.at[e, k])
            for k, (src, dst) in enumerate(zip(hbm, held))
        ]
        for e in range(2)
    ]
    for load in loads[0] + loads[1]:
        load.start()
    rows, grads, act, pre_grad, lin_grad = held
    stores = []
    for e in range(2):
        for load in loads[e]:
            load.wait()
        for k, (left, right) in enumerate(((pre_grad, rows), (lin_grad, rows), (act, grads))):
            results[e, k] = over(left[e], right[e], (0, 0))
            store = pltpu.make_async_copy(results.at[e, k], outs[k].at[e], out_sem.at[e, k])
            store.start()
            stores.append(store)
    for store in stores:
        store.wait()


def expert_grads(*operands):
    shape = jax.ShapeDtypeStruct((2, operands[2].shape[2], D), jnp.float32)
    scratch = [pltpu.VMEM(x.shape, x.dtype) for x in operands]
    scratch += [pltpu.VMEM((2, 3, *shape.shape[1:]), jnp.float32)]
    scratch += [pltpu.SemaphoreType.DMA((2, 5)), pltpu.SemaphoreType.DMA((2, 3))]
    anywhere = pl.BlockSpec(memory_space=pl.ANY)
    return pl.pallas_call(
        expert_grads_kernel,
        out_shape=[shape] * 3,
        in_specs=[anywhere] * 5,
        out_specs=[anywhere] * 3,
        scratch_shapes=scratch,
        compiler_params=pltpu.CompilerParams(vmem_limit_bytes=VMEM_LIMIT),
        name="expert_grads",
    )(*operands)


def turned_gather(arrays, axis):
    widths = [a.shape[1] for a in arrays]
    whole = lax.all_gather(jnp.concatenate(arrays, axis=1), axis, axis=0, tiled=True)
    return jnp.split(whole, [sum(widths[:k]) for k in range(1, len(widths))], axis=1)


def rope_tables(positions):
    half_width = HD // 2
    inverse = 1.0 / ROPE_BASE ** (jnp.arange(half_width, dtype=jnp.float32) * 2.0 / HD)
    angles = positions[:, None] * inverse[None, :]
    cosine, sine = jnp.cos(angles), jnp.sin(angles)
    return jnp.concatenate([cosine, cosine], axis=1), jnp.concatenate([-sine, sine], axis=1)


def dot(left, right, over, dtype=jnp.float32, **kept):
    return lax.dot_general(
        left, right, ((over[:1], over[1:]), ((), ())), preferred_element_type=dtype, **kept
    )


def shards(
    tokens,
    cotangent,
    routes,
    attn_gain,
    query_weight,
    key_weight,
    value_weight,
    output_weight,
    mlp_gain,
    router_weight,
    shared_gate,
    shared_up,
    shared_down,
    expert_gate,
    expert_up,
    expert_down,
):
    low = jnp.bfloat16
    local_tokens = tokens.shape[0]
    head_cols = query_weight.shape[1]
    experts_all = router_weight.shape[1]
    groups = ("sp", "ctx")
    place, core = lax.axis_index("wa") // 2, lax.axis_index("wa") % 2
    quarter_at = core * (D // 2) + place * (D // 4)

    def quarter(x):
        return lax.dynamic_slice_in_dim(x, quarter_at, D // 4, 1)

    hidden_cols = shared_gate.shape[1]
    def beside(arrays):
        return jnp.concatenate(
            [jnp.pad(x, ((0, 0), (0, -x.shape[1] % HD))) for x in arrays], axis=1
        )

    gate_router = jnp.concatenate([shared_gate, router_weight], axis=1)
    up_gain = jnp.concatenate([shared_up, mlp_gain[:, None]], axis=1)
    shared_whole = lax.all_gather(
        beside((gate_router, up_gain, shared_down.T)), groups, axis=0, tiled=True
    )
    tokens_f = tokens.astype(jnp.float32)
    inv_one = lax.rsqrt(jnp.mean(tokens_f * tokens_f, axis=-1, keepdims=True) + EPSILON)
    unit_one = tokens_f * inv_one
    gain_one = attn_gain.astype(jnp.float32)[:, None]
    heads = jnp.concatenate([query_weight, key_weight, value_weight], axis=1)
    scaled = (gain_one * heads.astype(jnp.float32)).astype(low)
    head_rows, head_weights = gather_head(unit_one.astype(low), scaled, 1)
    head_rows, head_weights = head_rows.reshape(-1, D), head_weights.reshape(D, -1)
    blocks = jnp.arange(4, dtype=jnp.int32)[:, None] * 8 + lax.axis_index("ctx")
    positions = blocks * local_tokens + jnp.arange(local_tokens, dtype=jnp.int32)[None, :]
    cosine, sine = rope_tables(positions.reshape(-1).astype(jnp.float32))
    by_head = (4, local_tokens, HD)
    head_queries, own_keys, own_values = (
        x.reshape(by_head) for x in project(head_rows, head_weights, cosine, sine)
    )
    attn_out, attended, head_keys, head_values, probs, exact, whole = attention(
        head_queries, own_keys, own_values, output_weight.T, 2
    )
    attn_out = attn_out.astype(jnp.float32)
    turned = whole.reshape(D, head_cols)
    full_router = shared_whole[:, hidden_cols : hidden_cols + experts_all]
    gain_two = shared_whole[:, shared_step(hidden_cols) + hidden_cols].astype(jnp.float32)
    hidden_state = tokens_f + attn_out
    inv_two = lax.rsqrt(jnp.mean(hidden_state * hidden_state, axis=-1, keepdims=True) + EPSILON)
    unit_two = hidden_state * inv_two
    mlp_in = (unit_two * gain_two).astype(low)

    logits = dot(mlp_in, full_router, (1, 0))
    logit_exp = jnp.exp(logits - jnp.max(logits, axis=-1, keepdims=True))
    router_probs = logit_exp / jnp.sum(logit_exp, axis=-1, keepdims=True)
    experts = jnp.arange(experts_all, dtype=jnp.int32)
    chosen = jnp.zeros((local_tokens, experts_all), jnp.bool_)
    for j in range(TOP):
        chosen = chosen | (routes[:, j : j + 1] == experts[None, :])
    ids = jnp.arange(local_tokens, dtype=jnp.int32)
    before = (ids[None, :] < ids[:, None]).astype(low)
    rank = dot(before, chosen.astype(low), (1, 0))
    slot_of = jnp.where(chosen, rank, -1.0).astype(low)
    slot_ids = jnp.arange(experts_all * SLOTS, dtype=jnp.int32)
    widen = (experts[:, None] == slot_ids[None, :] // SLOTS).astype(low)
    taken = dot(slot_of, widen, (1, 0)) == (slot_ids % SLOTS).astype(jnp.float32)[None, :]
    probs_high = router_probs.astype(low)
    probs_rest = (router_probs - probs_high.astype(jnp.float32)).astype(low)
    pick = taken.astype(low)
    gate_high = jnp.where(taken, dot(probs_high, widen, (1, 0)), 0.0).astype(low)
    gate_rest = jnp.where(taken, dot(probs_rest, widen, (1, 0)), 0.0).astype(low)
    grad_quarter = quarter(cotangent)
    send_rows = dot(pick, quarter(mlp_in), (0, 0)).astype(low)
    send_grads = (
        dot(gate_high, grad_quarter, (0, 0)) + dot(gate_rest, grad_quarter, (0, 0))
    ).astype(low)
    by_owner = (32, 2, SLOTS, D // 4)
    expert_weights = (expert_gate.transpose(0, 2, 1), expert_up.transpose(0, 2, 1), expert_down)
    (
        rows_in,
        grads_in,
        returned,
        rows_back,
        shared_part,
        shared_in_part,
        gate_share,
        up_share,
        down_share,
        *kept,
    ) = mlp(
        (send_rows.reshape(by_owner), send_grads.reshape(by_owner)),
        mlp_in,
        cotangent,
        shared_whole,
        hidden_cols,
        expert_weights,
        5,
    )
    gate_grad_turned, up_grad_turned, expert_down_grad = expert_grads(rows_in, grads_in, *kept)
    returned, rows_back = returned.reshape(-1, D // 4), rows_back.reshape(-1, D // 4)

    widen_all = jnp.pad(widen, ((0, HD - experts_all), (0, 0)))
    mixed, mixed_in, prob_grads = combine(
        (
            gate_high,
            gate_rest,
            pick,
            widen_all,
            grad_quarter,
            returned,
            rows_back,
            shared_part,
            shared_in_part,
        ),
        7,
    )
    block_out = (hidden_state + mixed.astype(jnp.float32)).astype(low)
    prob_grads = prob_grads[:, :experts_all]
    logit_grads = router_probs * (
        prob_grads - jnp.sum(router_probs * prob_grads, axis=-1, keepdims=True)
    )
    router_in_grad = dot(
        logit_grads, full_router.astype(jnp.float32), (1, 1), precision=PRECISE
    )
    mlp_in_grad = router_in_grad + mixed_in.astype(jnp.float32)
    gain_two_grad = jnp.sum(mlp_in_grad * unit_two, axis=0)
    scaled_two = mlp_in_grad * gain_two
    hidden_grad = cotangent.astype(jnp.float32) + inv_two * (
        scaled_two - unit_two * jnp.mean(scaled_two * unit_two, axis=-1, keepdims=True)
    )
    out_grad = hidden_grad.astype(low)
    router_grad = dot(mlp_in, logit_grads.astype(low), (0, 0))

    attended_grad = dot(out_grad, turned, (1, 0)).astype(low)
    def by_shard(x):
        return x.astype(low).reshape(4, 2, 4, x.shape[0] // 32, x.shape[1])

    small_grads = jnp.concatenate([router_grad, gain_two_grad[:, None]], axis=1)
    small_grads = jnp.pad(small_grads, ((0, 0), (0, HD - small_grads.shape[1])))
    summed = [by_shard(dot(out_grad, attended, (0, 0))), by_shard(small_grads)]
    scaled_one, head_shares, gain_terms, output_share, small_share = attention_back(
        (
            attended_grad,
            head_queries,
            head_keys,
            head_values,
            probs,
            exact,
            cosine,
            sine,
            head_rows,
            head_weights,
            heads,
        ),
        summed,
        9,
    )
    scaled_one = scaled_one.astype(jnp.float32)
    tokens_grad = (
        hidden_grad
        + inv_one
        * (scaled_one - unit_one * jnp.mean(scaled_one * unit_one, axis=-1, keepdims=True))
    ).astype(low)
    head_shares = head_shares.astype(jnp.float32) * gain_one
    query_share, key_share, value_share = (
        head_shares[..., k * HD : (k + 1) * HD].swapaxes(0, 1).reshape(-1, head_cols)
        for k in range(3)
    )
    return (
        block_out,
        tokens_grad,
        jnp.sum(gain_terms, axis=1),
        query_share,
        key_share,
        value_share,
        output_share.T,
        small_share[:, experts_all],
        small_share[:, :experts_all],
        gate_share,
        up_share,
        down_share.T,
        gate_grad_turned.transpose(0, 2, 1),
        up_grad_turned.transpose(0, 2, 1),
        expert_down_grad,
    )


def solution(mesh):
    placed = (
        P(("sp", "ctx"), None),
        P(("sp", "ctx"), None),
        P(("sp", "ctx"), None),
        P(("sp", "ctx")),
        P(("sp", "ctx"), "wa"),
        P(("sp", "ctx"), "wa"),
        P(("sp", "ctx"), "wa"),
        P("wa", ("sp", "ctx")),
        P(("sp", "ctx")),
        P(("sp", "ctx"), None),
        P(("sp", "ctx"), "wa"),
        P(("sp", "ctx"), "wa"),
        P("wa", ("sp", "ctx")),
        P(("sp", "ctx"), None, "wa"),
        P(("sp", "ctx"), None, "wa"),
        P(("sp", "ctx"), "wa", None),
    )
    return jax.shard_map(
        shards,
        mesh=mesh,
        in_specs=placed,
        out_specs=(
            P(("sp", "ctx"), None),
            P(("sp", "ctx"), None),
            P(("sp", "ctx")),
            P(("sp", "ctx"), "wa"),
            P(("sp", "ctx"), "wa"),
            P(("sp", "ctx"), "wa"),
            P("wa", ("sp", "ctx")),
            P(("sp", "ctx")),
            P(("sp", "ctx"), None),
            P(("sp", "ctx"), "wa"),
            P(("sp", "ctx"), "wa"),
            P("wa", ("sp", "ctx")),
            P(("sp", "ctx"), None, "wa"),
            P(("sp", "ctx"), None, "wa"),
            P(("sp", "ctx"), "wa", None),
        ),
        check_vma=False,
    )
```
